32 devices in a mesh: phase: 2 (over x), dp: 16 (over z, y, core).
Axes of the slice: x: 2, y: 2, z: 4, core: 2. Of those that a mesh axis runs over, the one named last changes fastest.
Arguments:
- hidden_in: bfloat16 [16384, 768], P('dp'), may hold values from -6 to 6
- out_grad: bfloat16 [16384, 768], P('dp'), may hold values from -6 to 6
- qkv_weight: bfloat16 [2, 768, 2304], P('phase'), may hold values from -0.3125 to 0.3125
- out_weight: bfloat16 [2, 768, 768], P('phase'), may hold values from -0.625 to 0.625
- rel_table: float32 [2, 256, 12], P('phase'), may hold values from -4 to 4
- norm1_gain: float32 [2, 768], P('phase'), may hold values from 0.25 to 1.75
- norm1_bias: float32 [2, 768], P('phase'), may hold values from -1.5 to 1.5
- up_weight: bfloat16 [2, 768, 3072], P('phase'), may hold values from -0.21875 to 0.21875
- down_weight: bfloat16 [2, 3072, 768], P('phase'), may hold values from -0.15625 to 0.15625
- norm2_gain: float32 [2, 768], P('phase'), may hold values from 0.25 to 1.75
- norm2_bias: float32 [2, 768], P('phase'), may hold values from -1.5 to 1.5
- seg_ids: int32 [16384], P('dp'), may hold values from 0 to 3, as said below
- pad_mask: int32 [16384], P('dp'), may hold values from 0 to 1, as said below
- rel_buckets: int32 [1023], replicated, may hold values from 0 to 255
Outputs:
- layer_out: bfloat16 [2, 16384, 768], P('phase', 'dp')
- input_grad: bfloat16 [2, 16384, 768], P('phase', 'dp')
- qkv_grad: float32 [2, 768, 2304], P('phase', 'dp')
- out_proj_grad: float32 [2, 768, 768], P('phase', 'dp')
- table_grad: float32 [2, 256, 12], P('phase', 'dp')
- norm1_gain_grad: float32 [2, 768], P('phase', 'dp')
- norm1_bias_grad: float32 [2, 768], P('phase', 'dp')
- up_grad: float32 [2, 768, 3072], P('phase', 'dp')
- down_grad: float32 [2, 3072, 768], P('phase', 'dp')
- norm2_gain_grad: float32 [2, 768], P('phase', 'dp')
- norm2_bias_grad: float32 [2, 768], P('phase', 'dp')
The draws below stay inside these ranges and needn't reach their ends.
Inputs may be any that keep to these rules, and one draw needn't show every extreme that they name: `seg_ids`: in each aligned block of 512 slots, either every slot has number 0 (one sequence; exactly a quarter of the blocks) or slot i of the block has number i // 128. `pad_mask`: the used slots of a sequence are its first ones: at least 256 of a whole-block sequence, at least 32 of a short one.
All inputs are finite; a program needn't handle non-finite values.
Results may differ from the reference program's by a relative error of at most 0.04.
Values may be sent and summed in bfloat16 or wider, within the bound.
No kernel may reach another device: no remote copies, remote signals or barrier semaphores. Data moves between devices by JAX's collectives and lax.ppermute only.
A program may use at most 512 MiB of HBM per device.

```python
import jax
import jax.numpy as jnp
from jax import lax

D = 768
HEADS = 12
FF = 3072
BUCKETS = 256
BLOCK = 512
PIECE = 128
TOKENS = 16384


def block_layout(key):
    block_count = TOKENS // BLOCK
    piece_count = BLOCK // PIECE
    shuffled = jax.random.permutation(jax.random.fold_in(key, 11), block_count)
    single = shuffled < block_count // 4
    long_length = jax.random.randint(jax.random.fold_in(key, 12), (block_count,), BLOCK // 2, BLOCK + 1)
    short_length = jax.random.randint(jax.random.fold_in(key, 13), (block_count, piece_count), PIECE // 4, PIECE + 1)
    slots = jnp.arange(BLOCK, dtype=jnp.int32)
    piece_of = slots // PIECE
    segment = jnp.where(single[:, None], 0, piece_of[None, :])
    limit = jnp.where(single[:, None], long_length[:, None], short_length[:, piece_of])
    within = jnp.where(single[:, None], slots[None, :], (slots % PIECE)[None, :])
    padding = (within < limit).astype(jnp.int32)
    return (segment.reshape(-1).astype(jnp.int32), padding.reshape(-1))


def draw_seg_ids(key, part):
    return block_layout(key)[0]


def draw_pad_mask(key, part):
    return block_layout(key)[1]


def place_ends(drawn, own_key, least, high):
    index_at = [jax.random.randint(jax.random.fold_in(own_key, axis), (), 0, length) for axis, length in enumerate(drawn.shape)]
    longest = drawn.shape.index(max(drawn.shape))
    next_to = index_at[:longest] + [(index_at[longest] + 1) % drawn.shape[longest]] + index_at[longest + 1:]
    return drawn.at[tuple(index_at)].set(least).at[tuple(next_to)].set(high)


def level_of(own_key, shape, shards, smallest, largest):
    level, own = 1.0, jax.random.fold_in(own_key, 6)
    for position, parts in shards:
        steps = jnp.exp(jax.random.uniform(jax.random.fold_in(own, position), (parts,), jnp.float32, smallest / len(shards), largest / len(shards)))
        level = level * jnp.repeat(steps, shape[position] // parts).reshape([-1 if axis == position else 1 for axis in range(len(shape))])
    return level


def bell_draw(rng, shape, spread, most, split=(), held_as=jnp.bfloat16):
    values = spread * jax.random.normal(rng, shape, jnp.float32)
    if split:
        values = values * level_of(rng, shape, split, -0.22, 0.18)
    return jnp.clip(values, -most, most).astype(held_as)


def setup_inputs(seed: int = 0) -> dict:
    arg_keys = jax.random.split(jax.random.key(seed), 15)
    return {
        "hidden_in": bell_draw(arg_keys[0], (TOKENS, D), 1.0, 6.0, ((0, 16),)),
        "out_grad": bell_draw(arg_keys[1], (TOKENS, D), 1.0, 6.0, ((0, 16),)),
        "qkv_weight": bell_draw(arg_keys[2], (2, D, 3 * D), (D // 2) ** -0.5, 0.3125, ((0, 2),)),
        "out_weight": bell_draw(arg_keys[3], (2, D, D), (D // 8) ** -0.5, 0.625, ((0, 2),)),
        "rel_table": bell_draw(arg_keys[4], (2, BUCKETS, HEADS), 1.0, 4.0, ((0, 2),), jnp.float32),
        "norm1_gain": jnp.clip(1.0 + 0.15 * jax.random.normal(arg_keys[5], (2, D), jnp.float32), 0.25, 1.75),
        "norm1_bias": bell_draw(arg_keys[6], (2, D), 0.3, 1.5, ((0, 2),), jnp.float32),
        "up_weight": bell_draw(arg_keys[7], (2, D, FF), D ** -0.5, 0.21875, ((0, 2),)),
        "down_weight": bell_draw(arg_keys[8], (2, FF, D), (FF // 2) ** -0.5, 0.15625, ((0, 2),)),
        "norm2_gain": jnp.clip(1.0 + 0.15 * jax.random.normal(arg_keys[9], (2, D), jnp.float32), 0.25, 1.75),
        "norm2_bias": bell_draw(arg_keys[10], (2, D), 0.3, 1.5, ((0, 2),), jnp.float32),
        "seg_ids": draw_seg_ids(jax.random.fold_in(arg_keys[14], 71), 0),
        "pad_mask": draw_pad_mask(jax.random.fold_in(arg_keys[14], 71), 0),
        "rel_buckets": place_ends(jax.random.randint(arg_keys[13], (2 * BLOCK - 1,), 0, BUCKETS), jax.random.fold_in(arg_keys[13], 1), 0, BUCKETS - 1).astype(jnp.int32),
    }


norm_eps = 1e-05
mask_fill = -1000000000.0
score_scale = 0.125
highest = lax.Precision.HIGHEST

@jax.custom_vjp
def low(v):
    return lax.optimization_barrier(v.astype(jnp.bfloat16)).astype(jnp.float32)

@jax.custom_vjp
def low_back(v):
    return v

def low_keep(v):
    return (low(v), None)

def low_pass(kept, grad):
    return (grad,)

def back_keep(v):
    return (v, None)

def back_low(kept, grad):
    return (low(grad),)
low.defvjp(low_keep, low_pass)
low_back.defvjp(back_keep, back_low)

def layer_norm(residual, norm_gain, norm_shift):
    row_mean = lax.optimization_barrier(jnp.mean(residual, -1, keepdims=True))
    centred = residual - row_mean
    inv_scale = lax.rsqrt(lax.optimization_barrier(jnp.mean(centred * centred, -1, keepdims=True)) + norm_eps)
    return centred * inv_scale * norm_gain + norm_shift

def encoder_layer(inputs, weights, segment_row, padding_row, bucket_row):
    in_matrix, out_matrix, bias_table, first_gain, first_shift, up_matrix, down_matrix, second_gain, second_shift = weights
    row_count = inputs.shape[0]
    model_width = inputs.shape[1]
    head_count = bias_table.shape[1]
    head_size = model_width // head_count
    inputs = low_back(inputs)
    projected = low(low_back(jnp.dot(inputs, in_matrix, precision=highest)))
    sections = projected.reshape(row_count, 3, head_count, head_size).transpose(1, 2, 0, 3)
    positions = jnp.arange(row_count, dtype=jnp.int32)
    offsets = positions[None, :] - positions[:, None] + row_count - 1
    pair_bias = jnp.take(bias_table[bucket_row], offsets, axis=0).transpose(2, 0, 1)
    scores = jnp.einsum('hqd,hkd->hqk', sections[0], sections[1], precision=highest) * score_scale + pair_bias
    scores = low_back(scores)
    allowed = (segment_row[:, None] == segment_row[None, :]) & (padding_row[None, :] == 1) | (positions[:, None] == positions[None, :])
    attention = low(jax.nn.softmax(jnp.where(allowed[None], scores, mask_fill), axis=-1))
    blended = jnp.einsum('hqk,hkd->hqd', attention, sections[2], precision=highest)
    context = low(low_back(blended.transpose(1, 0, 2).reshape(row_count, model_width)))
    residual = inputs + low_back(jnp.dot(context, out_matrix, precision=highest))
    normed = layer_norm(residual, first_gain, first_shift)
    hidden = low_back(jnp.dot(low(normed), up_matrix, precision=highest))
    active = low(jax.nn.gelu(hidden, approximate=False))
    outer_sum = normed + low_back(jnp.dot(active, down_matrix, precision=highest))
    return low(layer_norm(outer_sum, second_gain, second_shift))

def reference(hidden_in, out_grad, qkv_weight, out_weight, rel_table, norm1_gain, norm1_bias, up_weight, down_weight, norm2_gain, norm2_bias, seg_ids, pad_mask, rel_buckets):
    params = (qkv_weight.astype(jnp.float32), out_weight.astype(jnp.float32), rel_table, norm1_gain, norm1_bias, up_weight.astype(jnp.float32), down_weight.astype(jnp.float32), norm2_gain, norm2_bias)
    blocks = hidden_in.shape[0] // BLOCK
    inputs_all = hidden_in.astype(jnp.float32).reshape(blocks, BLOCK, D)
    cotangents = out_grad.astype(jnp.float32).reshape(blocks, BLOCK, D)
    segments = seg_ids.reshape(blocks, BLOCK)
    paddings = pad_mask.reshape(blocks, BLOCK)

    def both_layers(layer_in, middle_in, weights, segment_row, padding_row):
        first = encoder_layer(layer_in, jax.tree.map(lambda leaf_array: leaf_array[0], weights), segment_row, padding_row, rel_buckets)
        second = encoder_layer(first + middle_in, jax.tree.map(lambda leaf_array: leaf_array[1], weights), segment_row, padding_row, rel_buckets)
        return (first, second)

    def visit(totals, block_items):
        layer_in, cotangent, segment_row, padding_row = block_items
        middle_in = jnp.zeros_like(layer_in)
        outputs, pullback = jax.vjp(lambda first_in, spare_in, weights: both_layers(first_in, spare_in, weights, segment_row, padding_row), layer_in, middle_in, params)
        grad_first, grad_middle, grad_params = pullback((jnp.zeros_like(layer_in), cotangent))
        totals = jax.tree.map(jnp.add, totals, grad_params)
        return (totals, (outputs[0], outputs[1], grad_first, grad_middle))
    initial = jax.tree.map(jnp.zeros_like, params)
    sums, (first_out, second_out, grad_first, grad_middle) = lax.scan(visit, initial, (inputs_all, cotangents, segments, paddings))
    total_rows = blocks * BLOCK
    layer_out = jnp.stack([first_out.reshape(total_rows, D), second_out.reshape(total_rows, D)]).astype(jnp.bfloat16)
    input_grad = jnp.stack([grad_first.reshape(total_rows, D), grad_middle.reshape(total_rows, D)]).astype(jnp.bfloat16)
    return (layer_out, input_grad, sums[0], sums[1], sums[2], sums[3], sums[4], sums[5], sums[6], sums[7], sums[8])
```

```python
import functools

import jax
import jax.numpy as jnp
from jax import lax
from jax.experimental import pallas as pl
from jax.experimental.pallas import tpu as pltpu
from jax.sharding import PartitionSpec as P

BLOCK = 512
MICRO = 2
TILE = 128
LANES = 128
CHUNK = 512
SPAN = 2 * BLOCK
VMEM_BYTES = 58 * 1024 * 1024
SMALL_VMEM_BYTES = 20 * 1024 * 1024

norm_eps = 1e-05
mask_fill = -1000000000.0
score_scale = 0.125
inv_root_two = 0.7071067811865476
inv_root_tau = 0.3989422804014327
log2_e = 1.4426950408889634
highest = lax.Precision.HIGHEST

F32 = jnp.float32
BF16 = jnp.bfloat16
ANY = pl.BlockSpec(memory_space=pl.ANY)
VMEM = pl.BlockSpec(memory_space=pltpu.VMEM)
QUICK = pl.CostEstimate(flops=1, bytes_accessed=1, transcendentals=0)
SMEM = pl.BlockSpec(memory_space=pltpu.SMEM)


def dot_nn(a, b):
    return lax.dot_general(a, b, (((1,), (0,)), ((), ())), preferred_element_type=F32)


def dot_nt(a, b):
    return lax.dot_general(a, b, (((1,), (1,)), ((), ())), preferred_element_type=F32)


def dot_tn(a, b):
    return lax.dot_general(a, b, (((0,), (0,)), ((), ())), preferred_element_type=F32)


def row_mean(rows):
    return jnp.sum(rows, -1, keepdims=True) * (1.0 / rows.shape[-1])


def normal_parts(residual):
    centred = residual - row_mean(residual)
    inv_scale = lax.rsqrt(row_mean(centred * centred) + norm_eps)
    return centred * inv_scale, inv_scale


def norm_backward(grad_rows, normal_form, inv_scale):
    first = row_mean(grad_rows)
    second = row_mean(grad_rows * normal_form)
    return inv_scale * (grad_rows - first - normal_form * second)


def gelu_parts(hidden):
    size = jnp.abs(hidden)
    bell = jnp.exp2(hidden * hidden * (-0.5 * log2_e))
    t = pl.reciprocal(1.0 + (0.3275911 * inv_root_two) * size, approx=True)
    tail = 0.5 * 1.061405429
    for factor in (-1.453152027, 1.421413741, -0.284496736, 0.254829592):
        tail = tail * t + 0.5 * factor
    tail = tail * t * bell
    share = jnp.where(hidden < 0.0, tail, 1.0 - tail)
    return hidden * share, share + hidden * bell * inv_root_tau


def half_mask(which, shape):
    lane = lax.broadcasted_iota(jnp.int32, shape, 1)
    return (lane < LANES // 2) if which == 0 else (lane >= LANES // 2)


class Copies:
    def __init__(self, sems):
        self.sems = sems
        self.used = 0
        self.stores = []

    def take(self, count=1):
        self.used += count
        return self.used - count

    def load(self, source, target):
        copy = pltpu.make_async_copy(source, target, self.sems.at[self.take()])
        copy.start()
        return copy

    def store(self, source, target, when=True):
        if when:
            self.stores.append(self.load(source, target))

    def finish(self):
        for copy in self.stores:
            copy.wait()


def bias_kernel(buckets_ref, table_ref, seg_ref, pad_ref, bias_ref, shut_ref, values_v):
    step = pl.program_id(0)

    @pl.when(step == 0)
    def _():
        span = buckets_ref.shape[1]
        bucket_ids = lax.broadcasted_iota(jnp.int32, (table_ref.shape[1], span), 0)
        hot = (bucket_ids == buckets_ref[...]).astype(F32)
        values = lax.dot_general(
            table_ref[0], hot, (((0,), (0,)), ((), ())), precision=highest, preferred_element_type=F32
        )
        values_v[:, :span] = values
        values_v[:, span:] = jnp.zeros((values.shape[0], SPAN - span), F32)
        for block in range(MICRO):
            at = slice(block * BLOCK, (block + 1) * BLOCK)
            for tile in range(BLOCK // TILE):
                own = seg_ref[:, block * BLOCK + tile * TILE : block * BLOCK + tile * TILE + 1]
                open_pairs = (seg_ref[:, at] == own) & (pad_ref[:, at] == 1)
                shut_ref[block, tile : tile + 1, :] = jnp.where(open_pairs, 0.0, mask_fill)

    for i in range(bias_ref.shape[0]):
        wide = jnp.broadcast_to(values_v[pl.ds(bias_ref.shape[0] * step + i, 1), :], (TILE, SPAN))
        bias_ref[i] = pltpu.roll(wide, 1, 1, stride=1, stride_axis=0)


KEPT = (
    "xin", "qkv", "weights", "ctx", "form1", "scale1", "low1", "slope", "act", "form2", "scale2", "out",
    "outer_low", "hidden_low", "residual_low", "sums", "residual", "projected", "offsets", "input_grad",
)
INS = (
    "phase", "hidden_in", "received", "out_grad", "bias", "shut", "gain1", "shift1", "gain2", "shift2",
    "wqkv", "wout", "wup", "wdown",
)


class Layer:
    def __init__(self, refs):
        self.__dict__.update(refs)
        self.copies = Copies(self.sems)
        self.width = self.x_v.shape[1]
        self.inner = self.act_v.shape[1]
        self.pairs = self.width // LANES
        self.stages = self.inner // (2 * CHUNK)
        self.pair_sems = self.copies.take(self.pairs)
        self.chunk_sems = [self.copies.take(self.stages) for _ in range(3)]

    def lanes_of(self, pair, part):
        return pl.ds(pl.multiple_of(part * self.width + pair * LANES, LANES), LANES)

    def chunk(self, c):
        return pl.ds(pl.multiple_of(c * CHUNK, CHUNK), CHUNK)

    def stage(self, i):
        return pl.ds(pl.multiple_of(i * 2 * CHUNK, 2 * CHUNK), 2 * CHUNK)


    def rows(self, block):
        return pl.ds(block * BLOCK, BLOCK)

    def forward(self, block, keep):
        copies = self.copies
        rows = self.rows(block)
        load_x = copies.load(self.hidden_in.at[rows] if keep else self.received, self.x_v)
        width = self.width
        loads = [
            copies.load(self.wqkv.at[0, :, pl.ds(c, width)], self.wqkv_v.at[:, pl.ds(c, width)])
            for c in range(0, 3 * width, width)
        ]
        load_x.wait()

        def load_bias(pair):
            heads = pl.ds(2 * pair, 2)
            return pltpu.make_async_copy(self.bias.at[heads], self.bias_v.at[heads], self.sems.at[self.pair_sems + pair])

        for i, c in enumerate(range(0, 3 * width, width)):
            loads[i].wait()
            if i == 2:
                for pair in range(self.pairs):
                    load_bias(pair).start()
            self.qkv_v[:, c : c + width] = dot_nn(self.x_v[...], self.wqkv_v[:, c : c + width]).astype(BF16)
        copies.store(self.x_v, self.xin.at[rows])
        copies.store(self.qkv_v, self.qkv.at[rows], keep)
        weights_sem = self.sems.at[copies.take()]
        later_loads = [
            pltpu.make_async_copy(source.at[0], target, self.sems.at[copies.take()])
            for source, target in ((self.wout, self.wout_v), (self.wup, self.wup_v), (self.wdown, self.wdown_v))
        ]

        def own(pair, part, which):
            both = self.qkv_v[:, self.lanes_of(pair, part)]
            return jnp.where(half_mask(which, both.shape), both, jnp.zeros_like(both))

        def scores(pair, which):
            q_rows = self.qkv_v[:, self.lanes_of(pair, 0)] * jnp.asarray(score_scale, BF16)
            self.square_v[which] = dot_nt(q_rows, own(pair, 1, which))

        def bias_part(head, which):
            for r in range(0, BLOCK, 64):
                at = BLOCK - r // TILE * TILE
                own_tile = r // TILE * TILE
                bias_rows = self.bias_v[head, r % TILE : r % TILE + 64, at : at + BLOCK]
                shut = bias_rows + self.shut[block, r // TILE : r // TILE + 1, :]
                row_id = lax.broadcasted_iota(jnp.int32, (64, TILE), 0) + r % TILE
                diagonal = row_id == lax.broadcasted_iota(jnp.int32, (64, TILE), 1)
                shut = jnp.concatenate(
                    [
                        jnp.where(diagonal, bias_rows[:, c : c + TILE], shut[:, c : c + TILE])
                        if c == own_tile
                        else shut[:, c : c + TILE]
                        for c in range(0, BLOCK, TILE)
                    ],
                    1,
                )
                logits = self.square_v[which, r : r + 64, :] + shut
                self.square_v[which, r : r + 64, :] = logits
                self.top_v[which, r : r + 64, :] = jnp.max(logits, -1, keepdims=True)

        def weigh_part(head, which):
            for r in range(0, BLOCK, 64):
                tile = slice(r, r + 64)
                raised = jnp.exp(self.square_v[which, tile, :] - self.top_v[which, tile, :])
                share = pl.reciprocal(jnp.sum(raised, -1, keepdims=True), approx=True)
                self.weights_v[head, tile, :] = (raised * share).astype(BF16)

        def blend(pair, which):
            return dot_nn(self.weights_v[2 * pair + which], own(pair, 2, which))

        scores(0, 0)

        def head_pair(pair, carry):
            load_bias(pair).wait()

            @pl.when(pair == 0)
            def _():
                for load in later_loads:
                    load.start()

            scores(pair, 1)
            bias_part(2 * pair, 0)
            bias_part(2 * pair + 1, 1)
            weigh_part(2 * pair, 0)
            scores(jnp.minimum(pair + 1, self.pairs - 1), 0)
            first = blend(pair, 0)
            weigh_part(2 * pair + 1, 1)
            second = blend(pair, 1)
            self.ctx_v[:, self.lanes_of(pair, 0)] = (first + second).astype(BF16)
            if keep:
                heads = pl.ds(2 * pair, 2)
                pltpu.make_async_copy(self.weights_v.at[heads], self.weights.at[block, heads], weights_sem).start()
            return carry

        lax.fori_loop(0, self.pairs, head_pair, 0)
        if keep:
            copies.stores.append(pltpu.make_async_copy(self.weights_v, self.weights.at[block], weights_sem))
        copies.store(self.ctx_v, self.ctx.at[rows])
        load_out, load_up, load_down = later_loads
        load_out.wait()
        self.acc_v[...] = dot_nn(self.ctx_v[...], self.wout_v[...])
        for r in range(0, BLOCK, 64):
            tile = slice(r, r + 64)
            form, scale = normal_parts(self.acc_v[tile, :] + self.x_v[tile, :].astype(F32))
            normed = form * self.gain1[...] + self.shift1[...]
            self.form1_v[tile, :] = form
            self.scale1_v[tile, :] = scale
            self.acc_v[tile, :] = normed
            self.low1_v[tile, :] = normed.astype(BF16)
        copies.store(self.form1_v, self.form1.at[rows], keep)
        copies.store(self.scale1_v, self.scale1.at[rows], keep)
        copies.store(self.low1_v, self.low1.at[rows])
        load_up.wait()
        load_down.wait()
        act_sem = self.sems.at[copies.take()]
        slope_sem = self.sems.at[copies.take()]

        def up_part(c, slot):
            self.square_v[slot] = dot_nn(self.low1_v[...], self.wup_v[:, self.chunk(c)])

        def gelu_part(c, slot):
            for r in range(0, BLOCK, 32):
                active, grade = gelu_parts(self.square_v[slot, r : r + 32, :])
                self.act_v[r : r + 32, self.chunk(c)] = active.astype(BF16)
                self.slope_v[r : r + 32, self.chunk(c)] = grade.astype(BF16)

        def down_part(c):
            self.acc_v[...] += dot_nn(self.act_v[:, self.chunk(c)], self.wdown_v[self.chunk(c), :])

        up_part(0, 0)

        def two_chunks(i, carry):
            up_part(2 * i + 1, 1)
            gelu_part(2 * i, 0)
            up_part(jnp.minimum(2 * i + 2, 2 * self.stages - 2), 0)
            down_part(2 * i)
            gelu_part(2 * i + 1, 1)
            down_part(2 * i + 1)
            span = self.stage(i)
            pltpu.make_async_copy(self.act_v.at[:, span], self.act.at[rows, span], act_sem).start()
            if keep:
                pltpu.make_async_copy(self.slope_v.at[:, span], self.slope.at[rows, span], slope_sem).start()
            return carry

        lax.fori_loop(0, self.stages, two_chunks, 0)
        copies.stores.append(pltpu.make_async_copy(self.act_v, self.act.at[rows], act_sem))
        if keep:
            copies.stores.append(pltpu.make_async_copy(self.slope_v, self.slope.at[rows], slope_sem))
        for r in range(0, BLOCK, 64):
            tile = slice(r, r + 64)
            form, scale = normal_parts(self.acc_v[tile, :])
            self.form2_v[tile, :] = form
            self.scale2_v[tile, :] = scale
            self.out_v[tile, :] = (form * self.gain2[...] + self.shift2[...]).astype(BF16)
        copies.store(self.out_v, self.send, keep)
        copies.store(self.out_v, self.out.at[rows])
        copies.store(self.form2_v, self.form2.at[rows], keep)
        copies.store(self.scale2_v, self.scale2.at[rows], keep)


    def chunk_loads(self, i, rows):
        span = self.stage(i)
        return [
            pltpu.make_async_copy(source, target, self.sems.at[self.chunk_sems[k] + i])
            for k, (source, target) in enumerate(
                (
                    (self.wdown.at[0, span], self.wdown_v.at[span]),
                    (self.slope.at[rows, span], self.slope_v.at[:, span]),
                    (self.wup.at[0, :, span], self.wup_v.at[:, span]),
                )
            )
        ]

    def norm_sums(self, source, form_ref, at):
        gain_sum = jnp.zeros((1, self.width), F32)
        shift_sum = jnp.zeros((1, self.width), F32)
        for r in range(0, BLOCK, 64):
            grad_rows, form = source[r : r + 64, :].astype(F32), form_ref[r : r + 64, :]
            gain_sum += jnp.sum(grad_rows * form, 0, keepdims=True)
            shift_sum += jnp.sum(grad_rows, 0, keepdims=True)
        self.sums_v[at : at + 1, :] = gain_sum
        self.sums_v[at + 1 : at + 2, :] = shift_sum

    def ffn_back(self, block, staged=False, middle_loads=()):
        copies = self.copies
        rows = self.rows(block)
        for r in range(0, BLOCK, 64):
            tile = slice(r, r + 64)
            grad_rows = self.g_v[tile, :].astype(F32) * self.gain2[...]
            grad_outer = norm_backward(grad_rows, self.form2_v[tile, :], self.scale2_v[tile, :])
            self.acc_v[tile, :] = grad_outer
            self.outer_v[tile, :] = grad_outer.astype(BF16)
        copies.store(self.outer_v, self.outer_low.at[rows])
        hidden_sem = self.sems.at[copies.take()]

        def two_chunks(i, carry):
            parts = [self.chunk(2 * i + k) for k in range(2)]
            span = self.stage(i)
            if staged:
                load_down, load_slope, load_up = self.chunk_loads(i, rows)
                load_down.wait()
                load_slope.wait()
            for k in range(2):
                self.square_v[k] = dot_nt(self.outer_v[...], self.wdown_v[parts[k], :])
            for k in range(2):
                for r in range(0, BLOCK, 64):
                    tile = slice(r, r + 64)
                    self.slope_v[tile, parts[k]] = (
                        self.square_v[k, tile, :] * self.slope_v[tile, parts[k]].astype(F32)
                    ).astype(BF16)
            if staged:
                load_up.wait()

                @pl.when(i + 2 < self.stages)
                def _():
                    for load in self.chunk_loads(i + 2, rows):
                        load.start()

            self.acc_v[...] += dot_nt(self.slope_v[:, span], self.wup_v[:, span])
            pltpu.make_async_copy(self.slope_v.at[:, span], self.hidden_low.at[rows, span], hidden_sem).start()
            return carry

        lax.fori_loop(0, self.stages, two_chunks, 0)
        copies.stores.append(pltpu.make_async_copy(self.slope_v, self.hidden_low.at[rows], hidden_sem))
        for load in middle_loads:
            load.wait()
        self.norm_sums(self.g_v, self.form2_v, 2)
        self.norm_sums(self.acc_v, self.form1_v, 0)
        for r in range(0, BLOCK, 64):
            tile = slice(r, r + 64)
            grad_residual = norm_backward(
                self.acc_v[tile, :] * self.gain1[...], self.form1_v[tile, :], self.scale1_v[tile, :]
            )
            self.acc_v[tile, :] = grad_residual
            self.residual_low_v[tile, :] = grad_residual.astype(BF16)
        copies.store(self.residual_low_v, self.residual_low.at[rows])
        copies.store(self.sums_v, self.sums.at[block])

    def attn_back(self, block, load_pair=None, load_in=()):
        copies = self.copies
        rows = self.rows(block)
        self.dctx_v[...] = dot_nt(self.residual_low_v[...], self.wout_v[...]).astype(BF16)
        self.fold_v[:, :, 0:TILE] = jnp.zeros((2, TILE, TILE), F32)

        def head_pair(pair, carry):
            def lanes_of(part):
                return self.lanes_of(pair, part)

            q_pair, k_pair, v_pair = (self.qkv_v[:, lanes_of(part)] for part in range(3))
            grad_pair = self.dctx_v[:, lanes_of(0)]
            crossed = grad_pair.astype(F32) * self.ctx_v[:, lanes_of(0)].astype(F32)
            if load_pair is not None:
                load_pair(pair).wait()
            masks = [half_mask(which, k_pair.shape) for which in range(2)]

            def own(both, which):
                return jnp.where(masks[which], both, jnp.zeros_like(both))

            for which in range(2):
                self.square_v[which] = dot_nt(grad_pair, own(v_pair, which))
            q_grad = k_grad = v_grad = 0.0
            for which in range(2):
                head = 2 * pair + which
                delta = jnp.sum(own(crossed, which), -1, keepdims=True)
                for r in range(0, BLOCK, 64):
                    tile = slice(r, r + 64)
                    score_grad = (
                        self.weights_v[head, tile, :].astype(F32) * (self.square_v[which, tile, :] - delta[tile, :])
                    ).astype(BF16)
                    self.scores_v[which, tile, :] = score_grad
                    at = BLOCK - r // TILE * TILE
                    wide = score_grad.astype(F32)
                    half = slice(r % TILE, r % TILE + 64)
                    if r < TILE:
                        self.fold_v[which, half, at : at + BLOCK] = wide
                    else:
                        self.fold_v[which, half, at : at + TILE] = wide[:, :TILE]
                        self.fold_v[which, half, at + TILE : at + BLOCK] += wide[:, TILE:]
                v_grad += dot_tn(self.weights_v[head], own(grad_pair, which))
                q_grad += dot_nn(self.scores_v[which], own(k_pair, which))
                k_grad += dot_tn(self.scores_v[which], own(q_pair, which))
                folded = self.fold_v[which]
                size = TILE // 2
                while size >= 8:
                    folded = folded[:size, :] + pltpu.roll(folded[size:, :], SPAN - size, 1)
                    size //= 2
                self.eighth_v[head] = folded
            self.qkv_v[:, lanes_of(0)] = (q_grad * score_scale).astype(BF16)
            self.qkv_v[:, lanes_of(1)] = (k_grad * score_scale).astype(BF16)
            self.qkv_v[:, lanes_of(2)] = v_grad.astype(BF16)
            return carry

        lax.fori_loop(0, self.pairs, head_pair, 0)
        copies.store(self.eighth_v, self.offsets.at[block])
        copies.store(self.qkv_v, self.projected.at[rows])
        for load in load_in:
            load.wait()
        self.grad_v[...] = (self.acc_v[...] + dot_nt(self.qkv_v[...], self.wqkv_v[...])).astype(BF16)
        copies.store(self.grad_v, self.send)
        copies.store(self.grad_v, self.input_grad.at[rows])


    def do_forward(self, block):
        self.forward(block, True)

    def do_both(self, block):
        load = self.copies.load(self.out_grad.at[self.rows(block)], self.g_v)
        self.forward(block, False)
        load.wait()
        self.ffn_back(block)
        self.attn_back(block)

    def do_back(self, block):
        rows = self.rows(block)
        loads = [
            self.copies.load(source, target)
            for source, target in (
                (self.received, self.g_v),
                (self.form2.at[rows], self.form2_v),
                (self.scale2.at[rows], self.scale2_v),
                (self.slope.at[rows], self.slope_v),
                (self.wdown.at[0], self.wdown_v),
                (self.wup.at[0], self.wup_v),
                (self.form1.at[rows], self.form1_v),
                (self.scale1.at[rows], self.scale1_v),
                (self.qkv.at[rows], self.qkv_v),
                (self.weights.at[block], self.weights_v),
                (self.ctx.at[rows], self.ctx_v),
                (self.wout.at[0], self.wout_v),
                (self.wqkv.at[0], self.wqkv_v),
            )
        ]
        for load in loads:
            load.wait()
        self.ffn_back(block)
        self.attn_back(block)

    def do_ffn_back(self, block):
        rows = self.rows(block)
        loads = [
            self.copies.load(source, target)
            for source, target in (
                (self.received, self.g_v),
                (self.form2.at[rows], self.form2_v),
                (self.scale2.at[rows], self.scale2_v),
            )
        ]
        for i in range(min(2, self.stages)):
            for load in self.chunk_loads(i, rows):
                load.start()
        for load in loads:
            load.wait()
        middle = [
            self.copies.load(self.form1.at[rows], self.form1_v),
            self.copies.load(self.scale1.at[rows], self.scale1_v),
        ]
        self.ffn_back(block, True, middle)
        self.copies.store(self.acc_v, self.residual)

    def do_attn_back(self, block):
        rows = self.rows(block)
        loads = [
            self.copies.load(source, target)
            for source, target in (
                (self.residual_low.at[rows], self.residual_low_v),
                (self.wout.at[0], self.wout_v),
                (self.qkv.at[rows], self.qkv_v),
                (self.ctx.at[rows], self.ctx_v),
            )
        ]

        def load_pair(pair):
            heads = pl.ds(2 * pair, 2)
            return pltpu.make_async_copy(
                self.weights.at[block, heads], self.weights_v.at[heads], self.sems.at[self.pair_sems + pair]
            )

        for pair in range(self.pairs):
            load_pair(pair).start()
        for load in loads:
            load.wait()
        last = [
            self.copies.load(self.wqkv.at[0], self.wqkv_v),
            self.copies.load(self.residual, self.acc_v),
        ]
        self.attn_back(block, load_pair, last)


def layer_kernel(work, phase_on, block, ins, outs, scratch, after_count, kept_count, *refs):
    refs_in, refs = refs[: len(ins)], refs[len(ins) + after_count + kept_count :]
    named = dict(zip(ins, refs_in)) | dict(zip(outs, refs)) | dict(zip(scratch, refs[len(outs) :]))

    @pl.when(named["phase"][0] == phase_on)
    def _():
        layer = Layer(named)
        getattr(layer, f"do_{work}")(block)
        layer.copies.finish()


def layer_step(work, phase_on, block, values, afters, kept, kept_shapes, scratch):
    specs = [SMEM] + [ANY] * 4 + [VMEM] * 5 + [ANY] * 4
    names = list(scratch)
    kept = list(kept) if kept is not None else []
    sent = jax.ShapeDtypeStruct((BLOCK, values[1].shape[1]), BF16)
    count = len(values) + len(afters)
    results = pl.pallas_call(
        functools.partial(
            layer_kernel, work, phase_on, block, INS, KEPT + ("send",), names + ["sems"], len(afters), len(kept)
        ),
        out_shape=list(kept_shapes) + [sent],
        in_specs=specs + [ANY] * (len(afters) + len(kept)),
        out_specs=[ANY] * (len(kept_shapes) + 1),
        scratch_shapes=[pltpu.VMEM(*scratch[name]) for name in names] + [pltpu.SemaphoreType.DMA((80,))],
        input_output_aliases={count + i: i for i in range(len(kept))},
        compiler_params=pltpu.CompilerParams(vmem_limit_bytes=VMEM_BYTES),
        name=f"{work}_{phase_on}_{block}",
    )(*values, *afters, *kept)
    return dict(zip(KEPT, results)), results[-1]


def table_kernel(buckets_ref, offsets_ref, out_ref):
    row_of = lax.broadcasted_iota(jnp.int32, (8, SPAN), 0)
    lines = []
    for head in range(offsets_ref.shape[1]):
        eighth = offsets_ref[0, head] + offsets_ref[1, head]
        for size in (4, 2, 1):
            eighth = jnp.where((row_of & size) != 0, pltpu.roll(eighth, SPAN - size, 1), eighth)
        lines.append(jnp.sum(eighth, 0, keepdims=True))
    lines += [jnp.zeros((1, SPAN), F32)] * (out_ref.shape[0] - len(lines))
    span = buckets_ref.shape[1]
    bucket_ids = lax.broadcasted_iota(jnp.int32, (out_ref.shape[1], span), 0)
    hot = (bucket_ids == buckets_ref[...]).astype(F32)
    sums = pltpu.roll(jnp.concatenate(lines, 0), SPAN - 1, 1)
    out_ref[...] = lax.dot_general(
        sums[:, :span], hot, (((1,), (1,)), ((), ())), precision=highest, preferred_element_type=F32
    )


def halve_kernel(bits, counts, after_count, me_ref, *refs):
    used = sum(counts) + len(counts)
    outs = refs[used + after_count :]
    for i, count in enumerate(counts):
        kept_refs, arrived_ref = refs[:count], refs[count]
        refs = refs[count + 1 :]
        send_ref, rest_ref = outs[2 * i : 2 * i + 2]
        mine = (me_ref[0] >> bits[i]) & 1

        def total(which):
            kept = [
                (ref[0, which, 0, 0] if len(ref.shape) == 6 else ref[0, which, 0]).astype(F32)
                for ref in kept_refs
            ]
            return jnp.concatenate(kept, 1) + arrived_ref[0, which, 0].astype(F32)

        send_ref[0, 0] = total(1 - mine).astype(send_ref.dtype)
        rest_ref[0, 0] = total(mine)


def join_kernel(kept_near, arrived_near, kept_far, arrived_far, out_ref, qkv_ref, small_ref):
    near = kept_near[...] + arrived_near[...].astype(F32)
    wide = out_ref.shape[1]
    share = qkv_ref.shape[1] - kept_far.shape[1]
    out_ref[...] = near[:, :wide]
    qkv_ref[:, :share] = near[:, wide : wide + share]
    qkv_ref[:, share:] = kept_far[...] + arrived_far[...].astype(F32)
    small_ref[...] = near[:, wide + share :]


class Share:
    def __init__(self, parts, order):
        self.parts = parts
        self.order = order[1:]
        self.left = sorted(order)
        self.depth = parts[0].shape[1]
        self.wide = sum(part.shape[2] for part in parts)
        self.mine = None
        self.swap(order[0], self.of_core(1 - (lax.axis_index("dp") & 1)))

    def of_core(self, core):
        halves = [
            lax.dynamic_index_in_dim(
                part.reshape((part.shape[0] // 2, 2) + part.shape[1:]), core, 1, keepdims=False
            )
            for part in self.parts
        ]
        return halves[0] if len(halves) == 1 else jnp.concatenate(halves, 2)

    def swap(self, bit, theirs):
        count = lax.axis_size("dp")
        self.left.remove(bit)
        self.sent = theirs
        self.arrived = lax.ppermute(theirs, "dp", [(i, i ^ (1 << bit)) for i in range(count)])

    def total(self):
        kept = self.of_core(lax.axis_index("dp") & 1) if self.mine is None else self.mine
        return kept.astype(F32) + self.arrived.astype(F32)

    def split_at(self):
        bit = self.order[0]
        axis = len(self.left) - 1 - self.left.index(bit)
        return bit, 2**axis, 2 ** (len(self.left) - 1 - axis)

    def halve(self):
        bit, above, below = self.split_at()
        self.order = self.order[1:]
        split = self.total().reshape(above, 2, below, self.depth, self.wide)
        here = (lax.axis_index("dp") >> bit) & 1
        theirs = lax.dynamic_index_in_dim(split, 1 - here, 1, keepdims=False).astype(BF16)
        mine = lax.dynamic_index_in_dim(split, here, 1, keepdims=False)
        self.mine = mine.reshape(-1, self.depth, self.wide)
        self.swap(bit, theirs.reshape(-1, self.depth, self.wide))


def halve_all(me, shares, afters=()):
    if any(share.depth % 16 for share in shares):
        for share in shares:
            share.halve()
        return
    ins, in_specs, outs, out_specs, bits, counts = [], [], [], [], [], []
    for share in shares:
        bit, above, below = share.split_at()
        bits.append(bit)

        def halves(wide, b=below):
            return pl.BlockSpec((1, 2, 1, share.depth, wide), lambda i, me: (i // b, 0, i % b, 0, 0))

        if share.mine is None:
            counts.append(len(share.parts))
            for part in share.parts:
                wide = part.shape[2]
                ins.append(part.reshape(above, 2, below, 2, share.depth, wide))
                in_specs.append(
                    pl.BlockSpec(
                        (1, 2, 1, 1, share.depth, wide),
                        lambda i, me, b=below: (i // b, 0, i % b, me[0] & 1, 0, 0),
                    )
                )
        else:
            counts.append(1)
            ins.append(share.mine.reshape(above, 2, below, share.depth, share.wide))
            in_specs.append(halves(share.wide))
        ins.append(share.arrived.reshape(above, 2, below, share.depth, share.wide))
        in_specs.append(halves(share.wide))
        outs += [
            jax.ShapeDtypeStruct((above, below, share.depth, share.wide), kind) for kind in (BF16, F32)
        ]
        out_specs += [
            pl.BlockSpec((1, 1, share.depth, share.wide), lambda i, me, b=below: (i // b, i % b, 0, 0))
        ] * 2
        steps = above * below
    results = pl.pallas_call(
        functools.partial(halve_kernel, tuple(bits), tuple(counts), len(afters)),
        grid_spec=pltpu.PrefetchScalarGridSpec(
            num_scalar_prefetch=1,
            grid=(steps,),
            in_specs=in_specs + [ANY] * len(afters),
            out_specs=out_specs,
        ),
        out_shape=outs,
        compiler_params=pltpu.CompilerParams(vmem_limit_bytes=SMALL_VMEM_BYTES),
        name="halve",
    )(me, *ins, *afters)
    for i, share in enumerate(shares):
        share.order = share.order[1:]
        share.mine = results[2 * i + 1].reshape(-1, share.depth, share.wide)
        share.swap(bits[i], results[2 * i].reshape(-1, share.depth, share.wide))


def joined(near, far, width):
    parts = [x[0] for share in (near, far) for x in (share.mine, share.arrived)]
    small = LANES
    return pl.pallas_call(
        join_kernel,
        out_shape=[
            jax.ShapeDtypeStruct((near.depth, wide), F32) for wide in (width, near.wide + far.wide - width - small, small)
        ],
        in_specs=[VMEM] * len(parts),
        out_specs=[VMEM] * 3,
        compiler_params=pltpu.CompilerParams(vmem_limit_bytes=SMALL_VMEM_BYTES),
        name="join",
    )(*parts)


def passed_along(x, axis, by):
    length = lax.axis_size(axis)
    pairs = [(i, i + by) for i in range(length) if 0 <= i + by < length]
    return lax.ppermute(x, axis, pairs)


def shards(
    hidden_in, out_grad, qkv_weight, out_weight, rel_table, norm1_gain, norm1_bias,
    up_weight, down_weight, norm2_gain, norm2_bias, seg_ids, pad_mask, rel_buckets,
):
    phase = lax.axis_index("phase").astype(jnp.int32).reshape(1)
    ways = lax.axis_size("dp")
    slots, width = hidden_in.shape
    inner = up_weight.shape[2]
    buckets, heads = rel_table.shape[1:]
    head_rows = -(-heads // 8) * 8

    def shape(dims, kind):
        return jax.ShapeDtypeStruct(dims, kind)

    def whole(array):
        return pl.BlockSpec(array.shape, lambda i: (0,) * array.ndim)

    starts = (rel_buckets[None, :], rel_table, seg_ids[None, :], pad_mask[None, :])
    bias, shut = pl.pallas_call(
        bias_kernel,
        grid=(heads // 2,),
        out_shape=[shape((heads, TILE, SPAN), F32), shape((MICRO, BLOCK // TILE, BLOCK), F32)],
        in_specs=[whole(array) for array in starts],
        out_specs=[
            pl.BlockSpec((2, TILE, SPAN), lambda i: (i, 0, 0)),
            pl.BlockSpec((MICRO, BLOCK // TILE, BLOCK), lambda i: (0, 0, 0)),
        ],
        scratch_shapes=[pltpu.VMEM((heads, SPAN), F32)],
        compiler_params=pltpu.CompilerParams(vmem_limit_bytes=SMALL_VMEM_BYTES),
        name="pair_bias",
    )(*starts)

    rows_of = {
        "xin": (width, BF16), "qkv": (3 * width, BF16), "ctx": (width, BF16), "form1": (width, F32),
        "scale1": (1, F32), "low1": (width, BF16), "slope": (inner, BF16), "act": (inner, BF16),
        "form2": (width, F32), "scale2": (1, F32), "out": (width, BF16),
        "outer_low": (width, BF16), "hidden_low": (inner, BF16), "residual_low": (width, BF16),
        "projected": (3 * width, BF16), "input_grad": (width, BF16),
    }
    kept_shapes = [
        shape((slots, rows_of[name][0]), rows_of[name][1])
        if name in rows_of
        else {
            "weights": shape((MICRO, heads, BLOCK, BLOCK), BF16),
            "sums": shape((MICRO, 8, width), F32),
            "residual": shape((BLOCK, width), F32),
            "offsets": shape((MICRO, heads, 8, SPAN), F32),
        }[name]
        for name in KEPT
    ]
    in_forward = ("qkv", "ctx", "form1", "scale1", "low1", "slope", "act", "form2", "scale2", "out")
    scratch = {f"{name}_v": ((BLOCK, rows_of[name][0]), rows_of[name][1]) for name in in_forward}
    scratch |= {
        name: ((BLOCK, width), BF16) for name in ("x_v", "g_v", "outer_v", "residual_low_v", "dctx_v", "grad_v")
    }
    scratch |= {
        "weights_v": ((heads, BLOCK, BLOCK), BF16), "acc_v": ((BLOCK, width), F32), "square_v": ((2, BLOCK, BLOCK), F32),
        "top_v": ((2, BLOCK, 1), F32), "bias_v": ((heads, TILE, SPAN), F32), "sums_v": ((8, width), F32),
        "wqkv_v": ((width, 3 * width), BF16), "wout_v": ((width, width), BF16), "wup_v": ((width, inner), BF16),
        "wdown_v": ((inner, width), BF16), "fold_v": ((2, TILE, SPAN), F32), "eighth_v": ((heads, 8, SPAN), F32),
        "scores_v": ((2, BLOCK, BLOCK), BF16),
    }

    def step(work, phase_on, block, received, kept, afters=()):
        values = (
            phase, hidden_in, received, out_grad, bias, shut, norm1_gain, norm1_bias, norm2_gain, norm2_bias,
            qkv_weight, out_weight, up_weight, down_weight,
        )
        in_place = None if kept is None else [kept[name] for name in KEPT]
        return layer_step(work, phase_on, block, values, list(afters), in_place, kept_shapes, scratch)

    kept, sent = step("forward", 0, 0, hidden_in, None)
    first = passed_along(sent, "phase", 1)
    kept, sent = step("forward", 0, 1, hidden_in, kept)
    second = passed_along(sent, "phase", 1)
    kept, sent = step("both", 1, 0, first, kept)
    first_back = passed_along(sent, "phase", -1)
    kept, sent = step("both", 1, 1, second, kept)
    second_back = passed_along(sent, "phase", -1)
    kept, _ = step("back", 0, 0, first_back, kept)
    kept, _ = step("ffn_back", 0, 1, second_back, kept)

    bits = ways.bit_length() - 1
    near_first = list(range(bits))
    far_first = [0] + list(range(2, bits)) + [1] if bits > 1 else near_first
    me = lax.axis_index("dp").astype(jnp.int32).reshape(1)

    def weight_grad(left, right):
        product = dot_tn(left, right).astype(BF16)
        return product.reshape(ways, product.shape[0] // ways, product.shape[1])

    down = Share([weight_grad(kept["act"], kept["outer_low"])], near_first)
    up = Share([weight_grad(kept["low1"], kept["hidden_low"])], near_first)
    out_part = weight_grad(kept["ctx"], kept["residual_low"])
    halve_all(me, [down])
    halve_all(me, [up])
    kept, _ = step("attn_back", 0, 1, hidden_in, kept, [down.sent, up.sent])
    far = Share([weight_grad(kept["xin"], kept["projected"][:, width:])], far_first)
    near_part = weight_grad(kept["xin"], kept["projected"][:, :width])
    table_part = pl.pallas_call(
        table_kernel,
        out_shape=shape((head_rows, buckets), F32),
        in_specs=[VMEM, VMEM],
        out_specs=VMEM,
        compiler_params=pltpu.CompilerParams(vmem_limit_bytes=SMALL_VMEM_BYTES),
        name="table_grad",
    )(starts[0], kept["offsets"])[:heads].T
    sums = jnp.sum(kept["sums"], 0)[:4]
    table_size = buckets // ways * heads
    small = jnp.concatenate(
        [table_part.reshape(ways, -1), sums.reshape(4, ways, width // ways).transpose(1, 0, 2).reshape(ways, -1)],
        1,
    ).astype(BF16)
    depth = width // ways
    small = jnp.pad(small, ((0, 0), (0, depth * LANES - small.shape[1]))).reshape(ways, depth, LANES)
    near = Share([out_part, near_part, small], near_first)
    halve_all(me, [down])
    halve_all(me, [up], [down.sent])
    halve_all(me, [near, far], [down.sent, up.sent])
    halve_all(me, [down])
    halve_all(me, [up], [down.sent])
    halve_all(me, [near, far], [down.sent, up.sent])
    while down.order:
        halve_all(me, [down, up])
    while near.order:
        halve_all(me, [near, far])
    down_share = down.total()[0]
    up_share = up.total()[0]
    out_share, qkv_share, small_share = joined(near, far, width)
    small_share = small_share.reshape(-1)[: table_size + 4 * width // ways]
    norm_shares = small_share[table_size:].reshape(4, width // ways)
    return (
        kept["out"][None],
        kept["input_grad"][None],
        qkv_share[None],
        out_share[None],
        small_share[:table_size].reshape(1, buckets // ways, heads),
        norm_shares[0:1],
        norm_shares[1:2],
        up_share[None],
        down_share[None],
        norm_shares[2:3],
        norm_shares[3:4],
    )


def solution(mesh):
    return jax.shard_map(
        shards,
        mesh=mesh,
        in_specs=(
            P("dp", None),
            P("dp", None),
            P("phase", None, None),
            P("phase", None, None),
            P("phase", None, None),
            P("phase", None),
            P("phase", None),
            P("phase", None, None),
            P("phase", None, None),
            P("phase", None),
            P("phase", None),
            P("dp"),
            P("dp"),
            P(),
        ),
        out_specs=(
            P("phase", "dp", None),
            P("phase", "dp", None),
            P("phase", "dp", None),
            P("phase", "dp", None),
            P("phase", "dp", None),
            P("phase", "dp"),
            P("phase", "dp"),
            P("phase", "dp", None),
            P("phase", "dp", None),
            P("phase", "dp"),
            P("phase", "dp"),
        ),
        check_vma=False,
    )
```

```python
import functools

import jax
import jax.numpy as jnp
from jax import lax
from jax.experimental import pallas as pl
from jax.experimental.pallas import tpu as pltpu
from jax.sharding import PartitionSpec as P

BLOCK = 512
MICRO = 2
TILE = 128
LANES = 128
CHUNK = 512
SPAN = 2 * BLOCK
VMEM_BYTES = 58 * 1024 * 1024
SMALL_VMEM_BYTES = 20 * 1024 * 1024
NORM_LANE = 16

norm_eps = 1e-05
mask_fill = -1000000000.0
score_scale = 0.125
inv_root_two = 0.7071067811865476
inv_root_tau = 0.3989422804014327
log2_e = 1.4426950408889634
highest = lax.Precision.HIGHEST

F32 = jnp.float32
BF16 = jnp.bfloat16
ANY = pl.BlockSpec(memory_space=pl.ANY)
VMEM = pl.BlockSpec(memory_space=pltpu.VMEM)
QUICK = pl.CostEstimate(flops=1, bytes_accessed=1, transcendentals=0)
SMEM = pl.BlockSpec(memory_space=pltpu.SMEM)


def dot_nn(a, b):
    return lax.dot_general(a, b, (((1,), (0,)), ((), ())), preferred_element_type=F32)


def dot_nt(a, b):
    return lax.dot_general(a, b, (((1,), (1,)), ((), ())), preferred_element_type=F32)


def dot_tn(a, b):
    return lax.dot_general(a, b, (((0,), (0,)), ((), ())), preferred_element_type=F32)


def row_mean(rows):
    return jnp.sum(rows, -1, keepdims=True) * (1.0 / rows.shape[-1])


def normal_parts(residual):
    centred = residual - row_mean(residual)
    inv_scale = lax.rsqrt(row_mean(centred * centred) + norm_eps)
    return centred * inv_scale, inv_scale


def norm_backward(grad_rows, normal_form, inv_scale):
    first = row_mean(grad_rows)
    second = row_mean(grad_rows * normal_form)
    return inv_scale * (grad_rows - first - normal_form * second)


def gelu_parts(hidden):
    size = jnp.abs(hidden)
    bell = jnp.exp2(hidden * hidden * (-0.5 * log2_e))
    t = pl.reciprocal(1.0 + (0.3275911 * inv_root_two) * size, approx=True)
    tail = 0.5 * 1.061405429
    for factor in (-1.453152027, 1.421413741, -0.284496736, 0.254829592):
        tail = tail * t + 0.5 * factor
    tail = tail * t * bell
    share = jnp.where(hidden < 0.0, tail, 1.0 - tail)
    return hidden * share, share + hidden * bell * inv_root_tau


def half_mask(which, shape):
    lane = lax.broadcasted_iota(jnp.int32, shape, 1)
    return (lane < LANES // 2) if which == 0 else (lane >= LANES // 2)


class Copies:
    def __init__(self, sems):
        self.sems = sems
        self.used = 0
        self.stores = []

    def take(self, count=1):
        self.used += count
        return self.used - count

    def load(self, source, target):
        copy = pltpu.make_async_copy(source, target, self.sems.at[self.take()])
        copy.start()
        return copy

    def store(self, source, target, when=True):
        if when:
            self.stores.append(self.load(source, target))

    def finish(self):
        for copy in self.stores:
            copy.wait()


def bias_kernel(buckets_ref, table_ref, seg_ref, pad_ref, bias_ref, shut_ref, values_v):
    step = pl.program_id(0)

    @pl.when(step == 0)
    def _():
        span = buckets_ref.shape[1]
        bucket_ids = lax.broadcasted_iota(jnp.int32, (table_ref.shape[1], span), 0)
        hot = (bucket_ids == buckets_ref[...]).astype(F32)
        values = lax.dot_general(
            table_ref[0], hot, (((0,), (0,)), ((), ())), precision=highest, preferred_element_type=F32
        )
        values_v[:, :span] = values
        values_v[:, span:] = jnp.zeros((values.shape[0], SPAN - span), F32)
        for block in range(MICRO):
            at = slice(block * BLOCK, (block + 1) * BLOCK)
            for tile in range(BLOCK // TILE):
                own = seg_ref[:, block * BLOCK + tile * TILE : block * BLOCK + tile * TILE + 1]
                open_pairs = (seg_ref[:, at] == own) & (pad_ref[:, at] == 1)
                shut_ref[block, tile : tile + 1, :] = jnp.where(open_pairs, 0.0, mask_fill)

    for i in range(bias_ref.shape[0]):
        wide = jnp.broadcast_to(values_v[pl.ds(bias_ref.shape[0] * step + i, 1), :], (TILE, SPAN))
        bias_ref[i] = pltpu.roll(wide, 1, 1, stride=1, stride_axis=0)


KEPT = (
    "xin", "qkv", "weights", "ctx", "form1", "scale1", "low1", "slope", "act", "form2", "scale2", "out",
    "outer_low", "hidden_low", "residual_low", "sums1", "sums2", "residual", "projected", "offsets", "input_grad",
)
INS = (
    "phase", "hidden_in", "received", "out_grad", "bias", "shut", "gain1", "shift1", "gain2", "shift2",
    "wqkv", "wout", "wup", "wdown",
)


class Layer:
    def __init__(self, refs):
        self.__dict__.update(refs)
        self.copies = Copies(self.sems)
        self.width = self.hidden_in.shape[1]
        self.inner = self.wup.shape[2]
        self.pairs = self.width // LANES
        self.stages = self.inner // (2 * CHUNK)
        self.pair_sems = self.copies.take(self.pairs)
        self.chunk_sems = [self.copies.take(self.stages) for _ in range(3)]

    def lanes_of(self, pair, part):
        return pl.ds(pl.multiple_of(part * self.width + pair * LANES, LANES), LANES)

    def chunk(self, c):
        return pl.ds(pl.multiple_of(c * CHUNK, CHUNK), CHUNK)

    def stage(self, i):
        return pl.ds(pl.multiple_of(i * 2 * CHUNK, 2 * CHUNK), 2 * CHUNK)


    def rows(self, block):
        return pl.ds(block * BLOCK, BLOCK)

    def forward(self, block, keep):
        copies = self.copies
        rows = self.rows(block)
        load_x = copies.load(self.hidden_in.at[rows] if keep else self.received, self.x_v)
        width = self.width
        loads = [
            copies.load(self.wqkv.at[0, :, pl.ds(c, width)], self.wqkv_v.at[:, pl.ds(c, width)])
            for c in range(0, 3 * width, width)
        ]
        load_x.wait()

        def load_bias(pair):
            heads = pl.ds(2 * pair, 2)
            return pltpu.make_async_copy(self.bias.at[heads], self.bias_v.at[heads], self.sems.at[self.pair_sems + pair])

        for i, c in enumerate(range(0, 3 * width, width)):
            loads[i].wait()
            if i == 2:
                for pair in range(self.pairs):
                    load_bias(pair).start()
            self.qkv_v[:, c : c + width] = dot_nn(self.x_v[...], self.wqkv_v[:, c : c + width]).astype(BF16)
        copies.store(self.x_v, self.xin.at[rows])
        copies.store(self.qkv_v, self.qkv.at[rows], keep)
        weights_sem = self.sems.at[copies.take()]
        later_loads = [
            pltpu.make_async_copy(source.at[0], target, self.sems.at[copies.take()])
            for source, target in ((self.wout, self.wout_v), (self.wup, self.wup_v), (self.wdown, self.wdown_v))
        ]

        def own(pair, part, which):
            both = self.qkv_v[:, self.lanes_of(pair, part)]
            return jnp.where(half_mask(which, both.shape), both, jnp.zeros_like(both))

        def scores(pair, which):
            q_rows = self.qkv_v[:, self.lanes_of(pair, 0)] * jnp.asarray(score_scale, BF16)
            self.square_v[which] = dot_nt(q_rows, own(pair, 1, which))

        def bias_part(head, which):
            for r in range(0, BLOCK, 64):
                at = BLOCK - r // TILE * TILE
                own_tile = r // TILE * TILE
                bias_rows = self.bias_v[head, r % TILE : r % TILE + 64, at : at + BLOCK]
                shut = bias_rows + self.shut[block, r // TILE : r // TILE + 1, :]
                row_id = lax.broadcasted_iota(jnp.int32, (64, TILE), 0) + r % TILE
                diagonal = row_id == lax.broadcasted_iota(jnp.int32, (64, TILE), 1)
                shut = jnp.concatenate(
                    [
                        jnp.where(diagonal, bias_rows[:, c : c + TILE], shut[:, c : c + TILE])
                        if c == own_tile
                        else shut[:, c : c + TILE]
                        for c in range(0, BLOCK, TILE)
                    ],
                    1,
                )
                logits = self.square_v[which, r : r + 64, :] + shut
                self.square_v[which, r : r + 64, :] = logits
                self.top_v[which, r : r + 64, :] = jnp.max(logits, -1, keepdims=True)

        def weigh_part(head, which):
            for r in range(0, BLOCK, 64):
                tile = slice(r, r + 64)
                raised = jnp.exp(self.square_v[which, tile, :] - self.top_v[which, tile, :])
                share = pl.reciprocal(jnp.sum(raised, -1, keepdims=True), approx=True)
                weights = (raised * share).astype(BF16)
                self.weights_v[head, tile, :] = weights
                self.half_v[which, tile, :] = weights

        def blend(pair, which):
            return dot_nn(self.half_v[which], own(pair, 2, which))

        def put_context(pair):
            self.ctx_v[:, self.lanes_of(pair, 0)] = (self.part_v[...] + blend(pair, 1)).astype(BF16)

        scores(0, 0)

        def head_pair(pair, carry):
            load_bias(pair).wait()

            @pl.when(pair == 0)
            def _():
                for load in later_loads:
                    load.start()

            put_context(jnp.maximum(pair - 1, 0))
            scores(pair, 1)
            bias_part(2 * pair, 0)
            weigh_part(2 * pair, 0)
            self.part_v[...] = blend(pair, 0)
            scores(jnp.minimum(pair + 1, self.pairs - 1), 0)
            bias_part(2 * pair + 1, 1)
            weigh_part(2 * pair + 1, 1)
            if keep:
                heads = pl.ds(2 * pair, 2)
                pltpu.make_async_copy(self.weights_v.at[heads], self.weights.at[block, heads], weights_sem).start()
            return carry

        lax.fori_loop(0, self.pairs, head_pair, 0)
        put_context(self.pairs - 1)
        if keep:
            copies.stores.append(pltpu.make_async_copy(self.weights_v, self.weights.at[block], weights_sem))
        copies.store(self.ctx_v, self.ctx.at[rows])
        load_out, load_up, load_down = later_loads
        load_out.wait()
        self.acc_v[...] = dot_nn(self.ctx_v[...], self.wout_v[...])
        for r in range(0, BLOCK, 64):
            tile = slice(r, r + 64)
            form, scale = normal_parts(self.acc_v[tile, :] + self.x_v[tile, :].astype(F32))
            normed = form * self.gain1[...] + self.shift1[...]
            self.form1_v[tile, :] = form
            self.scale1_v[tile, :] = scale
            self.acc_v[tile, :] = normed
            self.low1_v[tile, :] = normed.astype(BF16)
        copies.store(self.form1_v, self.form1.at[rows], keep)
        copies.store(self.scale1_v, self.scale1.at[rows], keep)
        copies.store(self.low1_v, self.low1.at[rows])
        load_up.wait()
        load_down.wait()
        act_sem = self.sems.at[copies.take()]
        slope_sem = self.sems.at[copies.take()]

        def up_part(c, slot):
            self.square_v[slot] = dot_nn(self.low1_v[...], self.wup_v[:, self.chunk(c)])

        def gelu_part(c, slot):
            for r in range(0, BLOCK, 32):
                active, grade = gelu_parts(self.square_v[slot, r : r + 32, :])
                active = active.astype(BF16)
                self.act_v[r : r + 32, self.chunk(c)] = active
                self.half_v[slot, r : r + 32, :] = active
                self.slope_v[r : r + 32, self.chunk(c)] = grade.astype(BF16)

        def down_part(c, slot):
            self.acc_v[...] += dot_nn(self.half_v[slot], self.wdown_v[self.chunk(c), :])

        up_part(0, 0)
        self.half_v[1] = jnp.zeros((BLOCK, CHUNK), BF16)

        def two_chunks(i, carry):
            down_part(jnp.maximum(2 * i - 1, 0), 1)
            up_part(2 * i + 1, 1)
            gelu_part(2 * i, 0)
            down_part(2 * i, 0)
            up_part(jnp.minimum(2 * i + 2, 2 * self.stages - 2), 0)
            gelu_part(2 * i + 1, 1)
            span = self.stage(i)
            pltpu.make_async_copy(self.act_v.at[:, span], self.act.at[rows, span], act_sem).start()
            if keep:
                pltpu.make_async_copy(self.slope_v.at[:, span], self.slope.at[rows, span], slope_sem).start()
            return carry

        lax.fori_loop(0, self.stages, two_chunks, 0)
        down_part(2 * self.stages - 1, 1)
        copies.stores.append(pltpu.make_async_copy(self.act_v, self.act.at[rows], act_sem))
        if keep:
            copies.stores.append(pltpu.make_async_copy(self.slope_v, self.slope.at[rows], slope_sem))
        for r in range(0, BLOCK, 64):
            tile = slice(r, r + 64)
            form, scale = normal_parts(self.acc_v[tile, :])
            self.form2_v[tile, :] = form
            self.scale2_v[tile, :] = scale
            self.out_v[tile, :] = (form * self.gain2[...] + self.shift2[...]).astype(BF16)
        copies.store(self.out_v, self.send, keep)
        copies.store(self.out_v, self.out.at[rows])
        copies.store(self.form2_v, self.form2.at[rows], keep)
        copies.store(self.scale2_v, self.scale2.at[rows], keep)


    def chunk_loads(self, i, rows):
        span = self.stage(i)
        return [
            pltpu.make_async_copy(source, target, self.sems.at[self.chunk_sems[k] + i])
            for k, (source, target) in enumerate(
                (
                    (self.wdown.at[0, span], self.wdown_v.at[span]),
                    (self.slope.at[rows, span], self.slope_v.at[:, span]),
                    (self.wup.at[0, :, span], self.wup_v.at[:, span]),
                )
            )
        ]

    def norm_sums(self, source, form_ref, sums_ref):
        gain_sum = jnp.zeros((1, self.width), F32)
        shift_sum = jnp.zeros((1, self.width), F32)
        for r in range(0, BLOCK, 64):
            grad_rows, form = source[r : r + 64, :].astype(F32), form_ref[r : r + 64, :]
            gain_sum += jnp.sum(grad_rows * form, 0, keepdims=True)
            shift_sum += jnp.sum(grad_rows, 0, keepdims=True)
        sums_ref[...] = jnp.zeros(sums_ref.shape, F32)
        sums_ref[0:1, :] = gain_sum
        sums_ref[1:2, :] = shift_sum

    def norm_back(self, block):
        for r in range(0, BLOCK, 64):
            tile = slice(r, r + 64)
            grad_rows = self.g_v[tile, :].astype(F32) * self.gain2[...]
            grad_outer = norm_backward(grad_rows, self.form2_v[tile, :], self.scale2_v[tile, :])
            self.acc_v[tile, :] = grad_outer
            self.outer_v[tile, :] = grad_outer.astype(BF16)
        self.copies.store(self.outer_v, self.outer_low.at[self.rows(block)])

    def norm_sums_2(self, block):
        self.norm_sums(self.g_v, self.form2_v, self.sums2_v)
        self.copies.store(self.sums2_v, self.sums2.at[block])

    def ffn_back(self, block, staged=False, middle_loads=()):
        copies = self.copies
        rows = self.rows(block)
        hidden_sem = self.sems.at[copies.take()]

        def two_chunks(i, carry):
            parts = [self.chunk(2 * i + k) for k in range(2)]
            span = self.stage(i)
            if staged:
                load_down, load_slope, load_up = self.chunk_loads(i, rows)
                load_down.wait()
                load_slope.wait()
            for k in range(2):
                self.square_v[k] = dot_nt(self.outer_v[...], self.wdown_v[parts[k], :])
            for k in range(2):
                for r in range(0, BLOCK, 64):
                    tile = slice(r, r + 64)
                    hidden = (self.square_v[k, tile, :] * self.slope_v[tile, parts[k]].astype(F32)).astype(BF16)
                    self.slope_v[tile, parts[k]] = hidden
                    self.half_v[k, tile, :] = hidden
            if staged:
                load_up.wait()

                @pl.when(i + 2 < self.stages)
                def _():
                    for load in self.chunk_loads(i + 2, rows):
                        load.start()

            for k in range(2):
                self.acc_v[...] += dot_nt(self.half_v[k], self.wup_v[:, parts[k]])
            pltpu.make_async_copy(self.slope_v.at[:, span], self.hidden_low.at[rows, span], hidden_sem).start()
            return carry

        lax.fori_loop(0, self.stages, two_chunks, 0)
        copies.stores.append(pltpu.make_async_copy(self.slope_v, self.hidden_low.at[rows], hidden_sem))
        for load in middle_loads:
            load.wait()
        self.norm_sums(self.acc_v, self.form1_v, self.sums1_v)
        for r in range(0, BLOCK, 64):
            tile = slice(r, r + 64)
            grad_residual = norm_backward(
                self.acc_v[tile, :] * self.gain1[...], self.form1_v[tile, :], self.scale1_v[tile, :]
            )
            self.acc_v[tile, :] = grad_residual
            self.residual_low_v[tile, :] = grad_residual.astype(BF16)
        copies.store(self.residual_low_v, self.residual_low.at[rows])
        copies.store(self.sums1_v, self.sums1.at[block])

    def attn_back(self, block, load_pair=None, load_in=()):
        copies = self.copies
        rows = self.rows(block)
        self.dctx_v[...] = dot_nt(self.residual_low_v[...], self.wout_v[...]).astype(BF16)
        self.fold_v[:, :, 0:TILE] = jnp.zeros((2, TILE, TILE), F32)

        def head_pair(pair, carry):
            def lanes_of(part):
                return self.lanes_of(pair, part)

            q_pair, k_pair, v_pair = (self.qkv_v[:, lanes_of(part)] for part in range(3))
            grad_pair = self.dctx_v[:, lanes_of(0)]
            crossed = grad_pair.astype(F32) * self.ctx_v[:, lanes_of(0)].astype(F32)
            if load_pair is not None:
                load_pair(pair).wait()
            masks = [half_mask(which, k_pair.shape) for which in range(2)]

            def own(both, which):
                return jnp.where(masks[which], both, jnp.zeros_like(both))

            for which in range(2):
                self.square_v[which] = dot_nt(grad_pair, own(v_pair, which))
            q_grad = k_grad = v_grad = 0.0
            for which in range(2):
                head = 2 * pair + which
                delta = jnp.sum(own(crossed, which), -1, keepdims=True)
                for r in range(0, BLOCK, 64):
                    tile = slice(r, r + 64)
                    score_grad = (
                        self.weights_v[head, tile, :].astype(F32) * (self.square_v[which, tile, :] - delta[tile, :])
                    ).astype(BF16)
                    self.half_v[which, tile, :] = score_grad
                    at = BLOCK - r // TILE * TILE
                    wide = score_grad.astype(F32)
                    half = slice(r % TILE, r % TILE + 64)
                    if r < TILE:
                        self.fold_v[which, half, at : at + BLOCK] = wide
                    else:
                        self.fold_v[which, half, at : at + TILE] = wide[:, :TILE]
                        self.fold_v[which, half, at + TILE : at + BLOCK] += wide[:, TILE:]
                v_grad += dot_tn(self.weights_v[head], own(grad_pair, which))
                q_grad += dot_nn(self.half_v[which], own(k_pair, which))
                k_grad += dot_tn(self.half_v[which], own(q_pair, which))
                folded = self.fold_v[which]
                size = TILE // 2
                while size >= 8:
                    folded = folded[:size, :] + pltpu.roll(folded[size:, :], SPAN - size, 1)
                    size //= 2
                self.eighth_v[head] = folded
            self.qkv_v[:, lanes_of(0)] = (q_grad * score_scale).astype(BF16)
            self.qkv_v[:, lanes_of(1)] = (k_grad * score_scale).astype(BF16)
            self.qkv_v[:, lanes_of(2)] = v_grad.astype(BF16)
            return carry

        lax.fori_loop(0, self.pairs, head_pair, 0)
        copies.store(self.eighth_v, self.offsets.at[block])
        copies.store(self.qkv_v, self.projected.at[rows])
        for load in load_in:
            load.wait()
        self.grad_v[...] = (self.acc_v[...] + dot_nt(self.qkv_v[...], self.wqkv_v[...])).astype(BF16)
        copies.store(self.grad_v, self.send)
        copies.store(self.grad_v, self.input_grad.at[rows])


    def do_forward(self, block):
        self.forward(block, True)

    def do_both(self, block):
        load = self.copies.load(self.out_grad.at[self.rows(block)], self.g_v)
        self.forward(block, False)
        load.wait()
        self.norm_back(block)
        self.ffn_back(block)
        self.norm_sums_2(block)
        self.attn_back(block)

    def do_back(self, block):
        rows = self.rows(block)
        loads = [
            self.copies.load(source, target)
            for source, target in (
                (self.received, self.g_v),
                (self.form2.at[rows], self.form2_v),
                (self.scale2.at[rows], self.scale2_v),
                (self.slope.at[rows], self.slope_v),
                (self.wdown.at[0], self.wdown_v),
                (self.wup.at[0], self.wup_v),
                (self.form1.at[rows], self.form1_v),
                (self.scale1.at[rows], self.scale1_v),
                (self.qkv.at[rows], self.qkv_v),
                (self.weights.at[block], self.weights_v),
                (self.ctx.at[rows], self.ctx_v),
                (self.wout.at[0], self.wout_v),
                (self.wqkv.at[0], self.wqkv_v),
            )
        ]
        for load in loads:
            load.wait()
        self.norm_back(block)
        self.ffn_back(block)
        self.norm_sums_2(block)
        self.attn_back(block)

    def do_norm_back(self, block):
        rows = self.rows(block)
        loads = [
            self.copies.load(source, target)
            for source, target in (
                (self.received, self.g_v),
                (self.form2.at[rows], self.form2_v),
                (self.scale2.at[rows], self.scale2_v),
            )
        ]
        for load in loads:
            load.wait()
        self.norm_back(block)
        self.copies.store(self.acc_v, self.residual)
        self.norm_sums_2(block)

    def do_ffn_back(self, block):
        rows = self.rows(block)
        loads = [
            self.copies.load(self.outer_low.at[rows], self.outer_v),
            self.copies.load(self.residual, self.acc_v),
        ]
        for i in range(min(2, self.stages)):
            for load in self.chunk_loads(i, rows):
                load.start()
        for load in loads:
            load.wait()
        middle = [
            self.copies.load(self.form1.at[rows], self.form1_v),
            self.copies.load(self.scale1.at[rows], self.scale1_v),
        ]
        self.ffn_back(block, True, middle)
        self.copies.store(self.acc_v, self.residual)

    def do_attn_back(self, block):
        rows = self.rows(block)
        loads = [
            self.copies.load(source, target)
            for source, target in (
                (self.residual_low.at[rows], self.residual_low_v),
                (self.wout.at[0], self.wout_v),
                (self.qkv.at[rows], self.qkv_v),
                (self.ctx.at[rows], self.ctx_v),
            )
        ]

        def load_pair(pair):
            heads = pl.ds(2 * pair, 2)
            return pltpu.make_async_copy(
                self.weights.at[block, heads], self.weights_v.at[heads], self.sems.at[self.pair_sems + pair]
            )

        for pair in range(self.pairs):
            load_pair(pair).start()
        for load in loads:
            load.wait()
        last = [
            self.copies.load(self.wqkv.at[0], self.wqkv_v),
            self.copies.load(self.residual, self.acc_v),
        ]
        self.attn_back(block, load_pair, last)


def layer_kernel(work, phase_on, block, ins, outs, scratch, after_count, kept_count, *refs):
    refs_in, refs = refs[: len(ins)], refs[len(ins) + after_count + kept_count :]
    named = dict(zip(ins, refs_in)) | dict(zip(outs, refs)) | dict(zip(scratch, refs[len(outs) :]))

    @pl.when(named["phase"][0] == phase_on)
    def _():
        layer = Layer(named)
        getattr(layer, f"do_{work}")(block)
        layer.copies.finish()


def layer_step(work, phase_on, block, values, afters, kept, kept_shapes, scratch):
    specs = [SMEM] + [ANY] * 4 + [VMEM] * 5 + [ANY] * 4
    names = list(scratch)
    kept = list(kept) if kept is not None else []
    sent = jax.ShapeDtypeStruct((BLOCK, values[1].shape[1]), BF16)
    if work == "norm_back":
        names = [f"{name}_v" for name in ("g", "form2", "scale2", "acc", "outer", "sums2")]
    count = len(values) + len(afters)
    results = pl.pallas_call(
        functools.partial(
            layer_kernel, work, phase_on, block, INS, KEPT + ("send",), names + ["sems"], len(afters), len(kept)
        ),
        out_shape=list(kept_shapes) + [sent],
        in_specs=specs + [ANY] * (len(afters) + len(kept)),
        out_specs=[ANY] * (len(kept_shapes) + 1),
        scratch_shapes=[pltpu.VMEM(*scratch[name]) for name in names] + [pltpu.SemaphoreType.DMA((80,))],
        input_output_aliases={count + i: i for i in range(len(kept))},
        compiler_params=pltpu.CompilerParams(vmem_limit_bytes=VMEM_BYTES),
        name=f"{work}_{phase_on}_{block}",
    )(*values, *afters, *kept)
    return dict(zip(KEPT, results)), results[-1]


def pack_kernel(ways, buckets_ref, offsets_ref, sums1_ref, sums2_ref, out_ref, turn_v):
    row_of = lax.broadcasted_iota(jnp.int32, (8, SPAN), 0)
    lines = []
    for head in range(offsets_ref.shape[1]):
        eighth = offsets_ref[0, head] + offsets_ref[1, head]
        for size in (4, 2, 1):
            eighth = jnp.where((row_of & size) != 0, pltpu.roll(eighth, SPAN - size, 1), eighth)
        lines.append(jnp.sum(eighth, 0, keepdims=True))
    lines += [jnp.zeros((1, SPAN), F32)] * (NORM_LANE - len(lines))
    sums = pltpu.roll(jnp.concatenate(lines, 0), SPAN - 1, 1)
    span = buckets_ref.shape[1]
    buckets, depth = out_ref.shape[0] // 3, out_ref.shape[0] // ways
    share = buckets // ways
    bucket_ids = lax.broadcasted_iota(jnp.int32, (buckets, span), 0)
    hot = (bucket_ids == buckets_ref[...]).astype(F32)
    table = lax.dot_general(
        hot, sums[:, :span], (((1,), (1,)), ((), ())), precision=highest, preferred_element_type=F32
    ).astype(BF16)
    turn_v[...] = jnp.zeros(turn_v.shape, F32)
    for i, ref in enumerate((sums1_ref, sums2_ref)):
        at = NORM_LANE + 2 * i
        turn_v[at : at + 2, :] = ref[0, 0:2, :] + ref[1, 0:2, :]
    out_ref[...] = turn_v[...].T.astype(BF16)
    for i in range(ways):
        out_ref[i * depth : i * depth + share, 0:NORM_LANE] = table[i * share : (i + 1) * share, :]


def packed(ways, buckets, offset_buckets, kept):
    width = kept["sums1"].shape[2]
    depth, share = width // ways, buckets // ways
    arrays = (offset_buckets, kept["offsets"], kept["sums1"], kept["sums2"])
    if depth % 16 == 0 and share % 16 == 0 and 3 * buckets == width:
        rows = pl.pallas_call(
            functools.partial(pack_kernel, ways),
            out_shape=jax.ShapeDtypeStruct((width, LANES), BF16),
            in_specs=[VMEM] * len(arrays),
            out_specs=VMEM,
            scratch_shapes=[pltpu.VMEM((LANES, width), F32)],
            compiler_params=pltpu.CompilerParams(vmem_limit_bytes=SMALL_VMEM_BYTES),
            name="pack",
        )(*arrays)
        return rows.reshape(ways, depth, LANES)
    eighths = jnp.sum(kept["offsets"], 0)
    lines = sum(jnp.roll(eighths[:, i, :], -i, 1) for i in range(8))[:, 1:]
    hot = (offset_buckets[0][None, :] == jnp.arange(buckets, dtype=jnp.int32)[:, None]).astype(F32)
    table = jnp.dot(hot, lines.T, precision=highest).reshape(ways, share, -1)
    table = jnp.pad(table, ((0, 0), (0, depth - share), (0, NORM_LANE - table.shape[2])))
    norms = jnp.concatenate([jnp.sum(kept[name], 0)[:2] for name in ("sums1", "sums2")], 0)
    norms = norms.T.reshape(ways, depth, 4)
    rows = jnp.concatenate([table, norms], 2)
    return jnp.pad(rows, ((0, 0), (0, 0), (0, LANES - rows.shape[2]))).astype(BF16)


def halve_kernel(bits, counts, after_count, through_count, me_ref, *refs):
    used = sum(counts) + len(counts)
    outs = refs[used + after_count + through_count :]
    for i, count in enumerate(counts):
        kept_refs, arrived_ref = refs[:count], refs[count]
        refs = refs[count + 1 :]
        send_ref, rest_ref = outs[2 * i : 2 * i + 2]
        mine = (me_ref[0] >> bits[i]) & 1

        def total(which):
            kept = [
                (ref[0, which, 0, 0] if len(ref.shape) == 6 else ref[0, which, 0]).astype(F32)
                for ref in kept_refs
            ]
            return jnp.concatenate(kept, 1) + arrived_ref[0, which, 0].astype(F32)

        send_ref[0, 0] = total(1 - mine).astype(send_ref.dtype)
        rest_ref[0, 0] = total(mine)


def join_kernel(kept_near, arrived_near, kept_far, arrived_far, out_ref, qkv_ref, table_ref, *refs):
    norm_refs, turn_v = refs[:-1], refs[-1]
    near = kept_near[...] + arrived_near[...].astype(F32)
    wide = out_ref.shape[1]
    share = qkv_ref.shape[1] - kept_far.shape[1]
    out_ref[...] = near[:, :wide]
    qkv_ref[:, :share] = near[:, wide : wide + share]
    qkv_ref[:, share:] = kept_far[...] + arrived_far[...].astype(F32)
    small = near[:, wide + share :]
    table_ref[...] = small[: table_ref.shape[0], : table_ref.shape[1]]
    turn_v[...] = jnp.zeros(turn_v.shape, F32)
    turn_v[: small.shape[0], :] = small
    turned = turn_v[...].T
    for i, ref in enumerate(norm_refs):
        ref[...] = turned[NORM_LANE + i : NORM_LANE + i + 1, : ref.shape[1]]


class Share:
    def __init__(self, parts, order):
        self.parts = parts
        self.order = order[1:]
        self.left = sorted(order)
        self.depth = parts[0].shape[1]
        self.wide = sum(part.shape[2] for part in parts)
        self.mine = None
        self.swap(order[0], self.of_core(1 - (lax.axis_index("dp") & 1)))

    def of_core(self, core):
        halves = [
            lax.dynamic_index_in_dim(
                part.reshape((part.shape[0] // 2, 2) + part.shape[1:]), core, 1, keepdims=False
            )
            for part in self.parts
        ]
        return halves[0] if len(halves) == 1 else jnp.concatenate(halves, 2)

    def swap(self, bit, theirs):
        count = lax.axis_size("dp")
        self.left.remove(bit)
        self.sent = theirs
        self.arrived = lax.ppermute(theirs, "dp", [(i, i ^ (1 << bit)) for i in range(count)])

    def total(self):
        kept = self.of_core(lax.axis_index("dp") & 1) if self.mine is None else self.mine
        return kept.astype(F32) + self.arrived.astype(F32)

    def split_at(self):
        bit = self.order[0]
        axis = len(self.left) - 1 - self.left.index(bit)
        return bit, 2**axis, 2 ** (len(self.left) - 1 - axis)

    def halve(self):
        bit, above, below = self.split_at()
        self.order = self.order[1:]
        split = self.total().reshape(above, 2, below, self.depth, self.wide)
        here = (lax.axis_index("dp") >> bit) & 1
        theirs = lax.dynamic_index_in_dim(split, 1 - here, 1, keepdims=False).astype(BF16)
        mine = lax.dynamic_index_in_dim(split, here, 1, keepdims=False)
        self.mine = mine.reshape(-1, self.depth, self.wide)
        self.swap(bit, theirs.reshape(-1, self.depth, self.wide))


def halve_all(me, shares, afters=(), through=()):
    if any(share.depth % 16 for share in shares):
        for share in shares:
            share.halve()
        return through
    ins, in_specs, outs, out_specs, bits, counts = [], [], [], [], [], []
    for share in shares:
        bit, above, below = share.split_at()
        bits.append(bit)

        def halves(wide, b=below):
            return pl.BlockSpec((1, 2, 1, share.depth, wide), lambda i, me: (i // b, 0, i % b, 0, 0))

        if share.mine is None:
            counts.append(len(share.parts))
            for part in share.parts:
                wide = part.shape[2]
                ins.append(part.reshape(above, 2, below, 2, share.depth, wide))
                in_specs.append(
                    pl.BlockSpec(
                        (1, 2, 1, 1, share.depth, wide),
                        lambda i, me, b=below: (i // b, 0, i % b, me[0] & 1, 0, 0),
                    )
                )
        else:
            counts.append(1)
            ins.append(share.mine.reshape(above, 2, below, share.depth, share.wide))
            in_specs.append(halves(share.wide))
        ins.append(share.arrived.reshape(above, 2, below, share.depth, share.wide))
        in_specs.append(halves(share.wide))
        outs += [
            jax.ShapeDtypeStruct((above, below, share.depth, share.wide), kind) for kind in (BF16, F32)
        ]
        out_specs += [
            pl.BlockSpec((1, 1, share.depth, share.wide), lambda i, me, b=below: (i // b, i % b, 0, 0))
        ] * 2
        steps = above * below
    results = pl.pallas_call(
        functools.partial(halve_kernel, tuple(bits), tuple(counts), len(afters), len(through)),
        grid_spec=pltpu.PrefetchScalarGridSpec(
            num_scalar_prefetch=1,
            grid=(steps,),
            in_specs=in_specs + [ANY] * (len(afters) + len(through)),
            out_specs=out_specs + [ANY] * len(through),
        ),
        out_shape=outs + [jax.ShapeDtypeStruct(array.shape, array.dtype) for array in through],
        input_output_aliases={
            1 + len(ins) + len(afters) + i: len(outs) + i for i in range(len(through))
        },
        compiler_params=pltpu.CompilerParams(vmem_limit_bytes=VMEM_BYTES if through else SMALL_VMEM_BYTES),
        name="halve",
    )(me, *ins, *afters, *through)
    for i, share in enumerate(shares):
        share.order = share.order[1:]
        share.mine = results[2 * i + 1].reshape(-1, share.depth, share.wide)
        share.swap(bits[i], results[2 * i].reshape(-1, share.depth, share.wide))
    return results[len(outs) :]


def joined(near, far, width, table_shape):
    parts = [x[0] for share in (near, far) for x in (share.mine, share.arrived)]
    shapes = [(near.depth, width), (near.depth, near.wide + far.wide - width - LANES), table_shape]
    shapes += [(1, near.depth)] * 4
    return pl.pallas_call(
        join_kernel,
        out_shape=[jax.ShapeDtypeStruct(dims, F32) for dims in shapes],
        in_specs=[VMEM] * len(parts),
        out_specs=[VMEM] * len(shapes),
        scratch_shapes=[pltpu.VMEM((LANES, LANES), F32)],
        compiler_params=pltpu.CompilerParams(vmem_limit_bytes=SMALL_VMEM_BYTES),
        name="join",
    )(*parts)


def passed_along(x, axis, by):
    length = lax.axis_size(axis)
    pairs = [(i, i + by) for i in range(length) if 0 <= i + by < length]
    return lax.ppermute(x, axis, pairs)


def shards(
    hidden_in, out_grad, qkv_weight, out_weight, rel_table, norm1_gain, norm1_bias,
    up_weight, down_weight, norm2_gain, norm2_bias, seg_ids, pad_mask, rel_buckets,
):
    phase = lax.axis_index("phase").astype(jnp.int32).reshape(1)
    ways = lax.axis_size("dp")
    slots, width = hidden_in.shape
    inner = up_weight.shape[2]
    buckets, heads = rel_table.shape[1:]

    def shape(dims, kind):
        return jax.ShapeDtypeStruct(dims, kind)

    def whole(array):
        return pl.BlockSpec(array.shape, lambda i: (0,) * array.ndim)

    starts = (rel_buckets[None, :], rel_table, seg_ids[None, :], pad_mask[None, :])
    bias, shut = pl.pallas_call(
        bias_kernel,
        grid=(heads // 2,),
        out_shape=[shape((heads, TILE, SPAN), F32), shape((MICRO, BLOCK // TILE, BLOCK), F32)],
        in_specs=[whole(array) for array in starts],
        out_specs=[
            pl.BlockSpec((2, TILE, SPAN), lambda i: (i, 0, 0)),
            pl.BlockSpec((MICRO, BLOCK // TILE, BLOCK), lambda i: (0, 0, 0)),
        ],
        scratch_shapes=[pltpu.VMEM((heads, SPAN), F32)],
        compiler_params=pltpu.CompilerParams(vmem_limit_bytes=VMEM_BYTES),
        name="pair_bias",
    )(*starts)

    rows_of = {
        "xin": (width, BF16), "qkv": (3 * width, BF16), "ctx": (width, BF16), "form1": (width, F32),
        "scale1": (1, F32), "low1": (width, BF16), "slope": (inner, BF16), "act": (inner, BF16),
        "form2": (width, F32), "scale2": (1, F32), "out": (width, BF16),
        "outer_low": (width, BF16), "hidden_low": (inner, BF16), "residual_low": (width, BF16),
        "projected": (3 * width, BF16), "input_grad": (width, BF16),
    }
    kept_shapes = [
        shape((slots, rows_of[name][0]), rows_of[name][1])
        if name in rows_of
        else {
            "weights": shape((MICRO, heads, BLOCK, BLOCK), BF16),
            "sums1": shape((MICRO, 8, width), F32),
            "sums2": shape((MICRO, 8, width), F32),
            "residual": shape((BLOCK, width), F32),
            "offsets": shape((MICRO, heads, 8, SPAN), F32),
        }[name]
        for name in KEPT
    ]
    in_forward = ("qkv", "ctx", "form1", "scale1", "low1", "slope", "act", "form2", "scale2", "out")
    scratch = {f"{name}_v": ((BLOCK, rows_of[name][0]), rows_of[name][1]) for name in in_forward}
    scratch |= {
        name: ((BLOCK, width), BF16) for name in ("x_v", "g_v", "outer_v", "residual_low_v", "dctx_v", "grad_v")
    }
    scratch |= {
        "weights_v": ((heads, BLOCK, BLOCK), BF16), "acc_v": ((BLOCK, width), F32), "square_v": ((2, BLOCK, BLOCK), F32),
        "top_v": ((2, BLOCK, 1), F32), "bias_v": ((heads, TILE, SPAN), F32), "sums1_v": ((8, width), F32), "sums2_v": ((8, width), F32),
        "wqkv_v": ((width, 3 * width), BF16), "wout_v": ((width, width), BF16), "wup_v": ((width, inner), BF16),
        "wdown_v": ((inner, width), BF16), "fold_v": ((2, TILE, SPAN), F32), "eighth_v": ((heads, 8, SPAN), F32),
        "half_v": ((2, BLOCK, BLOCK), BF16), "part_v": ((BLOCK, LANES), F32),
    }

    def step(work, phase_on, block, received, kept, afters=()):
        values = (
            phase, hidden_in, received, out_grad, bias, shut, norm1_gain, norm1_bias, norm2_gain, norm2_bias,
            qkv_weight, out_weight, up_weight, down_weight,
        )
        in_place = None if kept is None else [kept[name] for name in KEPT]
        return layer_step(work, phase_on, block, values, list(afters), in_place, kept_shapes, scratch)

    kept, sent = step("forward", 0, 0, hidden_in, None)
    first = passed_along(sent, "phase", 1)
    kept, sent = step("forward", 0, 1, hidden_in, kept)
    second = passed_along(sent, "phase", 1)
    kept, sent = step("both", 1, 0, first, kept)
    first_back = passed_along(sent, "phase", -1)
    kept, sent = step("both", 1, 1, second, kept)
    second_back = passed_along(sent, "phase", -1)
    kept, _ = step("back", 0, 0, first_back, kept)
    kept, _ = step("norm_back", 0, 1, second_back, kept)

    bits = ways.bit_length() - 1
    near_first = list(range(bits))
    far_first = [0] + list(range(2, bits)) + [1] if bits > 1 else near_first
    me = lax.axis_index("dp").astype(jnp.int32).reshape(1)

    def weight_grad(left, right):
        product = dot_tn(left, right).astype(BF16)
        return product.reshape(ways, product.shape[0] // ways, product.shape[1])

    down = Share([weight_grad(kept["act"], kept["outer_low"])], far_first)
    kept, _ = step("ffn_back", 0, 1, hidden_in, kept, [down.sent])
    up = Share([weight_grad(kept["low1"], kept["hidden_low"])], near_first)
    out_part = weight_grad(kept["ctx"], kept["residual_low"])
    halve_all(me, [down])
    halve_all(me, [up])
    kept, _ = step("attn_back", 0, 1, hidden_in, kept, [down.sent, up.sent])
    (projected,) = halve_all(me, [down], through=[kept["projected"]])
    far = Share([weight_grad(kept["xin"], projected[:, width:])], far_first)
    near_part = weight_grad(kept["xin"], projected[:, :width])
    near = Share([out_part, near_part, packed(ways, buckets, starts[0], kept)], near_first)
    halve_all(me, [up], [down.sent])
    halve_all(me, [near, far], [up.sent])
    halve_all(me, [down])
    halve_all(me, [up])
    halve_all(me, [near, far], [down.sent, up.sent])
    while down.order:
        halve_all(me, [down, up])
    while near.order:
        halve_all(me, [near, far])
    down_share = down.total()[0]
    up_share = up.total()[0]
    out_share, qkv_share, table_share, *norm_shares = joined(near, far, width, (buckets // ways, heads))
    return (
        kept["out"][None],
        kept["input_grad"][None],
        qkv_share[None],
        out_share[None],
        table_share[None],
        norm_shares[0],
        norm_shares[1],
        up_share[None],
        down_share[None],
        norm_shares[2],
        norm_shares[3],
    )


def solution(mesh):
    return jax.shard_map(
        shards,
        mesh=mesh,
        in_specs=(
            P("dp", None),
            P("dp", None),
            P("phase", None, None),
            P("phase", None, None),
            P("phase", None, None),
            P("phase", None),
            P("phase", None),
            P("phase", None, None),
            P("phase", None, None),
            P("phase", None),
            P("phase", None),
            P("dp"),
            P("dp"),
            P(),
        ),
        out_specs=(
            P("phase", "dp", None),
            P("phase", "dp", None),
            P("phase", "dp", None),
            P("phase", "dp", None),
            P("phase", "dp", None),
            P("phase", "dp"),
            P("phase", "dp"),
            P("phase", "dp", None),
            P("phase", "dp", None),
            P("phase", "dp"),
            P("phase", "dp"),
        ),
        check_vma=False,
    )
```

```python
import functools

import jax
import jax.numpy as jnp
from jax import lax
from jax.experimental import pallas as pl
from jax.experimental.pallas import tpu as pltpu
from jax.sharding import PartitionSpec as P

BLOCK = 512
MICRO = 2
TILE = 128
LANES = 128
CHUNK = 512
SPAN = 2 * BLOCK
VMEM_BYTES = 58 * 1024 * 1024
SMALL_VMEM_BYTES = 20 * 1024 * 1024
NORM_LANE = 16

norm_eps = 1e-05
mask_fill = -1000000000.0
score_scale = 0.125
inv_root_two = 0.7071067811865476
inv_root_tau = 0.3989422804014327
log2_e = 1.4426950408889634
highest = lax.Precision.HIGHEST

F32 = jnp.float32
BF16 = jnp.bfloat16
ANY = pl.BlockSpec(memory_space=pl.ANY)
VMEM = pl.BlockSpec(memory_space=pltpu.VMEM)
QUICK = pl.CostEstimate(flops=1, bytes_accessed=1, transcendentals=0)
SMEM = pl.BlockSpec(memory_space=pltpu.SMEM)


def dot_nn(a, b):
    return lax.dot_general(a, b, (((1,), (0,)), ((), ())), preferred_element_type=F32)


def dot_nt(a, b):
    return lax.dot_general(a, b, (((1,), (1,)), ((), ())), preferred_element_type=F32)


def dot_tn(a, b):
    return lax.dot_general(a, b, (((0,), (0,)), ((), ())), preferred_element_type=F32)


def row_mean(rows):
    return jnp.sum(rows, -1, keepdims=True) * (1.0 / rows.shape[-1])


def normal_parts(residual):
    centred = residual - row_mean(residual)
    inv_scale = lax.rsqrt(row_mean(centred * centred) + norm_eps)
    return centred * inv_scale, inv_scale


def norm_backward(grad_rows, normal_form, inv_scale):
    first = row_mean(grad_rows)
    second = row_mean(grad_rows * normal_form)
    return inv_scale * (grad_rows - first - normal_form * second)


def gelu_parts(hidden):
    share = 0.5 + 0.5 * lax.erf(hidden * inv_root_two)
    bell = jnp.exp2(hidden * hidden * (-0.5 * log2_e))
    return hidden * share, share + hidden * bell * inv_root_tau


def half_mask(which, shape):
    lane = lax.broadcasted_iota(jnp.int32, shape, 1)
    return (lane < LANES // 2) if which == 0 else (lane >= LANES // 2)


class Copies:
    def __init__(self, sems):
        self.sems = sems
        self.used = 0
        self.stores = []

    def take(self, count=1):
        self.used += count
        return self.used - count

    def load(self, source, target):
        copy = pltpu.make_async_copy(source, target, self.sems.at[self.take()])
        copy.start()
        return copy

    def store(self, source, target, when=True):
        if when:
            self.stores.append(self.load(source, target))

    def finish(self):
        for copy in self.stores:
            copy.wait()


KEPT = (
    "xin", "qkv", "weights", "ctx", "form1", "scale1", "low1", "slope", "act", "form2", "scale2", "out",
    "bias", "outer_low", "hidden_low", "residual_low", "sums1", "sums2", "residual", "projected", "offsets", "input_grad",
)
INS = (
    "phase", "segments", "hidden_in", "received", "out_grad", "table", "padding", "buckets",
    "gain1", "shift1", "gain2", "shift2",
    "wqkv", "wout", "wup", "wdown",
)


class Layer:
    def __init__(self, refs):
        self.__dict__.update(refs)
        self.copies = Copies(self.sems)
        self.width = self.hidden_in.shape[1]
        self.inner = self.wup.shape[2]
        self.pairs = self.width // LANES
        self.stages = self.inner // (2 * CHUNK)
        self.pair_sems = self.copies.take(self.pairs)
        self.chunk_sems = [self.copies.take(self.stages) for _ in range(3)]

    def lanes_of(self, pair, part):
        return pl.ds(pl.multiple_of(part * self.width + pair * LANES, LANES), LANES)

    def stage(self, i):
        return pl.ds(pl.multiple_of(i * 2 * CHUNK, 2 * CHUNK), 2 * CHUNK)

    def build_bias(self):
        span = self.buckets.shape[1]
        bucket_ids = lax.broadcasted_iota(jnp.int32, (self.table.shape[1], span), 0)
        hot = (bucket_ids == self.buckets[...]).astype(F32)
        values = lax.dot_general(
            self.table[0], hot, (((0,), (0,)), ((), ())), precision=highest, preferred_element_type=F32
        )
        self.values_v[:, :span] = values
        self.values_v[:, span:] = jnp.zeros((values.shape[0], SPAN - span), F32)

        def one_head(head, carry):
            wide = jnp.broadcast_to(self.values_v[pl.ds(head, 1), :], (TILE, SPAN))
            self.bias_v[head] = pltpu.roll(wide, 1, 1, stride=1, stride_axis=0)
            return carry

        lax.fori_loop(0, values.shape[0], one_head, 0)
        self.copies.store(self.bias_v, self.bias)


    def rows(self, block):
        return pl.ds(block * BLOCK, BLOCK)

    def forward(self, block, keep, built):
        copies = self.copies
        rows = self.rows(block)
        load_x = copies.load(self.hidden_in.at[rows] if keep else self.received, self.x_v)
        width = self.width
        loads = [
            copies.load(self.wqkv.at[0, :, pl.ds(c, width)], self.wqkv_v.at[:, pl.ds(c, width)])
            for c in range(0, 3 * width, width)
        ]
        if not built:
            self.build_bias()
        load_x.wait()

        def load_bias(pair):
            heads = pl.ds(2 * pair, 2)
            return pltpu.make_async_copy(self.bias.at[heads], self.bias_v.at[heads], self.sems.at[self.pair_sems + pair])

        for i, c in enumerate(range(0, 3 * width, width)):
            loads[i].wait()
            if i == 2 and built:
                for pair in range(self.pairs):
                    load_bias(pair).start()
            self.qkv_v[:, c : c + width] = dot_nn(self.x_v[...], self.wqkv_v[:, c : c + width]).astype(BF16)
        copies.store(self.x_v, self.xin.at[rows])
        copies.store(self.qkv_v, self.qkv.at[rows], keep)
        weights_sem = self.sems.at[copies.take()]
        later_loads = [
            pltpu.make_async_copy(source.at[0], target, self.sems.at[copies.take()])
            for source, target in ((self.wout, self.wout_v), (self.wup, self.wup_v), (self.wdown, self.wdown_v))
        ]

        def own(pair, part, which):
            both = self.qkv_v[:, self.lanes_of(pair, part)]
            return jnp.where(half_mask(which, both.shape), both, jnp.zeros_like(both))

        single = self.segments[block * BLOCK + TILE] == self.segments[block * BLOCK]
        padding = self.padding[:, block * BLOCK : (block + 1) * BLOCK]
        tile_of = lax.broadcasted_iota(jnp.int32, (1, BLOCK), 1) // TILE
        shut = [
            jnp.where((padding == 1) & (single | (tile_of == tile)), 0.0, mask_fill) for tile in range(BLOCK // TILE)
        ]
        row_id = lax.broadcasted_iota(jnp.int32, (TILE, TILE), 0)
        diagonal = row_id == lax.broadcasted_iota(jnp.int32, (TILE, TILE), 1)

        def bias_rows(head, tile):
            at = BLOCK - tile * TILE
            rows = self.bias_v[head, :, at : at + BLOCK]
            masked = rows + shut[tile]
            own = slice(tile * TILE, (tile + 1) * TILE)
            parts = [masked[:, : own.start], jnp.where(diagonal, rows[:, own], masked[:, own]), masked[:, own.stop :]]
            return jnp.concatenate([part for part in parts if part.shape[1]], 1)

        def weigh(pair, which):
            head = 2 * pair + which
            k_own = own(pair, 1, which)
            for r in range(0, BLOCK, 2 * TILE):
                q_rows = self.qkv_v[r : r + 2 * TILE, self.lanes_of(pair, 0)] * jnp.asarray(score_scale, BF16)
                tiles = [bias_rows(head, tile) for tile in range(r // TILE, r // TILE + 2)]
                logits = dot_nt(q_rows, k_own) + jnp.concatenate(tiles, 0)
                raised = jnp.exp(logits - jnp.max(logits, -1, keepdims=True))
                share = pl.reciprocal(jnp.sum(raised, -1, keepdims=True), approx=True)
                self.weights_v[head, r : r + 2 * TILE, :] = (raised * share).astype(BF16)

        def head_pair(pair, carry):
            if built:
                load_bias(pair).wait()

            @pl.when(pair == 0)
            def _():
                for load in later_loads:
                    load.start()

            weigh(pair, 0)
            context = dot_nn(self.weights_v[2 * pair], own(pair, 2, 0))
            weigh(pair, 1)
            context += dot_nn(self.weights_v[2 * pair + 1], own(pair, 2, 1))
            self.ctx_v[:, self.lanes_of(pair, 0)] = context.astype(BF16)
            if keep:
                heads = pl.ds(2 * pair, 2)
                pltpu.make_async_copy(self.weights_v.at[heads], self.weights.at[block, heads], weights_sem).start()
            return carry

        lax.fori_loop(0, self.pairs, head_pair, 0)
        if keep:
            copies.stores.append(pltpu.make_async_copy(self.weights_v, self.weights.at[block], weights_sem))
        copies.store(self.ctx_v, self.ctx.at[rows])
        load_out, load_up, load_down = later_loads
        load_out.wait()
        self.acc_v[...] = dot_nn(self.ctx_v[...], self.wout_v[...])
        for r in range(0, BLOCK, 64):
            tile = slice(r, r + 64)
            form, scale = normal_parts(self.acc_v[tile, :] + self.x_v[tile, :].astype(F32))
            normed = form * self.gain1[...] + self.shift1[...]
            self.form1_v[tile, :] = form
            self.scale1_v[tile, :] = scale
            self.acc_v[tile, :] = normed
            self.low1_v[tile, :] = normed.astype(BF16)
        copies.store(self.form1_v, self.form1.at[rows], keep)
        copies.store(self.scale1_v, self.scale1.at[rows], keep)
        copies.store(self.low1_v, self.low1.at[rows])
        load_up.wait()
        load_down.wait()
        act_sem = self.sems.at[copies.take()]
        slope_sem = self.sems.at[copies.take()]

        def two_chunks(i, carry):
            span = self.stage(i)
            active, grade = gelu_parts(dot_nn(self.low1_v[...], self.wup_v[:, span]))
            active = active.astype(BF16)
            self.act_v[:, span] = active
            self.slope_v[:, span] = grade.astype(BF16)
            self.acc_v[...] += dot_nn(active, self.wdown_v[span, :])
            pltpu.make_async_copy(self.act_v.at[:, span], self.act.at[rows, span], act_sem).start()
            if keep:
                pltpu.make_async_copy(self.slope_v.at[:, span], self.slope.at[rows, span], slope_sem).start()
            return carry

        lax.fori_loop(0, self.stages, two_chunks, 0)
        copies.stores.append(pltpu.make_async_copy(self.act_v, self.act.at[rows], act_sem))
        if keep:
            copies.stores.append(pltpu.make_async_copy(self.slope_v, self.slope.at[rows], slope_sem))
        for r in range(0, BLOCK, 64):
            tile = slice(r, r + 64)
            form, scale = normal_parts(self.acc_v[tile, :])
            self.form2_v[tile, :] = form
            self.scale2_v[tile, :] = scale
            self.out_v[tile, :] = (form * self.gain2[...] + self.shift2[...]).astype(BF16)
        copies.store(self.out_v, self.send, keep)
        copies.store(self.out_v, self.out.at[rows])
        copies.store(self.form2_v, self.form2.at[rows], keep)
        copies.store(self.scale2_v, self.scale2.at[rows], keep)


    def chunk_loads(self, i, rows):
        span = self.stage(i)
        return [
            pltpu.make_async_copy(source, target, self.sems.at[self.chunk_sems[k] + i])
            for k, (source, target) in enumerate(
                (
                    (self.wdown.at[0, span], self.wdown_v.at[span]),
                    (self.slope.at[rows, span], self.slope_v.at[:, span]),
                    (self.wup.at[0, :, span], self.wup_v.at[:, span]),
                )
            )
        ]

    def norm_sums(self, source, form_ref, sums_ref):
        gain_sum = jnp.zeros((1, self.width), F32)
        shift_sum = jnp.zeros((1, self.width), F32)
        for r in range(0, BLOCK, 64):
            grad_rows, form = source[r : r + 64, :].astype(F32), form_ref[r : r + 64, :]
            gain_sum += jnp.sum(grad_rows * form, 0, keepdims=True)
            shift_sum += jnp.sum(grad_rows, 0, keepdims=True)
        sums_ref[...] = jnp.zeros(sums_ref.shape, F32)
        sums_ref[0:1, :] = gain_sum
        sums_ref[1:2, :] = shift_sum

    def norm_back(self, block):
        for r in range(0, BLOCK, 64):
            tile = slice(r, r + 64)
            grad_rows = self.g_v[tile, :].astype(F32) * self.gain2[...]
            grad_outer = norm_backward(grad_rows, self.form2_v[tile, :], self.scale2_v[tile, :])
            self.acc_v[tile, :] = grad_outer
            self.outer_v[tile, :] = grad_outer.astype(BF16)
        self.copies.store(self.outer_v, self.outer_low.at[self.rows(block)])

    def norm_sums_2(self, block):
        self.norm_sums(self.g_v, self.form2_v, self.sums2_v)
        self.copies.store(self.sums2_v, self.sums2.at[block])

    def ffn_back(self, block, staged=False, middle_loads=()):
        copies = self.copies
        rows = self.rows(block)
        hidden_sem = self.sems.at[copies.take()]

        def two_chunks(i, carry):
            span = self.stage(i)
            if staged:
                load_down, load_slope, load_up = self.chunk_loads(i, rows)
                load_down.wait()
                load_slope.wait()
            grad_active = dot_nt(self.outer_v[...], self.wdown_v[span, :])
            hidden = (grad_active * self.slope_v[:, span].astype(F32)).astype(BF16)
            self.slope_v[:, span] = hidden
            if staged:
                load_up.wait()

                @pl.when(i + 2 < self.stages)
                def _():
                    for load in self.chunk_loads(i + 2, rows):
                        load.start()

            self.acc_v[...] += dot_nt(hidden, self.wup_v[:, span])
            pltpu.make_async_copy(self.slope_v.at[:, span], self.hidden_low.at[rows, span], hidden_sem).start()
            return carry

        lax.fori_loop(0, self.stages, two_chunks, 0)
        copies.stores.append(pltpu.make_async_copy(self.slope_v, self.hidden_low.at[rows], hidden_sem))
        for load in middle_loads:
            load.wait()
        self.norm_sums(self.acc_v, self.form1_v, self.sums1_v)
        for r in range(0, BLOCK, 64):
            tile = slice(r, r + 64)
            grad_residual = norm_backward(
                self.acc_v[tile, :] * self.gain1[...], self.form1_v[tile, :], self.scale1_v[tile, :]
            )
            self.acc_v[tile, :] = grad_residual
            self.residual_low_v[tile, :] = grad_residual.astype(BF16)
        copies.store(self.residual_low_v, self.residual_low.at[rows])
        copies.store(self.sums1_v, self.sums1.at[block])

    def attn_back(self, block, load_pair=None, load_in=()):
        copies = self.copies
        rows = self.rows(block)
        self.dctx_v[...] = dot_nt(self.residual_low_v[...], self.wout_v[...]).astype(BF16)
        self.fold_v[:, :, 0:TILE] = jnp.zeros((2, TILE, TILE), F32)

        def head_pair(pair, carry):
            def lanes_of(part):
                return self.lanes_of(pair, part)

            q_pair, k_pair, v_pair = (self.qkv_v[:, lanes_of(part)] for part in range(3))
            grad_pair = self.dctx_v[:, lanes_of(0)]
            crossed = grad_pair.astype(F32) * self.ctx_v[:, lanes_of(0)].astype(F32)
            if load_pair is not None:
                load_pair(pair).wait()
            masks = [half_mask(which, k_pair.shape) for which in range(2)]

            def own(both, which):
                return jnp.where(masks[which], both, jnp.zeros_like(both))

            for which in range(2):
                self.square_v[which] = dot_nt(grad_pair, own(v_pair, which))
            q_grad = k_grad = v_grad = 0.0
            for which in range(2):
                head = 2 * pair + which
                delta = jnp.sum(own(crossed, which), -1, keepdims=True)
                for r in range(0, BLOCK, 64):
                    tile = slice(r, r + 64)
                    score_grad = (
                        self.weights_v[head, tile, :].astype(F32) * (self.square_v[which, tile, :] - delta[tile, :])
                    ).astype(BF16)
                    self.half_v[which, tile, :] = score_grad
                    at = BLOCK - r // TILE * TILE
                    wide = score_grad.astype(F32)
                    half = slice(r % TILE, r % TILE + 64)
                    if r < TILE:
                        self.fold_v[which, half, at : at + BLOCK] = wide
                    else:
                        self.fold_v[which, half, at : at + TILE] = wide[:, :TILE]
                        self.fold_v[which, half, at + TILE : at + BLOCK] += wide[:, TILE:]
                v_grad += dot_tn(self.weights_v[head], own(grad_pair, which))
                q_grad += dot_nn(self.half_v[which], own(k_pair, which))
                k_grad += dot_tn(self.half_v[which], own(q_pair, which))
                folded = self.fold_v[which]
                size = TILE // 2
                while size >= 8:
                    folded = folded[:size, :] + pltpu.roll(folded[size:, :], SPAN - size, 1)
                    size //= 2
                self.eighth_v[head] = folded
            self.qkv_v[:, lanes_of(0)] = (q_grad * score_scale).astype(BF16)
            self.qkv_v[:, lanes_of(1)] = (k_grad * score_scale).astype(BF16)
            self.qkv_v[:, lanes_of(2)] = v_grad.astype(BF16)
            return carry

        lax.fori_loop(0, self.pairs, head_pair, 0)
        copies.store(self.eighth_v, self.offsets.at[block])
        copies.store(self.qkv_v, self.projected.at[rows])
        for load in load_in:
            load.wait()
        self.grad_v[...] = (self.acc_v[...] + dot_nt(self.qkv_v[...], self.wqkv_v[...])).astype(BF16)
        copies.store(self.grad_v, self.send)
        copies.store(self.grad_v, self.input_grad.at[rows])


    def do_forward(self, block):
        self.forward(block, True, block > 0)

    def do_bias(self, block):
        self.build_bias()

    def do_both(self, block):
        load = self.copies.load(self.out_grad.at[self.rows(block)], self.g_v)
        self.forward(block, False, True)
        load.wait()
        self.norm_back(block)
        self.ffn_back(block)
        self.norm_sums_2(block)
        self.attn_back(block)

    def do_back(self, block):
        rows = self.rows(block)
        loads = [
            self.copies.load(source, target)
            for source, target in (
                (self.received, self.g_v),
                (self.form2.at[rows], self.form2_v),
                (self.scale2.at[rows], self.scale2_v),
                (self.slope.at[rows], self.slope_v),
                (self.wdown.at[0], self.wdown_v),
                (self.wup.at[0], self.wup_v),
                (self.form1.at[rows], self.form1_v),
                (self.scale1.at[rows], self.scale1_v),
                (self.qkv.at[rows], self.qkv_v),
                (self.weights.at[block], self.weights_v),
                (self.ctx.at[rows], self.ctx_v),
                (self.wout.at[0], self.wout_v),
                (self.wqkv.at[0], self.wqkv_v),
            )
        ]
        for load in loads:
            load.wait()
        self.norm_back(block)
        self.ffn_back(block)
        self.norm_sums_2(block)
        self.attn_back(block)

    def do_norm_back(self, block):
        rows = self.rows(block)
        loads = [
            self.copies.load(source, target)
            for source, target in (
                (self.received, self.g_v),
                (self.form2.at[rows], self.form2_v),
                (self.scale2.at[rows], self.scale2_v),
            )
        ]
        for load in loads:
            load.wait()
        self.norm_back(block)
        self.copies.store(self.acc_v, self.residual)
        self.norm_sums_2(block)

    def do_ffn_back(self, block):
        rows = self.rows(block)
        loads = [
            self.copies.load(self.outer_low.at[rows], self.outer_v),
            self.copies.load(self.residual, self.acc_v),
        ]
        for i in range(min(2, self.stages)):
            for load in self.chunk_loads(i, rows):
                load.start()
        for load in loads:
            load.wait()
        middle = [
            self.copies.load(self.form1.at[rows], self.form1_v),
            self.copies.load(self.scale1.at[rows], self.scale1_v),
        ]
        self.ffn_back(block, True, middle)
        self.copies.store(self.acc_v, self.residual)

    def do_attn_back(self, block):
        rows = self.rows(block)
        loads = [
            self.copies.load(source, target)
            for source, target in (
                (self.residual_low.at[rows], self.residual_low_v),
                (self.wout.at[0], self.wout_v),
                (self.qkv.at[rows], self.qkv_v),
                (self.ctx.at[rows], self.ctx_v),
            )
        ]

        def load_pair(pair):
            heads = pl.ds(2 * pair, 2)
            return pltpu.make_async_copy(
                self.weights.at[block, heads], self.weights_v.at[heads], self.sems.at[self.pair_sems + pair]
            )

        for pair in range(self.pairs):
            load_pair(pair).start()
        for load in loads:
            load.wait()
        last = [
            self.copies.load(self.wqkv.at[0], self.wqkv_v),
            self.copies.load(self.residual, self.acc_v),
        ]
        self.attn_back(block, load_pair, last)


def layer_kernel(work, phase_on, block, ins, outs, scratch, after_count, kept_count, *refs):
    refs_in, refs = refs[: len(ins)], refs[len(ins) + after_count + kept_count :]
    named = dict(zip(ins, refs_in)) | dict(zip(outs, refs)) | dict(zip(scratch, refs[len(outs) :]))

    @pl.when(named["phase"][0] == phase_on)
    def _():
        layer = Layer(named)
        getattr(layer, f"do_{work}")(block)
        layer.copies.finish()


def layer_step(work, phase_on, block, values, afters, kept, kept_shapes, scratch):
    specs = [SMEM] * 2 + [ANY] * 3 + [VMEM] * 7 + [ANY] * 4
    names = list(scratch)
    kept = list(kept) if kept is not None else []
    sent = jax.ShapeDtypeStruct((BLOCK, values[2].shape[1]), BF16)
    if work == "norm_back":
        names = [f"{name}_v" for name in ("g", "form2", "scale2", "acc", "outer", "sums2")]
    elif work == "bias":
        names = ["values_v", "bias_v"]
    count = len(values) + len(afters)
    results = pl.pallas_call(
        functools.partial(
            layer_kernel, work, phase_on, block, INS, KEPT + ("send",), names + ["sems"], len(afters), len(kept)
        ),
        out_shape=list(kept_shapes) + [sent],
        in_specs=specs + [ANY] * (len(afters) + len(kept)),
        out_specs=[ANY] * (len(kept_shapes) + 1),
        scratch_shapes=[pltpu.VMEM(*scratch[name]) for name in names] + [pltpu.SemaphoreType.DMA((80,))],
        input_output_aliases={count + i: i for i in range(len(kept))},
        compiler_params=pltpu.CompilerParams(vmem_limit_bytes=VMEM_BYTES),
        name=f"{work}_{phase_on}_{block}",
    )(*values, *afters, *kept)
    return dict(zip(KEPT, results)), results[-1]


def pack_kernel(ways, buckets_ref, offsets_ref, sums1_ref, sums2_ref, *refs):
    out_ref, turn_v = refs[-2:]
    row_of = lax.broadcasted_iota(jnp.int32, (8, SPAN), 0)
    lines = []
    for head in range(offsets_ref.shape[1]):
        eighth = offsets_ref[0, head] + offsets_ref[1, head]
        for size in (4, 2, 1):
            eighth = jnp.where((row_of & size) != 0, pltpu.roll(eighth, SPAN - size, 1), eighth)
        lines.append(jnp.sum(eighth, 0, keepdims=True))
    lines += [jnp.zeros((1, SPAN), F32)] * (NORM_LANE - len(lines))
    sums = pltpu.roll(jnp.concatenate(lines, 0), SPAN - 1, 1)
    span = buckets_ref.shape[1]
    buckets, depth = out_ref.shape[0] // 3, out_ref.shape[0] // ways
    share = buckets // ways
    bucket_ids = lax.broadcasted_iota(jnp.int32, (buckets, span), 0)
    hot = (bucket_ids == buckets_ref[...]).astype(F32)
    table = lax.dot_general(
        hot, sums[:, :span], (((1,), (1,)), ((), ())), precision=highest, preferred_element_type=F32
    ).astype(BF16)
    turn_v[...] = jnp.zeros(turn_v.shape, F32)
    for i, ref in enumerate((sums1_ref, sums2_ref)):
        at = NORM_LANE + 2 * i
        turn_v[at : at + 2, :] = ref[0, 0:2, :] + ref[1, 0:2, :]
    out_ref[...] = turn_v[...].T.astype(BF16)
    for i in range(ways):
        out_ref[i * depth : i * depth + share, 0:NORM_LANE] = table[i * share : (i + 1) * share, :]


def packed(ways, buckets, offset_buckets, kept, afters):
    width = kept["sums1"].shape[2]
    depth, share = width // ways, buckets // ways
    arrays = (offset_buckets, kept["offsets"], kept["sums1"], kept["sums2"])
    if depth % 16 == 0 and share % 16 == 0 and 3 * buckets == width:
        rows = pl.pallas_call(
            functools.partial(pack_kernel, ways),
            out_shape=jax.ShapeDtypeStruct((width, LANES), BF16),
            in_specs=[VMEM] * len(arrays) + [ANY] * len(afters),
            out_specs=VMEM,
            scratch_shapes=[pltpu.VMEM((LANES, width), F32)],
            compiler_params=pltpu.CompilerParams(vmem_limit_bytes=SMALL_VMEM_BYTES),
            name="pack",
        )(*arrays, *afters)
        return rows.reshape(ways, depth, LANES)
    eighths = jnp.sum(kept["offsets"], 0)
    lines = sum(jnp.roll(eighths[:, i, :], -i, 1) for i in range(8))[:, 1:]
    hot = (offset_buckets[0][None, :] == jnp.arange(buckets, dtype=jnp.int32)[:, None]).astype(F32)
    table = jnp.dot(hot, lines.T, precision=highest).reshape(ways, share, -1)
    table = jnp.pad(table, ((0, 0), (0, depth - share), (0, NORM_LANE - table.shape[2])))
    norms = jnp.concatenate([jnp.sum(kept[name], 0)[:2] for name in ("sums1", "sums2")], 0)
    norms = norms.T.reshape(ways, depth, 4)
    rows = jnp.concatenate([table, norms], 2)
    return jnp.pad(rows, ((0, 0), (0, 0), (0, LANES - rows.shape[2]))).astype(BF16)


def halve_kernel(bits, counts, after_count, through_count, me_ref, *refs):
    used = sum(counts) + len(counts)
    outs = refs[used + after_count + through_count :]
    for i, count in enumerate(counts):
        kept_refs, arrived_ref = refs[:count], refs[count]
        refs = refs[count + 1 :]
        send_ref, rest_ref = outs[2 * i : 2 * i + 2]
        mine = (me_ref[0] >> bits[i]) & 1

        def total(which):
            kept = [
                (ref[0, which, 0, 0] if len(ref.shape) == 6 else ref[0, which, 0]).astype(F32)
                for ref in kept_refs
            ]
            return jnp.concatenate(kept, 1) + arrived_ref[0, which, 0].astype(F32)

        send_ref[0, 0] = total(1 - mine).astype(send_ref.dtype)
        rest_ref[0, 0] = total(mine)


def join_kernel(kept_near, arrived_near, kept_far, arrived_far, out_ref, qkv_ref, table_ref, *refs):
    norm_refs, turn_v = refs[:-1], refs[-1]
    near = kept_near[...] + arrived_near[...].astype(F32)
    wide = out_ref.shape[1]
    share = qkv_ref.shape[1] - kept_far.shape[1]
    out_ref[...] = near[:, :wide]
    qkv_ref[:, :share] = near[:, wide : wide + share]
    qkv_ref[:, share:] = kept_far[...] + arrived_far[...].astype(F32)
    small = near[:, wide + share :]
    table_ref[...] = small[: table_ref.shape[0], : table_ref.shape[1]]
    turn_v[...] = jnp.zeros(turn_v.shape, F32)
    turn_v[: small.shape[0], :] = small
    turned = turn_v[...].T
    for i, ref in enumerate(norm_refs):
        ref[...] = turned[NORM_LANE + i : NORM_LANE + i + 1, : ref.shape[1]]


class Share:
    def __init__(self, parts, order):
        self.parts = parts
        self.order = order[1:]
        self.left = sorted(order)
        self.depth = parts[0].shape[1]
        self.wide = sum(part.shape[2] for part in parts)
        self.mine = None
        self.swap(order[0], self.of_core(1 - (lax.axis_index("dp") & 1)))

    def of_core(self, core):
        halves = [
            lax.dynamic_index_in_dim(
                part.reshape((part.shape[0] // 2, 2) + part.shape[1:]), core, 1, keepdims=False
            )
            for part in self.parts
        ]
        return halves[0] if len(halves) == 1 else jnp.concatenate(halves, 2)

    def swap(self, bit, theirs):
        count = lax.axis_size("dp")
        self.left.remove(bit)
        self.sent = theirs
        self.arrived = lax.ppermute(theirs, "dp", [(i, i ^ (1 << bit)) for i in range(count)])

    def total(self):
        kept = self.of_core(lax.axis_index("dp") & 1) if self.mine is None else self.mine
        return kept.astype(F32) + self.arrived.astype(F32)

    def split_at(self):
        bit = self.order[0]
        axis = len(self.left) - 1 - self.left.index(bit)
        return bit, 2**axis, 2 ** (len(self.left) - 1 - axis)

    def halve(self):
        bit, above, below = self.split_at()
        self.order = self.order[1:]
        split = self.total().reshape(above, 2, below, self.depth, self.wide)
        here = (lax.axis_index("dp") >> bit) & 1
        theirs = lax.dynamic_index_in_dim(split, 1 - here, 1, keepdims=False).astype(BF16)
        mine = lax.dynamic_index_in_dim(split, here, 1, keepdims=False)
        self.mine = mine.reshape(-1, self.depth, self.wide)
        self.swap(bit, theirs.reshape(-1, self.depth, self.wide))


def halve_all(me, shares, afters=(), through=()):
    if any(share.depth % 16 for share in shares):
        for share in shares:
            share.halve()
        return through
    ins, in_specs, outs, out_specs, bits, counts = [], [], [], [], [], []
    for share in shares:
        bit, above, below = share.split_at()
        bits.append(bit)

        def halves(wide, b=below):
            return pl.BlockSpec((1, 2, 1, share.depth, wide), lambda i, me: (i // b, 0, i % b, 0, 0))

        if share.mine is None:
            counts.append(len(share.parts))
            for part in share.parts:
                wide = part.shape[2]
                ins.append(part.reshape(above, 2, below, 2, share.depth, wide))
                in_specs.append(
                    pl.BlockSpec(
                        (1, 2, 1, 1, share.depth, wide),
                        lambda i, me, b=below: (i // b, 0, i % b, me[0] & 1, 0, 0),
                    )
                )
        else:
            counts.append(1)
            ins.append(share.mine.reshape(above, 2, below, share.depth, share.wide))
            in_specs.append(halves(share.wide))
        ins.append(share.arrived.reshape(above, 2, below, share.depth, share.wide))
        in_specs.append(halves(share.wide))
        outs += [
            jax.ShapeDtypeStruct((above, below, share.depth, share.wide), kind) for kind in (BF16, F32)
        ]
        out_specs += [
            pl.BlockSpec((1, 1, share.depth, share.wide), lambda i, me, b=below: (i // b, i % b, 0, 0))
        ] * 2
        steps = above * below
    results = pl.pallas_call(
        functools.partial(halve_kernel, tuple(bits), tuple(counts), len(afters), len(through)),
        grid_spec=pltpu.PrefetchScalarGridSpec(
            num_scalar_prefetch=1,
            grid=(steps,),
            in_specs=in_specs + [ANY] * (len(afters) + len(through)),
            out_specs=out_specs + [ANY] * len(through),
        ),
        out_shape=outs + [jax.ShapeDtypeStruct(array.shape, array.dtype) for array in through],
        input_output_aliases={
            1 + len(ins) + len(afters) + i: len(outs) + i for i in range(len(through))
        },
        compiler_params=pltpu.CompilerParams(vmem_limit_bytes=VMEM_BYTES if through else SMALL_VMEM_BYTES),
        name="halve",
    )(me, *ins, *afters, *through)
    for i, share in enumerate(shares):
        share.order = share.order[1:]
        share.mine = results[2 * i + 1].reshape(-1, share.depth, share.wide)
        share.swap(bits[i], results[2 * i].reshape(-1, share.depth, share.wide))
    return results[len(outs) :]


def joined(near, far, width, table_shape):
    parts = [x[0] for share in (near, far) for x in (share.mine, share.arrived)]
    shapes = [(near.depth, width), (near.depth, near.wide + far.wide - width - LANES), table_shape]
    shapes += [(1, near.depth)] * 4
    return pl.pallas_call(
        join_kernel,
        out_shape=[jax.ShapeDtypeStruct(dims, F32) for dims in shapes],
        in_specs=[VMEM] * len(parts),
        out_specs=[VMEM] * len(shapes),
        scratch_shapes=[pltpu.VMEM((LANES, LANES), F32)],
        compiler_params=pltpu.CompilerParams(vmem_limit_bytes=SMALL_VMEM_BYTES),
        name="join",
    )(*parts)


def passed_along(x, axis, by):
    length = lax.axis_size(axis)
    pairs = [(i, i + by) for i in range(length) if 0 <= i + by < length]
    return lax.ppermute(x, axis, pairs)


def shards(
    hidden_in, out_grad, qkv_weight, out_weight, rel_table, norm1_gain, norm1_bias,
    up_weight, down_weight, norm2_gain, norm2_bias, seg_ids, pad_mask, rel_buckets,
):
    phase = lax.axis_index("phase").astype(jnp.int32).reshape(1)
    ways = lax.axis_size("dp")
    slots, width = hidden_in.shape
    inner = up_weight.shape[2]
    buckets, heads = rel_table.shape[1:]

    def shape(dims, kind):
        return jax.ShapeDtypeStruct(dims, kind)

    rows_of = {
        "xin": (width, BF16), "qkv": (3 * width, BF16), "ctx": (width, BF16), "form1": (width, F32),
        "scale1": (1, F32), "low1": (width, BF16), "slope": (inner, BF16), "act": (inner, BF16),
        "form2": (width, F32), "scale2": (1, F32), "out": (width, BF16),
        "outer_low": (width, BF16), "hidden_low": (inner, BF16), "residual_low": (width, BF16),
        "projected": (3 * width, BF16), "input_grad": (width, BF16),
    }
    kept_shapes = [
        shape((slots, rows_of[name][0]), rows_of[name][1])
        if name in rows_of
        else {
            "weights": shape((MICRO, heads, BLOCK, BLOCK), BF16),
            "sums1": shape((MICRO, 8, width), F32),
            "sums2": shape((MICRO, 8, width), F32),
            "residual": shape((BLOCK, width), F32),
            "offsets": shape((MICRO, heads, 8, SPAN), F32),
            "bias": shape((heads, TILE, SPAN), F32),
        }[name]
        for name in KEPT
    ]
    in_forward = ("qkv", "ctx", "form1", "scale1", "low1", "slope", "act", "form2", "scale2", "out")
    scratch = {f"{name}_v": ((BLOCK, rows_of[name][0]), rows_of[name][1]) for name in in_forward}
    scratch |= {
        name: ((BLOCK, width), BF16) for name in ("x_v", "g_v", "outer_v", "residual_low_v", "dctx_v", "grad_v")
    }
    scratch |= {
        "weights_v": ((heads, BLOCK, BLOCK), BF16), "acc_v": ((BLOCK, width), F32), "square_v": ((2, BLOCK, BLOCK), F32),
        "values_v": ((heads, SPAN), F32), "bias_v": ((heads, TILE, SPAN), F32), "sums1_v": ((8, width), F32), "sums2_v": ((8, width), F32),
        "wqkv_v": ((width, 3 * width), BF16), "wout_v": ((width, width), BF16), "wup_v": ((width, inner), BF16),
        "wdown_v": ((inner, width), BF16), "fold_v": ((2, TILE, SPAN), F32), "eighth_v": ((heads, 8, SPAN), F32),
        "half_v": ((2, BLOCK, BLOCK), BF16),
    }

    def step(work, phase_on, block, received, kept, afters=()):
        values = (
            phase, seg_ids, hidden_in, received, out_grad, rel_table, pad_mask[None, :], rel_buckets[None, :],
            norm1_gain, norm1_bias, norm2_gain, norm2_bias, qkv_weight, out_weight, up_weight, down_weight,
        )
        in_place = None if kept is None else [kept[name] for name in KEPT]
        return layer_step(work, phase_on, block, values, list(afters), in_place, kept_shapes, scratch)

    kept, sent = step("forward", 0, 0, hidden_in, None)
    first = passed_along(sent, "phase", 1)
    kept, _ = step("bias", 1, 0, hidden_in, kept)
    kept, sent = step("forward", 0, 1, hidden_in, kept)
    second = passed_along(sent, "phase", 1)
    kept, sent = step("both", 1, 0, first, kept)
    first_back = passed_along(sent, "phase", -1)
    kept, sent = step("both", 1, 1, second, kept)
    second_back = passed_along(sent, "phase", -1)
    kept, _ = step("back", 0, 0, first_back, kept)
    kept, _ = step("norm_back", 0, 1, second_back, kept)

    bits = ways.bit_length() - 1
    near_first = list(range(bits))
    far_first = [0] + list(range(2, bits)) + [1] if bits > 1 else near_first
    me = lax.axis_index("dp").astype(jnp.int32).reshape(1)

    def weight_grad(left, right):
        product = dot_tn(left, right).astype(BF16)
        return product.reshape(ways, product.shape[0] // ways, product.shape[1])

    down = Share([weight_grad(kept["act"], kept["outer_low"])], far_first)
    kept, _ = step("ffn_back", 0, 1, hidden_in, kept, [down.sent])
    (hidden_low,) = halve_all(me, [down], through=[kept["hidden_low"]])
    up = Share([weight_grad(kept["low1"], hidden_low)], near_first)
    out_part = weight_grad(kept["ctx"], kept["residual_low"])
    kept["hidden_low"] = hidden_low
    halve_all(me, [up])
    kept, _ = step("attn_back", 0, 1, hidden_in, kept, [down.sent, up.sent])
    (projected,) = halve_all(me, [down], through=[kept["projected"]])
    far = Share([weight_grad(kept["xin"], projected[:, width:])], far_first)
    (slots_in,) = halve_all(me, [up], [down.sent, far.sent], [kept["xin"]])
    near_part = weight_grad(slots_in, projected[:, :width])
    small = packed(ways, buckets, rel_buckets[None, :], kept, [far.sent])
    near = Share([out_part, near_part, small], near_first)
    halve_all(me, [down])
    halve_all(me, [near, far], [up.sent])
    halve_all(me, [up])
    halve_all(me, [near, far], [up.sent])
    while down.order:
        halve_all(me, [down, up])
    while near.order:
        halve_all(me, [near, far])
    down_share = down.total()[0]
    up_share = up.total()[0]
    out_share, qkv_share, table_share, *norm_shares = joined(near, far, width, (buckets // ways, heads))
    return (
        kept["out"][None],
        kept["input_grad"][None],
        qkv_share[None],
        out_share[None],
        table_share[None],
        norm_shares[0],
        norm_shares[1],
        up_share[None],
        down_share[None],
        norm_shares[2],
        norm_shares[3],
    )


def solution(mesh):
    return jax.shard_map(
        shards,
        mesh=mesh,
        in_specs=(
            P("dp", None),
            P("dp", None),
            P("phase", None, None),
            P("phase", None, None),
            P("phase", None, None),
            P("phase", None),
            P("phase", None),
            P("phase", None, None),
            P("phase", None, None),
            P("phase", None),
            P("phase", None),
            P("dp"),
            P("dp"),
            P(),
        ),
        out_specs=(
            P("phase", "dp", None),
            P("phase", "dp", None),
            P("phase", "dp", None),
            P("phase", "dp", None),
            P("phase", "dp", None),
            P("phase", "dp"),
            P("phase", "dp"),
            P("phase", "dp", None),
            P("phase", "dp", None),
            P("phase", "dp"),
            P("phase", "dp"),
        ),
        check_vma=False,
    )
```

```python
import functools

import jax
import jax.numpy as jnp
from jax import lax
from jax.experimental import pallas as pl
from jax.experimental.pallas import tpu as pltpu
from jax.sharding import PartitionSpec as P

BLOCK = 512
MICRO = 2
TILE = 128
LANES = 128
CHUNK = 512
SPAN = 2 * BLOCK
VMEM_BYTES = 58 * 1024 * 1024
SMALL_VMEM_BYTES = 20 * 1024 * 1024
NORM_LANE = 16

norm_eps = 1e-05
mask_fill = -1000000000.0
score_scale = 0.125
inv_root_two = 0.7071067811865476
inv_root_tau = 0.3989422804014327
log2_e = 1.4426950408889634
highest = lax.Precision.HIGHEST

F32 = jnp.float32
BF16 = jnp.bfloat16
ANY = pl.BlockSpec(memory_space=pl.ANY)
VMEM = pl.BlockSpec(memory_space=pltpu.VMEM)
QUICK = pl.CostEstimate(flops=1, bytes_accessed=1, transcendentals=0)
SMEM = pl.BlockSpec(memory_space=pltpu.SMEM)


def dot_nn(a, b):
    return lax.dot_general(a, b, (((1,), (0,)), ((), ())), preferred_element_type=F32)


def dot_nt(a, b):
    return lax.dot_general(a, b, (((1,), (1,)), ((), ())), preferred_element_type=F32)


def dot_tn(a, b):
    return lax.dot_general(a, b, (((0,), (0,)), ((), ())), preferred_element_type=F32)


def row_mean(rows):
    return jnp.sum(rows, -1, keepdims=True) * (1.0 / rows.shape[-1])


def normal_parts(residual):
    centred = residual - row_mean(residual)
    inv_scale = lax.rsqrt(row_mean(centred * centred) + norm_eps)
    return centred * inv_scale, inv_scale


def norm_backward(grad_rows, normal_form, inv_scale):
    first = row_mean(grad_rows)
    second = row_mean(grad_rows * normal_form)
    return inv_scale * (grad_rows - first - normal_form * second)


def gelu_parts(hidden):
    share = 0.5 + 0.5 * lax.erf(hidden * inv_root_two)
    bell = jnp.exp2(hidden * hidden * (-0.5 * log2_e))
    return hidden * share, share + hidden * bell * inv_root_tau


def half_mask(which, shape):
    lane = lax.broadcasted_iota(jnp.int32, shape, 1)
    return (lane < LANES // 2) if which == 0 else (lane >= LANES // 2)


class Copies:
    def __init__(self, sems):
        self.sems = sems
        self.used = 0
        self.stores = []

    def take(self, count=1):
        self.used += count
        return self.used - count

    def load(self, source, target):
        copy = pltpu.make_async_copy(source, target, self.sems.at[self.take()])
        copy.start()
        return copy

    def store(self, source, target, when=True):
        if when:
            self.stores.append(self.load(source, target))

    def finish(self):
        for copy in self.stores:
            copy.wait()


KEPT = (
    "xin", "qkv", "weights", "ctx", "form1", "scale1", "low1", "slope", "act", "form2", "scale2", "out",
    "bias", "outer_low", "hidden_low", "residual_low", "sums1", "sums2", "residual", "projected", "offsets", "input_grad",
)
INS = (
    "phase", "segments", "hidden_in", "received", "out_grad", "table", "padding", "buckets",
    "gain1", "shift1", "gain2", "shift2",
    "wqkv", "wout", "wup", "wdown",
)


class Layer:
    def __init__(self, refs):
        self.__dict__.update(refs)
        self.copies = Copies(self.sems)
        self.width = self.hidden_in.shape[1]
        self.inner = self.wup.shape[2]
        self.pairs = self.width // LANES
        self.stages = self.inner // (2 * CHUNK)
        self.pair_sems = self.copies.take(self.pairs)
        self.chunk_sems = [self.copies.take(self.stages) for _ in range(3)]

    def lanes_of(self, pair, part):
        return pl.ds(pl.multiple_of(part * self.width + pair * LANES, LANES), LANES)

    def stage(self, i):
        return pl.ds(pl.multiple_of(i * 2 * CHUNK, 2 * CHUNK), 2 * CHUNK)

    def build_bias(self):
        span = self.buckets.shape[1]
        bucket_ids = lax.broadcasted_iota(jnp.int32, (self.table.shape[1], span), 0)
        hot = (bucket_ids == self.buckets[...]).astype(F32)
        values = lax.dot_general(
            self.table[0], hot, (((0,), (0,)), ((), ())), precision=highest, preferred_element_type=F32
        )
        self.values_v[:, :span] = values
        self.values_v[:, span:] = jnp.zeros((values.shape[0], SPAN - span), F32)

        def one_head(head, carry):
            wide = jnp.broadcast_to(self.values_v[pl.ds(head, 1), :], (TILE, SPAN))
            self.bias_v[head] = pltpu.roll(wide, 1, 1, stride=1, stride_axis=0)
            return carry

        lax.fori_loop(0, values.shape[0], one_head, 0)
        self.copies.store(self.bias_v, self.bias)


    def rows(self, block):
        return pl.ds(block * BLOCK, BLOCK)

    def forward(self, block, keep, built):
        copies = self.copies
        rows = self.rows(block)
        load_x = copies.load(self.hidden_in.at[rows] if keep else self.received, self.x_v)
        width = self.width
        loads = [
            copies.load(self.wqkv.at[0, :, pl.ds(c, width)], self.wqkv_v.at[:, pl.ds(c, width)])
            for c in range(0, 3 * width, width)
        ]
        if not built:
            self.build_bias()
        load_x.wait()

        def load_bias(pair):
            heads = pl.ds(2 * pair, 2)
            return pltpu.make_async_copy(self.bias.at[heads], self.bias_v.at[heads], self.sems.at[self.pair_sems + pair])

        for i, c in enumerate(range(0, 3 * width, width)):
            loads[i].wait()
            if i == 2 and built:
                for pair in range(self.pairs):
                    load_bias(pair).start()
            self.qkv_v[:, c : c + width] = dot_nn(self.x_v[...], self.wqkv_v[:, c : c + width]).astype(BF16)
        copies.store(self.x_v, self.xin.at[rows])
        copies.store(self.qkv_v, self.qkv.at[rows], keep)
        weights_sem = self.sems.at[copies.take()]
        later_loads = [
            pltpu.make_async_copy(source.at[0], target, self.sems.at[copies.take()])
            for source, target in ((self.wout, self.wout_v), (self.wup, self.wup_v), (self.wdown, self.wdown_v))
        ]

        def own(pair, part, which):
            both = self.qkv_v[:, self.lanes_of(pair, part)]
            return jnp.where(half_mask(which, both.shape), both, jnp.zeros_like(both))

        single = self.segments[block * BLOCK + TILE] == self.segments[block * BLOCK]
        padding = self.padding[:, block * BLOCK : (block + 1) * BLOCK]
        tile_of = lax.broadcasted_iota(jnp.int32, (1, BLOCK), 1) // TILE
        shut = [
            jnp.where((padding == 1) & (single | (tile_of == tile)), 0.0, mask_fill) for tile in range(BLOCK // TILE)
        ]
        row_id = lax.broadcasted_iota(jnp.int32, (TILE, TILE), 0)
        diagonal = row_id == lax.broadcasted_iota(jnp.int32, (TILE, TILE), 1)

        def bias_rows(head, tile):
            at = BLOCK - tile * TILE
            rows = self.bias_v[head, :, at : at + BLOCK]
            masked = rows + shut[tile]
            own = slice(tile * TILE, (tile + 1) * TILE)
            parts = [masked[:, : own.start], jnp.where(diagonal, rows[:, own], masked[:, own]), masked[:, own.stop :]]
            return jnp.concatenate([part for part in parts if part.shape[1]], 1)

        def weigh(pair, which):
            head = 2 * pair + which
            k_own = own(pair, 1, which)
            for r in range(0, BLOCK, 2 * TILE):
                q_rows = self.qkv_v[r : r + 2 * TILE, self.lanes_of(pair, 0)] * jnp.asarray(score_scale, BF16)
                tiles = [bias_rows(head, tile) for tile in range(r // TILE, r // TILE + 2)]
                logits = dot_nt(q_rows, k_own) + jnp.concatenate(tiles, 0)
                raised = jnp.exp(logits - jnp.max(logits, -1, keepdims=True))
                share = pl.reciprocal(jnp.sum(raised, -1, keepdims=True), approx=True)
                self.weights_v[head, r : r + 2 * TILE, :] = (raised * share).astype(BF16)

        def head_pair(pair, carry):
            if built:
                load_bias(pair).wait()

            @pl.when(pair == 0)
            def _():
                for load in later_loads:
                    load.start()

            weigh(pair, 0)
            context = dot_nn(self.weights_v[2 * pair], own(pair, 2, 0))
            weigh(pair, 1)
            context += dot_nn(self.weights_v[2 * pair + 1], own(pair, 2, 1))
            self.ctx_v[:, self.lanes_of(pair, 0)] = context.astype(BF16)
            if keep:
                heads = pl.ds(2 * pair, 2)
                pltpu.make_async_copy(self.weights_v.at[heads], self.weights.at[block, heads], weights_sem).start()
            return carry

        lax.fori_loop(0, self.pairs, head_pair, 0)
        if keep:
            copies.stores.append(pltpu.make_async_copy(self.weights_v, self.weights.at[block], weights_sem))
        copies.store(self.ctx_v, self.ctx.at[rows])
        load_out, load_up, load_down = later_loads
        load_out.wait()
        self.acc_v[...] = dot_nn(self.ctx_v[...], self.wout_v[...])
        for r in range(0, BLOCK, 64):
            tile = slice(r, r + 64)
            form, scale = normal_parts(self.acc_v[tile, :] + self.x_v[tile, :].astype(F32))
            normed = form * self.gain1[...] + self.shift1[...]
            self.form1_v[tile, :] = form
            self.scale1_v[tile, :] = scale
            self.acc_v[tile, :] = normed
            self.low1_v[tile, :] = normed.astype(BF16)
        copies.store(self.form1_v, self.form1.at[rows], keep)
        copies.store(self.scale1_v, self.scale1.at[rows], keep)
        copies.store(self.low1_v, self.low1.at[rows])
        load_up.wait()
        load_down.wait()
        act_sem = self.sems.at[copies.take()]
        slope_sem = self.sems.at[copies.take()]

        def two_chunks(i, carry):
            span = self.stage(i)
            active, grade = gelu_parts(dot_nn(self.low1_v[...], self.wup_v[:, span]))
            active = active.astype(BF16)
            self.act_v[:, span] = active
            self.slope_v[:, span] = grade.astype(BF16)
            self.acc_v[...] += dot_nn(active, self.wdown_v[span, :])
            pltpu.make_async_copy(self.act_v.at[:, span], self.act.at[rows, span], act_sem).start()
            if keep:
                pltpu.make_async_copy(self.slope_v.at[:, span], self.slope.at[rows, span], slope_sem).start()
            return carry

        lax.fori_loop(0, self.stages, two_chunks, 0)
        copies.stores.append(pltpu.make_async_copy(self.act_v, self.act.at[rows], act_sem))
        if keep:
            copies.stores.append(pltpu.make_async_copy(self.slope_v, self.slope.at[rows], slope_sem))
        for r in range(0, BLOCK, 64):
            tile = slice(r, r + 64)
            form, scale = normal_parts(self.acc_v[tile, :])
            self.form2_v[tile, :] = form
            self.scale2_v[tile, :] = scale
            self.out_v[tile, :] = (form * self.gain2[...] + self.shift2[...]).astype(BF16)
        copies.store(self.out_v, self.send, keep)
        copies.store(self.out_v, self.out.at[rows])
        copies.store(self.form2_v, self.form2.at[rows], keep)
        copies.store(self.scale2_v, self.scale2.at[rows], keep)


    def chunk_loads(self, i, rows):
        span = self.stage(i)
        return [
            pltpu.make_async_copy(source, target, self.sems.at[self.chunk_sems[k] + i])
            for k, (source, target) in enumerate(
                (
                    (self.wdown.at[0, span], self.wdown_v.at[span]),
                    (self.slope.at[rows, span], self.slope_v.at[:, span]),
                    (self.wup.at[0, :, span], self.wup_v.at[:, span]),
                )
            )
        ]

    def norm_sums(self, source, form_ref, sums_ref):
        gain_sum = jnp.zeros((1, self.width), F32)
        shift_sum = jnp.zeros((1, self.width), F32)
        for r in range(0, BLOCK, 64):
            grad_rows, form = source[r : r + 64, :].astype(F32), form_ref[r : r + 64, :]
            gain_sum += jnp.sum(grad_rows * form, 0, keepdims=True)
            shift_sum += jnp.sum(grad_rows, 0, keepdims=True)
        sums_ref[...] = jnp.zeros(sums_ref.shape, F32)
        sums_ref[0:1, :] = gain_sum
        sums_ref[1:2, :] = shift_sum

    def norm_back(self, block):
        for r in range(0, BLOCK, 64):
            tile = slice(r, r + 64)
            grad_rows = self.g_v[tile, :].astype(F32) * self.gain2[...]
            grad_outer = norm_backward(grad_rows, self.form2_v[tile, :], self.scale2_v[tile, :])
            self.acc_v[tile, :] = grad_outer
            self.outer_v[tile, :] = grad_outer.astype(BF16)
        self.copies.store(self.outer_v, self.outer_low.at[self.rows(block)])

    def norm_sums_2(self, block):
        self.norm_sums(self.g_v, self.form2_v, self.sums2_v)
        self.copies.store(self.sums2_v, self.sums2.at[block])

    def ffn_back(self, block, staged=False, middle_loads=()):
        copies = self.copies
        rows = self.rows(block)
        hidden_sem = self.sems.at[copies.take()]

        def two_chunks(i, carry):
            span = self.stage(i)
            if staged:
                load_down, load_slope, load_up = self.chunk_loads(i, rows)
                load_down.wait()
                load_slope.wait()
            grad_active = dot_nt(self.outer_v[...], self.wdown_v[span, :])
            hidden = (grad_active * self.slope_v[:, span].astype(F32)).astype(BF16)
            self.slope_v[:, span] = hidden
            if staged:
                load_up.wait()

                @pl.when(i + 2 < self.stages)
                def _():
                    for load in self.chunk_loads(i + 2, rows):
                        load.start()

            self.acc_v[...] += dot_nt(hidden, self.wup_v[:, span])
            pltpu.make_async_copy(self.slope_v.at[:, span], self.hidden_low.at[rows, span], hidden_sem).start()
            return carry

        lax.fori_loop(0, self.stages, two_chunks, 0)
        copies.stores.append(pltpu.make_async_copy(self.slope_v, self.hidden_low.at[rows], hidden_sem))
        for load in middle_loads:
            load.wait()
        self.norm_sums(self.acc_v, self.form1_v, self.sums1_v)
        for r in range(0, BLOCK, 64):
            tile = slice(r, r + 64)
            grad_residual = norm_backward(
                self.acc_v[tile, :] * self.gain1[...], self.form1_v[tile, :], self.scale1_v[tile, :]
            )
            self.acc_v[tile, :] = grad_residual
            self.residual_low_v[tile, :] = grad_residual.astype(BF16)
        copies.store(self.residual_low_v, self.residual_low.at[rows])
        copies.store(self.sums1_v, self.sums1.at[block])

    def attn_back(self, block, load_pair=None, load_in=()):
        copies = self.copies
        rows = self.rows(block)
        self.dctx_v[...] = dot_nt(self.residual_low_v[...], self.wout_v[...]).astype(BF16)
        self.fold_v[:, :, 0:TILE] = jnp.zeros((2, TILE, TILE), F32)

        def head_pair(pair, carry):
            def lanes_of(part):
                return self.lanes_of(pair, part)

            q_pair, k_pair, v_pair = (self.qkv_v[:, lanes_of(part)] for part in range(3))
            grad_pair = self.dctx_v[:, lanes_of(0)]
            crossed = grad_pair.astype(F32) * self.ctx_v[:, lanes_of(0)].astype(F32)
            if load_pair is not None:
                load_pair(pair).wait()
            masks = [half_mask(which, k_pair.shape) for which in range(2)]

            def own(both, which):
                return jnp.where(masks[which], both, jnp.zeros_like(both))

            for which in range(2):
                self.square_v[which] = dot_nt(grad_pair, own(v_pair, which))
            q_grad = k_grad = v_grad = 0.0
            for which in range(2):
                head = 2 * pair + which
                delta = jnp.sum(own(crossed, which), -1, keepdims=True)
                for r in range(0, BLOCK, 64):
                    tile = slice(r, r + 64)
                    score_grad = (
                        self.weights_v[head, tile, :].astype(F32) * (self.square_v[which, tile, :] - delta[tile, :])
                    ).astype(BF16)
                    self.half_v[which, tile, :] = score_grad
                    at = BLOCK - r // TILE * TILE
                    wide = score_grad.astype(F32)
                    half = slice(r % TILE, r % TILE + 64)
                    if r < TILE:
                        self.fold_v[which, half, at : at + BLOCK] = wide
                    else:
                        self.fold_v[which, half, at : at + TILE] = wide[:, :TILE]
                        self.fold_v[which, half, at + TILE : at + BLOCK] += wide[:, TILE:]
                v_grad += dot_tn(self.weights_v[head], own(grad_pair, which))
                q_grad += dot_nn(self.half_v[which], own(k_pair, which))
                k_grad += dot_tn(self.half_v[which], own(q_pair, which))
                folded = self.fold_v[which]
                size = TILE // 2
                while size >= 8:
                    folded = folded[:size, :] + pltpu.roll(folded[size:, :], SPAN - size, 1)
                    size //= 2
                self.eighth_v[head] = folded
            self.qkv_v[:, lanes_of(0)] = (q_grad * score_scale).astype(BF16)
            self.qkv_v[:, lanes_of(1)] = (k_grad * score_scale).astype(BF16)
            self.qkv_v[:, lanes_of(2)] = v_grad.astype(BF16)
            return carry

        lax.fori_loop(0, self.pairs, head_pair, 0)
        copies.store(self.eighth_v, self.offsets.at[block])
        copies.store(self.qkv_v, self.projected.at[rows])
        for load in load_in:
            load.wait()
        self.grad_v[...] = (self.acc_v[...] + dot_nt(self.qkv_v[...], self.wqkv_v[...])).astype(BF16)
        copies.store(self.grad_v, self.send)
        copies.store(self.grad_v, self.input_grad.at[rows])


    def do_forward(self, block):
        self.forward(block, True, block > 0)

    def do_bias(self, block):
        self.build_bias()

    def do_both(self, block):
        load = self.copies.load(self.out_grad.at[self.rows(block)], self.g_v)
        self.forward(block, False, True)
        load.wait()
        self.norm_back(block)
        self.ffn_back(block)
        self.norm_sums_2(block)
        self.attn_back(block)

    def do_back(self, block):
        rows = self.rows(block)
        loads = [
            self.copies.load(source, target)
            for source, target in (
                (self.received, self.g_v),
                (self.form2.at[rows], self.form2_v),
                (self.scale2.at[rows], self.scale2_v),
                (self.slope.at[rows], self.slope_v),
                (self.wdown.at[0], self.wdown_v),
                (self.wup.at[0], self.wup_v),
                (self.form1.at[rows], self.form1_v),
                (self.scale1.at[rows], self.scale1_v),
                (self.qkv.at[rows], self.qkv_v),
                (self.weights.at[block], self.weights_v),
                (self.ctx.at[rows], self.ctx_v),
                (self.wout.at[0], self.wout_v),
                (self.wqkv.at[0], self.wqkv_v),
            )
        ]
        for load in loads:
            load.wait()
        self.norm_back(block)
        self.ffn_back(block)
        self.norm_sums_2(block)
        self.attn_back(block)

    def do_ffn_back(self, block):
        rows = self.rows(block)
        loads = [
            self.copies.load(source, target)
            for source, target in (
                (self.received, self.g_v),
                (self.form2.at[rows], self.form2_v),
                (self.scale2.at[rows], self.scale2_v),
            )
        ]
        for i in range(min(2, self.stages)):
            for load in self.chunk_loads(i, rows):
                load.start()
        for load in loads:
            load.wait()
        middle = [
            self.copies.load(self.form1.at[rows], self.form1_v),
            self.copies.load(self.scale1.at[rows], self.scale1_v),
        ]
        self.norm_back(block)
        self.ffn_back(block, True, middle)
        self.copies.store(self.acc_v, self.residual)
        self.norm_sums_2(block)

    def do_attn_back(self, block):
        rows = self.rows(block)
        loads = [
            self.copies.load(source, target)
            for source, target in (
                (self.residual_low.at[rows], self.residual_low_v),
                (self.wout.at[0], self.wout_v),
                (self.qkv.at[rows], self.qkv_v),
                (self.ctx.at[rows], self.ctx_v),
            )
        ]

        def load_pair(pair):
            heads = pl.ds(2 * pair, 2)
            return pltpu.make_async_copy(
                self.weights.at[block, heads], self.weights_v.at[heads], self.sems.at[self.pair_sems + pair]
            )

        for pair in range(self.pairs):
            load_pair(pair).start()
        for load in loads:
            load.wait()
        last = [
            self.copies.load(self.wqkv.at[0], self.wqkv_v),
            self.copies.load(self.residual, self.acc_v),
        ]
        self.attn_back(block, load_pair, last)


def layer_kernel(work, phase_on, block, ins, outs, scratch, after_count, kept_count, *refs):
    refs_in, refs = refs[: len(ins)], refs[len(ins) + after_count + kept_count :]
    named = dict(zip(ins, refs_in)) | dict(zip(outs, refs)) | dict(zip(scratch, refs[len(outs) :]))

    @pl.when(named["phase"][0] == phase_on)
    def _():
        layer = Layer(named)
        getattr(layer, f"do_{work}")(block)
        layer.copies.finish()


def layer_step(work, phase_on, block, values, afters, kept, kept_shapes, scratch):
    specs = [SMEM] * 2 + [ANY] * 3 + [VMEM] * 7 + [ANY] * 4
    names = list(scratch)
    kept = list(kept) if kept is not None else []
    sent = jax.ShapeDtypeStruct((BLOCK, values[2].shape[1]), BF16)
    if work == "bias":
        names = ["values_v", "bias_v"]
    count = len(values) + len(afters)
    results = pl.pallas_call(
        functools.partial(
            layer_kernel, work, phase_on, block, INS, KEPT + ("send",), names + ["sems"], len(afters), len(kept)
        ),
        out_shape=list(kept_shapes) + [sent],
        in_specs=specs + [ANY] * (len(afters) + len(kept)),
        out_specs=[ANY] * (len(kept_shapes) + 1),
        scratch_shapes=[pltpu.VMEM(*scratch[name]) for name in names] + [pltpu.SemaphoreType.DMA((80,))],
        input_output_aliases={count + i: i for i in range(len(kept))},
        compiler_params=pltpu.CompilerParams(vmem_limit_bytes=VMEM_BYTES),
        name=f"{work}_{phase_on}_{block}",
    )(*values, *afters, *kept)
    return dict(zip(KEPT, results)), results[-1]


def pack_kernel(ways, buckets_ref, offsets_ref, sums1_ref, sums2_ref, *refs):
    out_ref, turn_v = refs[-2:]
    row_of = lax.broadcasted_iota(jnp.int32, (8, SPAN), 0)
    lines = []
    for head in range(offsets_ref.shape[1]):
        eighth = offsets_ref[0, head] + offsets_ref[1, head]
        for size in (4, 2, 1):
            eighth = jnp.where((row_of & size) != 0, pltpu.roll(eighth, SPAN - size, 1), eighth)
        lines.append(jnp.sum(eighth, 0, keepdims=True))
    lines += [jnp.zeros((1, SPAN), F32)] * (NORM_LANE - len(lines))
    sums = pltpu.roll(jnp.concatenate(lines, 0), SPAN - 1, 1)
    span = buckets_ref.shape[1]
    buckets, depth = out_ref.shape[0] // 3, out_ref.shape[0] // ways
    share = buckets // ways
    bucket_ids = lax.broadcasted_iota(jnp.int32, (buckets, span), 0)
    hot = (bucket_ids == buckets_ref[...]).astype(F32)
    table = lax.dot_general(
        hot, sums[:, :span], (((1,), (1,)), ((), ())), precision=highest, preferred_element_type=F32
    ).astype(BF16)
    turn_v[...] = jnp.zeros(turn_v.shape, F32)
    for i, ref in enumerate((sums1_ref, sums2_ref)):
        at = NORM_LANE + 2 * i
        turn_v[at : at + 2, :] = ref[0, 0:2, :] + ref[1, 0:2, :]
    out_ref[...] = turn_v[...].T.astype(BF16)
    for i in range(ways):
        out_ref[i * depth : i * depth + share, 0:NORM_LANE] = table[i * share : (i + 1) * share, :]


def packed(ways, buckets, offset_buckets, kept, afters):
    width = kept["sums1"].shape[2]
    depth, share = width // ways, buckets // ways
    arrays = (offset_buckets, kept["offsets"], kept["sums1"], kept["sums2"])
    if depth % 16 == 0 and share % 16 == 0 and 3 * buckets == width:
        rows = pl.pallas_call(
            functools.partial(pack_kernel, ways),
            out_shape=jax.ShapeDtypeStruct((width, LANES), BF16),
            in_specs=[VMEM] * len(arrays) + [ANY] * len(afters),
            out_specs=VMEM,
            scratch_shapes=[pltpu.VMEM((LANES, width), F32)],
            compiler_params=pltpu.CompilerParams(vmem_limit_bytes=SMALL_VMEM_BYTES),
            name="pack",
        )(*arrays, *afters)
        return rows.reshape(ways, depth, LANES)
    eighths = jnp.sum(kept["offsets"], 0)
    lines = sum(jnp.roll(eighths[:, i, :], -i, 1) for i in range(8))[:, 1:]
    hot = (offset_buckets[0][None, :] == jnp.arange(buckets, dtype=jnp.int32)[:, None]).astype(F32)
    table = jnp.dot(hot, lines.T, precision=highest).reshape(ways, share, -1)
    table = jnp.pad(table, ((0, 0), (0, depth - share), (0, NORM_LANE - table.shape[2])))
    norms = jnp.concatenate([jnp.sum(kept[name], 0)[:2] for name in ("sums1", "sums2")], 0)
    norms = norms.T.reshape(ways, depth, 4)
    rows = jnp.concatenate([table, norms], 2)
    return jnp.pad(rows, ((0, 0), (0, 0), (0, LANES - rows.shape[2]))).astype(BF16)


def halve_kernel(bits, counts, after_count, through_count, me_ref, *refs):
    used = sum(counts) + len(counts)
    outs = refs[used + after_count + through_count :]
    for i, count in enumerate(counts):
        kept_refs, arrived_ref = refs[:count], refs[count]
        refs = refs[count + 1 :]
        send_ref, rest_ref = outs[2 * i : 2 * i + 2]
        mine = (me_ref[0] >> bits[i]) & 1

        def total(which):
            kept = [
                (ref[0, which, 0, 0] if len(ref.shape) == 6 else ref[0, which, 0]).astype(F32)
                for ref in kept_refs
            ]
            return jnp.concatenate(kept, 1) + arrived_ref[0, which, 0].astype(F32)

        send_ref[0, 0] = total(1 - mine).astype(send_ref.dtype)
        rest_ref[0, 0] = total(mine)


def join_kernel(kept_near, arrived_near, kept_far, arrived_far, out_ref, qkv_ref, table_ref, *refs):
    norm_refs, turn_v = refs[:-1], refs[-1]
    near = kept_near[...] + arrived_near[...].astype(F32)
    wide = out_ref.shape[1]
    share = qkv_ref.shape[1] - kept_far.shape[1]
    out_ref[...] = near[:, :wide]
    qkv_ref[:, :share] = near[:, wide : wide + share]
    qkv_ref[:, share:] = kept_far[...] + arrived_far[...].astype(F32)
    small = near[:, wide + share :]
    table_ref[...] = small[: table_ref.shape[0], : table_ref.shape[1]]
    turn_v[...] = jnp.zeros(turn_v.shape, F32)
    turn_v[: small.shape[0], :] = small
    turned = turn_v[...].T
    for i, ref in enumerate(norm_refs):
        ref[...] = turned[NORM_LANE + i : NORM_LANE + i + 1, : ref.shape[1]]


class Share:
    def __init__(self, parts, order):
        self.parts = parts
        self.order = order[1:]
        self.left = sorted(order)
        self.depth = parts[0].shape[1]
        self.wide = sum(part.shape[2] for part in parts)
        self.mine = None
        self.swap(order[0], self.of_core(1 - (lax.axis_index("dp") & 1)))

    def of_core(self, core):
        halves = [
            lax.dynamic_index_in_dim(
                part.reshape((part.shape[0] // 2, 2) + part.shape[1:]), core, 1, keepdims=False
            )
            for part in self.parts
        ]
        return halves[0] if len(halves) == 1 else jnp.concatenate(halves, 2)

    def swap(self, bit, theirs):
        count = lax.axis_size("dp")
        self.left.remove(bit)
        self.sent = theirs
        self.arrived = lax.ppermute(theirs, "dp", [(i, i ^ (1 << bit)) for i in range(count)])

    def total(self):
        kept = self.of_core(lax.axis_index("dp") & 1) if self.mine is None else self.mine
        return kept.astype(F32) + self.arrived.astype(F32)

    def split_at(self):
        bit = self.order[0]
        axis = len(self.left) - 1 - self.left.index(bit)
        return bit, 2**axis, 2 ** (len(self.left) - 1 - axis)

    def halve(self):
        bit, above, below = self.split_at()
        self.order = self.order[1:]
        split = self.total().reshape(above, 2, below, self.depth, self.wide)
        here = (lax.axis_index("dp") >> bit) & 1
        theirs = lax.dynamic_index_in_dim(split, 1 - here, 1, keepdims=False).astype(BF16)
        mine = lax.dynamic_index_in_dim(split, here, 1, keepdims=False)
        self.mine = mine.reshape(-1, self.depth, self.wide)
        self.swap(bit, theirs.reshape(-1, self.depth, self.wide))


def halve_all(me, shares, afters=(), through=()):
    if any(share.depth % 16 for share in shares):
        for share in shares:
            share.halve()
        return through
    ins, in_specs, outs, out_specs, bits, counts = [], [], [], [], [], []
    for share in shares:
        bit, above, below = share.split_at()
        bits.append(bit)

        def halves(wide, b=below):
            return pl.BlockSpec((1, 2, 1, share.depth, wide), lambda i, me: (i // b, 0, i % b, 0, 0))

        if share.mine is None:
            counts.append(len(share.parts))
            for part in share.parts:
                wide = part.shape[2]
                ins.append(part.reshape(above, 2, below, 2, share.depth, wide))
                in_specs.append(
                    pl.BlockSpec(
                        (1, 2, 1, 1, share.depth, wide),
                        lambda i, me, b=below: (i // b, 0, i % b, me[0] & 1, 0, 0),
                    )
                )
        else:
            counts.append(1)
            ins.append(share.mine.reshape(above, 2, below, share.depth, share.wide))
            in_specs.append(halves(share.wide))
        ins.append(share.arrived.reshape(above, 2, below, share.depth, share.wide))
        in_specs.append(halves(share.wide))
        outs += [
            jax.ShapeDtypeStruct((above, below, share.depth, share.wide), kind) for kind in (BF16, F32)
        ]
        out_specs += [
            pl.BlockSpec((1, 1, share.depth, share.wide), lambda i, me, b=below: (i // b, i % b, 0, 0))
        ] * 2
        steps = above * below
    results = pl.pallas_call(
        functools.partial(halve_kernel, tuple(bits), tuple(counts), len(afters), len(through)),
        grid_spec=pltpu.PrefetchScalarGridSpec(
            num_scalar_prefetch=1,
            grid=(steps,),
            in_specs=in_specs + [ANY] * (len(afters) + len(through)),
            out_specs=out_specs + [ANY] * len(through),
        ),
        out_shape=outs + [jax.ShapeDtypeStruct(array.shape, array.dtype) for array in through],
        input_output_aliases={
            1 + len(ins) + len(afters) + i: len(outs) + i for i in range(len(through))
        },
        compiler_params=pltpu.CompilerParams(vmem_limit_bytes=VMEM_BYTES if through else SMALL_VMEM_BYTES),
        name="halve",
    )(me, *ins, *afters, *through)
    for i, share in enumerate(shares):
        share.order = share.order[1:]
        share.mine = results[2 * i + 1].reshape(-1, share.depth, share.wide)
        share.swap(bits[i], results[2 * i].reshape(-1, share.depth, share.wide))
    return results[len(outs) :]


def joined(near, far, width, table_shape):
    parts = [x[0] for share in (near, far) for x in (share.mine, share.arrived)]
    shapes = [(near.depth, width), (near.depth, near.wide + far.wide - width - LANES), table_shape]
    shapes += [(1, near.depth)] * 4
    return pl.pallas_call(
        join_kernel,
        out_shape=[jax.ShapeDtypeStruct(dims, F32) for dims in shapes],
        in_specs=[VMEM] * len(parts),
        out_specs=[VMEM] * len(shapes),
        scratch_shapes=[pltpu.VMEM((LANES, LANES), F32)],
        compiler_params=pltpu.CompilerParams(vmem_limit_bytes=SMALL_VMEM_BYTES),
        name="join",
    )(*parts)


def passed_along(x, axis, by):
    length = lax.axis_size(axis)
    pairs = [(i, i + by) for i in range(length) if 0 <= i + by < length]
    return lax.ppermute(x, axis, pairs)


def shards(
    hidden_in, out_grad, qkv_weight, out_weight, rel_table, norm1_gain, norm1_bias,
    up_weight, down_weight, norm2_gain, norm2_bias, seg_ids, pad_mask, rel_buckets,
):
    phase = lax.axis_index("phase").astype(jnp.int32).reshape(1)
    ways = lax.axis_size("dp")
    slots, width = hidden_in.shape
    inner = up_weight.shape[2]
    buckets, heads = rel_table.shape[1:]

    def shape(dims, kind):
        return jax.ShapeDtypeStruct(dims, kind)

    rows_of = {
        "xin": (width, BF16), "qkv": (3 * width, BF16), "ctx": (width, BF16), "form1": (width, F32),
        "scale1": (1, F32), "low1": (width, BF16), "slope": (inner, BF16), "act": (inner, BF16),
        "form2": (width, F32), "scale2": (1, F32), "out": (width, BF16),
        "outer_low": (width, BF16), "hidden_low": (inner, BF16), "residual_low": (width, BF16),
        "projected": (3 * width, BF16), "input_grad": (width, BF16),
    }
    kept_shapes = [
        shape((slots, rows_of[name][0]), rows_of[name][1])
        if name in rows_of
        else {
            "weights": shape((MICRO, heads, BLOCK, BLOCK), BF16),
            "sums1": shape((MICRO, 8, width), F32),
            "sums2": shape((MICRO, 8, width), F32),
            "residual": shape((BLOCK, width), F32),
            "offsets": shape((MICRO, heads, 8, SPAN), F32),
            "bias": shape((heads, TILE, SPAN), F32),
        }[name]
        for name in KEPT
    ]
    in_forward = ("qkv", "ctx", "form1", "scale1", "low1", "slope", "act", "form2", "scale2", "out")
    scratch = {f"{name}_v": ((BLOCK, rows_of[name][0]), rows_of[name][1]) for name in in_forward}
    scratch |= {
        name: ((BLOCK, width), BF16) for name in ("x_v", "g_v", "outer_v", "residual_low_v", "dctx_v", "grad_v")
    }
    scratch |= {
        "weights_v": ((heads, BLOCK, BLOCK), BF16), "acc_v": ((BLOCK, width), F32), "square_v": ((2, BLOCK, BLOCK), F32),
        "values_v": ((heads, SPAN), F32), "bias_v": ((heads, TILE, SPAN), F32), "sums1_v": ((8, width), F32), "sums2_v": ((8, width), F32),
        "wqkv_v": ((width, 3 * width), BF16), "wout_v": ((width, width), BF16), "wup_v": ((width, inner), BF16),
        "wdown_v": ((inner, width), BF16), "fold_v": ((2, TILE, SPAN), F32), "eighth_v": ((heads, 8, SPAN), F32),
        "half_v": ((2, BLOCK, BLOCK), BF16),
    }

    def step(work, phase_on, block, received, kept, afters=()):
        values = (
            phase, seg_ids, hidden_in, received, out_grad, rel_table, pad_mask[None, :], rel_buckets[None, :],
            norm1_gain, norm1_bias, norm2_gain, norm2_bias, qkv_weight, out_weight, up_weight, down_weight,
        )
        in_place = None if kept is None else [kept[name] for name in KEPT]
        return layer_step(work, phase_on, block, values, list(afters), in_place, kept_shapes, scratch)

    kept, sent = step("forward", 0, 0, hidden_in, None)
    first = passed_along(sent, "phase", 1)
    kept, _ = step("bias", 1, 0, hidden_in, kept)
    kept, sent = step("forward", 0, 1, hidden_in, kept)
    second = passed_along(sent, "phase", 1)
    kept, sent = step("both", 1, 0, first, kept)
    first_back = passed_along(sent, "phase", -1)
    kept, sent = step("both", 1, 1, second, kept)
    second_back = passed_along(sent, "phase", -1)
    kept, _ = step("back", 0, 0, first_back, kept)
    kept, _ = step("ffn_back", 0, 1, second_back, kept)

    bits = ways.bit_length() - 1
    near_first = list(range(bits))
    far_first = [0] + list(range(2, bits)) + [1] if bits > 1 else near_first
    me = lax.axis_index("dp").astype(jnp.int32).reshape(1)

    def weight_grad(left, right):
        product = dot_tn(left, right).astype(BF16)
        return product.reshape(ways, product.shape[0] // ways, product.shape[1])

    down = Share([weight_grad(kept["act"], kept["outer_low"])], near_first)
    up = Share([weight_grad(kept["low1"], kept["hidden_low"])], far_first)
    out_part = weight_grad(kept["ctx"], kept["residual_low"])
    halve_all(me, [down])
    halve_all(me, [up])
    kept, _ = step("attn_back", 0, 1, hidden_in, kept, [down.sent, up.sent])
    far = Share([weight_grad(kept["xin"], kept["projected"][:, width:])], far_first)
    (slots_in,) = halve_all(me, [down, up], [far.sent], [kept["xin"]])
    near_part = weight_grad(slots_in, kept["projected"][:, :width])
    small = packed(ways, buckets, rel_buckets[None, :], kept, [far.sent])
    near = Share([out_part, near_part, small], near_first)
    halve_all(me, [near, far], [down.sent, up.sent])
    halve_all(me, [down, up])
    halve_all(me, [near, far], [down.sent, up.sent])
    while down.order:
        halve_all(me, [down, up])
    while near.order:
        halve_all(me, [near, far])
    down_share = down.total()[0]
    up_share = up.total()[0]
    out_share, qkv_share, table_share, *norm_shares = joined(near, far, width, (buckets // ways, heads))
    return (
        kept["out"][None],
        kept["input_grad"][None],
        qkv_share[None],
        out_share[None],
        table_share[None],
        norm_shares[0],
        norm_shares[1],
        up_share[None],
        down_share[None],
        norm_shares[2],
        norm_shares[3],
    )


def solution(mesh):
    return jax.shard_map(
        shards,
        mesh=mesh,
        in_specs=(
            P("dp", None),
            P("dp", None),
            P("phase", None, None),
            P("phase", None, None),
            P("phase", None, None),
            P("phase", None),
            P("phase", None),
            P("phase", None, None),
            P("phase", None, None),
            P("phase", None),
            P("phase", None),
            P("dp"),
            P("dp"),
            P(),
        ),
        out_specs=(
            P("phase", "dp", None),
            P("phase", "dp", None),
            P("phase", "dp", None),
            P("phase", "dp", None),
            P("phase", "dp", None),
            P("phase", "dp"),
            P("phase", "dp"),
            P("phase", "dp", None),
            P("phase", "dp", None),
            P("phase", "dp"),
            P("phase", "dp"),
        ),
        check_vma=False,
    )
```

```python
import functools

import jax
import jax.numpy as jnp
from jax import lax
from jax.experimental import pallas as pl
from jax.experimental.pallas import tpu as pltpu
from jax.sharding import PartitionSpec as P

BLOCK = 512
MICRO = 2
TILE = 128
LANES = 128
CHUNK = 512
SPAN = 2 * BLOCK
VMEM_BYTES = 58 * 1024 * 1024
SMALL_VMEM_BYTES = 20 * 1024 * 1024
NORM_LANE = 16

norm_eps = 1e-05
mask_fill = -1000000000.0
score_scale = 0.125
inv_root_two = 0.7071067811865476
inv_root_tau = 0.3989422804014327
log2_e = 1.4426950408889634
highest = lax.Precision.HIGHEST

F32 = jnp.float32
BF16 = jnp.bfloat16
ANY = pl.BlockSpec(memory_space=pl.ANY)
VMEM = pl.BlockSpec(memory_space=pltpu.VMEM)
QUICK = pl.CostEstimate(flops=1, bytes_accessed=1, transcendentals=0)
SMEM = pl.BlockSpec(memory_space=pltpu.SMEM)


def dot_nn(a, b):
    return lax.dot_general(a, b, (((1,), (0,)), ((), ())), preferred_element_type=F32)


def dot_nt(a, b):
    return lax.dot_general(a, b, (((1,), (1,)), ((), ())), preferred_element_type=F32)


def dot_tn(a, b):
    return lax.dot_general(a, b, (((0,), (0,)), ((), ())), preferred_element_type=F32)


def row_mean(rows):
    return jnp.sum(rows, -1, keepdims=True) * (1.0 / rows.shape[-1])


def normal_parts(residual):
    centred = residual - row_mean(residual)
    inv_scale = lax.rsqrt(row_mean(centred * centred) + norm_eps)
    return centred * inv_scale, inv_scale


def norm_backward(grad_rows, normal_form, inv_scale):
    first = row_mean(grad_rows)
    second = row_mean(grad_rows * normal_form)
    return inv_scale * (grad_rows - first - normal_form * second)


def gelu_parts(hidden):
    share = 0.5 + 0.5 * lax.erf(hidden * inv_root_two)
    bell = jnp.exp2(hidden * hidden * (-0.5 * log2_e))
    return hidden * share, share + hidden * bell * inv_root_tau


def half_mask(which, shape):
    lane = lax.broadcasted_iota(jnp.int32, shape, 1)
    return (lane < LANES // 2) if which == 0 else (lane >= LANES // 2)


class Copies:
    def __init__(self, sems):
        self.sems = sems
        self.used = 0
        self.stores = []

    def take(self, count=1):
        self.used += count
        return self.used - count

    def load(self, source, target):
        copy = pltpu.make_async_copy(source, target, self.sems.at[self.take()])
        copy.start()
        return copy

    def store(self, source, target, when=True):
        if when:
            self.stores.append(self.load(source, target))

    def finish(self):
        for copy in self.stores:
            copy.wait()


KEPT = (
    "xin", "qkv", "weights", "ctx", "form1", "scale1", "low1", "slope", "act", "form2", "scale2", "out",
    "bias", "outer_low", "hidden_low", "residual_low", "sums1", "sums2", "residual", "projected", "offsets", "input_grad",
)
INS = (
    "phase", "segments", "hidden_in", "received", "out_grad", "table", "padding", "buckets",
    "gain1", "shift1", "gain2", "shift2",
    "wqkv", "wout", "wup", "wdown",
)


class Layer:
    def __init__(self, refs):
        self.__dict__.update(refs)
        self.copies = Copies(self.sems)
        self.width = self.hidden_in.shape[1]
        self.inner = self.wup.shape[2]
        self.pairs = self.width // LANES
        self.stages = self.inner // (2 * CHUNK)
        self.pair_sems = self.copies.take(self.pairs)
        self.chunk_sems = [self.copies.take(self.stages) for _ in range(3)]

    def lanes_of(self, pair, part):
        return pl.ds(pl.multiple_of(part * self.width + pair * LANES, LANES), LANES)

    def stage(self, i):
        return pl.ds(pl.multiple_of(i * 2 * CHUNK, 2 * CHUNK), 2 * CHUNK)

    def build_bias(self):
        span = self.buckets.shape[1]
        bucket_ids = lax.broadcasted_iota(jnp.int32, (self.table.shape[2], span), 0)
        hot = (bucket_ids == self.buckets[...]).astype(F32)
        table = jnp.concatenate([self.table[head] for head in range(self.table.shape[0])], 0)
        values = lax.dot_general(
            table, hot, (((1,), (0,)), ((), ())), precision=highest, preferred_element_type=F32
        )
        self.values_v[:, :span] = values
        self.values_v[:, span:] = jnp.zeros((values.shape[0], SPAN - span), F32)

        def one_head(head, carry):
            wide = jnp.broadcast_to(self.values_v[pl.ds(head, 1), :], (TILE, SPAN))
            self.bias_v[head] = pltpu.roll(wide, 1, 1, stride=1, stride_axis=0)
            return carry

        lax.fori_loop(0, values.shape[0], one_head, 0)
        self.copies.store(self.bias_v, self.bias)


    def rows(self, block):
        return pl.ds(block * BLOCK, BLOCK)

    def forward(self, block, keep, built):
        copies = self.copies
        rows = self.rows(block)
        load_x = copies.load(self.hidden_in.at[rows] if keep else self.received, self.x_v)
        width = self.width
        loads = [
            copies.load(self.wqkv.at[0, :, pl.ds(c, width)], self.wqkv_v.at[:, pl.ds(c, width)])
            for c in range(0, 3 * width, width)
        ]
        if not built:
            self.build_bias()
        load_x.wait()

        def load_bias(pair):
            heads = pl.ds(2 * pair, 2)
            return pltpu.make_async_copy(self.bias.at[heads], self.bias_v.at[heads], self.sems.at[self.pair_sems + pair])

        for i, c in enumerate(range(0, 3 * width, width)):
            loads[i].wait()
            if built and i < 2:
                load_bias(i).start()
            self.qkv_v[:, c : c + width] = dot_nn(self.x_v[...], self.wqkv_v[:, c : c + width]).astype(BF16)
        copies.store(self.x_v, self.xin.at[rows])
        copies.store(self.qkv_v, self.qkv.at[rows], keep)
        weights_sem = self.sems.at[copies.take()]
        later_loads = [
            pltpu.make_async_copy(source.at[0], target, self.sems.at[copies.take()])
            for source, target in ((self.wout, self.wout_v), (self.wup, self.wup_v), (self.wdown, self.wdown_v))
        ]

        def own(pair, part, which):
            both = self.qkv_v[:, self.lanes_of(pair, part)]
            return jnp.where(half_mask(which, both.shape), both, jnp.zeros_like(both))

        single = self.segments[block * BLOCK + TILE] == self.segments[block * BLOCK]
        padding = self.padding[:, block * BLOCK : (block + 1) * BLOCK]
        tile_of = lax.broadcasted_iota(jnp.int32, (1, BLOCK), 1) // TILE
        shut = [
            jnp.where((padding == 1) & (single | (tile_of == tile)), 0.0, mask_fill) for tile in range(BLOCK // TILE)
        ]
        row_id = lax.broadcasted_iota(jnp.int32, (TILE, TILE), 0)
        diagonal = row_id == lax.broadcasted_iota(jnp.int32, (TILE, TILE), 1)

        def bias_rows(head, tile):
            at = BLOCK - tile * TILE
            rows = self.bias_v[head, :, at : at + BLOCK]
            masked = rows + shut[tile]
            own = slice(tile * TILE, (tile + 1) * TILE)
            parts = [masked[:, : own.start], jnp.where(diagonal, rows[:, own], masked[:, own]), masked[:, own.stop :]]
            return jnp.concatenate([part for part in parts if part.shape[1]], 1)

        def weigh(pair, which):
            head = 2 * pair + which
            k_own = own(pair, 1, which)
            for r in range(0, BLOCK, 2 * TILE):
                q_rows = self.qkv_v[r : r + 2 * TILE, self.lanes_of(pair, 0)] * jnp.asarray(score_scale, BF16)
                tiles = [bias_rows(head, tile) for tile in range(r // TILE, r // TILE + 2)]
                logits = dot_nt(q_rows, k_own) + jnp.concatenate(tiles, 0)
                raised = jnp.exp(logits - jnp.max(logits, -1, keepdims=True))
                share = pl.reciprocal(jnp.sum(raised, -1, keepdims=True), approx=True)
                self.weights_v[head, r : r + 2 * TILE, :] = (raised * share).astype(BF16)

        def head_pair(pair, carry):
            if built:
                load_bias(pair).wait()

                @pl.when(pair + 2 < self.pairs)
                def _():
                    load_bias(pair + 2).start()

            @pl.when(pair == 1)
            def _():
                for load in later_loads:
                    load.start()

            weigh(pair, 0)
            context = dot_nn(self.weights_v[2 * pair], own(pair, 2, 0))
            weigh(pair, 1)
            context += dot_nn(self.weights_v[2 * pair + 1], own(pair, 2, 1))
            self.ctx_v[:, self.lanes_of(pair, 0)] = context.astype(BF16)
            if keep:
                heads = pl.ds(2 * pair, 2)
                pltpu.make_async_copy(self.weights_v.at[heads], self.weights.at[block, heads], weights_sem).start()
            return carry

        lax.fori_loop(0, self.pairs, head_pair, 0)
        if keep:
            copies.stores.append(pltpu.make_async_copy(self.weights_v, self.weights.at[block], weights_sem))
        copies.store(self.ctx_v, self.ctx.at[rows])
        load_out, load_up, load_down = later_loads
        load_out.wait()
        self.acc_v[...] = dot_nn(self.ctx_v[...], self.wout_v[...])
        for r in range(0, BLOCK, 64):
            tile = slice(r, r + 64)
            form, scale = normal_parts(self.acc_v[tile, :] + self.x_v[tile, :].astype(F32))
            normed = form * self.gain1[...] + self.shift1[...]
            self.form1_v[tile, :] = form
            self.scale1_v[tile, :] = scale
            self.acc_v[tile, :] = normed
            self.low1_v[tile, :] = normed.astype(BF16)
        copies.store(self.form1_v, self.form1.at[rows], keep)
        copies.store(self.scale1_v, self.scale1.at[rows], keep)
        copies.store(self.low1_v, self.low1.at[rows])
        load_up.wait()
        load_down.wait()
        act_sem = self.sems.at[copies.take()]
        slope_sem = self.sems.at[copies.take()]

        def two_chunks(i, carry):
            span = self.stage(i)
            active, grade = gelu_parts(dot_nn(self.low1_v[...], self.wup_v[:, span]))
            active = active.astype(BF16)
            self.act_v[:, span] = active
            self.slope_v[:, span] = grade.astype(BF16)
            self.acc_v[...] += dot_nn(active, self.wdown_v[span, :])
            pltpu.make_async_copy(self.act_v.at[:, span], self.act.at[rows, span], act_sem).start()
            if keep:
                pltpu.make_async_copy(self.slope_v.at[:, span], self.slope.at[rows, span], slope_sem).start()
            return carry

        lax.fori_loop(0, self.stages, two_chunks, 0)
        copies.stores.append(pltpu.make_async_copy(self.act_v, self.act.at[rows], act_sem))
        if keep:
            copies.stores.append(pltpu.make_async_copy(self.slope_v, self.slope.at[rows], slope_sem))
        for r in range(0, BLOCK, 64):
            tile = slice(r, r + 64)
            form, scale = normal_parts(self.acc_v[tile, :])
            self.form2_v[tile, :] = form
            self.scale2_v[tile, :] = scale
            self.out_v[tile, :] = (form * self.gain2[...] + self.shift2[...]).astype(BF16)
        copies.store(self.out_v, self.send, keep)
        copies.store(self.out_v, self.out.at[rows])
        copies.store(self.form2_v, self.form2.at[rows], keep)
        copies.store(self.scale2_v, self.scale2.at[rows], keep)


    def chunk_loads(self, i, rows):
        span = self.stage(i)
        return [
            pltpu.make_async_copy(source, target, self.sems.at[self.chunk_sems[k] + i])
            for k, (source, target) in enumerate(
                (
                    (self.wdown.at[0, span], self.wdown_v.at[span]),
                    (self.slope.at[rows, span], self.slope_v.at[:, span]),
                    (self.wup.at[0, :, span], self.wup_v.at[:, span]),
                )
            )
        ]

    def norm_sums(self, source, form_ref, sums_ref):
        gain_sum = jnp.zeros((1, self.width), F32)
        shift_sum = jnp.zeros((1, self.width), F32)
        for r in range(0, BLOCK, 64):
            grad_rows, form = source[r : r + 64, :].astype(F32), form_ref[r : r + 64, :]
            gain_sum += jnp.sum(grad_rows * form, 0, keepdims=True)
            shift_sum += jnp.sum(grad_rows, 0, keepdims=True)
        sums_ref[...] = jnp.zeros(sums_ref.shape, F32)
        sums_ref[0:1, :] = gain_sum
        sums_ref[1:2, :] = shift_sum

    def norm_back(self, block):
        for r in range(0, BLOCK, 64):
            tile = slice(r, r + 64)
            grad_rows = self.g_v[tile, :].astype(F32) * self.gain2[...]
            grad_outer = norm_backward(grad_rows, self.form2_v[tile, :], self.scale2_v[tile, :])
            self.acc_v[tile, :] = grad_outer
            self.outer_v[tile, :] = grad_outer.astype(BF16)
        self.copies.store(self.outer_v, self.outer_low.at[self.rows(block)])

    def norm_sums_2(self, block):
        self.norm_sums(self.g_v, self.form2_v, self.sums2_v)
        self.copies.store(self.sums2_v, self.sums2.at[block])

    def ffn_back(self, block, staged=False, middle_loads=()):
        copies = self.copies
        rows = self.rows(block)
        hidden_sem = self.sems.at[copies.take()]

        def two_chunks(i, carry):
            span = self.stage(i)
            if staged:
                load_down, load_slope, load_up = self.chunk_loads(i, rows)
                load_down.wait()
                load_slope.wait()
            grad_active = dot_nt(self.outer_v[...], self.wdown_v[span, :])
            hidden = (grad_active * self.slope_v[:, span].astype(F32)).astype(BF16)
            self.slope_v[:, span] = hidden
            if staged:
                load_up.wait()

                @pl.when(i + 2 < self.stages)
                def _():
                    for load in self.chunk_loads(i + 2, rows):
                        load.start()

            self.acc_v[...] += dot_nt(hidden, self.wup_v[:, span])
            pltpu.make_async_copy(self.slope_v.at[:, span], self.hidden_low.at[rows, span], hidden_sem).start()
            return carry

        lax.fori_loop(0, self.stages, two_chunks, 0)
        copies.stores.append(pltpu.make_async_copy(self.slope_v, self.hidden_low.at[rows], hidden_sem))
        for load in middle_loads:
            load.wait()
        self.norm_sums(self.acc_v, self.form1_v, self.sums1_v)
        for r in range(0, BLOCK, 64):
            tile = slice(r, r + 64)
            grad_residual = norm_backward(
                self.acc_v[tile, :] * self.gain1[...], self.form1_v[tile, :], self.scale1_v[tile, :]
            )
            self.acc_v[tile, :] = grad_residual
            self.residual_low_v[tile, :] = grad_residual.astype(BF16)
        copies.store(self.residual_low_v, self.residual_low.at[rows])
        copies.store(self.sums1_v, self.sums1.at[block])

    def attn_back(self, block, next_loads=None, load_in=()):
        copies = self.copies
        rows = self.rows(block)
        self.dctx_v[...] = dot_nt(self.residual_low_v[...], self.wout_v[...]).astype(BF16)
        self.fold_v[:, :, 0:TILE] = jnp.zeros((2, TILE, TILE), F32)

        def head_pair(pair, carry):
            def lanes_of(part):
                return self.lanes_of(pair, part)

            if next_loads is not None:
                next_loads(pair)
            q_pair, k_pair, v_pair = (self.qkv_v[:, lanes_of(part)] for part in range(3))
            grad_pair = self.dctx_v[:, lanes_of(0)]
            crossed = grad_pair.astype(F32) * self.ctx_v[:, lanes_of(0)].astype(F32)
            masks = [half_mask(which, k_pair.shape) for which in range(2)]

            def own(both, which):
                return jnp.where(masks[which], both, jnp.zeros_like(both))

            for which in range(2):
                self.square_v[which] = dot_nt(grad_pair, own(v_pair, which))
            q_grad = k_grad = v_grad = 0.0
            for which in range(2):
                head = 2 * pair + which
                delta = jnp.sum(own(crossed, which), -1, keepdims=True)
                for r in range(0, BLOCK, 64):
                    tile = slice(r, r + 64)
                    score_grad = (
                        self.weights_v[head, tile, :].astype(F32) * (self.square_v[which, tile, :] - delta[tile, :])
                    ).astype(BF16)
                    self.half_v[which, tile, :] = score_grad
                    at = BLOCK - r // TILE * TILE
                    wide = score_grad.astype(F32)
                    half = slice(r % TILE, r % TILE + 64)
                    if r < TILE:
                        self.fold_v[which, half, at : at + BLOCK] = wide
                    else:
                        self.fold_v[which, half, at : at + TILE] = wide[:, :TILE]
                        self.fold_v[which, half, at + TILE : at + BLOCK] += wide[:, TILE:]
                v_grad += dot_tn(self.weights_v[head], own(grad_pair, which))
                q_grad += dot_nn(self.half_v[which], own(k_pair, which))
                k_grad += dot_tn(self.half_v[which], own(q_pair, which))
                folded = self.fold_v[which]
                size = TILE // 2
                while size >= 8:
                    folded = folded[:size, :] + pltpu.roll(folded[size:, :], SPAN - size, 1)
                    size //= 2
                self.eighth_v[head] = folded
            self.qkv_v[:, lanes_of(0)] = (q_grad * score_scale).astype(BF16)
            self.qkv_v[:, lanes_of(1)] = (k_grad * score_scale).astype(BF16)
            self.qkv_v[:, lanes_of(2)] = v_grad.astype(BF16)
            return carry

        lax.fori_loop(0, self.pairs, head_pair, 0)
        copies.store(self.eighth_v, self.offsets.at[block])
        copies.store(self.qkv_v, self.projected.at[rows])
        for load in load_in:
            load.wait()
        self.grad_v[...] = (self.acc_v[...] + dot_nt(self.qkv_v[...], self.wqkv_v[...])).astype(BF16)
        copies.store(self.grad_v, self.send)
        copies.store(self.grad_v, self.input_grad.at[rows])


    def do_forward(self, block):
        self.forward(block, True, block > 0)

    def do_bias(self, block):
        self.build_bias()

    def do_both(self, block):
        load = self.copies.load(self.out_grad.at[self.rows(block)], self.g_v)
        self.forward(block, False, True)
        load.wait()
        self.norm_back(block)
        self.ffn_back(block)
        self.norm_sums_2(block)
        self.attn_back(block)

    def do_back(self, block):
        rows = self.rows(block)
        loads = [
            self.copies.load(source, target)
            for source, target in (
                (self.received, self.g_v),
                (self.form2.at[rows], self.form2_v),
                (self.scale2.at[rows], self.scale2_v),
                (self.slope.at[rows], self.slope_v),
                (self.wdown.at[0], self.wdown_v),
                (self.wup.at[0], self.wup_v),
                (self.form1.at[rows], self.form1_v),
                (self.scale1.at[rows], self.scale1_v),
                (self.qkv.at[rows], self.qkv_v),
                (self.weights.at[block], self.weights_v),
                (self.ctx.at[rows], self.ctx_v),
                (self.wout.at[0], self.wout_v),
                (self.wqkv.at[0], self.wqkv_v),
            )
        ]
        for load in loads:
            load.wait()
        self.norm_back(block)
        self.ffn_back(block)
        self.norm_sums_2(block)
        self.attn_back(block)

    def do_ffn_back(self, block):
        rows = self.rows(block)
        loads = [
            self.copies.load(source, target)
            for source, target in (
                (self.received, self.g_v),
                (self.form2.at[rows], self.form2_v),
                (self.scale2.at[rows], self.scale2_v),
            )
        ]
        self.chunk_loads(0, rows)[0].start()
        for load in loads:
            load.wait()
        for load in self.chunk_loads(0, rows)[1:] + self.chunk_loads(1, rows):
            load.start()
        middle = [
            self.copies.load(self.form1.at[rows], self.form1_v),
            self.copies.load(self.scale1.at[rows], self.scale1_v),
        ]
        self.norm_back(block)
        self.ffn_back(block, True, middle)
        self.copies.store(self.acc_v, self.residual)
        self.norm_sums_2(block)

    def do_attn_back(self, block):
        rows = self.rows(block)
        loads = [
            self.copies.load(source, target)
            for source, target in ((self.residual_low.at[rows], self.residual_low_v), (self.wout.at[0], self.wout_v))
        ]
        first = self.copies.take(5 * self.pairs)

        def pair_loads(pair):
            heads = pl.ds(2 * pair, 2)
            sources = [(self.weights.at[block, heads], self.weights_v.at[heads])]
            for source, target, parts in ((self.qkv, self.qkv_v, 3), (self.ctx, self.ctx_v, 1)):
                for part in range(parts):
                    lanes = self.lanes_of(pair, part)
                    sources.append((source.at[rows, lanes], target.at[:, lanes]))
            return [
                pltpu.make_async_copy(source, target, self.sems.at[first + 5 * pair + k])
                for k, (source, target) in enumerate(sources)
            ]

        for pair in range(2):
            for load in pair_loads(pair):
                load.start()
        for load in loads:
            load.wait()
        last = [
            pltpu.make_async_copy(source, target, self.sems.at[self.copies.take()])
            for source, target in ((self.wqkv.at[0], self.wqkv_v), (self.residual, self.acc_v))
        ]

        def next_loads(pair):
            for load in pair_loads(pair):
                load.wait()

            @pl.when(pair + 2 < self.pairs)
            def _():
                for load in pair_loads(pair + 2):
                    load.start()

            @pl.when(pair == self.pairs - 3)
            def _():
                for load in last:
                    load.start()

        self.attn_back(block, next_loads, last)


def layer_kernel(work, phase_on, block, ins, outs, scratch, after_count, kept_count, *refs):
    refs_in, refs = refs[: len(ins)], refs[len(ins) + after_count + kept_count :]
    named = dict(zip(ins, refs_in)) | dict(zip(outs, refs)) | dict(zip(scratch, refs[len(outs) :]))

    @pl.when(named["phase"][0] == phase_on)
    def _():
        layer = Layer(named)
        getattr(layer, f"do_{work}")(block)
        layer.copies.finish()


def layer_step(work, phase_on, block, values, afters, kept, kept_shapes, scratch):
    specs = [SMEM] * 2 + [ANY] * 3 + [VMEM] * 7 + [ANY] * 4
    names = list(scratch)
    kept = list(kept) if kept is not None else []
    sent = jax.ShapeDtypeStruct((BLOCK, values[2].shape[1]), BF16)
    if work == "bias":
        names = ["values_v", "bias_v"]
    count = len(values) + len(afters)
    results = pl.pallas_call(
        functools.partial(
            layer_kernel, work, phase_on, block, INS, KEPT + ("send",), names + ["sems"], len(afters), len(kept)
        ),
        out_shape=list(kept_shapes) + [sent],
        in_specs=specs + [ANY] * (len(afters) + len(kept)),
        out_specs=[ANY] * (len(kept_shapes) + 1),
        scratch_shapes=[pltpu.VMEM(*scratch[name]) for name in names] + [pltpu.SemaphoreType.DMA((96,))],
        input_output_aliases={count + i: i for i in range(len(kept))},
        compiler_params=pltpu.CompilerParams(vmem_limit_bytes=VMEM_BYTES),
        name=f"{work}_{phase_on}_{block}",
    )(*values, *afters, *kept)
    return dict(zip(KEPT, results)), results[-1]


def pack_kernel(ways, buckets_ref, offsets_ref, sums1_ref, sums2_ref, *refs):
    out_ref, turn_v = refs[-2:]
    row_of = lax.broadcasted_iota(jnp.int32, (8, SPAN), 0)
    lines = []
    for head in range(offsets_ref.shape[1]):
        eighth = offsets_ref[0, head] + offsets_ref[1, head]
        for size in (4, 2, 1):
            eighth = jnp.where((row_of & size) != 0, pltpu.roll(eighth, SPAN - size, 1), eighth)
        lines.append(jnp.sum(eighth, 0, keepdims=True))
    lines += [jnp.zeros((1, SPAN), F32)] * (NORM_LANE - len(lines))
    sums = pltpu.roll(jnp.concatenate(lines, 0), SPAN - 1, 1)
    span = buckets_ref.shape[1]
    buckets, depth = out_ref.shape[0] // 3, out_ref.shape[0] // ways
    share = buckets // ways
    bucket_ids = lax.broadcasted_iota(jnp.int32, (buckets, span), 0)
    hot = (bucket_ids == buckets_ref[...]).astype(F32)
    table = lax.dot_general(
        hot, sums[:, :span], (((1,), (1,)), ((), ())), precision=highest, preferred_element_type=F32
    ).astype(BF16)
    turn_v[...] = jnp.zeros(turn_v.shape, F32)
    for i, ref in enumerate((sums1_ref, sums2_ref)):
        at = NORM_LANE + 2 * i
        turn_v[at : at + 2, :] = ref[0, 0:2, :] + ref[1, 0:2, :]
    out_ref[...] = turn_v[...].T.astype(BF16)
    for i in range(ways):
        out_ref[i * depth : i * depth + share, 0:NORM_LANE] = table[i * share : (i + 1) * share, :]


def packed(ways, buckets, offset_buckets, kept, afters):
    width = kept["sums1"].shape[2]
    depth, share = width // ways, buckets // ways
    arrays = (offset_buckets, kept["offsets"], kept["sums1"], kept["sums2"])
    if depth % 16 == 0 and share % 16 == 0 and 3 * buckets == width:
        rows = pl.pallas_call(
            functools.partial(pack_kernel, ways),
            out_shape=jax.ShapeDtypeStruct((width, LANES), BF16),
            in_specs=[VMEM] * len(arrays) + [ANY] * len(afters),
            out_specs=VMEM,
            scratch_shapes=[pltpu.VMEM((LANES, width), F32)],
            compiler_params=pltpu.CompilerParams(vmem_limit_bytes=SMALL_VMEM_BYTES),
            name="pack",
        )(*arrays, *afters)
        return rows.reshape(ways, depth, LANES)
    eighths = jnp.sum(kept["offsets"], 0)
    lines = sum(jnp.roll(eighths[:, i, :], -i, 1) for i in range(8))[:, 1:]
    hot = (offset_buckets[0][None, :] == jnp.arange(buckets, dtype=jnp.int32)[:, None]).astype(F32)
    table = jnp.dot(hot, lines.T, precision=highest).reshape(ways, share, -1)
    table = jnp.pad(table, ((0, 0), (0, depth - share), (0, NORM_LANE - table.shape[2])))
    norms = jnp.concatenate([jnp.sum(kept[name], 0)[:2] for name in ("sums1", "sums2")], 0)
    norms = norms.T.reshape(ways, depth, 4)
    rows = jnp.concatenate([table, norms], 2)
    return jnp.pad(rows, ((0, 0), (0, 0), (0, LANES - rows.shape[2]))).astype(BF16)


def halve_kernel(bits, counts, after_count, through_count, me_ref, *refs):
    used = sum(counts) + len(counts)
    outs = refs[used + after_count + through_count :]
    for i, count in enumerate(counts):
        kept_refs, arrived_ref = refs[:count], refs[count]
        refs = refs[count + 1 :]
        send_ref, rest_ref = outs[2 * i : 2 * i + 2]
        mine = (me_ref[0] >> bits[i]) & 1

        def total(which):
            kept = [
                (ref[0, which, 0, 0] if len(ref.shape) == 6 else ref[0, which, 0]).astype(F32)
                for ref in kept_refs
            ]
            return jnp.concatenate(kept, 1) + arrived_ref[0, which, 0].astype(F32)

        send_ref[0, 0] = total(1 - mine).astype(send_ref.dtype)
        rest_ref[0, 0] = total(mine)


def join_kernel(kept_ref, arrived_ref, out_ref, qkv_ref, table_ref, *refs):
    norm_refs, turn_v = refs[:-1], refs[-1]
    total = kept_ref[...] + arrived_ref[...].astype(F32)
    wide = out_ref.shape[1]
    out_ref[...] = total[:, :wide]
    qkv_ref[...] = total[:, wide : 4 * wide]
    small = total[:, 4 * wide :]
    turn_v[...] = jnp.zeros(turn_v.shape, F32)
    turn_v[: small.shape[0], :] = small
    turned = turn_v[...].T
    for head in range(table_ref.shape[0]):
        table_ref[head] = turned[head : head + 1, : table_ref.shape[2]]
    for i, ref in enumerate(norm_refs):
        ref[...] = turned[NORM_LANE + i : NORM_LANE + i + 1, : ref.shape[1]]


class Share:
    def __init__(self, parts, order):
        self.parts = parts
        self.order = order[1:]
        self.left = sorted(order)
        self.depth = parts[0].shape[1]
        self.wide = sum(part.shape[2] for part in parts)
        self.mine = None
        self.swap(order[0], self.of_core(1 - (lax.axis_index("dp") & 1)))

    def of_core(self, core):
        halves = [
            lax.dynamic_index_in_dim(
                part.reshape((part.shape[0] // 2, 2) + part.shape[1:]), core, 1, keepdims=False
            )
            for part in self.parts
        ]
        return halves[0] if len(halves) == 1 else jnp.concatenate(halves, 2)

    def swap(self, bit, theirs):
        count = lax.axis_size("dp")
        self.left.remove(bit)
        self.sent = theirs
        self.arrived = lax.ppermute(theirs, "dp", [(i, i ^ (1 << bit)) for i in range(count)])

    def total(self):
        kept = self.of_core(lax.axis_index("dp") & 1) if self.mine is None else self.mine
        return kept.astype(F32) + self.arrived.astype(F32)

    def split_at(self):
        bit = self.order[0]
        axis = len(self.left) - 1 - self.left.index(bit)
        return bit, 2**axis, 2 ** (len(self.left) - 1 - axis)

    def halve(self):
        bit, above, below = self.split_at()
        self.order = self.order[1:]
        split = self.total().reshape(above, 2, below, self.depth, self.wide)
        here = (lax.axis_index("dp") >> bit) & 1
        theirs = lax.dynamic_index_in_dim(split, 1 - here, 1, keepdims=False).astype(BF16)
        mine = lax.dynamic_index_in_dim(split, here, 1, keepdims=False)
        self.mine = mine.reshape(-1, self.depth, self.wide)
        self.swap(bit, theirs.reshape(-1, self.depth, self.wide))


def halve_all(me, shares, afters=(), through=()):
    if any(share.depth % 16 for share in shares):
        for share in shares:
            share.halve()
        return through
    ins, in_specs, outs, out_specs, bits, counts = [], [], [], [], [], []
    for share in shares:
        bit, above, below = share.split_at()
        bits.append(bit)

        def halves(wide, b=below):
            return pl.BlockSpec((1, 2, 1, share.depth, wide), lambda i, me: (i // b, 0, i % b, 0, 0))

        if share.mine is None:
            counts.append(len(share.parts))
            for part in share.parts:
                wide = part.shape[2]
                ins.append(part.reshape(above, 2, below, 2, share.depth, wide))
                in_specs.append(
                    pl.BlockSpec(
                        (1, 2, 1, 1, share.depth, wide),
                        lambda i, me, b=below: (i // b, 0, i % b, me[0] & 1, 0, 0),
                    )
                )
        else:
            counts.append(1)
            ins.append(share.mine.reshape(above, 2, below, share.depth, share.wide))
            in_specs.append(halves(share.wide))
        ins.append(share.arrived.reshape(above, 2, below, share.depth, share.wide))
        in_specs.append(halves(share.wide))
        outs += [
            jax.ShapeDtypeStruct((above, below, share.depth, share.wide), kind) for kind in (BF16, F32)
        ]
        out_specs += [
            pl.BlockSpec((1, 1, share.depth, share.wide), lambda i, me, b=below: (i // b, i % b, 0, 0))
        ] * 2
        steps = above * below
    results = pl.pallas_call(
        functools.partial(halve_kernel, tuple(bits), tuple(counts), len(afters), len(through)),
        grid_spec=pltpu.PrefetchScalarGridSpec(
            num_scalar_prefetch=1,
            grid=(steps,),
            in_specs=in_specs + [ANY] * (len(afters) + len(through)),
            out_specs=out_specs + [ANY] * len(through),
        ),
        out_shape=outs + [jax.ShapeDtypeStruct(array.shape, array.dtype) for array in through],
        input_output_aliases={
            1 + len(ins) + len(afters) + i: len(outs) + i for i in range(len(through))
        },
        compiler_params=pltpu.CompilerParams(vmem_limit_bytes=VMEM_BYTES if through else SMALL_VMEM_BYTES),
        name="halve",
    )(me, *ins, *afters, *through)
    for i, share in enumerate(shares):
        share.order = share.order[1:]
        share.mine = results[2 * i + 1].reshape(-1, share.depth, share.wide)
        share.swap(bits[i], results[2 * i].reshape(-1, share.depth, share.wide))
    return results[len(outs) :]


def joined(share, width, table_shape):
    shapes = [(share.depth, width), (share.depth, 3 * width), table_shape] + [(1, share.depth)] * 4
    return pl.pallas_call(
        join_kernel,
        out_shape=[jax.ShapeDtypeStruct(dims, F32) for dims in shapes],
        in_specs=[VMEM] * 2,
        out_specs=[VMEM] * len(shapes),
        scratch_shapes=[pltpu.VMEM((LANES, LANES), F32)],
        compiler_params=pltpu.CompilerParams(vmem_limit_bytes=SMALL_VMEM_BYTES),
        name="join",
    )(share.mine[0], share.arrived[0])


def passed_along(x, axis, by):
    length = lax.axis_size(axis)
    pairs = [(i, i + by) for i in range(length) if 0 <= i + by < length]
    return lax.ppermute(x, axis, pairs)


def shards(
    hidden_in, out_grad, qkv_weight, out_weight, rel_table, norm1_gain, norm1_bias,
    up_weight, down_weight, norm2_gain, norm2_bias, seg_ids, pad_mask, rel_buckets,
):
    phase = lax.axis_index("phase").astype(jnp.int32).reshape(1)
    ways = lax.axis_size("dp")
    slots, width = hidden_in.shape
    inner = up_weight.shape[2]
    buckets, heads = rel_table.shape[1:]

    def shape(dims, kind):
        return jax.ShapeDtypeStruct(dims, kind)

    rows_of = {
        "xin": (width, BF16), "qkv": (3 * width, BF16), "ctx": (width, BF16), "form1": (width, F32),
        "scale1": (1, F32), "low1": (width, BF16), "slope": (inner, BF16), "act": (inner, BF16),
        "form2": (width, F32), "scale2": (1, F32), "out": (width, BF16),
        "outer_low": (width, BF16), "hidden_low": (inner, BF16), "residual_low": (width, BF16),
        "projected": (3 * width, BF16), "input_grad": (width, BF16),
    }
    kept_shapes = [
        shape((slots, rows_of[name][0]), rows_of[name][1])
        if name in rows_of
        else {
            "weights": shape((MICRO, heads, BLOCK, BLOCK), BF16),
            "sums1": shape((MICRO, 8, width), F32),
            "sums2": shape((MICRO, 8, width), F32),
            "residual": shape((BLOCK, width), F32),
            "offsets": shape((MICRO, heads, 8, SPAN), F32),
            "bias": shape((heads, TILE, SPAN), F32),
        }[name]
        for name in KEPT
    ]
    in_forward = ("qkv", "ctx", "form1", "scale1", "low1", "slope", "act", "form2", "scale2", "out")
    scratch = {f"{name}_v": ((BLOCK, rows_of[name][0]), rows_of[name][1]) for name in in_forward}
    scratch |= {
        name: ((BLOCK, width), BF16) for name in ("x_v", "g_v", "outer_v", "residual_low_v", "dctx_v", "grad_v")
    }
    scratch |= {
        "weights_v": ((heads, BLOCK, BLOCK), BF16), "acc_v": ((BLOCK, width), F32), "square_v": ((2, BLOCK, BLOCK), F32),
        "values_v": ((heads, SPAN), F32), "bias_v": ((heads, TILE, SPAN), F32), "sums1_v": ((8, width), F32), "sums2_v": ((8, width), F32),
        "wqkv_v": ((width, 3 * width), BF16), "wout_v": ((width, width), BF16), "wup_v": ((width, inner), BF16),
        "wdown_v": ((inner, width), BF16), "fold_v": ((2, TILE, SPAN), F32), "eighth_v": ((heads, 8, SPAN), F32),
        "half_v": ((2, BLOCK, BLOCK), BF16),
    }

    def step(work, phase_on, block, received, kept, afters=()):
        values = (
            phase, seg_ids, hidden_in, received, out_grad, rel_table.transpose(2, 0, 1), pad_mask[None, :], rel_buckets[None, :],
            norm1_gain, norm1_bias, norm2_gain, norm2_bias, qkv_weight, out_weight, up_weight, down_weight,
        )
        in_place = None if kept is None else [kept[name] for name in KEPT]
        return layer_step(work, phase_on, block, values, list(afters), in_place, kept_shapes, scratch)

    kept, sent = step("forward", 0, 0, hidden_in, None)
    first = passed_along(sent, "phase", 1)
    kept, _ = step("bias", 1, 0, hidden_in, kept)
    kept, sent = step("forward", 0, 1, hidden_in, kept)
    second = passed_along(sent, "phase", 1)
    kept, sent = step("both", 1, 0, first, kept)
    first_back = passed_along(sent, "phase", -1)
    kept, sent = step("both", 1, 1, second, kept)
    second_back = passed_along(sent, "phase", -1)
    kept, _ = step("back", 0, 0, first_back, kept)
    kept, _ = step("ffn_back", 0, 1, second_back, kept)

    bits = ways.bit_length() - 1
    near_first = list(range(bits))
    far_first = [0] + list(range(2, bits)) + [1] if bits > 1 else near_first
    me = lax.axis_index("dp").astype(jnp.int32).reshape(1)

    def weight_grad(left, right):
        product = dot_tn(left, right).astype(BF16)
        return product.reshape(ways, product.shape[0] // ways, product.shape[1])

    down = Share([weight_grad(kept["act"], kept["outer_low"])], near_first)
    up = Share([weight_grad(kept["low1"], kept["hidden_low"])], far_first)
    out_part = weight_grad(kept["ctx"], kept["residual_low"])
    halve_all(me, [down])
    halve_all(me, [up])
    kept, _ = step("attn_back", 0, 1, hidden_in, kept, [down.sent, up.sent])
    parts = [weight_grad(kept["xin"], kept["projected"][:, width:])]
    (slots_in,) = halve_all(me, [down, up], [parts[0]], [kept["xin"]])
    parts.append(weight_grad(slots_in, kept["projected"][:, :width]))
    small = packed(ways, buckets, rel_buckets[None, :], kept, [])
    last = Share([out_part, parts[1], parts[0], small], near_first)
    halve_all(me, [last], [down.sent, up.sent])
    halve_all(me, [down, up])
    halve_all(me, [last], [down.sent, up.sent])
    while down.order:
        halve_all(me, [down, up])
    while last.order:
        halve_all(me, [last])
    down_share = down.total()[0]
    up_share = up.total()[0]
    out_share, qkv_share, table_share, *norm_shares = joined(last, width, (heads, 1, buckets // ways))
    return (
        kept["out"][None],
        kept["input_grad"][None],
        qkv_share[None],
        out_share[None],
        table_share.transpose(1, 2, 0),
        norm_shares[0],
        norm_shares[1],
        up_share[None],
        down_share[None],
        norm_shares[2],
        norm_shares[3],
    )


def solution(mesh):
    return jax.shard_map(
        shards,
        mesh=mesh,
        in_specs=(
            P("dp", None),
            P("dp", None),
            P("phase", None, None),
            P("phase", None, None),
            P("phase", None, None),
            P("phase", None),
            P("phase", None),
            P("phase", None, None),
            P("phase", None, None),
            P("phase", None),
            P("phase", None),
            P("dp"),
            P("dp"),
            P(),
        ),
        out_specs=(
            P("phase", "dp", None),
            P("phase", "dp", None),
            P("phase", "dp", None),
            P("phase", "dp", None),
            P("phase", "dp", None),
            P("phase", "dp"),
            P("phase", "dp"),
            P("phase", "dp", None),
            P("phase", "dp", None),
            P("phase", "dp"),
            P("phase", "dp"),
        ),
        check_vma=False,
    )
```

```python
import functools

import jax
import jax.numpy as jnp
from jax import lax
from jax.experimental import pallas as pl
from jax.experimental.pallas import tpu as pltpu
from jax.sharding import PartitionSpec as P

BLOCK = 512
MICRO = 2
TILE = 128
LANES = 128
CHUNK = 512
SPAN = 2 * BLOCK
VMEM_BYTES = 58 * 1024 * 1024
SMALL_VMEM_BYTES = 20 * 1024 * 1024
NORM_LANE = 16

norm_eps = 1e-05
mask_fill = -1000000000.0
score_scale = 0.125
inv_root_two = 0.7071067811865476
inv_root_tau = 0.3989422804014327
log2_e = 1.4426950408889634
highest = lax.Precision.HIGHEST

F32 = jnp.float32
BF16 = jnp.bfloat16
ANY = pl.BlockSpec(memory_space=pl.ANY)
VMEM = pl.BlockSpec(memory_space=pltpu.VMEM)
QUICK = pl.CostEstimate(flops=1, bytes_accessed=1, transcendentals=0)
SMEM = pl.BlockSpec(memory_space=pltpu.SMEM)


def dot_nn(a, b):
    return lax.dot_general(a, b, (((1,), (0,)), ((), ())), preferred_element_type=F32)


def dot_nt(a, b):
    return lax.dot_general(a, b, (((1,), (1,)), ((), ())), preferred_element_type=F32)


def dot_tn(a, b):
    return lax.dot_general(a, b, (((0,), (0,)), ((), ())), preferred_element_type=F32)


def row_mean(rows):
    return jnp.sum(rows, -1, keepdims=True) * (1.0 / rows.shape[-1])


def normal_parts(residual):
    centred = residual - row_mean(residual)
    inv_scale = lax.rsqrt(row_mean(centred * centred) + norm_eps)
    return centred * inv_scale, inv_scale


def norm_backward(grad_rows, normal_form, inv_scale):
    first = row_mean(grad_rows)
    second = row_mean(grad_rows * normal_form)
    return inv_scale * (grad_rows - first - normal_form * second)


def gelu_parts(hidden):
    share = 0.5 + 0.5 * lax.erf(hidden * inv_root_two)
    bell = jnp.exp2(hidden * hidden * (-0.5 * log2_e))
    return hidden * share, share + hidden * bell * inv_root_tau


def half_mask(which, shape):
    lane = lax.broadcasted_iota(jnp.int32, shape, 1)
    return (lane < LANES // 2) if which == 0 else (lane >= LANES // 2)


class Copies:
    def __init__(self, sems):
        self.sems = sems
        self.used = 0
        self.stores = []

    def take(self, count=1):
        self.used += count
        return self.used - count

    def load(self, source, target):
        copy = pltpu.make_async_copy(source, target, self.sems.at[self.take()])
        copy.start()
        return copy

    def store(self, source, target, when=True):
        if when:
            self.stores.append(self.load(source, target))

    def finish(self):
        for copy in self.stores:
            copy.wait()


KEPT = (
    "xin", "qkv", "weights", "ctx", "form1", "scale1", "low1", "slope", "act", "form2", "scale2", "out",
    "bias", "outer_low", "hidden_low", "residual_low", "sums1", "sums2", "residual", "projected", "offsets", "input_grad",
)
INS = (
    "phase", "segments", "hidden_in", "received", "out_grad", "table", "padding", "buckets",
    "gain1", "shift1", "gain2", "shift2",
    "wqkv", "wout", "wup", "wdown",
)


class Layer:
    def __init__(self, refs):
        self.__dict__.update(refs)
        self.copies = Copies(self.sems)
        self.width = self.hidden_in.shape[1]
        self.inner = self.wup.shape[2]
        self.pairs = self.width // LANES
        self.stages = self.inner // (2 * CHUNK)
        self.pair_sems = self.copies.take(self.pairs)
        self.chunk_sems = [self.copies.take(self.stages) for _ in range(3)]

    def lanes_of(self, pair, part):
        return pl.ds(pl.multiple_of(part * self.width + pair * LANES, LANES), LANES)

    def stage(self, i):
        return pl.ds(pl.multiple_of(i * 2 * CHUNK, 2 * CHUNK), 2 * CHUNK)

    def build_bias(self):
        span = self.buckets.shape[1]
        bucket_ids = lax.broadcasted_iota(jnp.int32, (self.table.shape[2], span), 0)
        hot = (bucket_ids == self.buckets[...]).astype(F32)
        table = jnp.concatenate([self.table[head] for head in range(self.table.shape[0])], 0)
        values = lax.dot_general(
            table, hot, (((1,), (0,)), ((), ())), precision=highest, preferred_element_type=F32
        )
        self.values_v[:, :span] = values
        self.values_v[:, span:] = jnp.zeros((values.shape[0], SPAN - span), F32)

        def one_head(head, carry):
            wide = jnp.broadcast_to(self.values_v[pl.ds(head, 1), :], (TILE, SPAN))
            self.bias_v[head] = pltpu.roll(wide, 1, 1, stride=1, stride_axis=0)
            return carry

        lax.fori_loop(0, values.shape[0], one_head, 0)
        self.copies.store(self.bias_v, self.bias)


    def rows(self, block):
        return pl.ds(block * BLOCK, BLOCK)

    def forward(self, block, keep, built):
        copies = self.copies
        rows = self.rows(block)
        load_x = copies.load(self.hidden_in.at[rows] if keep else self.received, self.x_v)
        width = self.width
        loads = [
            copies.load(self.wqkv.at[0, :, pl.ds(c, width)], self.wqkv_v.at[:, pl.ds(c, width)])
            for c in range(0, 3 * width, width)
        ]
        if not built:
            self.build_bias()
        load_x.wait()

        def load_bias(pair):
            heads = pl.ds(2 * pair, 2)
            return pltpu.make_async_copy(self.bias.at[heads], self.bias_v.at[heads], self.sems.at[self.pair_sems + pair])

        for i, c in enumerate(range(0, 3 * width, width)):
            loads[i].wait()
            if built and i < 2:
                load_bias(i).start()
            self.qkv_v[:, c : c + width] = dot_nn(self.x_v[...], self.wqkv_v[:, c : c + width]).astype(BF16)
        copies.store(self.x_v, self.xin.at[rows])
        copies.store(self.qkv_v, self.qkv.at[rows], keep)
        weights_sem = self.sems.at[copies.take()]
        later_loads = [
            pltpu.make_async_copy(source.at[0], target, self.sems.at[copies.take()])
            for source, target in ((self.wout, self.wout_v), (self.wup, self.wup_v), (self.wdown, self.wdown_v))
        ]

        def own(pair, part, which):
            both = self.qkv_v[:, self.lanes_of(pair, part)]
            return jnp.where(half_mask(which, both.shape), both, jnp.zeros_like(both))

        single = self.segments[block * BLOCK + TILE] == self.segments[block * BLOCK]
        padding = self.padding[:, block * BLOCK : (block + 1) * BLOCK]
        tile_of = lax.broadcasted_iota(jnp.int32, (1, BLOCK), 1) // TILE
        shut = [
            jnp.where((padding == 1) & (single | (tile_of == tile)), 0.0, mask_fill) for tile in range(BLOCK // TILE)
        ]
        row_id = lax.broadcasted_iota(jnp.int32, (TILE, TILE), 0)
        diagonal = row_id == lax.broadcasted_iota(jnp.int32, (TILE, TILE), 1)

        def bias_rows(head, tile):
            at = BLOCK - tile * TILE
            rows = self.bias_v[head, :, at : at + BLOCK]
            masked = rows + shut[tile]
            own = slice(tile * TILE, (tile + 1) * TILE)
            parts = [masked[:, : own.start], jnp.where(diagonal, rows[:, own], masked[:, own]), masked[:, own.stop :]]
            return jnp.concatenate([part for part in parts if part.shape[1]], 1)

        def weigh(pair, which):
            head = 2 * pair + which
            k_own = own(pair, 1, which)
            for r in range(0, BLOCK, 2 * TILE):
                q_rows = self.qkv_v[r : r + 2 * TILE, self.lanes_of(pair, 0)] * jnp.asarray(score_scale, BF16)
                tiles = [bias_rows(head, tile) for tile in range(r // TILE, r // TILE + 2)]
                logits = dot_nt(q_rows, k_own) + jnp.concatenate(tiles, 0)
                raised = jnp.exp(logits - jnp.max(logits, -1, keepdims=True))
                share = pl.reciprocal(jnp.sum(raised, -1, keepdims=True), approx=True)
                self.weights_v[head, r : r + 2 * TILE, :] = (raised * share).astype(BF16)

        def head_pair(pair, carry):
            if built:
                load_bias(pair).wait()

                @pl.when(pair + 2 < self.pairs)
                def _():
                    load_bias(pair + 2).start()

            @pl.when(pair == 1)
            def _():
                for load in later_loads:
                    load.start()

            weigh(pair, 0)
            context = dot_nn(self.weights_v[2 * pair], own(pair, 2, 0))
            weigh(pair, 1)
            context += dot_nn(self.weights_v[2 * pair + 1], own(pair, 2, 1))
            self.ctx_v[:, self.lanes_of(pair, 0)] = context.astype(BF16)
            if keep:
                heads = pl.ds(2 * pair, 2)
                pltpu.make_async_copy(self.weights_v.at[heads], self.weights.at[block, heads], weights_sem).start()
            return carry

        lax.fori_loop(0, self.pairs, head_pair, 0)
        if keep:
            copies.stores.append(pltpu.make_async_copy(self.weights_v, self.weights.at[block], weights_sem))
        copies.store(self.ctx_v, self.ctx.at[rows])
        load_out, load_up, load_down = later_loads
        load_out.wait()
        self.acc_v[...] = dot_nn(self.ctx_v[...], self.wout_v[...])
        for r in range(0, BLOCK, 64):
            tile = slice(r, r + 64)
            form, scale = normal_parts(self.acc_v[tile, :] + self.x_v[tile, :].astype(F32))
            normed = form * self.gain1[...] + self.shift1[...]
            self.form1_v[tile, :] = form
            self.scale1_v[tile, :] = scale
            self.acc_v[tile, :] = normed
            self.low1_v[tile, :] = normed.astype(BF16)
        copies.store(self.form1_v, self.form1.at[rows], keep)
        copies.store(self.scale1_v, self.scale1.at[rows], keep)
        copies.store(self.low1_v, self.low1.at[rows])
        load_up.wait()
        load_down.wait()
        act_sem = self.sems.at[copies.take()]
        slope_sem = self.sems.at[copies.take()]

        def two_chunks(i, carry):
            span = self.stage(i)
            active, grade = gelu_parts(dot_nn(self.low1_v[...], self.wup_v[:, span]))
            active = active.astype(BF16)
            self.act_v[:, span] = active
            self.slope_v[:, span] = grade.astype(BF16)
            self.acc_v[...] += dot_nn(active, self.wdown_v[span, :])
            pltpu.make_async_copy(self.act_v.at[:, span], self.act.at[rows, span], act_sem).start()
            if keep:
                pltpu.make_async_copy(self.slope_v.at[:, span], self.slope.at[rows, span], slope_sem).start()
            return carry

        lax.fori_loop(0, self.stages, two_chunks, 0)
        copies.stores.append(pltpu.make_async_copy(self.act_v, self.act.at[rows], act_sem))
        if keep:
            copies.stores.append(pltpu.make_async_copy(self.slope_v, self.slope.at[rows], slope_sem))
        for r in range(0, BLOCK, 64):
            tile = slice(r, r + 64)
            form, scale = normal_parts(self.acc_v[tile, :])
            self.form2_v[tile, :] = form
            self.scale2_v[tile, :] = scale
            self.out_v[tile, :] = (form * self.gain2[...] + self.shift2[...]).astype(BF16)
        copies.store(self.out_v, self.send, keep)
        copies.store(self.out_v, self.out.at[rows])
        copies.store(self.form2_v, self.form2.at[rows], keep)
        copies.store(self.scale2_v, self.scale2.at[rows], keep)


    def chunk_loads(self, i, rows):
        span = self.stage(i)
        return [
            pltpu.make_async_copy(source, target, self.sems.at[self.chunk_sems[k] + i])
            for k, (source, target) in enumerate(
                (
                    (self.wdown.at[0, span], self.wdown_v.at[span]),
                    (self.slope.at[rows, span], self.slope_v.at[:, span]),
                    (self.wup.at[0, :, span], self.wup_v.at[:, span]),
                )
            )
        ]

    def over_rows(self, size, body):
        if not self.compact:
            for r in range(0, BLOCK, size):
                body(slice(r, r + size))
            return

        def one_tile(i, carry):
            body(pl.ds(pl.multiple_of(i * size, size), size))
            return carry

        lax.fori_loop(0, BLOCK // size, one_tile, 0)

    def over_columns(self, body):
        size = 2 * LANES
        if not self.compact:
            body(pl.ds(0, self.width))
            return

        def one_part(i, carry):
            body(pl.ds(pl.multiple_of(i * size, size), size))
            return carry

        lax.fori_loop(0, self.width // size, one_part, 0)

    def norm_sums(self, source, form_ref, sums_ref):
        sums_ref[...] = jnp.zeros(sums_ref.shape, F32)

        def add_tile(tile):
            grad_rows = source[tile, :].astype(F32)
            sums_ref[0:1, :] += jnp.sum(grad_rows * form_ref[tile, :], 0, keepdims=True)
            sums_ref[1:2, :] += jnp.sum(grad_rows, 0, keepdims=True)

        self.over_rows(TILE, add_tile)

    def norm_back(self, block):
        def one_tile(tile):
            grad_rows = self.g_v[tile, :].astype(F32) * self.gain2[...]
            grad_outer = norm_backward(grad_rows, self.form2_v[tile, :], self.scale2_v[tile, :])
            self.acc_v[tile, :] = grad_outer
            self.outer_v[tile, :] = grad_outer.astype(BF16)

        self.over_rows(TILE, one_tile)
        self.copies.store(self.outer_v, self.outer_low.at[self.rows(block)])

    def norm_sums_2(self, block):
        self.norm_sums(self.g_v, self.form2_v, self.sums2_v)
        self.copies.store(self.sums2_v, self.sums2.at[block])

    def ffn_back(self, block, staged=False, middle_loads=()):
        copies = self.copies
        rows = self.rows(block)
        hidden_sem = self.sems.at[copies.take()]

        def two_chunks(i, carry):
            span = self.stage(i)
            if staged:
                load_down, load_slope, load_up = self.chunk_loads(i, rows)
                load_down.wait()
                load_slope.wait()
            grad_active = dot_nt(self.outer_v[...], self.wdown_v[span, :])
            hidden = (grad_active * self.slope_v[:, span].astype(F32)).astype(BF16)
            self.slope_v[:, span] = hidden
            if staged:
                load_up.wait()

                @pl.when(i + 2 < self.stages)
                def _():
                    for load in self.chunk_loads(i + 2, rows):
                        load.start()

            self.acc_v[...] += dot_nt(hidden, self.wup_v[:, span])
            pltpu.make_async_copy(self.slope_v.at[:, span], self.hidden_low.at[rows, span], hidden_sem).start()
            return carry

        lax.fori_loop(0, self.stages, two_chunks, 0)
        copies.stores.append(pltpu.make_async_copy(self.slope_v, self.hidden_low.at[rows], hidden_sem))
        for load in middle_loads:
            load.wait()
        self.norm_sums(self.acc_v, self.form1_v, self.sums1_v)

        def one_tile(tile):
            grad_residual = norm_backward(
                self.acc_v[tile, :] * self.gain1[...], self.form1_v[tile, :], self.scale1_v[tile, :]
            )
            self.acc_v[tile, :] = grad_residual
            self.residual_low_v[tile, :] = grad_residual.astype(BF16)

        self.over_rows(TILE, one_tile)
        copies.store(self.residual_low_v, self.residual_low.at[rows])
        copies.store(self.sums1_v, self.sums1.at[block])

    def attn_back(self, block, next_loads=None, load_in=()):
        copies = self.copies
        rows = self.rows(block)

        def context_part(part):
            self.dctx_v[:, part] = dot_nt(self.residual_low_v[...], self.wout_v[part, :]).astype(BF16)

        self.over_columns(context_part)
        self.fold_v[:, :, 0:TILE] = jnp.zeros((2, TILE, TILE), F32)

        def head_pair(pair, carry):
            def lanes_of(part):
                return self.lanes_of(pair, part)

            if next_loads is not None:
                next_loads(pair)
            q_pair, k_pair, v_pair = (self.qkv_v[:, lanes_of(part)] for part in range(3))
            grad_pair = self.dctx_v[:, lanes_of(0)]
            crossed = grad_pair.astype(F32) * self.ctx_v[:, lanes_of(0)].astype(F32)
            masks = [half_mask(which, k_pair.shape) for which in range(2)]

            def own(both, which):
                return jnp.where(masks[which], both, jnp.zeros_like(both))

            for which in range(2):
                self.square_v[which] = dot_nt(grad_pair, own(v_pair, which))
            q_grad = k_grad = v_grad = 0.0
            for which in range(2):
                head = 2 * pair + which
                delta = jnp.sum(own(crossed, which), -1, keepdims=True)
                for r in range(0, BLOCK, 64):
                    tile = slice(r, r + 64)
                    score_grad = (
                        self.weights_v[head, tile, :].astype(F32) * (self.square_v[which, tile, :] - delta[tile, :])
                    ).astype(BF16)
                    self.half_v[which, tile, :] = score_grad
                    at = BLOCK - r // TILE * TILE
                    wide = score_grad.astype(F32)
                    half = slice(r % TILE, r % TILE + 64)
                    if r < TILE:
                        self.fold_v[which, half, at : at + BLOCK] = wide
                    else:
                        self.fold_v[which, half, at : at + TILE] = wide[:, :TILE]
                        self.fold_v[which, half, at + TILE : at + BLOCK] += wide[:, TILE:]
                v_grad += dot_tn(self.weights_v[head], own(grad_pair, which))
                q_grad += dot_nn(self.half_v[which], own(k_pair, which))
                k_grad += dot_tn(self.half_v[which], own(q_pair, which))
                folded = self.fold_v[which]
                size = TILE // 2
                while size >= 8:
                    folded = folded[:size, :] + pltpu.roll(folded[size:, :], SPAN - size, 1)
                    size //= 2
                self.eighth_v[head] = folded
            self.qkv_v[:, lanes_of(0)] = (q_grad * score_scale).astype(BF16)
            self.qkv_v[:, lanes_of(1)] = (k_grad * score_scale).astype(BF16)
            self.qkv_v[:, lanes_of(2)] = v_grad.astype(BF16)
            return carry

        lax.fori_loop(0, self.pairs, head_pair, 0)
        copies.store(self.eighth_v, self.offsets.at[block])
        copies.store(self.qkv_v, self.projected.at[rows])
        for load in load_in:
            load.wait()

        def input_part(part):
            self.grad_v[:, part] = (self.acc_v[:, part] + dot_nt(self.qkv_v[...], self.wqkv_v[part, :])).astype(BF16)

        self.over_columns(input_part)
        copies.store(self.grad_v, self.send)
        copies.store(self.grad_v, self.input_grad.at[rows])


    def do_forward(self, block):
        self.forward(block, True, block > 0)

    def do_bias(self, block):
        self.build_bias()

    def do_both(self, block):
        load = self.copies.load(self.out_grad.at[self.rows(block)], self.g_v)
        self.forward(block, False, True)
        load.wait()
        self.norm_back(block)
        self.ffn_back(block)
        self.norm_sums_2(block)
        self.attn_back(block)

    def do_back(self, block):
        rows = self.rows(block)
        loads = [
            self.copies.load(source, target)
            for source, target in (
                (self.received, self.g_v),
                (self.form2.at[rows], self.form2_v),
                (self.scale2.at[rows], self.scale2_v),
                (self.slope.at[rows], self.slope_v),
                (self.wdown.at[0], self.wdown_v),
                (self.wup.at[0], self.wup_v),
                (self.form1.at[rows], self.form1_v),
                (self.scale1.at[rows], self.scale1_v),
                (self.qkv.at[rows], self.qkv_v),
                (self.weights.at[block], self.weights_v),
                (self.ctx.at[rows], self.ctx_v),
                (self.wout.at[0], self.wout_v),
                (self.wqkv.at[0], self.wqkv_v),
            )
        ]
        for load in loads:
            load.wait()
        self.norm_back(block)
        self.ffn_back(block)
        self.norm_sums_2(block)
        self.attn_back(block)

    def do_ffn_back(self, block):
        rows = self.rows(block)
        loads = [
            self.copies.load(source, target)
            for source, target in (
                (self.received, self.g_v),
                (self.form2.at[rows], self.form2_v),
                (self.scale2.at[rows], self.scale2_v),
            )
        ]
        self.chunk_loads(0, rows)[0].start()
        for load in loads:
            load.wait()
        for load in self.chunk_loads(0, rows)[1:] + self.chunk_loads(1, rows):
            load.start()
        middle = [
            self.copies.load(self.form1.at[rows], self.form1_v),
            self.copies.load(self.scale1.at[rows], self.scale1_v),
        ]
        self.norm_back(block)
        self.ffn_back(block, True, middle)
        self.copies.store(self.acc_v, self.residual)
        self.norm_sums_2(block)

    def do_attn_back(self, block):
        rows = self.rows(block)
        loads = [
            self.copies.load(source, target)
            for source, target in ((self.residual_low.at[rows], self.residual_low_v), (self.wout.at[0], self.wout_v))
        ]
        first = self.copies.take(5 * self.pairs)

        def pair_loads(pair):
            heads = pl.ds(2 * pair, 2)
            sources = [(self.weights.at[block, heads], self.weights_v.at[heads])]
            for source, target, parts in ((self.qkv, self.qkv_v, 3), (self.ctx, self.ctx_v, 1)):
                for part in range(parts):
                    lanes = self.lanes_of(pair, part)
                    sources.append((source.at[rows, lanes], target.at[:, lanes]))
            return [
                pltpu.make_async_copy(source, target, self.sems.at[first + 5 * pair + k])
                for k, (source, target) in enumerate(sources)
            ]

        for pair in range(2):
            for load in pair_loads(pair):
                load.start()
        for load in loads:
            load.wait()
        last = [
            pltpu.make_async_copy(source, target, self.sems.at[self.copies.take()])
            for source, target in ((self.wqkv.at[0], self.wqkv_v), (self.residual, self.acc_v))
        ]

        def next_loads(pair):
            for load in pair_loads(pair):
                load.wait()

            @pl.when(pair + 2 < self.pairs)
            def _():
                for load in pair_loads(pair + 2):
                    load.start()

            @pl.when(pair == self.pairs - 3)
            def _():
                for load in last:
                    load.start()

        self.attn_back(block, next_loads, last)


def layer_kernel(work, phase_on, block, ins, outs, scratch, after_count, kept_count, *refs):
    refs_in, refs = refs[: len(ins)], refs[len(ins) + after_count + kept_count :]
    named = dict(zip(ins, refs_in)) | dict(zip(outs, refs)) | dict(zip(scratch, refs[len(outs) :]))

    @pl.when(named["phase"][0] == phase_on)
    def _():
        layer = Layer(named)
        layer.compact = work not in ("forward", "both")
        getattr(layer, f"do_{work}")(block)
        layer.copies.finish()


def layer_step(work, phase_on, block, values, afters, kept, kept_shapes, scratch):
    specs = [SMEM] * 2 + [ANY] * 3 + [VMEM] * 7 + [ANY] * 4
    names = list(scratch)
    kept = list(kept) if kept is not None else []
    sent = jax.ShapeDtypeStruct((BLOCK, values[2].shape[1]), BF16)
    if work == "bias":
        names = ["values_v", "bias_v"]
    count = len(values) + len(afters)
    results = pl.pallas_call(
        functools.partial(
            layer_kernel, work, phase_on, block, INS, KEPT + ("send",), names + ["sems"], len(afters), len(kept)
        ),
        out_shape=list(kept_shapes) + [sent],
        in_specs=specs + [ANY] * (len(afters) + len(kept)),
        out_specs=[ANY] * (len(kept_shapes) + 1),
        scratch_shapes=[pltpu.VMEM(*scratch[name]) for name in names] + [pltpu.SemaphoreType.DMA((96,))],
        input_output_aliases={count + i: i for i in range(len(kept))},
        compiler_params=pltpu.CompilerParams(vmem_limit_bytes=VMEM_BYTES),
        name=f"{work}_{phase_on}_{block}",
    )(*values, *afters, *kept)
    return dict(zip(KEPT, results)), results[-1]


def pack_kernel(ways, buckets_ref, offsets_ref, sums1_ref, sums2_ref, *refs):
    out_ref, turn_v = refs[-2:]
    row_of = lax.broadcasted_iota(jnp.int32, (8, SPAN), 0)
    lines = []
    for head in range(offsets_ref.shape[1]):
        eighth = offsets_ref[0, head] + offsets_ref[1, head]
        for size in (4, 2, 1):
            eighth = jnp.where((row_of & size) != 0, pltpu.roll(eighth, SPAN - size, 1), eighth)
        lines.append(jnp.sum(eighth, 0, keepdims=True))
    lines += [jnp.zeros((1, SPAN), F32)] * (NORM_LANE - len(lines))
    sums = pltpu.roll(jnp.concatenate(lines, 0), SPAN - 1, 1)
    span = buckets_ref.shape[1]
    buckets, depth = out_ref.shape[0] // 3, out_ref.shape[0] // ways
    share = buckets // ways
    bucket_ids = lax.broadcasted_iota(jnp.int32, (buckets, span), 0)
    hot = (bucket_ids == buckets_ref[...]).astype(F32)
    table = lax.dot_general(
        hot, sums[:, :span], (((1,), (1,)), ((), ())), precision=highest, preferred_element_type=F32
    ).astype(BF16)
    turn_v[...] = jnp.zeros(turn_v.shape, F32)
    for i, ref in enumerate((sums1_ref, sums2_ref)):
        at = NORM_LANE + 2 * i
        turn_v[at : at + 2, :] = ref[0, 0:2, :] + ref[1, 0:2, :]
    out_ref[...] = turn_v[...].T.astype(BF16)
    for i in range(ways):
        out_ref[i * depth : i * depth + share, 0:NORM_LANE] = table[i * share : (i + 1) * share, :]


def packed(ways, buckets, offset_buckets, kept, afters):
    width = kept["sums1"].shape[2]
    depth, share = width // ways, buckets // ways
    arrays = (offset_buckets, kept["offsets"], kept["sums1"], kept["sums2"])
    if depth % 16 == 0 and share % 16 == 0 and 3 * buckets == width:
        rows = pl.pallas_call(
            functools.partial(pack_kernel, ways),
            out_shape=jax.ShapeDtypeStruct((width, LANES), BF16),
            in_specs=[VMEM] * len(arrays) + [ANY] * len(afters),
            out_specs=VMEM,
            scratch_shapes=[pltpu.VMEM((LANES, width), F32)],
            compiler_params=pltpu.CompilerParams(vmem_limit_bytes=SMALL_VMEM_BYTES),
            name="pack",
        )(*arrays, *afters)
        return rows.reshape(ways, depth, LANES)
    eighths = jnp.sum(kept["offsets"], 0)
    lines = sum(jnp.roll(eighths[:, i, :], -i, 1) for i in range(8))[:, 1:]
    hot = (offset_buckets[0][None, :] == jnp.arange(buckets, dtype=jnp.int32)[:, None]).astype(F32)
    table = jnp.dot(hot, lines.T, precision=highest).reshape(ways, share, -1)
    table = jnp.pad(table, ((0, 0), (0, depth - share), (0, NORM_LANE - table.shape[2])))
    norms = jnp.concatenate([jnp.sum(kept[name], 0)[:2] for name in ("sums1", "sums2")], 0)
    norms = norms.T.reshape(ways, depth, 4)
    rows = jnp.concatenate([table, norms], 2)
    return jnp.pad(rows, ((0, 0), (0, 0), (0, LANES - rows.shape[2]))).astype(BF16)


def halve_kernel(bits, counts, after_count, through_count, me_ref, *refs):
    used = sum(counts) + len(counts)
    outs = refs[used + after_count + through_count :]
    for i, count in enumerate(counts):
        kept_refs, arrived_ref = refs[:count], refs[count]
        refs = refs[count + 1 :]
        send_ref, rest_ref = outs[2 * i : 2 * i + 2]
        mine = (me_ref[0] >> bits[i]) & 1

        def total(which):
            kept = [
                (ref[0, which, 0, 0] if len(ref.shape) == 6 else ref[0, which, 0]).astype(F32)
                for ref in kept_refs
            ]
            return jnp.concatenate(kept, 1) + arrived_ref[0, which, 0].astype(F32)

        send_ref[0, 0] = total(1 - mine).astype(send_ref.dtype)
        rest_ref[0, 0] = total(mine)


def join_kernel(kept_near, arrived_near, kept_far, arrived_far, out_ref, qkv_ref, table_ref, *refs):
    norm_refs, turn_v = refs[:-1], refs[-1]
    near = kept_near[...] + arrived_near[...].astype(F32)
    wide = out_ref.shape[1]
    out_ref[...] = near[:, :wide]
    qkv_ref[:, :wide] = near[:, wide : 2 * wide]
    qkv_ref[:, wide:] = kept_far[...] + arrived_far[...].astype(F32)
    small = near[:, 2 * wide :]
    turn_v[...] = jnp.zeros(turn_v.shape, F32)
    turn_v[: small.shape[0], :] = small
    turned = turn_v[...].T
    for head in range(table_ref.shape[0]):
        table_ref[head] = turned[head : head + 1, : table_ref.shape[2]]
    for i, ref in enumerate(norm_refs):
        ref[...] = turned[NORM_LANE + i : NORM_LANE + i + 1, : ref.shape[1]]


class Share:
    def __init__(self, parts, order):
        self.parts = parts
        self.order = order[1:]
        self.left = sorted(order)
        self.depth = parts[0].shape[1]
        self.wide = sum(part.shape[2] for part in parts)
        self.mine = None
        self.swap(order[0], self.of_core(1 - (lax.axis_index("dp") & 1)))

    def of_core(self, core):
        halves = [
            lax.dynamic_index_in_dim(
                part.reshape((part.shape[0] // 2, 2) + part.shape[1:]), core, 1, keepdims=False
            )
            for part in self.parts
        ]
        return halves[0] if len(halves) == 1 else jnp.concatenate(halves, 2)

    def swap(self, bit, theirs):
        count = lax.axis_size("dp")
        self.left.remove(bit)
        self.sent = theirs
        self.arrived = lax.ppermute(theirs, "dp", [(i, i ^ (1 << bit)) for i in range(count)])

    def total(self):
        kept = self.of_core(lax.axis_index("dp") & 1) if self.mine is None else self.mine
        return kept.astype(F32) + self.arrived.astype(F32)

    def split_at(self):
        bit = self.order[0]
        axis = len(self.left) - 1 - self.left.index(bit)
        return bit, 2**axis, 2 ** (len(self.left) - 1 - axis)

    def halve(self):
        bit, above, below = self.split_at()
        self.order = self.order[1:]
        split = self.total().reshape(above, 2, below, self.depth, self.wide)
        here = (lax.axis_index("dp") >> bit) & 1
        theirs = lax.dynamic_index_in_dim(split, 1 - here, 1, keepdims=False).astype(BF16)
        mine = lax.dynamic_index_in_dim(split, here, 1, keepdims=False)
        self.mine = mine.reshape(-1, self.depth, self.wide)
        self.swap(bit, theirs.reshape(-1, self.depth, self.wide))


def halve_all(me, shares, afters=(), through=()):
    if any(share.depth % 16 for share in shares):
        for share in shares:
            share.halve()
        return through
    ins, in_specs, outs, out_specs, bits, counts = [], [], [], [], [], []
    for share in shares:
        bit, above, below = share.split_at()
        bits.append(bit)

        def halves(wide, b=below):
            return pl.BlockSpec((1, 2, 1, share.depth, wide), lambda i, me: (i // b, 0, i % b, 0, 0))

        if share.mine is None:
            counts.append(len(share.parts))
            for part in share.parts:
                wide = part.shape[2]
                ins.append(part.reshape(above, 2, below, 2, share.depth, wide))
                in_specs.append(
                    pl.BlockSpec(
                        (1, 2, 1, 1, share.depth, wide),
                        lambda i, me, b=below: (i // b, 0, i % b, me[0] & 1, 0, 0),
                    )
                )
        else:
            counts.append(1)
            ins.append(share.mine.reshape(above, 2, below, share.depth, share.wide))
            in_specs.append(halves(share.wide))
        ins.append(share.arrived.reshape(above, 2, below, share.depth, share.wide))
        in_specs.append(halves(share.wide))
        outs += [
            jax.ShapeDtypeStruct((above, below, share.depth, share.wide), kind) for kind in (BF16, F32)
        ]
        out_specs += [
            pl.BlockSpec((1, 1, share.depth, share.wide), lambda i, me, b=below: (i // b, i % b, 0, 0))
        ] * 2
        steps = above * below
    results = pl.pallas_call(
        functools.partial(halve_kernel, tuple(bits), tuple(counts), len(afters), len(through)),
        grid_spec=pltpu.PrefetchScalarGridSpec(
            num_scalar_prefetch=1,
            grid=(steps,),
            in_specs=in_specs + [ANY] * (len(afters) + len(through)),
            out_specs=out_specs + [ANY] * len(through),
        ),
        out_shape=outs + [jax.ShapeDtypeStruct(array.shape, array.dtype) for array in through],
        input_output_aliases={
            1 + len(ins) + len(afters) + i: len(outs) + i for i in range(len(through))
        },
        compiler_params=pltpu.CompilerParams(vmem_limit_bytes=VMEM_BYTES if through else SMALL_VMEM_BYTES),
        name="halve",
    )(me, *ins, *afters, *through)
    for i, share in enumerate(shares):
        share.order = share.order[1:]
        share.mine = results[2 * i + 1].reshape(-1, share.depth, share.wide)
        share.swap(bits[i], results[2 * i].reshape(-1, share.depth, share.wide))
    return results[len(outs) :]


def joined(near, far, width, table_shape):
    parts = [x[0] for share in (near, far) for x in (share.mine, share.arrived)]
    shapes = [(near.depth, width), (near.depth, 3 * width), table_shape] + [(1, near.depth)] * 4
    return pl.pallas_call(
        join_kernel,
        out_shape=[jax.ShapeDtypeStruct(dims, F32) for dims in shapes],
        in_specs=[VMEM] * len(parts),
        out_specs=[VMEM] * len(shapes),
        scratch_shapes=[pltpu.VMEM((LANES, LANES), F32)],
        compiler_params=pltpu.CompilerParams(vmem_limit_bytes=SMALL_VMEM_BYTES),
        name="join",
    )(*parts)


def passed_along(x, axis, by):
    length = lax.axis_size(axis)
    pairs = [(i, i + by) for i in range(length) if 0 <= i + by < length]
    return lax.ppermute(x, axis, pairs)


def shards(
    hidden_in, out_grad, qkv_weight, out_weight, rel_table, norm1_gain, norm1_bias,
    up_weight, down_weight, norm2_gain, norm2_bias, seg_ids, pad_mask, rel_buckets,
):
    phase = lax.axis_index("phase").astype(jnp.int32).reshape(1)
    ways = lax.axis_size("dp")
    slots, width = hidden_in.shape
    inner = up_weight.shape[2]
    buckets, heads = rel_table.shape[1:]

    def shape(dims, kind):
        return jax.ShapeDtypeStruct(dims, kind)

    rows_of = {
        "xin": (width, BF16), "qkv": (3 * width, BF16), "ctx": (width, BF16), "form1": (width, F32),
        "scale1": (1, F32), "low1": (width, BF16), "slope": (inner, BF16), "act": (inner, BF16),
        "form2": (width, F32), "scale2": (1, F32), "out": (width, BF16),
        "outer_low": (width, BF16), "hidden_low": (inner, BF16), "residual_low": (width, BF16),
        "projected": (3 * width, BF16), "input_grad": (width, BF16),
    }
    kept_shapes = [
        shape((slots, rows_of[name][0]), rows_of[name][1])
        if name in rows_of
        else {
            "weights": shape((MICRO, heads, BLOCK, BLOCK), BF16),
            "sums1": shape((MICRO, 8, width), F32),
            "sums2": shape((MICRO, 8, width), F32),
            "residual": shape((BLOCK, width), F32),
            "offsets": shape((MICRO, heads, 8, SPAN), F32),
            "bias": shape((heads, TILE, SPAN), F32),
        }[name]
        for name in KEPT
    ]
    in_forward = ("qkv", "ctx", "form1", "scale1", "low1", "slope", "act", "form2", "scale2", "out")
    scratch = {f"{name}_v": ((BLOCK, rows_of[name][0]), rows_of[name][1]) for name in in_forward}
    scratch |= {
        name: ((BLOCK, width), BF16) for name in ("x_v", "g_v", "outer_v", "residual_low_v", "dctx_v", "grad_v")
    }
    scratch |= {
        "weights_v": ((heads, BLOCK, BLOCK), BF16), "acc_v": ((BLOCK, width), F32), "square_v": ((2, BLOCK, BLOCK), F32),
        "values_v": ((heads, SPAN), F32), "bias_v": ((heads, TILE, SPAN), F32), "sums1_v": ((8, width), F32), "sums2_v": ((8, width), F32),
        "wqkv_v": ((width, 3 * width), BF16), "wout_v": ((width, width), BF16), "wup_v": ((width, inner), BF16),
        "wdown_v": ((inner, width), BF16), "fold_v": ((2, TILE, SPAN), F32), "eighth_v": ((heads, 8, SPAN), F32),
        "half_v": ((2, BLOCK, BLOCK), BF16),
    }

    def step(work, phase_on, block, received, kept, afters=()):
        values = (
            phase, seg_ids, hidden_in, received, out_grad, rel_table.transpose(2, 0, 1), pad_mask[None, :], rel_buckets[None, :],
            norm1_gain, norm1_bias, norm2_gain, norm2_bias, qkv_weight, out_weight, up_weight, down_weight,
        )
        in_place = None if kept is None else [kept[name] for name in KEPT]
        return layer_step(work, phase_on, block, values, list(afters), in_place, kept_shapes, scratch)

    kept, sent = step("forward", 0, 0, hidden_in, None)
    first = passed_along(sent, "phase", 1)
    kept, _ = step("bias", 1, 0, hidden_in, kept)
    kept, sent = step("forward", 0, 1, hidden_in, kept)
    second = passed_along(sent, "phase", 1)
    kept, sent = step("both", 1, 0, first, kept)
    first_back = passed_along(sent, "phase", -1)
    kept, sent = step("both", 1, 1, second, kept)
    second_back = passed_along(sent, "phase", -1)
    kept, _ = step("back", 0, 0, first_back, kept)
    kept, _ = step("ffn_back", 0, 1, second_back, kept)

    bits = ways.bit_length() - 1
    near_first = list(range(bits))
    far_first = [0] + list(range(2, bits)) + [1] if bits > 1 else near_first
    me = lax.axis_index("dp").astype(jnp.int32).reshape(1)

    def weight_grad(left, right):
        product = dot_tn(left, right).astype(BF16)
        return product.reshape(ways, product.shape[0] // ways, product.shape[1])

    down = Share([weight_grad(kept["act"], kept["outer_low"])], near_first)
    up = Share([weight_grad(kept["low1"], kept["hidden_low"])], far_first)
    out_part = weight_grad(kept["ctx"], kept["residual_low"])
    halve_all(me, [down])
    halve_all(me, [up])
    kept, _ = step("attn_back", 0, 1, hidden_in, kept, [down.sent, up.sent])
    far_part = weight_grad(kept["xin"], kept["projected"][:, width:])
    (slots_in,) = halve_all(me, [down, up], [far_part], [kept["xin"]])
    near_part = weight_grad(slots_in, kept["projected"][:, :width])
    small = packed(ways, buckets, rel_buckets[None, :], kept, [far_part])
    near_part, far_part, small = halve_all(me, [down, up], [], [near_part, far_part, small])
    near = Share([out_part, near_part, small], near_first)
    far = Share([far_part], far_first)
    halve_all(me, [near, far])
    halve_all(me, [near, far])
    while down.order:
        halve_all(me, [down, up])
    while near.order:
        halve_all(me, [near, far])
    down_share = down.total()[0]
    up_share = up.total()[0]
    out_share, qkv_share, table_share, *norm_shares = joined(near, far, width, (heads, 1, buckets // ways))
    return (
        kept["out"][None],
        kept["input_grad"][None],
        qkv_share[None],
        out_share[None],
        table_share.transpose(1, 2, 0),
        norm_shares[0],
        norm_shares[1],
        up_share[None],
        down_share[None],
        norm_shares[2],
        norm_shares[3],
    )


def solution(mesh):
    return jax.shard_map(
        shards,
        mesh=mesh,
        in_specs=(
            P("dp", None),
            P("dp", None),
            P("phase", None, None),
            P("phase", None, None),
            P("phase", None, None),
            P("phase", None),
            P("phase", None),
            P("phase", None, None),
            P("phase", None, None),
            P("phase", None),
            P("phase", None),
            P("dp"),
            P("dp"),
            P(),
        ),
        out_specs=(
            P("phase", "dp", None),
            P("phase", "dp", None),
            P("phase", "dp", None),
            P("phase", "dp", None),
            P("phase", "dp", None),
            P("phase", "dp"),
            P("phase", "dp"),
            P("phase", "dp", None),
            P("phase", "dp", None),
            P("phase", "dp"),
            P("phase", "dp"),
        ),
        check_vma=False,
    )
```

```python
import functools

import jax
import jax.numpy as jnp
from jax import lax
from jax.experimental import pallas as pl
from jax.experimental.pallas import tpu as pltpu
from jax.sharding import PartitionSpec as P

BLOCK = 512
MICRO = 2
TILE = 128
LANES = 128
CHUNK = 768
SPAN = 2 * BLOCK
VMEM_BYTES = 58 * 1024 * 1024
SMALL_VMEM_BYTES = 20 * 1024 * 1024
NORM_LANE = 16

norm_eps = 1e-05
mask_fill = -1000000000.0
score_scale = 0.125
inv_root_two = 0.7071067811865476
inv_root_tau = 0.3989422804014327
log2_e = 1.4426950408889634
highest = lax.Precision.HIGHEST

F32 = jnp.float32
BF16 = jnp.bfloat16
ANY = pl.BlockSpec(memory_space=pl.ANY)
VMEM = pl.BlockSpec(memory_space=pltpu.VMEM)
QUICK = pl.CostEstimate(flops=1, bytes_accessed=1, transcendentals=0)
SMEM = pl.BlockSpec(memory_space=pltpu.SMEM)


def dot_nn(a, b):
    return lax.dot_general(a, b, (((1,), (0,)), ((), ())), preferred_element_type=F32)


def dot_nt(a, b):
    return lax.dot_general(a, b, (((1,), (1,)), ((), ())), preferred_element_type=F32)


def dot_tn(a, b):
    return lax.dot_general(a, b, (((0,), (0,)), ((), ())), preferred_element_type=F32)


def row_mean(rows):
    return jnp.sum(rows, -1, keepdims=True) * (1.0 / rows.shape[-1])


def normal_parts(residual):
    centred = residual - row_mean(residual)
    inv_scale = lax.rsqrt(row_mean(centred * centred) + norm_eps)
    return centred * inv_scale, inv_scale


def norm_backward(grad_rows, normal_form, inv_scale):
    first = row_mean(grad_rows)
    second = row_mean(grad_rows * normal_form)
    return inv_scale * (grad_rows - first - normal_form * second)


def gelu_parts(hidden):
    share = 0.5 + 0.5 * lax.erf(hidden * inv_root_two)
    bell = jnp.exp2(hidden * hidden * (-0.5 * log2_e))
    return hidden * share, share + hidden * bell * inv_root_tau


def half_mask(which, shape):
    lane = lax.broadcasted_iota(jnp.int32, shape, 1)
    return (lane < LANES // 2) if which == 0 else (lane >= LANES // 2)


class Copies:
    def __init__(self, sems):
        self.sems = sems
        self.used = 0
        self.stores = []

    def take(self, count=1):
        self.used += count
        return self.used - count

    def load(self, source, target):
        copy = pltpu.make_async_copy(source, target, self.sems.at[self.take()])
        copy.start()
        return copy

    def store(self, source, target, when=True):
        if when:
            self.stores.append(self.load(source, target))

    def finish(self):
        for copy in self.stores:
            copy.wait()


KEPT = (
    "xin", "qkv", "weights", "ctx", "form1", "scale1", "low1", "slope", "act", "form2", "scale2", "out",
    "bias", "outer_low", "hidden_low", "residual_low", "sums1", "sums2", "residual", "projected", "offsets", "input_grad",
)
INS = (
    "phase", "segments", "hidden_in", "received", "out_grad", "table", "padding", "buckets",
    "gain1", "shift1", "gain2", "shift2",
    "wqkv", "wout", "wup", "wdown",
)


class Layer:
    def __init__(self, refs):
        self.__dict__.update(refs)
        self.copies = Copies(self.sems)
        self.width = self.hidden_in.shape[1]
        self.inner = self.wup.shape[2]
        self.pairs = self.width // LANES
        self.stages = self.inner // (2 * CHUNK)
        self.pair_sems = self.copies.take(self.pairs)
        self.chunk_sems = [self.copies.take(self.stages) for _ in range(3)]

    def lanes_of(self, pair, part):
        return pl.ds(pl.multiple_of(part * self.width + pair * LANES, LANES), LANES)

    def stage(self, i):
        return pl.ds(pl.multiple_of(i * 2 * CHUNK, 2 * CHUNK), 2 * CHUNK)

    def build_bias(self):
        span = self.buckets.shape[1]
        bucket_ids = lax.broadcasted_iota(jnp.int32, (self.table.shape[2], span), 0)
        hot = (bucket_ids == self.buckets[...]).astype(F32)
        table = jnp.concatenate([self.table[head] for head in range(self.table.shape[0])], 0)
        values = lax.dot_general(
            table, hot, (((1,), (0,)), ((), ())), precision=highest, preferred_element_type=F32
        )
        self.values_v[:, :span] = values
        self.values_v[:, span:] = jnp.zeros((values.shape[0], SPAN - span), F32)

        def one_head(head, carry):
            wide = jnp.broadcast_to(self.values_v[pl.ds(head, 1), :], (TILE, SPAN))
            self.bias_v[head] = pltpu.roll(wide, 1, 1, stride=1, stride_axis=0)
            return carry

        lax.fori_loop(0, values.shape[0], one_head, 0)
        self.copies.store(self.bias_v, self.bias)


    def rows(self, block):
        return pl.ds(block * BLOCK, BLOCK)

    def forward(self, block, keep, built):
        copies = self.copies
        rows = self.rows(block)
        load_x = copies.load(self.hidden_in.at[rows] if keep else self.received, self.x_v)
        width = self.width
        loads = [
            copies.load(self.wqkv.at[0, :, pl.ds(c, width)], self.wqkv_v.at[:, pl.ds(c, width)])
            for c in range(0, 3 * width, width)
        ]
        if not built:
            self.build_bias()
        load_x.wait()

        def load_bias(pair):
            heads = pl.ds(2 * pair, 2)
            return pltpu.make_async_copy(self.bias.at[heads], self.bias_v.at[heads], self.sems.at[self.pair_sems + pair])

        for i, c in enumerate(range(0, 3 * width, width)):
            loads[i].wait()
            if built and i == 2:
                for pair in range(self.pairs):
                    load_bias(pair).start()
            self.qkv_v[:, c : c + width] = dot_nn(self.x_v[...], self.wqkv_v[:, c : c + width]).astype(BF16)
        copies.store(self.x_v, self.xin.at[rows])
        copies.store(self.qkv_v, self.qkv.at[rows], keep)
        weights_sem = self.sems.at[copies.take()]
        later_loads = [
            pltpu.make_async_copy(source.at[0], target, self.sems.at[copies.take()])
            for source, target in ((self.wout, self.wout_v), (self.wup, self.wup_v), (self.wdown, self.wdown_v))
        ]

        def own(pair, part, which):
            both = self.qkv_v[:, self.lanes_of(pair, part)]
            return jnp.where(half_mask(which, both.shape), both, jnp.zeros_like(both))

        single = self.segments[block * BLOCK + TILE] == self.segments[block * BLOCK]
        padding = self.padding[:, block * BLOCK : (block + 1) * BLOCK]
        tile_of = lax.broadcasted_iota(jnp.int32, (1, BLOCK), 1) // TILE
        shut = [
            jnp.where((padding == 1) & (single | (tile_of == tile)), 0.0, mask_fill) for tile in range(BLOCK // TILE)
        ]
        row_id = lax.broadcasted_iota(jnp.int32, (TILE, TILE), 0)
        diagonal = row_id == lax.broadcasted_iota(jnp.int32, (TILE, TILE), 1)

        def bias_rows(head, tile):
            at = BLOCK - tile * TILE
            rows = self.bias_v[head, :, at : at + BLOCK]
            masked = rows + shut[tile]
            own = slice(tile * TILE, (tile + 1) * TILE)
            parts = [masked[:, : own.start], jnp.where(diagonal, rows[:, own], masked[:, own]), masked[:, own.stop :]]
            return jnp.concatenate([part for part in parts if part.shape[1]], 1)

        def weigh(pair, which):
            head = 2 * pair + which
            k_own = own(pair, 1, which)
            for r in range(0, BLOCK, 2 * TILE):
                q_rows = self.qkv_v[r : r + 2 * TILE, self.lanes_of(pair, 0)] * jnp.asarray(score_scale, BF16)
                tiles = [bias_rows(head, tile) for tile in range(r // TILE, r // TILE + 2)]
                logits = dot_nt(q_rows, k_own) + jnp.concatenate(tiles, 0)
                raised = jnp.exp(logits - jnp.max(logits, -1, keepdims=True))
                share = pl.reciprocal(jnp.sum(raised, -1, keepdims=True), approx=True)
                self.weights_v[head, r : r + 2 * TILE, :] = (raised * share).astype(BF16)

        def head_pair(pair, carry):
            if built:
                load_bias(pair).wait()

            @pl.when(pair == 0)
            def _():
                for load in later_loads:
                    load.start()

            weigh(pair, 0)
            context = dot_nn(self.weights_v[2 * pair], own(pair, 2, 0))
            weigh(pair, 1)
            context += dot_nn(self.weights_v[2 * pair + 1], own(pair, 2, 1))
            self.ctx_v[:, self.lanes_of(pair, 0)] = context.astype(BF16)
            if keep:
                heads = pl.ds(2 * pair, 2)
                pltpu.make_async_copy(self.weights_v.at[heads], self.weights.at[block, heads], weights_sem).start()
            return carry

        lax.fori_loop(0, self.pairs, head_pair, 0)
        if keep:
            copies.stores.append(pltpu.make_async_copy(self.weights_v, self.weights.at[block], weights_sem))
        copies.store(self.ctx_v, self.ctx.at[rows])
        load_out, load_up, load_down = later_loads
        load_out.wait()
        self.acc_v[...] = dot_nn(self.ctx_v[...], self.wout_v[...])
        for r in range(0, BLOCK, 64):
            tile = slice(r, r + 64)
            form, scale = normal_parts(self.acc_v[tile, :] + self.x_v[tile, :].astype(F32))
            normed = form * self.gain1[...] + self.shift1[...]
            self.form1_v[tile, :] = form
            self.scale1_v[tile, :] = scale
            self.acc_v[tile, :] = normed
            self.low1_v[tile, :] = normed.astype(BF16)
        copies.store(self.form1_v, self.form1.at[rows], keep)
        copies.store(self.scale1_v, self.scale1.at[rows], keep)
        copies.store(self.low1_v, self.low1.at[rows])
        load_up.wait()
        load_down.wait()
        act_sem = self.sems.at[copies.take()]
        slope_sem = self.sems.at[copies.take()]

        def two_chunks(i, carry):
            span = self.stage(i)
            active, grade = gelu_parts(dot_nn(self.low1_v[...], self.wup_v[:, span]))
            active = active.astype(BF16)
            self.act_v[:, span] = active
            self.slope_v[:, span] = grade.astype(BF16)
            self.acc_v[...] += dot_nn(active, self.wdown_v[span, :])
            pltpu.make_async_copy(self.act_v.at[:, span], self.act.at[rows, span], act_sem).start()
            if keep:
                pltpu.make_async_copy(self.slope_v.at[:, span], self.slope.at[rows, span], slope_sem).start()
            return carry

        lax.fori_loop(0, self.stages, two_chunks, 0)
        copies.stores.append(pltpu.make_async_copy(self.act_v, self.act.at[rows], act_sem))
        if keep:
            copies.stores.append(pltpu.make_async_copy(self.slope_v, self.slope.at[rows], slope_sem))
        for r in range(0, BLOCK, 64):
            tile = slice(r, r + 64)
            form, scale = normal_parts(self.acc_v[tile, :])
            self.form2_v[tile, :] = form
            self.scale2_v[tile, :] = scale
            self.out_v[tile, :] = (form * self.gain2[...] + self.shift2[...]).astype(BF16)
        copies.store(self.out_v, self.send, keep)
        copies.store(self.out_v, self.out.at[rows])
        copies.store(self.form2_v, self.form2.at[rows], keep)
        copies.store(self.scale2_v, self.scale2.at[rows], keep)


    def chunk_loads(self, i, rows):
        span = self.stage(i)
        return [
            pltpu.make_async_copy(source, target, self.sems.at[self.chunk_sems[k] + i])
            for k, (source, target) in enumerate(
                (
                    (self.wdown.at[0, span], self.wdown_v.at[span]),
                    (self.slope.at[rows, span], self.slope_v.at[:, span]),
                    (self.wup.at[0, :, span], self.wup_v.at[:, span]),
                )
            )
        ]

    def norm_sums(self, source, form_ref, sums_ref):
        gain_sum = jnp.zeros((1, self.width), F32)
        shift_sum = jnp.zeros((1, self.width), F32)
        for r in range(0, BLOCK, 64):
            grad_rows, form = source[r : r + 64, :].astype(F32), form_ref[r : r + 64, :]
            gain_sum += jnp.sum(grad_rows * form, 0, keepdims=True)
            shift_sum += jnp.sum(grad_rows, 0, keepdims=True)
        sums_ref[...] = jnp.zeros(sums_ref.shape, F32)
        sums_ref[0:1, :] = gain_sum
        sums_ref[1:2, :] = shift_sum

    def norm_back(self, block):
        for r in range(0, BLOCK, 64):
            tile = slice(r, r + 64)
            grad_rows = self.g_v[tile, :].astype(F32) * self.gain2[...]
            grad_outer = norm_backward(grad_rows, self.form2_v[tile, :], self.scale2_v[tile, :])
            self.acc_v[tile, :] = grad_outer
            self.outer_v[tile, :] = grad_outer.astype(BF16)
        self.copies.store(self.outer_v, self.outer_low.at[self.rows(block)])

    def norm_sums_2(self, block):
        self.norm_sums(self.g_v, self.form2_v, self.sums2_v)
        self.copies.store(self.sums2_v, self.sums2.at[block])

    def ffn_back(self, block, staged=False, middle_loads=()):
        copies = self.copies
        rows = self.rows(block)
        hidden_sem = self.sems.at[copies.take()]

        def two_chunks(i, carry):
            span = self.stage(i)
            if staged:
                load_down, load_slope, load_up = self.chunk_loads(i, rows)
                load_down.wait()
                load_slope.wait()
            grad_active = dot_nt(self.outer_v[...], self.wdown_v[span, :])
            hidden = (grad_active * self.slope_v[:, span].astype(F32)).astype(BF16)
            self.slope_v[:, span] = hidden
            if staged:
                load_up.wait()

                @pl.when(i + 2 < self.stages)
                def _():
                    for load in self.chunk_loads(i + 2, rows):
                        load.start()

            self.acc_v[...] += dot_nt(hidden, self.wup_v[:, span])
            pltpu.make_async_copy(self.slope_v.at[:, span], self.hidden_low.at[rows, span], hidden_sem).start()
            return carry

        lax.fori_loop(0, self.stages, two_chunks, 0)
        copies.stores.append(pltpu.make_async_copy(self.slope_v, self.hidden_low.at[rows], hidden_sem))
        for load in middle_loads:
            load.wait()
        self.norm_sums(self.acc_v, self.form1_v, self.sums1_v)
        for r in range(0, BLOCK, 64):
            tile = slice(r, r + 64)
            grad_residual = norm_backward(
                self.acc_v[tile, :] * self.gain1[...], self.form1_v[tile, :], self.scale1_v[tile, :]
            )
            self.acc_v[tile, :] = grad_residual
            self.residual_low_v[tile, :] = grad_residual.astype(BF16)
        copies.store(self.residual_low_v, self.residual_low.at[rows])
        copies.store(self.sums1_v, self.sums1.at[block])

    def attn_back(self, block, next_loads=None, load_in=()):
        copies = self.copies
        rows = self.rows(block)
        self.dctx_v[...] = dot_nt(self.residual_low_v[...], self.wout_v[...]).astype(BF16)
        self.fold_v[:, :, 0:TILE] = jnp.zeros((2, TILE, TILE), F32)

        def head_pair(pair, carry):
            def lanes_of(part):
                return self.lanes_of(pair, part)

            if next_loads is not None:
                next_loads(pair)
            q_pair, k_pair, v_pair = (self.qkv_v[:, lanes_of(part)] for part in range(3))
            grad_pair = self.dctx_v[:, lanes_of(0)]
            crossed = grad_pair.astype(F32) * self.ctx_v[:, lanes_of(0)].astype(F32)
            masks = [half_mask(which, k_pair.shape) for which in range(2)]

            def own(both, which):
                return jnp.where(masks[which], both, jnp.zeros_like(both))

            for which in range(2):
                self.square_v[which] = dot_nt(grad_pair, own(v_pair, which))
            q_grad = k_grad = v_grad = 0.0
            for which in range(2):
                head = 2 * pair + which
                delta = jnp.sum(own(crossed, which), -1, keepdims=True)
                for r in range(0, BLOCK, 64):
                    tile = slice(r, r + 64)
                    score_grad = (
                        self.weights_v[head, tile, :].astype(F32) * (self.square_v[which, tile, :] - delta[tile, :])
                    ).astype(BF16)
                    self.half_v[which, tile, :] = score_grad
                    at = BLOCK - r // TILE * TILE
                    wide = score_grad.astype(F32)
                    half = slice(r % TILE, r % TILE + 64)
                    if r < TILE:
                        self.fold_v[which, half, at : at + BLOCK] = wide
                    else:
                        self.fold_v[which, half, at : at + TILE] = wide[:, :TILE]
                        self.fold_v[which, half, at + TILE : at + BLOCK] += wide[:, TILE:]
                v_grad += dot_tn(self.weights_v[head], own(grad_pair, which))
                q_grad += dot_nn(self.half_v[which], own(k_pair, which))
                k_grad += dot_tn(self.half_v[which], own(q_pair, which))
                folded = self.fold_v[which]
                size = TILE // 2
                while size >= 8:
                    folded = folded[:size, :] + pltpu.roll(folded[size:, :], SPAN - size, 1)
                    size //= 2
                self.eighth_v[head] = folded
            self.qkv_v[:, lanes_of(0)] = (q_grad * score_scale).astype(BF16)
            self.qkv_v[:, lanes_of(1)] = (k_grad * score_scale).astype(BF16)
            self.qkv_v[:, lanes_of(2)] = v_grad.astype(BF16)
            return carry

        lax.fori_loop(0, self.pairs, head_pair, 0)
        copies.store(self.eighth_v, self.offsets.at[block])
        copies.store(self.qkv_v, self.projected.at[rows])
        for load in load_in:
            load.wait()
        self.grad_v[...] = (self.acc_v[...] + dot_nt(self.qkv_v[...], self.wqkv_v[...])).astype(BF16)
        copies.store(self.grad_v, self.send)
        copies.store(self.grad_v, self.input_grad.at[rows])


    def do_forward(self, block):
        self.forward(block, True, block > 0)

    def do_bias(self, block):
        self.build_bias()

    def do_both(self, block):
        load = self.copies.load(self.out_grad.at[self.rows(block)], self.g_v)
        self.forward(block, False, True)
        load.wait()
        self.norm_back(block)
        self.ffn_back(block)
        self.norm_sums_2(block)
        self.attn_back(block)

    def do_back(self, block):
        rows = self.rows(block)
        loads = [
            self.copies.load(source, target)
            for source, target in (
                (self.received, self.g_v),
                (self.form2.at[rows], self.form2_v),
                (self.scale2.at[rows], self.scale2_v),
                (self.slope.at[rows], self.slope_v),
                (self.wdown.at[0], self.wdown_v),
                (self.wup.at[0], self.wup_v),
                (self.form1.at[rows], self.form1_v),
                (self.scale1.at[rows], self.scale1_v),
                (self.qkv.at[rows], self.qkv_v),
                (self.weights.at[block], self.weights_v),
                (self.ctx.at[rows], self.ctx_v),
                (self.wout.at[0], self.wout_v),
                (self.wqkv.at[0], self.wqkv_v),
            )
        ]
        for load in loads:
            load.wait()
        self.norm_back(block)
        self.ffn_back(block)
        self.norm_sums_2(block)
        self.attn_back(block)

    def do_ffn_back(self, block):
        rows = self.rows(block)
        loads = [
            self.copies.load(source, target)
            for source, target in (
                (self.received, self.g_v),
                (self.form2.at[rows], self.form2_v),
                (self.scale2.at[rows], self.scale2_v),
            )
        ]
        self.chunk_loads(0, rows)[0].start()
        for load in loads:
            load.wait()
        for load in self.chunk_loads(0, rows)[1:] + self.chunk_loads(1, rows):
            load.start()
        middle = [
            self.copies.load(self.form1.at[rows], self.form1_v),
            self.copies.load(self.scale1.at[rows], self.scale1_v),
        ]
        self.norm_back(block)
        self.ffn_back(block, True, middle)
        self.copies.store(self.acc_v, self.residual)
        self.norm_sums_2(block)

    def do_attn_back(self, block):
        rows = self.rows(block)
        loads = [
            self.copies.load(source, target)
            for source, target in ((self.residual_low.at[rows], self.residual_low_v), (self.wout.at[0], self.wout_v))
        ]
        first = self.copies.take(5 * self.pairs)

        def pair_loads(pair):
            heads = pl.ds(2 * pair, 2)
            sources = [(self.weights.at[block, heads], self.weights_v.at[heads])]
            for source, target, parts in ((self.qkv, self.qkv_v, 3), (self.ctx, self.ctx_v, 1)):
                for part in range(parts):
                    lanes = self.lanes_of(pair, part)
                    sources.append((source.at[rows, lanes], target.at[:, lanes]))
            return [
                pltpu.make_async_copy(source, target, self.sems.at[first + 5 * pair + k])
                for k, (source, target) in enumerate(sources)
            ]

        for pair in range(2):
            for load in pair_loads(pair):
                load.start()
        for load in loads:
            load.wait()
        last = [
            pltpu.make_async_copy(source, target, self.sems.at[self.copies.take()])
            for source, target in ((self.wqkv.at[0], self.wqkv_v), (self.residual, self.acc_v))
        ]

        def next_loads(pair):
            for load in pair_loads(pair):
                load.wait()

            @pl.when(pair + 2 < self.pairs)
            def _():
                for load in pair_loads(pair + 2):
                    load.start()

            @pl.when(pair == self.pairs - 3)
            def _():
                for load in last:
                    load.start()

        self.attn_back(block, next_loads, last)


def layer_kernel(work, phase_on, block, ins, outs, scratch, after_count, kept_count, *refs):
    refs_in, refs = refs[: len(ins)], refs[len(ins) + after_count + kept_count :]
    named = dict(zip(ins, refs_in)) | dict(zip(outs, refs)) | dict(zip(scratch, refs[len(outs) :]))

    @pl.when(named["phase"][0] == phase_on)
    def _():
        layer = Layer(named)
        getattr(layer, f"do_{work}")(block)
        layer.copies.finish()


def layer_step(work, phase_on, block, values, afters, kept, kept_shapes, scratch):
    specs = [SMEM] * 2 + [ANY] * 3 + [VMEM] * 7 + [ANY] * 4
    names = list(scratch)
    kept = list(kept) if kept is not None else []
    sent = jax.ShapeDtypeStruct((BLOCK, values[2].shape[1]), BF16)
    if work == "bias":
        names = ["values_v", "bias_v"]
    count = len(values) + len(afters)
    results = pl.pallas_call(
        functools.partial(
            layer_kernel, work, phase_on, block, INS, KEPT + ("send",), names + ["sems"], len(afters), len(kept)
        ),
        out_shape=list(kept_shapes) + [sent],
        in_specs=specs + [ANY] * (len(afters) + len(kept)),
        out_specs=[ANY] * (len(kept_shapes) + 1),
        scratch_shapes=[pltpu.VMEM(*scratch[name]) for name in names] + [pltpu.SemaphoreType.DMA((96,))],
        input_output_aliases={count + i: i for i in range(len(kept))},
        compiler_params=pltpu.CompilerParams(vmem_limit_bytes=VMEM_BYTES),
        name=f"{work}_{phase_on}_{block}",
    )(*values, *afters, *kept)
    return dict(zip(KEPT, results)), results[-1]


def pack_kernel(ways, buckets_ref, offsets_ref, sums1_ref, sums2_ref, *refs):
    out_ref, turn_v = refs[-2:]
    row_of = lax.broadcasted_iota(jnp.int32, (8, SPAN), 0)
    lines = []
    for head in range(offsets_ref.shape[1]):
        eighth = offsets_ref[0, head] + offsets_ref[1, head]
        for size in (4, 2, 1):
            eighth = jnp.where((row_of & size) != 0, pltpu.roll(eighth, SPAN - size, 1), eighth)
        lines.append(jnp.sum(eighth, 0, keepdims=True))
    lines += [jnp.zeros((1, SPAN), F32)] * (NORM_LANE - len(lines))
    sums = pltpu.roll(jnp.concatenate(lines, 0), SPAN - 1, 1)
    span = buckets_ref.shape[1]
    buckets, depth = out_ref.shape[0] // 3, out_ref.shape[0] // ways
    share = buckets // ways
    bucket_ids = lax.broadcasted_iota(jnp.int32, (buckets, span), 0)
    hot = (bucket_ids == buckets_ref[...]).astype(F32)
    table = lax.dot_general(
        hot, sums[:, :span], (((1,), (1,)), ((), ())), precision=highest, preferred_element_type=F32
    ).astype(BF16)
    turn_v[...] = jnp.zeros(turn_v.shape, F32)
    for i, ref in enumerate((sums1_ref, sums2_ref)):
        at = NORM_LANE + 2 * i
        turn_v[at : at + 2, :] = ref[0, 0:2, :] + ref[1, 0:2, :]
    out_ref[...] = turn_v[...].T.astype(BF16)
    for i in range(ways):
        out_ref[i * depth : i * depth + share, 0:NORM_LANE] = table[i * share : (i + 1) * share, :]


def packed(ways, buckets, offset_buckets, kept, afters):
    width = kept["sums1"].shape[2]
    depth, share = width // ways, buckets // ways
    arrays = (offset_buckets, kept["offsets"], kept["sums1"], kept["sums2"])
    if depth % 16 == 0 and share % 16 == 0 and 3 * buckets == width:
        rows = pl.pallas_call(
            functools.partial(pack_kernel, ways),
            out_shape=jax.ShapeDtypeStruct((width, LANES), BF16),
            in_specs=[VMEM] * len(arrays) + [ANY] * len(afters),
            out_specs=VMEM,
            scratch_shapes=[pltpu.VMEM((LANES, width), F32)],
            compiler_params=pltpu.CompilerParams(vmem_limit_bytes=SMALL_VMEM_BYTES),
            name="pack",
        )(*arrays, *afters)
        return rows.reshape(ways, depth, LANES)
    eighths = jnp.sum(kept["offsets"], 0)
    lines = sum(jnp.roll(eighths[:, i, :], -i, 1) for i in range(8))[:, 1:]
    hot = (offset_buckets[0][None, :] == jnp.arange(buckets, dtype=jnp.int32)[:, None]).astype(F32)
    table = jnp.dot(hot, lines.T, precision=highest).reshape(ways, share, -1)
    table = jnp.pad(table, ((0, 0), (0, depth - share), (0, NORM_LANE - table.shape[2])))
    norms = jnp.concatenate([jnp.sum(kept[name], 0)[:2] for name in ("sums1", "sums2")], 0)
    norms = norms.T.reshape(ways, depth, 4)
    rows = jnp.concatenate([table, norms], 2)
    return jnp.pad(rows, ((0, 0), (0, 0), (0, LANES - rows.shape[2]))).astype(BF16)


def halve_kernel(bits, counts, after_count, through_count, me_ref, *refs):
    outs = refs[2 * sum(counts) + after_count + through_count :]
    for i, count in enumerate(counts):
        pieces, refs = [refs[2 * k : 2 * k + 2] for k in range(count)], refs[2 * count :]
        send_ref, rest_ref = outs[2 * i : 2 * i + 2]
        mine = (me_ref[0] >> bits[i]) & 1

        def total(which):
            parts = [
                (kept[0, which, 0, 0] if len(kept.shape) == 6 else kept[0, which, 0]).astype(F32)
                + arrived[0, which, 0].astype(F32)
                for kept, arrived in pieces
            ]
            return jnp.concatenate(parts, 1)

        send_ref[0, 0] = total(1 - mine).astype(send_ref.dtype)
        rest_ref[0, 0] = total(mine)


def join_kernel(kept_ref, arrived_ref, out_ref, qkv_ref, table_ref, *refs):
    norm_refs, turn_v = refs[:-1], refs[-1]
    total = kept_ref[...] + arrived_ref[...].astype(F32)
    wide = out_ref.shape[1]
    out_ref[...] = total[:, :wide]
    qkv_ref[...] = total[:, wide : 4 * wide]
    small = total[:, 4 * wide :]
    turn_v[...] = jnp.zeros(turn_v.shape, F32)
    turn_v[: small.shape[0], :] = small
    turned = turn_v[...].T
    for head in range(table_ref.shape[0]):
        table_ref[head] = turned[head : head + 1, : table_ref.shape[2]]
    for i, ref in enumerate(norm_refs):
        ref[...] = turned[NORM_LANE + i : NORM_LANE + i + 1, : ref.shape[1]]


class Part:
    def __init__(self, whole):
        self.whole = whole
        self.sent = self.of_core(1 - (lax.axis_index("dp") & 1))
        self.arrived = swapped(self.sent, 0)

    def of_core(self, core):
        split = self.whole.reshape((self.whole.shape[0] // 2, 2) + self.whole.shape[1:])
        return lax.dynamic_index_in_dim(split, core, 1, keepdims=False)


def swapped(array, bit):
    count = lax.axis_size("dp")
    return lax.ppermute(array, "dp", [(i, i ^ (1 << bit)) for i in range(count)])


class Share:
    def __init__(self, parts, order):
        self.parts = parts
        self.order = order[1:]
        self.left = sorted(order[1:])
        self.depth = parts[0].whole.shape[1]
        self.wide = sum(part.whole.shape[2] for part in parts)
        self.mine = None

    def swap(self, bit, theirs):
        self.left.remove(bit)
        self.sent = theirs
        self.arrived = swapped(theirs, bit)

    def total(self):
        if self.mine is not None:
            return self.mine + self.arrived.astype(F32)
        here = lax.axis_index("dp") & 1
        return jnp.concatenate(
            [part.of_core(here).astype(F32) + part.arrived.astype(F32) for part in self.parts], 2
        )

    def split_at(self):
        bit = self.order[0]
        axis = len(self.left) - 1 - self.left.index(bit)
        return bit, 2**axis, 2 ** (len(self.left) - 1 - axis)

    def halve(self):
        bit, above, below = self.split_at()
        self.order = self.order[1:]
        split = self.total().reshape(above, 2, below, self.depth, self.wide)
        here = (lax.axis_index("dp") >> bit) & 1
        theirs = lax.dynamic_index_in_dim(split, 1 - here, 1, keepdims=False).astype(BF16)
        mine = lax.dynamic_index_in_dim(split, here, 1, keepdims=False)
        self.mine = mine.reshape(-1, self.depth, self.wide)
        self.swap(bit, theirs.reshape(-1, self.depth, self.wide))


def halve_all(me, shares, afters=(), through=()):
    if any(share.depth % 16 for share in shares):
        for share in shares:
            share.halve()
        return through
    ins, in_specs, outs, out_specs, bits, counts = [], [], [], [], [], []
    for share in shares:
        bit, above, below = share.split_at()
        bits.append(bit)

        def halves(wide, b=below):
            return pl.BlockSpec((1, 2, 1, share.depth, wide), lambda i, me: (i // b, 0, i % b, 0, 0))

        if share.mine is None:
            counts.append(len(share.parts))
            for part in share.parts:
                wide = part.whole.shape[2]
                ins.append(part.whole.reshape(above, 2, below, 2, share.depth, wide))
                in_specs.append(
                    pl.BlockSpec(
                        (1, 2, 1, 1, share.depth, wide),
                        lambda i, me, b=below: (i // b, 0, i % b, me[0] & 1, 0, 0),
                    )
                )
                ins.append(part.arrived.reshape(above, 2, below, share.depth, wide))
                in_specs.append(halves(wide))
        else:
            counts.append(1)
            for array in (share.mine, share.arrived):
                ins.append(array.reshape(above, 2, below, share.depth, share.wide))
                in_specs.append(halves(share.wide))
        outs += [
            jax.ShapeDtypeStruct((above, below, share.depth, share.wide), kind) for kind in (BF16, F32)
        ]
        out_specs += [
            pl.BlockSpec((1, 1, share.depth, share.wide), lambda i, me, b=below: (i // b, i % b, 0, 0))
        ] * 2
        steps = above * below
    results = pl.pallas_call(
        functools.partial(halve_kernel, tuple(bits), tuple(counts), len(afters), len(through)),
        grid_spec=pltpu.PrefetchScalarGridSpec(
            num_scalar_prefetch=1,
            grid=(steps,),
            in_specs=in_specs + [ANY] * (len(afters) + len(through)),
            out_specs=out_specs + [ANY] * len(through),
        ),
        out_shape=outs + [jax.ShapeDtypeStruct(array.shape, array.dtype) for array in through],
        input_output_aliases={
            1 + len(ins) + len(afters) + i: len(outs) + i for i in range(len(through))
        },
        compiler_params=pltpu.CompilerParams(vmem_limit_bytes=VMEM_BYTES if through else SMALL_VMEM_BYTES),
        name="halve",
    )(me, *ins, *afters, *through)
    for i, share in enumerate(shares):
        share.order = share.order[1:]
        share.mine = results[2 * i + 1].reshape(-1, share.depth, share.wide)
        share.swap(bits[i], results[2 * i].reshape(-1, share.depth, share.wide))
    return results[len(outs) :]


def joined(share, width, table_shape):
    shapes = [(share.depth, width), (share.depth, 3 * width), table_shape] + [(1, share.depth)] * 4
    return pl.pallas_call(
        join_kernel,
        out_shape=[jax.ShapeDtypeStruct(dims, F32) for dims in shapes],
        in_specs=[VMEM] * 2,
        out_specs=[VMEM] * len(shapes),
        scratch_shapes=[pltpu.VMEM((LANES, LANES), F32)],
        compiler_params=pltpu.CompilerParams(vmem_limit_bytes=SMALL_VMEM_BYTES),
        name="join",
    )(share.mine[0], share.arrived[0])


def passed_along(x, axis, by):
    length = lax.axis_size(axis)
    pairs = [(i, i + by) for i in range(length) if 0 <= i + by < length]
    return lax.ppermute(x, axis, pairs)


def shards(
    hidden_in, out_grad, qkv_weight, out_weight, rel_table, norm1_gain, norm1_bias,
    up_weight, down_weight, norm2_gain, norm2_bias, seg_ids, pad_mask, rel_buckets,
):
    phase = lax.axis_index("phase").astype(jnp.int32).reshape(1)
    ways = lax.axis_size("dp")
    slots, width = hidden_in.shape
    inner = up_weight.shape[2]
    buckets, heads = rel_table.shape[1:]

    def shape(dims, kind):
        return jax.ShapeDtypeStruct(dims, kind)

    rows_of = {
        "xin": (width, BF16), "qkv": (3 * width, BF16), "ctx": (width, BF16), "form1": (width, F32),
        "scale1": (1, F32), "low1": (width, BF16), "slope": (inner, BF16), "act": (inner, BF16),
        "form2": (width, F32), "scale2": (1, F32), "out": (width, BF16),
        "outer_low": (width, BF16), "hidden_low": (inner, BF16), "residual_low": (width, BF16),
        "projected": (3 * width, BF16), "input_grad": (width, BF16),
    }
    kept_shapes = [
        shape((slots, rows_of[name][0]), rows_of[name][1])
        if name in rows_of
        else {
            "weights": shape((MICRO, heads, BLOCK, BLOCK), BF16),
            "sums1": shape((MICRO, 8, width), F32),
            "sums2": shape((MICRO, 8, width), F32),
            "residual": shape((BLOCK, width), F32),
            "offsets": shape((MICRO, heads, 8, SPAN), F32),
            "bias": shape((heads, TILE, SPAN), F32),
        }[name]
        for name in KEPT
    ]
    in_forward = ("qkv", "ctx", "form1", "scale1", "low1", "slope", "act", "form2", "scale2", "out")
    scratch = {f"{name}_v": ((BLOCK, rows_of[name][0]), rows_of[name][1]) for name in in_forward}
    scratch |= {
        name: ((BLOCK, width), BF16) for name in ("x_v", "g_v", "outer_v", "residual_low_v", "dctx_v", "grad_v")
    }
    scratch |= {
        "weights_v": ((heads, BLOCK, BLOCK), BF16), "acc_v": ((BLOCK, width), F32), "square_v": ((2, BLOCK, BLOCK), F32),
        "values_v": ((heads, SPAN), F32), "bias_v": ((heads, TILE, SPAN), F32), "sums1_v": ((8, width), F32), "sums2_v": ((8, width), F32),
        "wqkv_v": ((width, 3 * width), BF16), "wout_v": ((width, width), BF16), "wup_v": ((width, inner), BF16),
        "wdown_v": ((inner, width), BF16), "fold_v": ((2, TILE, SPAN), F32), "eighth_v": ((heads, 8, SPAN), F32),
        "half_v": ((2, BLOCK, BLOCK), BF16),
    }

    def step(work, phase_on, block, received, kept, afters=()):
        values = (
            phase, seg_ids, hidden_in, received, out_grad, rel_table.transpose(2, 0, 1), pad_mask[None, :], rel_buckets[None, :],
            norm1_gain, norm1_bias, norm2_gain, norm2_bias, qkv_weight, out_weight, up_weight, down_weight,
        )
        in_place = None if kept is None else [kept[name] for name in KEPT]
        return layer_step(work, phase_on, block, values, list(afters), in_place, kept_shapes, scratch)

    kept, sent = step("forward", 0, 0, hidden_in, None)
    first = passed_along(sent, "phase", 1)
    kept, _ = step("bias", 1, 0, hidden_in, kept)
    kept, sent = step("forward", 0, 1, hidden_in, kept)
    second = passed_along(sent, "phase", 1)
    kept, sent = step("both", 1, 0, first, kept)
    first_back = passed_along(sent, "phase", -1)
    kept, sent = step("both", 1, 1, second, kept)
    second_back = passed_along(sent, "phase", -1)
    kept, _ = step("back", 0, 0, first_back, kept)
    kept, _ = step("ffn_back", 0, 1, second_back, kept)

    bits = ways.bit_length() - 1
    near_first = list(range(bits))
    far_first = [0] + list(range(2, bits)) + [1] if bits > 1 else near_first
    me = lax.axis_index("dp").astype(jnp.int32).reshape(1)

    def weight_grad(left, right):
        product = dot_tn(left, right).astype(BF16)
        return product.reshape(ways, product.shape[0] // ways, product.shape[1])

    down = Share([Part(weight_grad(kept["act"], kept["outer_low"]))], near_first)
    up = Share([Part(weight_grad(kept["low1"], kept["hidden_low"]))], far_first)
    out_part = Part(weight_grad(kept["ctx"], kept["residual_low"]))
    halve_all(me, [down])
    halve_all(me, [up])
    kept, _ = step("attn_back", 0, 1, hidden_in, kept, [down.sent, up.sent])
    far_part = Part(weight_grad(kept["xin"], kept["projected"][:, width:]))
    (slots_in,) = halve_all(me, [down, up], [far_part.sent], [kept["xin"]])
    near_part = Part(weight_grad(slots_in, kept["projected"][:, :width]))
    small_part = Part(packed(ways, buckets, rel_buckets[None, :], kept, [near_part.sent]))
    last = Share([out_part, near_part, far_part, small_part], near_first)
    halve_all(me, [last], [down.sent, up.sent])
    halve_all(me, [down, up])
    halve_all(me, [last], [down.sent, up.sent])
    while down.order:
        halve_all(me, [down, up])
    while last.order:
        halve_all(me, [last])
    down_share = down.total()[0]
    up_share = up.total()[0]
    out_share, qkv_share, table_share, *norm_shares = joined(last, width, (heads, 1, buckets // ways))
    return (
        kept["out"][None],
        kept["input_grad"][None],
        qkv_share[None],
        out_share[None],
        table_share.transpose(1, 2, 0),
        norm_shares[0],
        norm_shares[1],
        up_share[None],
        down_share[None],
        norm_shares[2],
        norm_shares[3],
    )


def solution(mesh):
    return jax.shard_map(
        shards,
        mesh=mesh,
        in_specs=(
            P("dp", None),
            P("dp", None),
            P("phase", None, None),
            P("phase", None, None),
            P("phase", None, None),
            P("phase", None),
            P("phase", None),
            P("phase", None, None),
            P("phase", None, None),
            P("phase", None),
            P("phase", None),
            P("dp"),
            P("dp"),
            P(),
        ),
        out_specs=(
            P("phase", "dp", None),
            P("phase", "dp", None),
            P("phase", "dp", None),
            P("phase", "dp", None),
            P("phase", "dp", None),
            P("phase", "dp"),
            P("phase", "dp"),
            P("phase", "dp", None),
            P("phase", "dp", None),
            P("phase", "dp"),
            P("phase", "dp"),
        ),
        check_vma=False,
    )
```

```python
import functools

import jax
import jax.numpy as jnp
from jax import lax
from jax.experimental import pallas as pl
from jax.experimental.pallas import tpu as pltpu
from jax.sharding import PartitionSpec as P

BLOCK = 512
MICRO = 2
TILE = 128
LANES = 128
CHUNK = 768
SPAN = 2 * BLOCK
VMEM_BYTES = 58 * 1024 * 1024
SMALL_VMEM_BYTES = 20 * 1024 * 1024
NORM_LANE = 16

norm_eps = 1e-05
mask_fill = -1000000000.0
score_scale = 0.125
inv_root_two = 0.7071067811865476
inv_root_tau = 0.3989422804014327
log2_e = 1.4426950408889634
highest = lax.Precision.HIGHEST

F32 = jnp.float32
BF16 = jnp.bfloat16
ANY = pl.BlockSpec(memory_space=pl.ANY)
VMEM = pl.BlockSpec(memory_space=pltpu.VMEM)
QUICK = pl.CostEstimate(flops=1, bytes_accessed=1, transcendentals=0)
SMEM = pl.BlockSpec(memory_space=pltpu.SMEM)


def dot_nn(a, b):
    return lax.dot_general(a, b, (((1,), (0,)), ((), ())), preferred_element_type=F32)


def dot_nt(a, b):
    return lax.dot_general(a, b, (((1,), (1,)), ((), ())), preferred_element_type=F32)


def dot_tn(a, b):
    return lax.dot_general(a, b, (((0,), (0,)), ((), ())), preferred_element_type=F32)


def row_mean(rows):
    return jnp.sum(rows, -1, keepdims=True) * (1.0 / rows.shape[-1])


def normal_parts(residual):
    centred = residual - row_mean(residual)
    inv_scale = lax.rsqrt(row_mean(centred * centred) + norm_eps)
    return centred * inv_scale, inv_scale


def norm_backward(grad_rows, normal_form, inv_scale):
    first = row_mean(grad_rows)
    second = row_mean(grad_rows * normal_form)
    return inv_scale * (grad_rows - first - normal_form * second)


def gelu_parts(hidden):
    share = 0.5 + 0.5 * lax.erf(hidden * inv_root_two)
    bell = jnp.exp2(hidden * hidden * (-0.5 * log2_e))
    return hidden * share, share + hidden * bell * inv_root_tau


def half_mask(which, shape):
    lane = lax.broadcasted_iota(jnp.int32, shape, 1)
    return (lane < LANES // 2) if which == 0 else (lane >= LANES // 2)


class Copies:
    def __init__(self, sems):
        self.sems = sems
        self.used = 0
        self.stores = []

    def take(self, count=1):
        self.used += count
        return self.used - count

    def load(self, source, target):
        copy = pltpu.make_async_copy(source, target, self.sems.at[self.take()])
        copy.start()
        return copy

    def store(self, source, target, when=True):
        if when:
            self.stores.append(self.load(source, target))

    def finish(self):
        for copy in self.stores:
            copy.wait()


KEPT = (
    "xin", "qkv", "weights", "ctx", "form1", "scale1", "low1", "slope", "act", "form2", "scale2", "out",
    "bias", "outer_low", "hidden_low", "residual_low", "sums1", "sums2", "residual", "projected", "offsets", "input_grad",
)
INS = (
    "phase", "segments", "hidden_in", "received", "out_grad", "table", "padding", "buckets",
    "gain1", "shift1", "gain2", "shift2",
    "wqkv", "wout", "wup", "wdown",
)


class Layer:
    def __init__(self, refs):
        self.__dict__.update(refs)
        self.copies = Copies(self.sems)
        self.width = self.hidden_in.shape[1]
        self.inner = self.wup.shape[2]
        self.pairs = self.width // LANES
        self.stages = self.inner // (2 * CHUNK)
        self.pair_sems = self.copies.take(self.pairs)
        self.chunk_sems = [self.copies.take(self.stages) for _ in range(3)]

    def fetch(self, names):
        loads = [self.copies.load(getattr(self, name), getattr(self, f"{name}_v")) for name in names.split()]
        for name in names.split():
            setattr(self, name, getattr(self, f"{name}_v"))
        return loads

    def lanes_of(self, pair, part):
        return pl.ds(pl.multiple_of(part * self.width + pair * LANES, LANES), LANES)

    def stage(self, i):
        return pl.ds(pl.multiple_of(i * 2 * CHUNK, 2 * CHUNK), 2 * CHUNK)

    def build_bias(self):
        for load in self.fetch("table buckets"):
            load.wait()
        span = self.buckets.shape[1]
        bucket_ids = lax.broadcasted_iota(jnp.int32, (self.table.shape[2], span), 0)
        hot = (bucket_ids == self.buckets[...]).astype(F32)
        table = jnp.concatenate([self.table[head] for head in range(self.table.shape[0])], 0)
        values = lax.dot_general(
            table, hot, (((1,), (0,)), ((), ())), precision=highest, preferred_element_type=F32
        )
        self.values_v[:, :span] = values
        self.values_v[:, span:] = jnp.zeros((values.shape[0], SPAN - span), F32)

        def one_head(head, carry):
            wide = jnp.broadcast_to(self.values_v[pl.ds(head, 1), :], (TILE, SPAN))
            self.bias_v[head] = pltpu.roll(wide, 1, 1, stride=1, stride_axis=0)
            return carry

        lax.fori_loop(0, values.shape[0], one_head, 0)
        self.copies.store(self.bias_v, self.bias)


    def rows(self, block):
        return pl.ds(block * BLOCK, BLOCK)

    def forward(self, block, keep, built):
        copies = self.copies
        rows = self.rows(block)
        load_x = copies.load(self.hidden_in.at[rows] if keep else self.received, self.x_v)
        small = self.fetch("segments padding gain1 shift1 gain2 shift2")
        width = self.width
        loads = [
            copies.load(self.wqkv.at[0, :, pl.ds(c, width)], self.wqkv_v.at[:, pl.ds(c, width)])
            for c in range(0, 3 * width, width)
        ]
        if not built:
            self.build_bias()
        load_x.wait()

        def load_bias(pair):
            heads = pl.ds(2 * pair, 2)
            return pltpu.make_async_copy(self.bias.at[heads], self.bias_v.at[heads], self.sems.at[self.pair_sems + pair])

        for i, c in enumerate(range(0, 3 * width, width)):
            loads[i].wait()
            if built and i == 2:
                for pair in range(self.pairs):
                    load_bias(pair).start()
            self.qkv_v[:, c : c + width] = dot_nn(self.x_v[...], self.wqkv_v[:, c : c + width]).astype(BF16)
        copies.store(self.x_v, self.xin.at[rows])
        copies.store(self.qkv_v, self.qkv.at[rows], keep)
        weights_sem = self.sems.at[copies.take()]
        later_loads = [
            pltpu.make_async_copy(source.at[0], target, self.sems.at[copies.take()])
            for source, target in ((self.wout, self.wout_v), (self.wup, self.wup_v), (self.wdown, self.wdown_v))
        ]

        def own(pair, part, which):
            both = self.qkv_v[:, self.lanes_of(pair, part)]
            return jnp.where(half_mask(which, both.shape), both, jnp.zeros_like(both))

        for load in small:
            load.wait()
        at = block * BLOCK
        single = self.segments[:, at + TILE : at + TILE + 1] == self.segments[:, at : at + 1]
        padding = self.padding[:, block * BLOCK : (block + 1) * BLOCK]
        tile_of = lax.broadcasted_iota(jnp.int32, (1, BLOCK), 1) // TILE
        shut = [
            jnp.where((padding == 1) & (single | (tile_of == tile)), 0.0, mask_fill) for tile in range(BLOCK // TILE)
        ]
        row_id = lax.broadcasted_iota(jnp.int32, (TILE, TILE), 0)
        diagonal = row_id == lax.broadcasted_iota(jnp.int32, (TILE, TILE), 1)

        def bias_rows(head, tile):
            at = BLOCK - tile * TILE
            rows = self.bias_v[head, :, at : at + BLOCK]
            masked = rows + shut[tile]
            own = slice(tile * TILE, (tile + 1) * TILE)
            parts = [masked[:, : own.start], jnp.where(diagonal, rows[:, own], masked[:, own]), masked[:, own.stop :]]
            return jnp.concatenate([part for part in parts if part.shape[1]], 1)

        def weigh(pair, which):
            head = 2 * pair + which
            k_own = own(pair, 1, which)
            for r in range(0, BLOCK, 2 * TILE):
                q_rows = self.qkv_v[r : r + 2 * TILE, self.lanes_of(pair, 0)] * jnp.asarray(score_scale, BF16)
                tiles = [bias_rows(head, tile) for tile in range(r // TILE, r // TILE + 2)]
                logits = dot_nt(q_rows, k_own) + jnp.concatenate(tiles, 0)
                raised = jnp.exp(logits - jnp.max(logits, -1, keepdims=True))
                share = pl.reciprocal(jnp.sum(raised, -1, keepdims=True), approx=True)
                self.weights_v[head, r : r + 2 * TILE, :] = (raised * share).astype(BF16)

        def head_pair(pair, carry):
            if built:
                load_bias(pair).wait()

            @pl.when(pair == 0)
            def _():
                for load in later_loads:
                    load.start()

            weigh(pair, 0)
            context = dot_nn(self.weights_v[2 * pair], own(pair, 2, 0))
            weigh(pair, 1)
            context += dot_nn(self.weights_v[2 * pair + 1], own(pair, 2, 1))
            self.ctx_v[:, self.lanes_of(pair, 0)] = context.astype(BF16)
            if keep:
                heads = pl.ds(2 * pair, 2)
                pltpu.make_async_copy(self.weights_v.at[heads], self.weights.at[block, heads], weights_sem).start()
            return carry

        lax.fori_loop(0, self.pairs, head_pair, 0)
        if keep:
            copies.stores.append(pltpu.make_async_copy(self.weights_v, self.weights.at[block], weights_sem))
        copies.store(self.ctx_v, self.ctx.at[rows])
        load_out, load_up, load_down = later_loads
        load_out.wait()
        self.acc_v[...] = dot_nn(self.ctx_v[...], self.wout_v[...])
        for r in range(0, BLOCK, 64):
            tile = slice(r, r + 64)
            form, scale = normal_parts(self.acc_v[tile, :] + self.x_v[tile, :].astype(F32))
            normed = form * self.gain1[...] + self.shift1[...]
            self.form1_v[tile, :] = form
            self.scale1_v[tile, :] = scale
            self.acc_v[tile, :] = normed
            self.low1_v[tile, :] = normed.astype(BF16)
        copies.store(self.form1_v, self.form1.at[rows], keep)
        copies.store(self.scale1_v, self.scale1.at[rows], keep)
        copies.store(self.low1_v, self.low1.at[rows])
        load_up.wait()
        load_down.wait()
        act_sem = self.sems.at[copies.take()]
        slope_sem = self.sems.at[copies.take()]

        def two_chunks(i, carry):
            span = self.stage(i)
            active, grade = gelu_parts(dot_nn(self.low1_v[...], self.wup_v[:, span]))
            active = active.astype(BF16)
            self.act_v[:, span] = active
            self.slope_v[:, span] = grade.astype(BF16)
            self.acc_v[...] += dot_nn(active, self.wdown_v[span, :])
            pltpu.make_async_copy(self.act_v.at[:, span], self.act.at[rows, span], act_sem).start()
            if keep:
                pltpu.make_async_copy(self.slope_v.at[:, span], self.slope.at[rows, span], slope_sem).start()
            return carry

        lax.fori_loop(0, self.stages, two_chunks, 0)
        copies.stores.append(pltpu.make_async_copy(self.act_v, self.act.at[rows], act_sem))
        if keep:
            copies.stores.append(pltpu.make_async_copy(self.slope_v, self.slope.at[rows], slope_sem))
        for r in range(0, BLOCK, 64):
            tile = slice(r, r + 64)
            form, scale = normal_parts(self.acc_v[tile, :])
            self.form2_v[tile, :] = form
            self.scale2_v[tile, :] = scale
            self.out_v[tile, :] = (form * self.gain2[...] + self.shift2[...]).astype(BF16)
        copies.store(self.out_v, self.send, keep)
        copies.store(self.out_v, self.out.at[rows])
        copies.store(self.form2_v, self.form2.at[rows], keep)
        copies.store(self.scale2_v, self.scale2.at[rows], keep)


    def chunk_loads(self, i, rows):
        span = self.stage(i)
        return [
            pltpu.make_async_copy(source, target, self.sems.at[self.chunk_sems[k] + i])
            for k, (source, target) in enumerate(
                (
                    (self.wdown.at[0, span], self.wdown_v.at[span]),
                    (self.slope.at[rows, span], self.slope_v.at[:, span]),
                    (self.wup.at[0, :, span], self.wup_v.at[:, span]),
                )
            )
        ]

    def norm_sums(self, source, form_ref, sums_ref):
        gain_sum = jnp.zeros((1, self.width), F32)
        shift_sum = jnp.zeros((1, self.width), F32)
        for r in range(0, BLOCK, 64):
            grad_rows, form = source[r : r + 64, :].astype(F32), form_ref[r : r + 64, :]
            gain_sum += jnp.sum(grad_rows * form, 0, keepdims=True)
            shift_sum += jnp.sum(grad_rows, 0, keepdims=True)
        sums_ref[...] = jnp.zeros(sums_ref.shape, F32)
        sums_ref[0:1, :] = gain_sum
        sums_ref[1:2, :] = shift_sum

    def norm_back(self, block):
        for r in range(0, BLOCK, 64):
            tile = slice(r, r + 64)
            grad_rows = self.g_v[tile, :].astype(F32) * self.gain2[...]
            grad_outer = norm_backward(grad_rows, self.form2_v[tile, :], self.scale2_v[tile, :])
            self.acc_v[tile, :] = grad_outer
            self.outer_v[tile, :] = grad_outer.astype(BF16)
        self.copies.store(self.outer_v, self.outer_low.at[self.rows(block)])

    def norm_sums_2(self, block):
        self.norm_sums(self.g_v, self.form2_v, self.sums2_v)
        self.copies.store(self.sums2_v, self.sums2.at[block])

    def ffn_back(self, block, staged=False, middle_loads=()):
        copies = self.copies
        rows = self.rows(block)
        hidden_sem = self.sems.at[copies.take()]

        def two_chunks(i, carry):
            span = self.stage(i)
            if staged:
                load_down, load_slope, load_up = self.chunk_loads(i, rows)
                load_down.wait()
                load_slope.wait()
            grad_active = dot_nt(self.outer_v[...], self.wdown_v[span, :])
            hidden = (grad_active * self.slope_v[:, span].astype(F32)).astype(BF16)
            self.slope_v[:, span] = hidden
            if staged:
                load_up.wait()

                @pl.when(i + 2 < self.stages)
                def _():
                    for load in self.chunk_loads(i + 2, rows):
                        load.start()

            self.acc_v[...] += dot_nt(hidden, self.wup_v[:, span])
            pltpu.make_async_copy(self.slope_v.at[:, span], self.hidden_low.at[rows, span], hidden_sem).start()
            return carry

        lax.fori_loop(0, self.stages, two_chunks, 0)
        copies.stores.append(pltpu.make_async_copy(self.slope_v, self.hidden_low.at[rows], hidden_sem))
        for load in middle_loads:
            load.wait()
        self.norm_sums(self.acc_v, self.form1_v, self.sums1_v)
        for r in range(0, BLOCK, 64):
            tile = slice(r, r + 64)
            grad_residual = norm_backward(
                self.acc_v[tile, :] * self.gain1[...], self.form1_v[tile, :], self.scale1_v[tile, :]
            )
            self.acc_v[tile, :] = grad_residual
            self.residual_low_v[tile, :] = grad_residual.astype(BF16)
        copies.store(self.residual_low_v, self.residual_low.at[rows])
        copies.store(self.sums1_v, self.sums1.at[block])

    def attn_back(self, block, next_loads=None, load_in=()):
        copies = self.copies
        rows = self.rows(block)
        self.dctx_v[...] = dot_nt(self.residual_low_v[...], self.wout_v[...]).astype(BF16)
        self.fold_v[:, :, 0:TILE] = jnp.zeros((2, TILE, TILE), F32)

        def head_pair(pair, carry):
            def lanes_of(part):
                return self.lanes_of(pair, part)

            if next_loads is not None:
                next_loads(pair)
            q_pair, k_pair, v_pair = (self.qkv_v[:, lanes_of(part)] for part in range(3))
            grad_pair = self.dctx_v[:, lanes_of(0)]
            crossed = grad_pair.astype(F32) * self.ctx_v[:, lanes_of(0)].astype(F32)
            masks = [half_mask(which, k_pair.shape) for which in range(2)]

            def own(both, which):
                return jnp.where(masks[which], both, jnp.zeros_like(both))

            for which in range(2):
                self.square_v[which] = dot_nt(grad_pair, own(v_pair, which))
            q_grad = k_grad = v_grad = 0.0
            for which in range(2):
                head = 2 * pair + which
                delta = jnp.sum(own(crossed, which), -1, keepdims=True)
                for r in range(0, BLOCK, 64):
                    tile = slice(r, r + 64)
                    score_grad = (
                        self.weights_v[head, tile, :].astype(F32) * (self.square_v[which, tile, :] - delta[tile, :])
                    ).astype(BF16)
                    self.half_v[which, tile, :] = score_grad
                    at = BLOCK - r // TILE * TILE
                    wide = score_grad.astype(F32)
                    half = slice(r % TILE, r % TILE + 64)
                    if r < TILE:
                        self.fold_v[which, half, at : at + BLOCK] = wide
                    else:
                        self.fold_v[which, half, at : at + TILE] = wide[:, :TILE]
                        self.fold_v[which, half, at + TILE : at + BLOCK] += wide[:, TILE:]
                v_grad += dot_tn(self.weights_v[head], own(grad_pair, which))
                q_grad += dot_nn(self.half_v[which], own(k_pair, which))
                k_grad += dot_tn(self.half_v[which], own(q_pair, which))
                folded = self.fold_v[which]
                size = TILE // 2
                while size >= 8:
                    folded = folded[:size, :] + pltpu.roll(folded[size:, :], SPAN - size, 1)
                    size //= 2
                self.eighth_v[head] = folded
            self.qkv_v[:, lanes_of(0)] = (q_grad * score_scale).astype(BF16)
            self.qkv_v[:, lanes_of(1)] = (k_grad * score_scale).astype(BF16)
            self.qkv_v[:, lanes_of(2)] = v_grad.astype(BF16)
            return carry

        lax.fori_loop(0, self.pairs, head_pair, 0)
        copies.store(self.eighth_v, self.offsets.at[block])
        copies.store(self.qkv_v, self.projected.at[rows])
        for load in load_in:
            load.wait()
        self.grad_v[...] = (self.acc_v[...] + dot_nt(self.qkv_v[...], self.wqkv_v[...])).astype(BF16)
        copies.store(self.grad_v, self.send)
        copies.store(self.grad_v, self.input_grad.at[rows])


    def do_forward(self, block):
        self.forward(block, True, block > 0)

    def do_bias(self, block):
        self.build_bias()

    def do_both(self, block):
        load = self.copies.load(self.out_grad.at[self.rows(block)], self.g_v)
        self.forward(block, False, True)
        load.wait()
        self.norm_back(block)
        self.ffn_back(block)
        self.norm_sums_2(block)
        self.attn_back(block)

    def do_back(self, block):
        rows = self.rows(block)
        loads = [
            self.copies.load(source, target)
            for source, target in (
                (self.received, self.g_v),
                (self.form2.at[rows], self.form2_v),
                (self.scale2.at[rows], self.scale2_v),
                (self.slope.at[rows], self.slope_v),
                (self.wdown.at[0], self.wdown_v),
                (self.wup.at[0], self.wup_v),
                (self.form1.at[rows], self.form1_v),
                (self.scale1.at[rows], self.scale1_v),
                (self.qkv.at[rows], self.qkv_v),
                (self.weights.at[block], self.weights_v),
                (self.ctx.at[rows], self.ctx_v),
                (self.wout.at[0], self.wout_v),
                (self.wqkv.at[0], self.wqkv_v),
            )
        ]
        for load in loads + self.fetch("gain1 gain2"):
            load.wait()
        self.norm_back(block)
        self.ffn_back(block)
        self.norm_sums_2(block)
        self.attn_back(block)

    def do_ffn_back(self, block):
        rows = self.rows(block)
        loads = [
            self.copies.load(source, target)
            for source, target in (
                (self.received, self.g_v),
                (self.form2.at[rows], self.form2_v),
                (self.scale2.at[rows], self.scale2_v),
            )
        ]
        loads += self.fetch("gain1 gain2")
        self.chunk_loads(0, rows)[0].start()
        for load in loads:
            load.wait()
        for load in self.chunk_loads(0, rows)[1:] + self.chunk_loads(1, rows):
            load.start()
        middle = [
            self.copies.load(self.form1.at[rows], self.form1_v),
            self.copies.load(self.scale1.at[rows], self.scale1_v),
        ]
        self.norm_back(block)
        self.norm_sums_2(block)
        self.ffn_back(block, True, middle)
        self.copies.store(self.acc_v, self.residual)

    def do_attn_back(self, block):
        rows = self.rows(block)
        loads = [
            self.copies.load(source, target)
            for source, target in ((self.residual_low.at[rows], self.residual_low_v), (self.wout.at[0], self.wout_v))
        ]
        first = self.copies.take(5 * self.pairs)

        def pair_loads(pair):
            heads = pl.ds(2 * pair, 2)
            sources = [(self.weights.at[block, heads], self.weights_v.at[heads])]
            for source, target, parts in ((self.qkv, self.qkv_v, 3), (self.ctx, self.ctx_v, 1)):
                for part in range(parts):
                    lanes = self.lanes_of(pair, part)
                    sources.append((source.at[rows, lanes], target.at[:, lanes]))
            return [
                pltpu.make_async_copy(source, target, self.sems.at[first + 5 * pair + k])
                for k, (source, target) in enumerate(sources)
            ]

        for pair in range(2):
            for load in pair_loads(pair):
                load.start()
        for load in loads:
            load.wait()
        last = [
            pltpu.make_async_copy(source, target, self.sems.at[self.copies.take()])
            for source, target in ((self.wqkv.at[0], self.wqkv_v), (self.residual, self.acc_v))
        ]

        def next_loads(pair):
            for load in pair_loads(pair):
                load.wait()

            @pl.when(pair + 2 < self.pairs)
            def _():
                for load in pair_loads(pair + 2):
                    load.start()

            @pl.when(pair == self.pairs - 3)
            def _():
                for load in last:
                    load.start()

        self.attn_back(block, next_loads, last)


def layer_kernel(work, phase_on, block, ins, outs, scratch, after_count, kept_count, *refs):
    refs_in, refs = refs[: len(ins)], refs[len(ins) + after_count + kept_count :]
    named = dict(zip(ins, refs_in)) | dict(zip(outs, refs)) | dict(zip(scratch, refs[len(outs) :]))

    @pl.when(named["phase"][0] == phase_on)
    def _():
        layer = Layer(named)
        getattr(layer, f"do_{work}")(block)
        layer.copies.finish()


def layer_step(work, phase_on, block, values, afters, kept, kept_shapes, scratch):
    specs = [SMEM] + [ANY] * (len(values) - 1)
    names = list(scratch)
    kept = list(kept) if kept is not None else []
    sent = jax.ShapeDtypeStruct((BLOCK, values[2].shape[1]), BF16)
    if work == "bias":
        names = ["values_v", "bias_v", "table_v", "buckets_v"]
    count = len(values) + len(afters)
    results = pl.pallas_call(
        functools.partial(
            layer_kernel, work, phase_on, block, INS, KEPT + ("send",), names + ["sems"], len(afters), len(kept)
        ),
        out_shape=list(kept_shapes) + [sent],
        in_specs=specs + [ANY] * (len(afters) + len(kept)),
        out_specs=[ANY] * (len(kept_shapes) + 1),
        scratch_shapes=[pltpu.VMEM(*scratch[name]) for name in names] + [pltpu.SemaphoreType.DMA((96,))],
        input_output_aliases={count + i: i for i in range(len(kept))},
        compiler_params=pltpu.CompilerParams(vmem_limit_bytes=VMEM_BYTES),
        name=f"{work}_{phase_on}_{block}",
    )(*values, *afters, *kept)
    return dict(zip(KEPT, results)), results[-1]


def pack_kernel(ways, buckets_ref, offsets_ref, sums1_ref, sums2_ref, *refs):
    out_ref, turn_v = refs[-2:]
    row_of = lax.broadcasted_iota(jnp.int32, (8, SPAN), 0)
    lines = []
    for head in range(offsets_ref.shape[1]):
        eighth = offsets_ref[0, head] + offsets_ref[1, head]
        for size in (4, 2, 1):
            eighth = jnp.where((row_of & size) != 0, pltpu.roll(eighth, SPAN - size, 1), eighth)
        lines.append(jnp.sum(eighth, 0, keepdims=True))
    lines += [jnp.zeros((1, SPAN), F32)] * (NORM_LANE - len(lines))
    sums = pltpu.roll(jnp.concatenate(lines, 0), SPAN - 1, 1)
    span = buckets_ref.shape[1]
    buckets, depth = out_ref.shape[0] // 3, out_ref.shape[0] // ways
    share = buckets // ways
    bucket_ids = lax.broadcasted_iota(jnp.int32, (buckets, span), 0)
    hot = (bucket_ids == buckets_ref[...]).astype(F32)
    table = lax.dot_general(
        hot, sums[:, :span], (((1,), (1,)), ((), ())), precision=highest, preferred_element_type=F32
    ).astype(BF16)
    turn_v[...] = jnp.zeros(turn_v.shape, F32)
    for i, ref in enumerate((sums1_ref, sums2_ref)):
        at = NORM_LANE + 2 * i
        turn_v[at : at + 2, :] = ref[0, 0:2, :] + ref[1, 0:2, :]
    out_ref[...] = turn_v[...].T.astype(BF16)
    for i in range(ways):
        out_ref[i * depth : i * depth + share, 0:NORM_LANE] = table[i * share : (i + 1) * share, :]


def packed(ways, buckets, offset_buckets, kept, afters):
    width = kept["sums1"].shape[2]
    depth, share = width // ways, buckets // ways
    arrays = (offset_buckets, kept["offsets"], kept["sums1"], kept["sums2"])
    if depth % 16 == 0 and share % 16 == 0 and 3 * buckets == width:
        rows = pl.pallas_call(
            functools.partial(pack_kernel, ways),
            out_shape=jax.ShapeDtypeStruct((width, LANES), BF16),
            in_specs=[VMEM] * len(arrays) + [ANY] * len(afters),
            out_specs=VMEM,
            scratch_shapes=[pltpu.VMEM((LANES, width), F32)],
            compiler_params=pltpu.CompilerParams(vmem_limit_bytes=SMALL_VMEM_BYTES),
            name="pack",
        )(*arrays, *afters)
        return rows.reshape(ways, depth, LANES)
    eighths = jnp.sum(kept["offsets"], 0)
    lines = sum(jnp.roll(eighths[:, i, :], -i, 1) for i in range(8))[:, 1:]
    hot = (offset_buckets[0][None, :] == jnp.arange(buckets, dtype=jnp.int32)[:, None]).astype(F32)
    table = jnp.dot(hot, lines.T, precision=highest).reshape(ways, share, -1)
    table = jnp.pad(table, ((0, 0), (0, depth - share), (0, NORM_LANE - table.shape[2])))
    norms = jnp.concatenate([jnp.sum(kept[name], 0)[:2] for name in ("sums1", "sums2")], 0)
    norms = norms.T.reshape(ways, depth, 4)
    rows = jnp.concatenate([table, norms], 2)
    return jnp.pad(rows, ((0, 0), (0, 0), (0, LANES - rows.shape[2]))).astype(BF16)


def halve_kernel(bits, counts, after_count, through_count, me_ref, *refs):
    outs = refs[2 * sum(counts) + after_count + through_count :]
    for i, count in enumerate(counts):
        pieces, refs = [refs[2 * k : 2 * k + 2] for k in range(count)], refs[2 * count :]
        send_ref, rest_ref = outs[2 * i : 2 * i + 2]
        mine = (me_ref[0] >> bits[i]) & 1

        def total(which):
            parts = [
                (kept[0, which, 0, 0] if len(kept.shape) == 6 else kept[0, which, 0]).astype(F32)
                + arrived[0, which, 0].astype(F32)
                for kept, arrived in pieces
            ]
            return jnp.concatenate(parts, 1)

        send_ref[0, 0] = total(1 - mine).astype(send_ref.dtype)
        rest_ref[0, 0] = total(mine)


def join_kernel(kept_ref, arrived_ref, out_ref, qkv_ref, table_ref, *refs):
    norm_refs, turn_v = refs[:-1], refs[-1]
    total = kept_ref[...] + arrived_ref[...].astype(F32)
    wide = out_ref.shape[1]
    out_ref[...] = total[:, :wide]
    qkv_ref[...] = total[:, wide : 4 * wide]
    small = total[:, 4 * wide :]
    turn_v[...] = jnp.zeros(turn_v.shape, F32)
    turn_v[: small.shape[0], :] = small
    turned = turn_v[...].T
    for head in range(table_ref.shape[0]):
        table_ref[head] = turned[head : head + 1, : table_ref.shape[2]]
    for i, ref in enumerate(norm_refs):
        ref[...] = turned[NORM_LANE + i : NORM_LANE + i + 1, : ref.shape[1]]


class Part:
    def __init__(self, whole):
        self.whole = whole
        self.sent = self.of_core(1 - (lax.axis_index("dp") & 1))
        self.arrived = swapped(self.sent, 0)

    def of_core(self, core):
        split = self.whole.reshape((self.whole.shape[0] // 2, 2) + self.whole.shape[1:])
        return lax.dynamic_index_in_dim(split, core, 1, keepdims=False)


def swapped(array, bit):
    count = lax.axis_size("dp")
    return lax.ppermute(array, "dp", [(i, i ^ (1 << bit)) for i in range(count)])


class Share:
    def __init__(self, parts, order):
        self.parts = parts
        self.order = order[1:]
        self.left = sorted(order[1:])
        self.depth = parts[0].whole.shape[1]
        self.wide = sum(part.whole.shape[2] for part in parts)
        self.mine = None

    def swap(self, bit, theirs):
        self.left.remove(bit)
        self.sent = theirs
        self.arrived = swapped(theirs, bit)

    def total(self):
        if self.mine is not None:
            return self.mine + self.arrived.astype(F32)
        here = lax.axis_index("dp") & 1
        return jnp.concatenate(
            [part.of_core(here).astype(F32) + part.arrived.astype(F32) for part in self.parts], 2
        )

    def split_at(self):
        bit = self.order[0]
        axis = len(self.left) - 1 - self.left.index(bit)
        return bit, 2**axis, 2 ** (len(self.left) - 1 - axis)

    def halve(self):
        bit, above, below = self.split_at()
        self.order = self.order[1:]
        split = self.total().reshape(above, 2, below, self.depth, self.wide)
        here = (lax.axis_index("dp") >> bit) & 1
        theirs = lax.dynamic_index_in_dim(split, 1 - here, 1, keepdims=False).astype(BF16)
        mine = lax.dynamic_index_in_dim(split, here, 1, keepdims=False)
        self.mine = mine.reshape(-1, self.depth, self.wide)
        self.swap(bit, theirs.reshape(-1, self.depth, self.wide))


def halve_all(me, shares, afters=(), through=()):
    if any(share.depth % 16 for share in shares):
        for share in shares:
            share.halve()
        return through
    ins, in_specs, outs, out_specs, bits, counts = [], [], [], [], [], []
    for share in shares:
        bit, above, below = share.split_at()
        bits.append(bit)

        def halves(wide, b=below):
            return pl.BlockSpec((1, 2, 1, share.depth, wide), lambda i, me: (i // b, 0, i % b, 0, 0))

        if share.mine is None:
            counts.append(len(share.parts))
            for part in share.parts:
                wide = part.whole.shape[2]
                ins.append(part.whole.reshape(above, 2, below, 2, share.depth, wide))
                in_specs.append(
                    pl.BlockSpec(
                        (1, 2, 1, 1, share.depth, wide),
                        lambda i, me, b=below: (i // b, 0, i % b, me[0] & 1, 0, 0),
                    )
                )
                ins.append(part.arrived.reshape(above, 2, below, share.depth, wide))
                in_specs.append(halves(wide))
        else:
            counts.append(1)
            for array in (share.mine, share.arrived):
                ins.append(array.reshape(above, 2, below, share.depth, share.wide))
                in_specs.append(halves(share.wide))
        outs += [
            jax.ShapeDtypeStruct((above, below, share.depth, share.wide), kind) for kind in (BF16, F32)
        ]
        out_specs += [
            pl.BlockSpec((1, 1, share.depth, share.wide), lambda i, me, b=below: (i // b, i % b, 0, 0))
        ] * 2
        steps = above * below
    results = pl.pallas_call(
        functools.partial(halve_kernel, tuple(bits), tuple(counts), len(afters), len(through)),
        grid_spec=pltpu.PrefetchScalarGridSpec(
            num_scalar_prefetch=1,
            grid=(steps,),
            in_specs=in_specs + [ANY] * (len(afters) + len(through)),
            out_specs=out_specs + [ANY] * len(through),
        ),
        out_shape=outs + [jax.ShapeDtypeStruct(array.shape, array.dtype) for array in through],
        input_output_aliases={
            1 + len(ins) + len(afters) + i: len(outs) + i for i in range(len(through))
        },
        compiler_params=pltpu.CompilerParams(vmem_limit_bytes=SMALL_VMEM_BYTES),
        name="halve",
    )(me, *ins, *afters, *through)
    for i, share in enumerate(shares):
        share.order = share.order[1:]
        share.mine = results[2 * i + 1].reshape(-1, share.depth, share.wide)
        share.swap(bits[i], results[2 * i].reshape(-1, share.depth, share.wide))
    return results[len(outs) :]


def joined(share, width, table_shape):
    shapes = [(share.depth, width), (share.depth, 3 * width), table_shape] + [(1, share.depth)] * 4
    return pl.pallas_call(
        join_kernel,
        out_shape=[jax.ShapeDtypeStruct(dims, F32) for dims in shapes],
        in_specs=[VMEM] * 2,
        out_specs=[VMEM] * len(shapes),
        scratch_shapes=[pltpu.VMEM((LANES, LANES), F32)],
        compiler_params=pltpu.CompilerParams(vmem_limit_bytes=SMALL_VMEM_BYTES),
        name="join",
    )(share.mine[0], share.arrived[0])


def passed_along(x, axis, by):
    length = lax.axis_size(axis)
    pairs = [(i, i + by) for i in range(length) if 0 <= i + by < length]
    return lax.ppermute(x, axis, pairs)


def shards(
    hidden_in, out_grad, qkv_weight, out_weight, rel_table, norm1_gain, norm1_bias,
    up_weight, down_weight, norm2_gain, norm2_bias, seg_ids, pad_mask, rel_buckets,
):
    phase = lax.axis_index("phase").astype(jnp.int32).reshape(1)
    ways = lax.axis_size("dp")
    slots, width = hidden_in.shape
    inner = up_weight.shape[2]
    buckets, heads = rel_table.shape[1:]

    def shape(dims, kind):
        return jax.ShapeDtypeStruct(dims, kind)

    rows_of = {
        "xin": (width, BF16), "qkv": (3 * width, BF16), "ctx": (width, BF16), "form1": (width, F32),
        "scale1": (1, F32), "low1": (width, BF16), "slope": (inner, BF16), "act": (inner, BF16),
        "form2": (width, F32), "scale2": (1, F32), "out": (width, BF16),
        "outer_low": (width, BF16), "hidden_low": (inner, BF16), "residual_low": (width, BF16),
        "projected": (3 * width, BF16), "input_grad": (width, BF16),
    }
    kept_shapes = [
        shape((slots, rows_of[name][0]), rows_of[name][1])
        if name in rows_of
        else {
            "weights": shape((MICRO, heads, BLOCK, BLOCK), BF16),
            "sums1": shape((MICRO, 8, width), F32),
            "sums2": shape((MICRO, 8, width), F32),
            "residual": shape((BLOCK, width), F32),
            "offsets": shape((MICRO, heads, 8, SPAN), F32),
            "bias": shape((heads, TILE, SPAN), F32),
        }[name]
        for name in KEPT
    ]
    small = {
        "segments_v": ((1, slots), jnp.int32), "padding_v": ((1, slots), jnp.int32),
        "buckets_v": ((1, rel_buckets.shape[0]), jnp.int32), "table_v": ((heads, 1, buckets), F32),
        "gain1_v": ((1, width), F32), "shift1_v": ((1, width), F32), "gain2_v": ((1, width), F32),
        "shift2_v": ((1, width), F32),
    }
    in_forward = ("qkv", "ctx", "form1", "scale1", "low1", "slope", "act", "form2", "scale2", "out")
    scratch = {f"{name}_v": ((BLOCK, rows_of[name][0]), rows_of[name][1]) for name in in_forward}
    scratch |= small
    scratch |= {
        name: ((BLOCK, width), BF16) for name in ("x_v", "g_v", "outer_v", "residual_low_v", "dctx_v", "grad_v")
    }
    scratch |= {
        "weights_v": ((heads, BLOCK, BLOCK), BF16), "acc_v": ((BLOCK, width), F32), "square_v": ((2, BLOCK, BLOCK), F32),
        "values_v": ((heads, SPAN), F32), "bias_v": ((heads, TILE, SPAN), F32), "sums1_v": ((8, width), F32), "sums2_v": ((8, width), F32),
        "wqkv_v": ((width, 3 * width), BF16), "wout_v": ((width, width), BF16), "wup_v": ((width, inner), BF16),
        "wdown_v": ((inner, width), BF16), "fold_v": ((2, TILE, SPAN), F32), "eighth_v": ((heads, 8, SPAN), F32),
        "half_v": ((2, BLOCK, BLOCK), BF16),
    }

    def step(work, phase_on, block, received, kept, afters=()):
        values = (
            phase, seg_ids[None, :], hidden_in, received, out_grad, rel_table.transpose(2, 0, 1), pad_mask[None, :], rel_buckets[None, :],
            norm1_gain, norm1_bias, norm2_gain, norm2_bias, qkv_weight, out_weight, up_weight, down_weight,
        )
        in_place = None if kept is None else [kept[name] for name in KEPT]
        return layer_step(work, phase_on, block, values, list(afters), in_place, kept_shapes, scratch)

    kept, sent = step("forward", 0, 0, hidden_in, None)
    first = passed_along(sent, "phase", 1)
    kept, _ = step("bias", 1, 0, hidden_in, kept)
    kept, sent = step("forward", 0, 1, hidden_in, kept)
    second = passed_along(sent, "phase", 1)
    kept, sent = step("both", 1, 0, first, kept)
    first_back = passed_along(sent, "phase", -1)
    kept, sent = step("both", 1, 1, second, kept)
    second_back = passed_along(sent, "phase", -1)
    kept, _ = step("back", 0, 0, first_back, kept)
    kept, _ = step("ffn_back", 0, 1, second_back, kept)

    bits = ways.bit_length() - 1
    near_first = list(range(bits))
    far_first = [0] + list(range(2, bits)) + [1] if bits > 1 else near_first
    me = lax.axis_index("dp").astype(jnp.int32).reshape(1)

    def weight_grad(left, right):
        product = dot_tn(left, right).astype(BF16)
        return product.reshape(ways, product.shape[0] // ways, product.shape[1])

    down = Share([Part(weight_grad(kept["act"], kept["outer_low"]))], near_first)
    up = Share([Part(weight_grad(kept["low1"], kept["hidden_low"]))], far_first)
    out_part = Part(weight_grad(kept["ctx"], kept["residual_low"]))
    halve_all(me, [down])
    halve_all(me, [up])
    kept, _ = step("attn_back", 0, 1, hidden_in, kept, [down.sent, up.sent])
    far_part = Part(weight_grad(kept["xin"], kept["projected"][:, width:]))
    (slots_in,) = halve_all(me, [down, up], [far_part.sent], [kept["xin"]])
    near_part = Part(weight_grad(slots_in, kept["projected"][:, :width]))
    small_part = Part(packed(ways, buckets, rel_buckets[None, :], kept, [near_part.sent]))
    last = Share([out_part, near_part, far_part, small_part], near_first)
    halve_all(me, [last], [down.sent, up.sent])
    halve_all(me, [down, up])
    halve_all(me, [last], [down.sent, up.sent])
    while down.order:
        halve_all(me, [down, up])
    while last.order:
        halve_all(me, [last])
    down_share = down.total()[0]
    up_share = up.total()[0]
    out_share, qkv_share, table_share, *norm_shares = joined(last, width, (heads, 1, buckets // ways))
    return (
        kept["out"][None],
        kept["input_grad"][None],
        qkv_share[None],
        out_share[None],
        table_share.transpose(1, 2, 0),
        norm_shares[0],
        norm_shares[1],
        up_share[None],
        down_share[None],
        norm_shares[2],
        norm_shares[3],
    )


def solution(mesh):
    return jax.shard_map(
        shards,
        mesh=mesh,
        in_specs=(
            P("dp", None),
            P("dp", None),
            P("phase", None, None),
            P("phase", None, None),
            P("phase", None, None),
            P("phase", None),
            P("phase", None),
            P("phase", None, None),
            P("phase", None, None),
            P("phase", None),
            P("phase", None),
            P("dp"),
            P("dp"),
            P(),
        ),
        out_specs=(
            P("phase", "dp", None),
            P("phase", "dp", None),
            P("phase", "dp", None),
            P("phase", "dp", None),
            P("phase", "dp", None),
            P("phase", "dp"),
            P("phase", "dp"),
            P("phase", "dp", None),
            P("phase", "dp", None),
            P("phase", "dp"),
            P("phase", "dp"),
        ),
        check_vma=False,
    )
```

```python
import functools

import jax
import jax.numpy as jnp
from jax import lax
from jax.experimental import pallas as pl
from jax.experimental.pallas import tpu as pltpu
from jax.sharding import PartitionSpec as P

BLOCK = 512
MICRO = 2
TILE = 128
LANES = 128
CHUNK = 768
SPAN = 2 * BLOCK
VMEM_BYTES = 58 * 1024 * 1024
SMALL_VMEM_BYTES = 20 * 1024 * 1024
NORM_LANE = 16

norm_eps = 1e-05
mask_fill = -1000000000.0
score_scale = 0.125
inv_root_two = 0.7071067811865476
inv_root_tau = 0.3989422804014327
log2_e = 1.4426950408889634
highest = lax.Precision.HIGHEST

F32 = jnp.float32
BF16 = jnp.bfloat16
ANY = pl.BlockSpec(memory_space=pl.ANY)
VMEM = pl.BlockSpec(memory_space=pltpu.VMEM)
QUICK = pl.CostEstimate(flops=1, bytes_accessed=1, transcendentals=0)
SMEM = pl.BlockSpec(memory_space=pltpu.SMEM)


def dot_nn(a, b):
    return lax.dot_general(a, b, (((1,), (0,)), ((), ())), preferred_element_type=F32)


def dot_nt(a, b):
    return lax.dot_general(a, b, (((1,), (1,)), ((), ())), preferred_element_type=F32)


def dot_tn(a, b):
    return lax.dot_general(a, b, (((0,), (0,)), ((), ())), preferred_element_type=F32)


def row_mean(rows):
    return jnp.sum(rows, -1, keepdims=True) * (1.0 / rows.shape[-1])


def normal_parts(residual):
    centred = residual - row_mean(residual)
    inv_scale = lax.rsqrt(row_mean(centred * centred) + norm_eps)
    return centred * inv_scale, inv_scale


def norm_backward(grad_rows, normal_form, inv_scale):
    first = row_mean(grad_rows)
    second = row_mean(grad_rows * normal_form)
    return inv_scale * (grad_rows - first - normal_form * second)


def gelu_parts(hidden):
    share = 0.5 + 0.5 * lax.erf(hidden * inv_root_two)
    bell = jnp.exp2(hidden * hidden * (-0.5 * log2_e))
    return hidden * share, share + hidden * bell * inv_root_tau


def half_mask(which, shape):
    lane = lax.broadcasted_iota(jnp.int32, shape, 1)
    return (lane < LANES // 2) if which == 0 else (lane >= LANES // 2)


class Copies:
    def __init__(self, sems):
        self.sems = sems
        self.used = 0
        self.stores = []

    def take(self, count=1):
        self.used += count
        return self.used - count

    def load(self, source, target):
        copy = pltpu.make_async_copy(source, target, self.sems.at[self.take()])
        copy.start()
        return copy

    def store(self, source, target, when=True):
        if when:
            self.stores.append(self.load(source, target))

    def finish(self):
        for copy in self.stores:
            copy.wait()


KEPT = (
    "xin", "qkv", "weights", "ctx", "form1", "scale1", "low1", "slope", "act", "form2", "scale2", "out",
    "bias", "outer_low", "hidden_low", "residual_low", "sums1", "sums2", "residual", "projected", "offsets", "input_grad",
)
INS = (
    "phase", "segments", "hidden_in", "received", "out_grad", "table", "padding", "buckets",
    "gain1", "shift1", "gain2", "shift2",
    "wqkv", "wout", "wup", "wdown",
)


class Layer:
    def __init__(self, refs):
        self.__dict__.update(refs)
        self.copies = Copies(self.sems)
        self.width = self.hidden_in.shape[1]
        self.inner = self.wup.shape[2]
        self.pairs = self.width // LANES
        self.stages = self.inner // (2 * CHUNK)
        self.pair_sems = self.copies.take(self.pairs)
        self.chunk_sems = [self.copies.take(self.stages) for _ in range(3)]

    def fetch(self, *names):
        loads = [self.copies.load(getattr(self, name), getattr(self, f"{name}_v")) for name in names]
        for name in names:
            setattr(self, name, getattr(self, f"{name}_v"))
        return loads

    def lanes_of(self, pair, part):
        return pl.ds(pl.multiple_of(part * self.width + pair * LANES, LANES), LANES)

    def stage(self, i):
        return pl.ds(pl.multiple_of(i * 2 * CHUNK, 2 * CHUNK), 2 * CHUNK)

    def build_bias(self, table_loads):
        for load in table_loads:
            load.wait()
        span = self.buckets.shape[1]
        bucket_ids = lax.broadcasted_iota(jnp.int32, (self.table.shape[2], span), 0)
        hot = (bucket_ids == self.buckets[...]).astype(F32)
        table = jnp.concatenate([self.table[head] for head in range(self.table.shape[0])], 0)
        values = lax.dot_general(
            table, hot, (((1,), (0,)), ((), ())), precision=highest, preferred_element_type=F32
        )
        self.values_v[:, :span] = values
        self.values_v[:, span:] = jnp.zeros((values.shape[0], SPAN - span), F32)

        def one_head(head, carry):
            wide = jnp.broadcast_to(self.values_v[pl.ds(head, 1), :], (TILE, SPAN))
            self.bias_v[head] = pltpu.roll(wide, 1, 1, stride=1, stride_axis=0)
            return carry

        lax.fori_loop(0, values.shape[0], one_head, 0)
        self.copies.store(self.bias_v, self.bias)


    def rows(self, block):
        return pl.ds(block * BLOCK, BLOCK)

    def forward(self, block, keep, built):
        copies = self.copies
        rows = self.rows(block)
        table_loads = [] if built else self.fetch("table", "buckets")
        load_x = copies.load(self.hidden_in.at[rows] if keep else self.received, self.x_v)
        small = self.fetch("segments", "padding", "gain1", "shift1", "gain2", "shift2")
        width = self.width
        loads = [
            copies.load(self.wqkv.at[0, :, pl.ds(c, width)], self.wqkv_v.at[:, pl.ds(c, width)])
            for c in range(0, 3 * width, width)
        ]
        if not built:
            self.build_bias(table_loads)
        load_x.wait()

        def load_bias(pair):
            heads = pl.ds(2 * pair, 2)
            return pltpu.make_async_copy(self.bias.at[heads], self.bias_v.at[heads], self.sems.at[self.pair_sems + pair])

        for i, c in enumerate(range(0, 3 * width, width)):
            loads[i].wait()
            if built and i == 2:
                for pair in range(self.pairs):
                    load_bias(pair).start()
            self.qkv_v[:, c : c + width] = dot_nn(self.x_v[...], self.wqkv_v[:, c : c + width]).astype(BF16)
        copies.store(self.x_v, self.xin.at[rows])
        copies.store(self.qkv_v, self.qkv.at[rows], keep)
        weights_sem = self.sems.at[copies.take()]
        later_loads = [
            pltpu.make_async_copy(source.at[0], target, self.sems.at[copies.take()])
            for source, target in ((self.wout, self.wout_v), (self.wup, self.wup_v), (self.wdown, self.wdown_v))
        ]

        def own(pair, part, which):
            both = self.qkv_v[:, self.lanes_of(pair, part)]
            return jnp.where(half_mask(which, both.shape), both, jnp.zeros_like(both))

        for load in small:
            load.wait()
        at = block * BLOCK
        single = self.segments[:, at + TILE : at + TILE + 1] == self.segments[:, at : at + 1]
        padding = self.padding[:, block * BLOCK : (block + 1) * BLOCK]
        tile_of = lax.broadcasted_iota(jnp.int32, (1, BLOCK), 1) // TILE
        shut = [
            jnp.where((padding == 1) & (single | (tile_of == tile)), 0.0, mask_fill) for tile in range(BLOCK // TILE)
        ]
        row_id = lax.broadcasted_iota(jnp.int32, (TILE, TILE), 0)
        diagonal = row_id == lax.broadcasted_iota(jnp.int32, (TILE, TILE), 1)

        def bias_rows(head, tile):
            at = BLOCK - tile * TILE
            rows = self.bias_v[head, :, at : at + BLOCK]
            masked = rows + shut[tile]
            own = slice(tile * TILE, (tile + 1) * TILE)
            parts = [masked[:, : own.start], jnp.where(diagonal, rows[:, own], masked[:, own]), masked[:, own.stop :]]
            return jnp.concatenate([part for part in parts if part.shape[1]], 1)

        def weigh(pair, which):
            head = 2 * pair + which
            k_own = own(pair, 1, which)
            for r in range(0, BLOCK, 2 * TILE):
                q_rows = self.qkv_v[r : r + 2 * TILE, self.lanes_of(pair, 0)] * jnp.asarray(score_scale, BF16)
                tiles = [bias_rows(head, tile) for tile in range(r // TILE, r // TILE + 2)]
                logits = dot_nt(q_rows, k_own) + jnp.concatenate(tiles, 0)
                raised = jnp.exp(logits - jnp.max(logits, -1, keepdims=True))
                share = pl.reciprocal(jnp.sum(raised, -1, keepdims=True), approx=True)
                self.weights_v[head, r : r + 2 * TILE, :] = (raised * share).astype(BF16)

        def head_pair(pair, carry):
            if built:
                load_bias(pair).wait()

            @pl.when(pair == 0)
            def _():
                for load in later_loads:
                    load.start()

            weigh(pair, 0)
            context = dot_nn(self.weights_v[2 * pair], own(pair, 2, 0))
            weigh(pair, 1)
            context += dot_nn(self.weights_v[2 * pair + 1], own(pair, 2, 1))
            self.ctx_v[:, self.lanes_of(pair, 0)] = context.astype(BF16)
            if keep:
                heads = pl.ds(2 * pair, 2)
                pltpu.make_async_copy(self.weights_v.at[heads], self.weights.at[block, heads], weights_sem).start()
            return carry

        lax.fori_loop(0, self.pairs, head_pair, 0)
        if keep:
            copies.stores.append(pltpu.make_async_copy(self.weights_v, self.weights.at[block], weights_sem))
        copies.store(self.ctx_v, self.ctx.at[rows])
        load_out, load_up, load_down = later_loads
        load_out.wait()
        self.acc_v[...] = dot_nn(self.ctx_v[...], self.wout_v[...])
        for r in range(0, BLOCK, 64):
            tile = slice(r, r + 64)
            form, scale = normal_parts(self.acc_v[tile, :] + self.x_v[tile, :].astype(F32))
            normed = form * self.gain1[...] + self.shift1[...]
            self.form1_v[tile, :] = form
            self.scale1_v[tile, :] = scale
            self.acc_v[tile, :] = normed
            self.low1_v[tile, :] = normed.astype(BF16)
        copies.store(self.form1_v, self.form1.at[rows], keep)
        copies.store(self.scale1_v, self.scale1.at[rows], keep)
        copies.store(self.low1_v, self.low1.at[rows])
        load_up.wait()
        load_down.wait()
        act_sem = self.sems.at[copies.take()]
        slope_sem = self.sems.at[copies.take()]

        def two_chunks(i, carry):
            span = self.stage(i)
            active, grade = gelu_parts(dot_nn(self.low1_v[...], self.wup_v[:, span]))
            active = active.astype(BF16)
            self.act_v[:, span] = active
            self.slope_v[:, span] = grade.astype(BF16)
            self.acc_v[...] += dot_nn(active, self.wdown_v[span, :])
            pltpu.make_async_copy(self.act_v.at[:, span], self.act.at[rows, span], act_sem).start()
            if keep:
                pltpu.make_async_copy(self.slope_v.at[:, span], self.slope.at[rows, span], slope_sem).start()
            return carry

        lax.fori_loop(0, self.stages, two_chunks, 0)
        copies.stores.append(pltpu.make_async_copy(self.act_v, self.act.at[rows], act_sem))
        if keep:
            copies.stores.append(pltpu.make_async_copy(self.slope_v, self.slope.at[rows], slope_sem))
        for r in range(0, BLOCK, 64):
            tile = slice(r, r + 64)
            form, scale = normal_parts(self.acc_v[tile, :])
            self.form2_v[tile, :] = form
            self.scale2_v[tile, :] = scale
            self.out_v[tile, :] = (form * self.gain2[...] + self.shift2[...]).astype(BF16)
        copies.store(self.out_v, self.send, keep)
        copies.store(self.out_v, self.out.at[rows])
        copies.store(self.form2_v, self.form2.at[rows], keep)
        copies.store(self.scale2_v, self.scale2.at[rows], keep)


    def chunk_loads(self, i, rows):
        span = self.stage(i)
        return [
            pltpu.make_async_copy(source, target, self.sems.at[self.chunk_sems[k] + i])
            for k, (source, target) in enumerate(
                (
                    (self.wdown.at[0, span], self.wdown_v.at[span]),
                    (self.slope.at[rows, span], self.slope_v.at[:, span]),
                    (self.wup.at[0, :, span], self.wup_v.at[:, span]),
                )
            )
        ]

    def norm_sums(self, source, form_ref, sums_ref):
        gain_sum = jnp.zeros((1, self.width), F32)
        shift_sum = jnp.zeros((1, self.width), F32)
        for r in range(0, BLOCK, 64):
            grad_rows, form = source[r : r + 64, :].astype(F32), form_ref[r : r + 64, :]
            gain_sum += jnp.sum(grad_rows * form, 0, keepdims=True)
            shift_sum += jnp.sum(grad_rows, 0, keepdims=True)
        sums_ref[...] = jnp.zeros(sums_ref.shape, F32)
        sums_ref[0:1, :] = gain_sum
        sums_ref[1:2, :] = shift_sum

    def norm_back(self, block):
        for r in range(0, BLOCK, 64):
            tile = slice(r, r + 64)
            grad_rows = self.g_v[tile, :].astype(F32) * self.gain2[...]
            grad_outer = norm_backward(grad_rows, self.form2_v[tile, :], self.scale2_v[tile, :])
            self.acc_v[tile, :] = grad_outer
            self.outer_v[tile, :] = grad_outer.astype(BF16)
        self.copies.store(self.outer_v, self.outer_low.at[self.rows(block)])

    def norm_sums_2(self, block):
        self.norm_sums(self.g_v, self.form2_v, self.sums2_v)
        self.copies.store(self.sums2_v, self.sums2.at[block])

    def ffn_back(self, block, staged=False, middle_loads=()):
        copies = self.copies
        rows = self.rows(block)
        hidden_sem = self.sems.at[copies.take()]

        def two_chunks(i, carry):
            span = self.stage(i)
            if staged:
                load_down, load_slope, load_up = self.chunk_loads(i, rows)
                load_down.wait()
                load_slope.wait()
            grad_active = dot_nt(self.outer_v[...], self.wdown_v[span, :])
            hidden = (grad_active * self.slope_v[:, span].astype(F32)).astype(BF16)
            self.slope_v[:, span] = hidden
            if staged:
                load_up.wait()

                @pl.when(i + 2 < self.stages)
                def _():
                    for load in self.chunk_loads(i + 2, rows):
                        load.start()

            self.acc_v[...] += dot_nt(hidden, self.wup_v[:, span])
            pltpu.make_async_copy(self.slope_v.at[:, span], self.hidden_low.at[rows, span], hidden_sem).start()
            return carry

        lax.fori_loop(0, self.stages, two_chunks, 0)
        copies.stores.append(pltpu.make_async_copy(self.slope_v, self.hidden_low.at[rows], hidden_sem))
        for load in middle_loads:
            load.wait()
        self.norm_sums(self.acc_v, self.form1_v, self.sums1_v)
        for r in range(0, BLOCK, 64):
            tile = slice(r, r + 64)
            grad_residual = norm_backward(
                self.acc_v[tile, :] * self.gain1[...], self.form1_v[tile, :], self.scale1_v[tile, :]
            )
            self.acc_v[tile, :] = grad_residual
            self.residual_low_v[tile, :] = grad_residual.astype(BF16)
        copies.store(self.residual_low_v, self.residual_low.at[rows])
        copies.store(self.sums1_v, self.sums1.at[block])

    def attn_back(self, block, next_loads=None, load_in=()):
        copies = self.copies
        rows = self.rows(block)
        self.dctx_v[...] = dot_nt(self.residual_low_v[...], self.wout_v[...]).astype(BF16)
        self.fold_v[:, :, 0:TILE] = jnp.zeros((2, TILE, TILE), F32)

        def head_pair(pair, carry):
            def lanes_of(part):
                return self.lanes_of(pair, part)

            if next_loads is not None:
                next_loads(pair)
            q_pair, k_pair, v_pair = (self.qkv_v[:, lanes_of(part)] for part in range(3))
            grad_pair = self.dctx_v[:, lanes_of(0)]
            crossed = grad_pair.astype(F32) * self.ctx_v[:, lanes_of(0)].astype(F32)
            masks = [half_mask(which, k_pair.shape) for which in range(2)]

            def own(both, which):
                return jnp.where(masks[which], both, jnp.zeros_like(both))

            for which in range(2):
                self.square_v[which] = dot_nt(grad_pair, own(v_pair, which))
            q_grad = k_grad = v_grad = 0.0
            for which in range(2):
                head = 2 * pair + which
                delta = jnp.sum(own(crossed, which), -1, keepdims=True)
                for r in range(0, BLOCK, 64):
                    tile = slice(r, r + 64)
                    score_grad = (
                        self.weights_v[head, tile, :].astype(F32) * (self.square_v[which, tile, :] - delta[tile, :])
                    ).astype(BF16)
                    self.half_v[which, tile, :] = score_grad
                    at = BLOCK - r // TILE * TILE
                    wide = score_grad.astype(F32)
                    half = slice(r % TILE, r % TILE + 64)
                    if r < TILE:
                        self.fold_v[which, half, at : at + BLOCK] = wide
                    else:
                        self.fold_v[which, half, at : at + TILE] = wide[:, :TILE]
                        self.fold_v[which, half, at + TILE : at + BLOCK] += wide[:, TILE:]
                v_grad += dot_tn(self.weights_v[head], own(grad_pair, which))
                q_grad += dot_nn(self.half_v[which], own(k_pair, which))
                k_grad += dot_tn(self.half_v[which], own(q_pair, which))
                folded = self.fold_v[which]
                size = TILE // 2
                while size >= 8:
                    folded = folded[:size, :] + pltpu.roll(folded[size:, :], SPAN - size, 1)
                    size //= 2
                self.eighth_v[head] = folded
            self.qkv_v[:, lanes_of(0)] = (q_grad * score_scale).astype(BF16)
            self.qkv_v[:, lanes_of(1)] = (k_grad * score_scale).astype(BF16)
            self.qkv_v[:, lanes_of(2)] = v_grad.astype(BF16)
            return carry

        lax.fori_loop(0, self.pairs, head_pair, 0)
        copies.store(self.eighth_v, self.offsets.at[block])
        copies.store(self.qkv_v, self.projected.at[rows])
        for load in load_in:
            load.wait()
        self.grad_v[...] = (self.acc_v[...] + dot_nt(self.qkv_v[...], self.wqkv_v[...])).astype(BF16)
        copies.store(self.grad_v, self.send)
        copies.store(self.grad_v, self.input_grad.at[rows])


    def do_forward(self, block):
        self.forward(block, True, block > 0)

    def do_bias(self, block):
        self.build_bias(self.fetch("table", "buckets"))

    def do_both(self, block):
        load = self.copies.load(self.out_grad.at[self.rows(block)], self.g_v)
        self.forward(block, False, True)
        load.wait()
        self.norm_back(block)
        self.ffn_back(block)
        self.norm_sums_2(block)
        self.attn_back(block)

    def do_back(self, block):
        rows = self.rows(block)
        loads = [
            self.copies.load(source, target)
            for source, target in (
                (self.received, self.g_v),
                (self.form2.at[rows], self.form2_v),
                (self.scale2.at[rows], self.scale2_v),
                (self.slope.at[rows], self.slope_v),
                (self.wdown.at[0], self.wdown_v),
                (self.wup.at[0], self.wup_v),
                (self.form1.at[rows], self.form1_v),
                (self.scale1.at[rows], self.scale1_v),
                (self.qkv.at[rows], self.qkv_v),
                (self.weights.at[block], self.weights_v),
                (self.ctx.at[rows], self.ctx_v),
                (self.wout.at[0], self.wout_v),
                (self.wqkv.at[0], self.wqkv_v),
            )
        ]
        for load in loads + self.fetch("gain1", "gain2"):
            load.wait()
        self.norm_back(block)
        self.ffn_back(block)
        self.norm_sums_2(block)
        self.attn_back(block)

    def do_ffn_back(self, block):
        rows = self.rows(block)
        loads = [
            self.copies.load(source, target)
            for source, target in (
                (self.received, self.g_v),
                (self.form2.at[rows], self.form2_v),
                (self.scale2.at[rows], self.scale2_v),
            )
        ]
        loads += self.fetch("gain1", "gain2")
        self.chunk_loads(0, rows)[0].start()
        for load in loads:
            load.wait()
        for load in self.chunk_loads(0, rows)[1:] + self.chunk_loads(1, rows):
            load.start()
        middle = [
            self.copies.load(self.form1.at[rows], self.form1_v),
            self.copies.load(self.scale1.at[rows], self.scale1_v),
        ]
        self.norm_back(block)
        self.norm_sums_2(block)
        self.ffn_back(block, True, middle)
        self.copies.store(self.acc_v, self.residual)

    def do_attn_back(self, block):
        rows = self.rows(block)
        loads = [
            self.copies.load(source, target)
            for source, target in ((self.residual_low.at[rows], self.residual_low_v), (self.wout.at[0], self.wout_v))
        ]
        first = self.copies.take(5 * self.pairs)

        def pair_loads(pair):
            heads = pl.ds(2 * pair, 2)
            sources = [(self.weights.at[block, heads], self.weights_v.at[heads])]
            for source, target, parts in ((self.qkv, self.qkv_v, 3), (self.ctx, self.ctx_v, 1)):
                for part in range(parts):
                    lanes = self.lanes_of(pair, part)
                    sources.append((source.at[rows, lanes], target.at[:, lanes]))
            return [
                pltpu.make_async_copy(source, target, self.sems.at[first + 5 * pair + k])
                for k, (source, target) in enumerate(sources)
            ]

        for pair in range(2):
            for load in pair_loads(pair):
                load.start()
        for load in loads:
            load.wait()
        last = [
            pltpu.make_async_copy(source, target, self.sems.at[self.copies.take()])
            for source, target in ((self.wqkv.at[0], self.wqkv_v), (self.residual, self.acc_v))
        ]

        def next_loads(pair):
            for load in pair_loads(pair):
                load.wait()

            @pl.when(pair + 2 < self.pairs)
            def _():
                for load in pair_loads(pair + 2):
                    load.start()

            @pl.when(pair == self.pairs - 3)
            def _():
                for load in last:
                    load.start()

        self.attn_back(block, next_loads, last)


def layer_kernel(work, phase_on, block, ins, outs, scratch, after_count, kept_count, *refs):
    refs_in, refs = refs[: len(ins)], refs[len(ins) + after_count + kept_count :]
    named = dict(zip(ins, refs_in)) | dict(zip(outs, refs)) | dict(zip(scratch, refs[len(outs) :]))

    @pl.when(named["phase"][0] == phase_on)
    def _():
        layer = Layer(named)
        getattr(layer, f"do_{work}")(block)
        layer.copies.finish()


def layer_step(work, phase_on, block, values, afters, kept, kept_shapes, scratch):
    specs = [SMEM] + [ANY] * (len(values) - 1)
    names = list(scratch)
    kept = list(kept) if kept is not None else []
    sent = jax.ShapeDtypeStruct((BLOCK, values[2].shape[1]), BF16)
    if work == "bias":
        names = ["values_v", "bias_v", "table_v", "buckets_v"]
    count = len(values) + len(afters)
    results = pl.pallas_call(
        functools.partial(
            layer_kernel, work, phase_on, block, INS, KEPT + ("send",), names + ["sems"], len(afters), len(kept)
        ),
        out_shape=list(kept_shapes) + [sent],
        in_specs=specs + [ANY] * (len(afters) + len(kept)),
        out_specs=[ANY] * (len(kept_shapes) + 1),
        scratch_shapes=[pltpu.VMEM(*scratch[name]) for name in names] + [pltpu.SemaphoreType.DMA((96,))],
        input_output_aliases={count + i: i for i in range(len(kept))},
        compiler_params=pltpu.CompilerParams(vmem_limit_bytes=VMEM_BYTES),
        name=f"{work}_{phase_on}_{block}",
    )(*values, *afters, *kept)
    return dict(zip(KEPT, results)), results[-1]


def pack_kernel(ways, buckets_ref, offsets_ref, sums1_ref, sums2_ref, *refs):
    out_ref, turn_v = refs[-2:]
    row_of = lax.broadcasted_iota(jnp.int32, (8, SPAN), 0)
    lines = []
    for head in range(offsets_ref.shape[1]):
        eighth = offsets_ref[0, head] + offsets_ref[1, head]
        for size in (4, 2, 1):
            eighth = jnp.where((row_of & size) != 0, pltpu.roll(eighth, SPAN - size, 1), eighth)
        lines.append(jnp.sum(eighth, 0, keepdims=True))
    lines += [jnp.zeros((1, SPAN), F32)] * (NORM_LANE - len(lines))
    sums = pltpu.roll(jnp.concatenate(lines, 0), SPAN - 1, 1)
    span = buckets_ref.shape[1]
    buckets, depth = out_ref.shape[0] // 3, out_ref.shape[0] // ways
    share = buckets // ways
    bucket_ids = lax.broadcasted_iota(jnp.int32, (buckets, span), 0)
    hot = (bucket_ids == buckets_ref[...]).astype(F32)
    table = lax.dot_general(
        hot, sums[:, :span], (((1,), (1,)), ((), ())), precision=highest, preferred_element_type=F32
    ).astype(BF16)
    turn_v[...] = jnp.zeros(turn_v.shape, F32)
    for i, ref in enumerate((sums1_ref, sums2_ref)):
        at = NORM_LANE + 2 * i
        turn_v[at : at + 2, :] = ref[0, 0:2, :] + ref[1, 0:2, :]
    out_ref[...] = turn_v[...].T.astype(BF16)
    for i in range(ways):
        out_ref[i * depth : i * depth + share, 0:NORM_LANE] = table[i * share : (i + 1) * share, :]


def packed(ways, buckets, offset_buckets, kept, afters):
    width = kept["sums1"].shape[2]
    depth, share = width // ways, buckets // ways
    arrays = (offset_buckets, kept["offsets"], kept["sums1"], kept["sums2"])
    if depth % 16 == 0 and share % 16 == 0 and 3 * buckets == width:
        rows = pl.pallas_call(
            functools.partial(pack_kernel, ways),
            out_shape=jax.ShapeDtypeStruct((width, LANES), BF16),
            in_specs=[VMEM] * len(arrays) + [ANY] * len(afters),
            out_specs=VMEM,
            scratch_shapes=[pltpu.VMEM((LANES, width), F32)],
            compiler_params=pltpu.CompilerParams(vmem_limit_bytes=SMALL_VMEM_BYTES),
            name="pack",
        )(*arrays, *afters)
        return rows.reshape(ways, depth, LANES)
    eighths = jnp.sum(kept["offsets"], 0)
    lines = sum(jnp.roll(eighths[:, i, :], -i, 1) for i in range(8))[:, 1:]
    hot = (offset_buckets[0][None, :] == jnp.arange(buckets, dtype=jnp.int32)[:, None]).astype(F32)
    table = jnp.dot(hot, lines.T, precision=highest).reshape(ways, share, -1)
    table = jnp.pad(table, ((0, 0), (0, depth - share), (0, NORM_LANE - table.shape[2])))
    norms = jnp.concatenate([jnp.sum(kept[name], 0)[:2] for name in ("sums1", "sums2")], 0)
    norms = norms.T.reshape(ways, depth, 4)
    rows = jnp.concatenate([table, norms], 2)
    return jnp.pad(rows, ((0, 0), (0, 0), (0, LANES - rows.shape[2]))).astype(BF16)


def halve_kernel(bits, counts, after_count, through_count, me_ref, *refs):
    outs = refs[2 * sum(counts) + after_count + through_count :]
    for i, count in enumerate(counts):
        pieces, refs = [refs[2 * k : 2 * k + 2] for k in range(count)], refs[2 * count :]
        send_ref, rest_ref = outs[2 * i : 2 * i + 2]
        mine = (me_ref[0] >> bits[i]) & 1

        def total(which):
            parts = [
                (kept[0, which, 0, 0] if len(kept.shape) == 6 else kept[0, which, 0]).astype(F32)
                + arrived[0, which, 0].astype(F32)
                for kept, arrived in pieces
            ]
            return jnp.concatenate(parts, 1)

        send_ref[0, 0] = total(1 - mine).astype(send_ref.dtype)
        rest_ref[0, 0] = total(mine)


def spread_kernel(bit, me_ref, kept_ref, arrived_ref, *refs):
    own = (me_ref[0] >> bit) & 3
    for i, ref in enumerate(refs):
        total = kept_ref[own ^ i] + arrived_ref[own ^ i].astype(F32)
        ref[...] = total.astype(ref.dtype)


def join_kernel(count, kept_ref, *refs):
    arrived_refs, (out_ref, qkv_ref, table_ref, *norm_refs, turn_v) = refs[:count], refs[count:]
    total = kept_ref[...]
    for ref in arrived_refs:
        total = total + ref[...].astype(F32)
    wide = out_ref.shape[1]
    out_ref[...] = total[:, :wide]
    qkv_ref[...] = total[:, wide : 4 * wide]
    small = total[:, 4 * wide :]
    turn_v[...] = jnp.zeros(turn_v.shape, F32)
    turn_v[: small.shape[0], :] = small
    turned = turn_v[...].T
    for head in range(table_ref.shape[0]):
        table_ref[head] = turned[head : head + 1, : table_ref.shape[2]]
    for i, ref in enumerate(norm_refs):
        ref[...] = turned[NORM_LANE + i : NORM_LANE + i + 1, : ref.shape[1]]


class Part:
    def __init__(self, whole):
        self.whole = whole
        self.sent = self.of_core(1 - (lax.axis_index("dp") & 1))
        self.arrived = swapped(self.sent, 0)

    def of_core(self, core):
        split = self.whole.reshape((self.whole.shape[0] // 2, 2) + self.whole.shape[1:])
        return lax.dynamic_index_in_dim(split, core, 1, keepdims=False)


def swapped(array, bit):
    count = lax.axis_size("dp")
    return lax.ppermute(array, "dp", [(i, i ^ (1 << bit)) for i in range(count)])


class Share:
    def __init__(self, parts, order):
        self.parts = parts
        self.order = order[1:]
        self.left = sorted(order[1:])
        self.depth = parts[0].whole.shape[1]
        self.wide = sum(part.whole.shape[2] for part in parts)
        self.mine = None

    def swap(self, bit, theirs):
        self.left.remove(bit)
        self.sent = theirs
        self.arrived = swapped(theirs, bit)

    def total(self):
        if self.mine is not None:
            return self.mine + self.arrived.astype(F32)
        here = lax.axis_index("dp") & 1
        return jnp.concatenate(
            [part.of_core(here).astype(F32) + part.arrived.astype(F32) for part in self.parts], 2
        )

    def split_at(self):
        bit = self.order[0]
        axis = len(self.left) - 1 - self.left.index(bit)
        return bit, 2**axis, 2 ** (len(self.left) - 1 - axis)

    def halve(self):
        bit, above, below = self.split_at()
        self.order = self.order[1:]
        split = self.total().reshape(above, 2, below, self.depth, self.wide)
        here = (lax.axis_index("dp") >> bit) & 1
        theirs = lax.dynamic_index_in_dim(split, 1 - here, 1, keepdims=False).astype(BF16)
        mine = lax.dynamic_index_in_dim(split, here, 1, keepdims=False)
        self.mine = mine.reshape(-1, self.depth, self.wide)
        self.swap(bit, theirs.reshape(-1, self.depth, self.wide))


def halve_all(me, shares, afters=(), through=()):
    if any(share.depth % 16 for share in shares):
        for share in shares:
            share.halve()
        return through
    ins, in_specs, outs, out_specs, bits, counts = [], [], [], [], [], []
    for share in shares:
        bit, above, below = share.split_at()
        bits.append(bit)

        def halves(wide, b=below):
            return pl.BlockSpec((1, 2, 1, share.depth, wide), lambda i, me: (i // b, 0, i % b, 0, 0))

        if share.mine is None:
            counts.append(len(share.parts))
            for part in share.parts:
                wide = part.whole.shape[2]
                ins.append(part.whole.reshape(above, 2, below, 2, share.depth, wide))
                in_specs.append(
                    pl.BlockSpec(
                        (1, 2, 1, 1, share.depth, wide),
                        lambda i, me, b=below: (i // b, 0, i % b, me[0] & 1, 0, 0),
                    )
                )
                ins.append(part.arrived.reshape(above, 2, below, share.depth, wide))
                in_specs.append(halves(wide))
        else:
            counts.append(1)
            for array in (share.mine, share.arrived):
                ins.append(array.reshape(above, 2, below, share.depth, share.wide))
                in_specs.append(halves(share.wide))
        outs += [
            jax.ShapeDtypeStruct((above, below, share.depth, share.wide), kind) for kind in (BF16, F32)
        ]
        out_specs += [
            pl.BlockSpec((1, 1, share.depth, share.wide), lambda i, me, b=below: (i // b, i % b, 0, 0))
        ] * 2
        steps = above * below
    results = pl.pallas_call(
        functools.partial(halve_kernel, tuple(bits), tuple(counts), len(afters), len(through)),
        grid_spec=pltpu.PrefetchScalarGridSpec(
            num_scalar_prefetch=1,
            grid=(steps,),
            in_specs=in_specs + [ANY] * (len(afters) + len(through)),
            out_specs=out_specs + [ANY] * len(through),
        ),
        out_shape=outs + [jax.ShapeDtypeStruct(array.shape, array.dtype) for array in through],
        input_output_aliases={
            1 + len(ins) + len(afters) + i: len(outs) + i for i in range(len(through))
        },
        compiler_params=pltpu.CompilerParams(vmem_limit_bytes=SMALL_VMEM_BYTES),
        name="halve",
    )(me, *ins, *afters, *through)
    for i, share in enumerate(shares):
        share.order = share.order[1:]
        share.mine = results[2 * i + 1].reshape(-1, share.depth, share.wide)
        share.swap(bits[i], results[2 * i].reshape(-1, share.depth, share.wide))
    return results[len(outs) :]


def spread(me, share):
    if share.depth % 16 or len(share.left) != 2 or share.left[1] != share.left[0] + 1:
        while share.order:
            share.halve()
        return share.mine[0], [share.arrived[0]]
    bit = share.left[0]
    tail = (share.depth, share.wide)
    own, *sent = pl.pallas_call(
        functools.partial(spread_kernel, bit),
        out_shape=[jax.ShapeDtypeStruct(tail, kind) for kind in (F32, BF16, BF16, BF16)],
        in_specs=[SMEM, VMEM, VMEM],
        out_specs=[VMEM] * 4,
        compiler_params=pltpu.CompilerParams(vmem_limit_bytes=SMALL_VMEM_BYTES),
        name="spread",
    )(me, share.mine.reshape((4,) + tail), share.arrived.reshape((4,) + tail))
    count = lax.axis_size("dp")
    arrived = [
        lax.ppermute(array, "dp", [(i, i ^ ((k + 1) << bit)) for i in range(count)]) for k, array in enumerate(sent)
    ]
    return own, arrived


def joined(own, arrived, width, table_shape):
    depth = own.shape[0]
    shapes = [(depth, width), (depth, 3 * width), table_shape] + [(1, depth)] * 4
    return pl.pallas_call(
        functools.partial(join_kernel, len(arrived)),
        out_shape=[jax.ShapeDtypeStruct(dims, F32) for dims in shapes],
        in_specs=[VMEM] * (1 + len(arrived)),
        out_specs=[VMEM] * len(shapes),
        scratch_shapes=[pltpu.VMEM((LANES, LANES), F32)],
        compiler_params=pltpu.CompilerParams(vmem_limit_bytes=SMALL_VMEM_BYTES),
        name="join",
    )(own, *arrived)


def passed_along(x, axis, by):
    length = lax.axis_size(axis)
    pairs = [(i, i + by) for i in range(length) if 0 <= i + by < length]
    return lax.ppermute(x, axis, pairs)


def shards(
    hidden_in, out_grad, qkv_weight, out_weight, rel_table, norm1_gain, norm1_bias,
    up_weight, down_weight, norm2_gain, norm2_bias, seg_ids, pad_mask, rel_buckets,
):
    phase = lax.axis_index("phase").astype(jnp.int32).reshape(1)
    ways = lax.axis_size("dp")
    slots, width = hidden_in.shape
    inner = up_weight.shape[2]
    buckets, heads = rel_table.shape[1:]

    def shape(dims, kind):
        return jax.ShapeDtypeStruct(dims, kind)

    rows_of = {
        "xin": (width, BF16), "qkv": (3 * width, BF16), "ctx": (width, BF16), "form1": (width, F32),
        "scale1": (1, F32), "low1": (width, BF16), "slope": (inner, BF16), "act": (inner, BF16),
        "form2": (width, F32), "scale2": (1, F32), "out": (width, BF16),
        "outer_low": (width, BF16), "hidden_low": (inner, BF16), "residual_low": (width, BF16),
        "projected": (3 * width, BF16), "input_grad": (width, BF16),
    }
    kept_shapes = [
        shape((slots, rows_of[name][0]), rows_of[name][1])
        if name in rows_of
        else {
            "weights": shape((MICRO, heads, BLOCK, BLOCK), BF16),
            "sums1": shape((MICRO, 8, width), F32),
            "sums2": shape((MICRO, 8, width), F32),
            "residual": shape((BLOCK, width), F32),
            "offsets": shape((MICRO, heads, 8, SPAN), F32),
            "bias": shape((heads, TILE, SPAN), F32),
        }[name]
        for name in KEPT
    ]
    small = {
        "segments_v": ((1, slots), jnp.int32), "padding_v": ((1, slots), jnp.int32),
        "buckets_v": ((1, rel_buckets.shape[0]), jnp.int32), "table_v": ((heads, 1, buckets), F32),
        "gain1_v": ((1, width), F32), "shift1_v": ((1, width), F32), "gain2_v": ((1, width), F32),
        "shift2_v": ((1, width), F32),
    }
    in_forward = ("qkv", "ctx", "form1", "scale1", "low1", "slope", "act", "form2", "scale2", "out")
    scratch = {f"{name}_v": ((BLOCK, rows_of[name][0]), rows_of[name][1]) for name in in_forward}
    scratch |= small
    scratch |= {
        name: ((BLOCK, width), BF16) for name in ("x_v", "g_v", "outer_v", "residual_low_v", "dctx_v", "grad_v")
    }
    scratch |= {
        "weights_v": ((heads, BLOCK, BLOCK), BF16), "acc_v": ((BLOCK, width), F32), "square_v": ((2, BLOCK, BLOCK), F32),
        "values_v": ((heads, SPAN), F32), "bias_v": ((heads, TILE, SPAN), F32), "sums1_v": ((8, width), F32), "sums2_v": ((8, width), F32),
        "wqkv_v": ((width, 3 * width), BF16), "wout_v": ((width, width), BF16), "wup_v": ((width, inner), BF16),
        "wdown_v": ((inner, width), BF16), "fold_v": ((2, TILE, SPAN), F32), "eighth_v": ((heads, 8, SPAN), F32),
        "half_v": ((2, BLOCK, BLOCK), BF16),
    }

    def step(work, phase_on, block, received, kept, afters=()):
        values = (
            phase, seg_ids[None, :], hidden_in, received, out_grad, rel_table.transpose(2, 0, 1), pad_mask[None, :], rel_buckets[None, :],
            norm1_gain, norm1_bias, norm2_gain, norm2_bias, qkv_weight, out_weight, up_weight, down_weight,
        )
        in_place = None if kept is None else [kept[name] for name in KEPT]
        return layer_step(work, phase_on, block, values, list(afters), in_place, kept_shapes, scratch)

    kept, sent = step("forward", 0, 0, hidden_in, None)
    first = passed_along(sent, "phase", 1)
    kept, _ = step("bias", 1, 0, hidden_in, kept)
    kept, sent = step("forward", 0, 1, hidden_in, kept)
    second = passed_along(sent, "phase", 1)
    kept, sent = step("both", 1, 0, first, kept)
    first_back = passed_along(sent, "phase", -1)
    kept, sent = step("both", 1, 1, second, kept)
    second_back = passed_along(sent, "phase", -1)
    kept, _ = step("back", 0, 0, first_back, kept)
    kept, _ = step("ffn_back", 0, 1, second_back, kept)

    bits = ways.bit_length() - 1
    near_first = list(range(bits))
    far_first = [0] + list(range(2, bits)) + [1] if bits > 1 else near_first
    me = lax.axis_index("dp").astype(jnp.int32).reshape(1)

    def weight_grad(left, right):
        product = dot_tn(left, right).astype(BF16)
        return product.reshape(ways, product.shape[0] // ways, product.shape[1])

    down = Share([Part(weight_grad(kept["act"], kept["outer_low"]))], near_first)
    up = Share([Part(weight_grad(kept["low1"], kept["hidden_low"]))], far_first)
    out_part = Part(weight_grad(kept["ctx"], kept["residual_low"]))
    halve_all(me, [down])
    halve_all(me, [up])
    kept, _ = step("attn_back", 0, 1, hidden_in, kept, [down.sent, up.sent])
    far_part = Part(weight_grad(kept["xin"], kept["projected"][:, width:]))
    (slots_in,) = halve_all(me, [down, up], [far_part.sent], [kept["xin"]])
    near_part = Part(weight_grad(slots_in, kept["projected"][:, :width]))
    small_part = Part(packed(ways, buckets, rel_buckets[None, :], kept, [near_part.sent]))
    last = Share([out_part, near_part, far_part, small_part], near_first)
    halve_all(me, [last], [down.sent, up.sent])
    halve_all(me, [down, up])
    own, arrived = spread(me, last)
    while down.order:
        halve_all(me, [down, up])
    down_share = down.total()[0]
    up_share = up.total()[0]
    out_share, qkv_share, table_share, *norm_shares = joined(own, arrived, width, (heads, 1, buckets // ways))
    return (
        kept["out"][None],
        kept["input_grad"][None],
        qkv_share[None],
        out_share[None],
        table_share.transpose(1, 2, 0),
        norm_shares[0],
        norm_shares[1],
        up_share[None],
        down_share[None],
        norm_shares[2],
        norm_shares[3],
    )


def solution(mesh):
    return jax.shard_map(
        shards,
        mesh=mesh,
        in_specs=(
            P("dp", None),
            P("dp", None),
            P("phase", None, None),
            P("phase", None, None),
            P("phase", None, None),
            P("phase", None),
            P("phase", None),
            P("phase", None, None),
            P("phase", None, None),
            P("phase", None),
            P("phase", None),
            P("dp"),
            P("dp"),
            P(),
        ),
        out_specs=(
            P("phase", "dp", None),
            P("phase", "dp", None),
            P("phase", "dp", None),
            P("phase", "dp", None),
            P("phase", "dp", None),
            P("phase", "dp"),
            P("phase", "dp"),
            P("phase", "dp", None),
            P("phase", "dp", None),
            P("phase", "dp"),
            P("phase", "dp"),
        ),
        check_vma=False,
    )
```

```python
import functools

import jax
import jax.numpy as jnp
from jax import lax
from jax.experimental import pallas as pl
from jax.experimental.pallas import tpu as pltpu
from jax.sharding import PartitionSpec as P

BLOCK = 512
MICRO = 2
TILE = 128
LANES = 128
CHUNK = 768
SPAN = 2 * BLOCK
VMEM_BYTES = 58 * 1024 * 1024
SMALL_VMEM_BYTES = 20 * 1024 * 1024
NORM_LANE = 16
PHASE, DP = "phase", "dp"

norm_eps = 1e-05
mask_fill = -1000000000.0
score_scale = 0.125
inv_root_two = 0.7071067811865476
inv_root_tau = 0.3989422804014327
log2_e = 1.4426950408889634
highest = lax.Precision.HIGHEST

F32 = jnp.float32
BF16 = jnp.bfloat16
ANY = pl.BlockSpec(memory_space=pl.ANY)
VMEM = pl.BlockSpec(memory_space=pltpu.VMEM)
QUICK = pl.CostEstimate(flops=1, bytes_accessed=1, transcendentals=0)
SMEM = pl.BlockSpec(memory_space=pltpu.SMEM)


def dot_nn(a, b):
    return lax.dot_general(a, b, (((1,), (0,)), ((), ())), preferred_element_type=F32)


def dot_nt(a, b):
    return lax.dot_general(a, b, (((1,), (1,)), ((), ())), preferred_element_type=F32)


def dot_tn(a, b):
    return lax.dot_general(a, b, (((0,), (0,)), ((), ())), preferred_element_type=F32)


def row_mean(rows):
    return jnp.sum(rows, -1, keepdims=True) * (1.0 / rows.shape[-1])


def normal_parts(residual):
    centred = residual - row_mean(residual)
    inv_scale = lax.rsqrt(row_mean(centred * centred) + norm_eps)
    return centred * inv_scale, inv_scale


def norm_backward(grad_rows, normal_form, inv_scale):
    first = row_mean(grad_rows)
    second = row_mean(grad_rows * normal_form)
    return inv_scale * (grad_rows - first - normal_form * second)


def gelu_parts(hidden):
    share = 0.5 + 0.5 * lax.erf(hidden * inv_root_two)
    bell = jnp.exp2(hidden * hidden * (-0.5 * log2_e))
    return hidden * share, share + hidden * bell * inv_root_tau


def half_mask(which, shape):
    lane = lax.broadcasted_iota(jnp.int32, shape, 1)
    return (lane < LANES // 2) if which == 0 else (lane >= LANES // 2)


class Copies:
    def __init__(self, sems):
        self.sems = sems
        self.used = 0
        self.stores = []

    def take(self, count=1):
        self.used += count
        return self.used - count

    def load(self, source, target):
        copy = pltpu.make_async_copy(source, target, self.sems.at[self.take()])
        copy.start()
        return copy

    def store(self, source, target, when=True):
        if when:
            self.stores.append(self.load(source, target))

    def finish(self):
        for copy in self.stores:
            copy.wait()


KEPT = (
    "xin", "qkv", "weights", "ctx", "form1", "scale1", "low1", "slope", "act", "form2", "scale2", "out",
    "bias", "outer_low", "hidden_low", "residual_low", "sums1", "sums2", "residual", "projected", "offsets", "input_grad",
)
INS = (
    "phase", "segments", "hidden_in", "received", "out_grad", "table", "padding", "buckets",
    "gain1", "shift1", "gain2", "shift2",
    "wqkv", "wout", "wup", "wdown",
)


class Layer:
    def __init__(self, refs):
        self.__dict__.update(refs)
        self.copies = Copies(self.sems)
        self.width = self.hidden_in.shape[1]
        self.inner = self.wup.shape[2]
        self.pairs = self.width // LANES
        self.stages = self.inner // (2 * CHUNK)
        self.pair_sems = self.copies.take(self.pairs)
        self.chunk_sems = [self.copies.take(self.stages) for _ in range(3)]

    def fetch(self, *names):
        loads = [self.copies.load(getattr(self, name), getattr(self, f"{name}_v")) for name in names]
        for name in names:
            setattr(self, name, getattr(self, f"{name}_v"))
        return loads

    def lanes_of(self, pair, part):
        return pl.ds(pl.multiple_of(part * self.width + pair * LANES, LANES), LANES)

    def stage(self, i):
        return pl.ds(pl.multiple_of(i * 2 * CHUNK, 2 * CHUNK), 2 * CHUNK)

    def build_bias(self, table_loads):
        for load in table_loads:
            load.wait()
        span = self.buckets.shape[1]
        bucket_ids = lax.broadcasted_iota(jnp.int32, (self.table.shape[2], span), 0)
        hot = (bucket_ids == self.buckets[...]).astype(F32)
        table = jnp.concatenate([self.table[head] for head in range(self.table.shape[0])], 0)
        values = lax.dot_general(
            table, hot, (((1,), (0,)), ((), ())), precision=highest, preferred_element_type=F32
        )
        self.values_v[:, :span] = values
        self.values_v[:, span:] = jnp.zeros((values.shape[0], SPAN - span), F32)

        def one_head(head, carry):
            wide = jnp.broadcast_to(self.values_v[pl.ds(head, 1), :], (TILE, SPAN))
            self.bias_v[head] = pltpu.roll(wide, 1, 1, stride=1, stride_axis=0)
            return carry

        lax.fori_loop(0, values.shape[0], one_head, 0)
        self.copies.store(self.bias_v, self.bias)


    def rows(self, block):
        return pl.ds(block * BLOCK, BLOCK)

    def forward(self, block, keep, built):
        copies = self.copies
        rows = self.rows(block)
        table_loads = [] if built else self.fetch("table", "buckets")
        load_x = copies.load(self.hidden_in.at[rows] if keep else self.received, self.x_v)
        small = self.fetch("segments", "padding", "gain1", "shift1", "gain2", "shift2")
        width = self.width
        loads = [
            copies.load(self.wqkv.at[0, :, pl.ds(c, width)], self.wqkv_v.at[:, pl.ds(c, width)])
            for c in range(0, 3 * width, width)
        ]
        if not built:
            self.build_bias(table_loads)
        load_x.wait()

        def load_bias(pair):
            heads = pl.ds(2 * pair, 2)
            return pltpu.make_async_copy(self.bias.at[heads], self.bias_v.at[heads], self.sems.at[self.pair_sems + pair])

        for i, c in enumerate(range(0, 3 * width, width)):
            loads[i].wait()
            if built and i == 2:
                for pair in range(self.pairs):
                    load_bias(pair).start()
            self.qkv_v[:, c : c + width] = dot_nn(self.x_v[...], self.wqkv_v[:, c : c + width]).astype(BF16)
        copies.store(self.x_v, self.xin.at[rows])
        copies.store(self.qkv_v, self.qkv.at[rows], keep)
        weights_sem = self.sems.at[copies.take()]
        later_loads = [
            pltpu.make_async_copy(source.at[0], target, self.sems.at[copies.take()])
            for source, target in ((self.wout, self.wout_v), (self.wup, self.wup_v), (self.wdown, self.wdown_v))
        ]

        def own(pair, part, which):
            both = self.qkv_v[:, self.lanes_of(pair, part)]
            return jnp.where(half_mask(which, both.shape), both, jnp.zeros_like(both))

        for load in small:
            load.wait()
        at = block * BLOCK
        single = self.segments[:, at + TILE : at + TILE + 1] == self.segments[:, at : at + 1]
        padding = self.padding[:, block * BLOCK : (block + 1) * BLOCK]
        tile_of = lax.broadcasted_iota(jnp.int32, (1, BLOCK), 1) // TILE
        shut = [
            jnp.where((padding == 1) & (single | (tile_of == tile)), 0.0, mask_fill) for tile in range(BLOCK // TILE)
        ]
        row_id = lax.broadcasted_iota(jnp.int32, (TILE, TILE), 0)
        diagonal = row_id == lax.broadcasted_iota(jnp.int32, (TILE, TILE), 1)

        def bias_rows(head, tile):
            at = BLOCK - tile * TILE
            rows = self.bias_v[head, :, at : at + BLOCK]
            masked = rows + shut[tile]
            own = slice(tile * TILE, (tile + 1) * TILE)
            parts = [masked[:, : own.start], jnp.where(diagonal, rows[:, own], masked[:, own]), masked[:, own.stop :]]
            return jnp.concatenate([part for part in parts if part.shape[1]], 1)

        def weigh(pair, which):
            head = 2 * pair + which
            k_own = own(pair, 1, which)
            for r in range(0, BLOCK, 2 * TILE):
                q_rows = self.qkv_v[r : r + 2 * TILE, self.lanes_of(pair, 0)] * jnp.asarray(score_scale, BF16)
                tiles = [bias_rows(head, tile) for tile in range(r // TILE, r // TILE + 2)]
                logits = dot_nt(q_rows, k_own) + jnp.concatenate(tiles, 0)
                raised = jnp.exp(logits - jnp.max(logits, -1, keepdims=True))
                share = pl.reciprocal(jnp.sum(raised, -1, keepdims=True), approx=True)
                self.weights_v[head, r : r + 2 * TILE, :] = (raised * share).astype(BF16)

        def head_pair(pair, carry):
            if built:
                load_bias(pair).wait()

            @pl.when(pair == 0)
            def _():
                for load in later_loads:
                    load.start()

            weigh(pair, 0)
            context = dot_nn(self.weights_v[2 * pair], own(pair, 2, 0))
            weigh(pair, 1)
            context += dot_nn(self.weights_v[2 * pair + 1], own(pair, 2, 1))
            self.ctx_v[:, self.lanes_of(pair, 0)] = context.astype(BF16)
            if keep:
                heads = pl.ds(2 * pair, 2)
                pltpu.make_async_copy(self.weights_v.at[heads], self.weights.at[block, heads], weights_sem).start()
            return carry

        lax.fori_loop(0, self.pairs, head_pair, 0)
        if keep:
            copies.stores.append(pltpu.make_async_copy(self.weights_v, self.weights.at[block], weights_sem))
        copies.store(self.ctx_v, self.ctx.at[rows])
        load_out, load_up, load_down = later_loads
        load_out.wait()
        self.acc_v[...] = dot_nn(self.ctx_v[...], self.wout_v[...])
        for r in range(0, BLOCK, 64):
            tile = slice(r, r + 64)
            form, scale = normal_parts(self.acc_v[tile, :] + self.x_v[tile, :].astype(F32))
            normed = form * self.gain1[...] + self.shift1[...]
            self.form1_v[tile, :] = form
            self.scale1_v[tile, :] = scale
            self.acc_v[tile, :] = normed
            self.low1_v[tile, :] = normed.astype(BF16)
        copies.store(self.form1_v, self.form1.at[rows], keep)
        copies.store(self.scale1_v, self.scale1.at[rows], keep)
        copies.store(self.low1_v, self.low1.at[rows])
        load_up.wait()
        load_down.wait()
        act_sem = self.sems.at[copies.take()]
        slope_sem = self.sems.at[copies.take()]

        def two_chunks(i, carry):
            span = self.stage(i)
            active, grade = gelu_parts(dot_nn(self.low1_v[...], self.wup_v[:, span]))
            active = active.astype(BF16)
            self.act_v[:, span] = active
            self.slope_v[:, span] = grade.astype(BF16)
            self.acc_v[...] += dot_nn(active, self.wdown_v[span, :])
            pltpu.make_async_copy(self.act_v.at[:, span], self.act.at[rows, span], act_sem).start()
            if keep:
                pltpu.make_async_copy(self.slope_v.at[:, span], self.slope.at[rows, span], slope_sem).start()
            return carry

        lax.fori_loop(0, self.stages, two_chunks, 0)
        copies.stores.append(pltpu.make_async_copy(self.act_v, self.act.at[rows], act_sem))
        if keep:
            copies.stores.append(pltpu.make_async_copy(self.slope_v, self.slope.at[rows], slope_sem))
        for r in range(0, BLOCK, 64):
            tile = slice(r, r + 64)
            form, scale = normal_parts(self.acc_v[tile, :])
            self.form2_v[tile, :] = form
            self.scale2_v[tile, :] = scale
            self.out_v[tile, :] = (form * self.gain2[...] + self.shift2[...]).astype(BF16)
        copies.store(self.out_v, self.send, keep)
        copies.store(self.out_v, self.out.at[rows])
        copies.store(self.form2_v, self.form2.at[rows], keep)
        copies.store(self.scale2_v, self.scale2.at[rows], keep)


    def chunk_loads(self, i, rows):
        span = self.stage(i)
        return [
            pltpu.make_async_copy(source, target, self.sems.at[self.chunk_sems[k] + i])
            for k, (source, target) in enumerate(
                (
                    (self.wdown.at[0, span], self.wdown_v.at[span]),
                    (self.slope.at[rows, span], self.slope_v.at[:, span]),
                    (self.wup.at[0, :, span], self.wup_v.at[:, span]),
                )
            )
        ]

    def norm_sums(self, source, form_ref, sums_ref):
        gain_sum = jnp.zeros((1, self.width), F32)
        shift_sum = jnp.zeros((1, self.width), F32)
        for r in range(0, BLOCK, 64):
            grad_rows, form = source[r : r + 64, :].astype(F32), form_ref[r : r + 64, :]
            gain_sum += jnp.sum(grad_rows * form, 0, keepdims=True)
            shift_sum += jnp.sum(grad_rows, 0, keepdims=True)
        sums_ref[...] = jnp.zeros(sums_ref.shape, F32)
        sums_ref[0:1, :] = gain_sum
        sums_ref[1:2, :] = shift_sum

    def norm_back(self, block):
        for r in range(0, BLOCK, 64):
            tile = slice(r, r + 64)
            grad_rows = self.g_v[tile, :].astype(F32) * self.gain2[...]
            grad_outer = norm_backward(grad_rows, self.form2_v[tile, :], self.scale2_v[tile, :])
            self.acc_v[tile, :] = grad_outer
            self.outer_v[tile, :] = grad_outer.astype(BF16)
        self.copies.store(self.outer_v, self.outer_low.at[self.rows(block)])

    def norm_sums_2(self, block):
        self.norm_sums(self.g_v, self.form2_v, self.sums2_v)
        self.copies.store(self.sums2_v, self.sums2.at[block])

    def ffn_back(self, block, staged=False, middle_loads=()):
        copies = self.copies
        rows = self.rows(block)
        hidden_sem = self.sems.at[copies.take()]

        def two_chunks(i, carry):
            span = self.stage(i)
            if staged:
                load_down, load_slope, load_up = self.chunk_loads(i, rows)
                load_down.wait()
                load_slope.wait()
            grad_active = dot_nt(self.outer_v[...], self.wdown_v[span, :])
            hidden = (grad_active * self.slope_v[:, span].astype(F32)).astype(BF16)
            self.slope_v[:, span] = hidden
            if staged:
                load_up.wait()

                @pl.when(i + 2 < self.stages)
                def _():
                    for load in self.chunk_loads(i + 2, rows):
                        load.start()

            self.acc_v[...] += dot_nt(hidden, self.wup_v[:, span])
            pltpu.make_async_copy(self.slope_v.at[:, span], self.hidden_low.at[rows, span], hidden_sem).start()
            return carry

        lax.fori_loop(0, self.stages, two_chunks, 0)
        copies.stores.append(pltpu.make_async_copy(self.slope_v, self.hidden_low.at[rows], hidden_sem))
        for load in middle_loads:
            load.wait()
        self.norm_sums(self.acc_v, self.form1_v, self.sums1_v)
        for r in range(0, BLOCK, 64):
            tile = slice(r, r + 64)
            grad_residual = norm_backward(
                self.acc_v[tile, :] * self.gain1[...], self.form1_v[tile, :], self.scale1_v[tile, :]
            )
            self.acc_v[tile, :] = grad_residual
            self.residual_low_v[tile, :] = grad_residual.astype(BF16)
        copies.store(self.residual_low_v, self.residual_low.at[rows])
        copies.store(self.sums1_v, self.sums1.at[block])

    def attn_back(self, block, next_loads=None, load_in=()):
        copies = self.copies
        rows = self.rows(block)
        self.dctx_v[...] = dot_nt(self.residual_low_v[...], self.wout_v[...]).astype(BF16)
        self.fold_v[:, :, 0:TILE] = jnp.zeros((2, TILE, TILE), F32)

        def head_pair(pair, carry):
            def lanes_of(part):
                return self.lanes_of(pair, part)

            if next_loads is not None:
                next_loads(pair)
            q_pair, k_pair, v_pair = (self.qkv_v[:, lanes_of(part)] for part in range(3))
            grad_pair = self.dctx_v[:, lanes_of(0)]
            crossed = grad_pair.astype(F32) * self.ctx_v[:, lanes_of(0)].astype(F32)
            masks = [half_mask(which, k_pair.shape) for which in range(2)]

            def own(both, which):
                return jnp.where(masks[which], both, jnp.zeros_like(both))

            for which in range(2):
                self.square_v[which] = dot_nt(grad_pair, own(v_pair, which))
            q_grad = k_grad = v_grad = 0.0
            for which in range(2):
                head = 2 * pair + which
                delta = jnp.sum(own(crossed, which), -1, keepdims=True)
                for r in range(0, BLOCK, 64):
                    tile = slice(r, r + 64)
                    score_grad = (
                        self.weights_v[head, tile, :].astype(F32) * (self.square_v[which, tile, :] - delta[tile, :])
                    ).astype(BF16)
                    self.half_v[which, tile, :] = score_grad
                    at = BLOCK - r // TILE * TILE
                    wide = score_grad.astype(F32)
                    half = slice(r % TILE, r % TILE + 64)
                    if r < TILE:
                        self.fold_v[which, half, at : at + BLOCK] = wide
                    else:
                        self.fold_v[which, half, at : at + TILE] = wide[:, :TILE]
                        self.fold_v[which, half, at + TILE : at + BLOCK] += wide[:, TILE:]
                v_grad += dot_tn(self.weights_v[head], own(grad_pair, which))
                q_grad += dot_nn(self.half_v[which], own(k_pair, which))
                k_grad += dot_tn(self.half_v[which], own(q_pair, which))
                folded = self.fold_v[which]
                size = TILE // 2
                while size >= 8:
                    folded = folded[:size, :] + pltpu.roll(folded[size:, :], SPAN - size, 1)
                    size //= 2
                self.eighth_v[head] = folded
            self.qkv_v[:, lanes_of(0)] = (q_grad * score_scale).astype(BF16)
            self.qkv_v[:, lanes_of(1)] = (k_grad * score_scale).astype(BF16)
            self.qkv_v[:, lanes_of(2)] = v_grad.astype(BF16)
            return carry

        lax.fori_loop(0, self.pairs, head_pair, 0)
        copies.store(self.eighth_v, self.offsets.at[block])
        copies.store(self.qkv_v, self.projected.at[rows])
        for load in load_in:
            load.wait()
        self.grad_v[...] = (self.acc_v[...] + dot_nt(self.qkv_v[...], self.wqkv_v[...])).astype(BF16)
        copies.store(self.grad_v, self.send)
        copies.store(self.grad_v, self.input_grad.at[rows])


    def do_forward(self, block):
        self.forward(block, True, block > 0)

    def do_bias(self, block):
        self.build_bias(self.fetch("table", "buckets"))

    def do_both(self, block):
        load = self.copies.load(self.out_grad.at[self.rows(block)], self.g_v)
        self.forward(block, False, True)
        load.wait()
        self.norm_back(block)
        self.ffn_back(block)
        self.norm_sums_2(block)
        self.attn_back(block)

    def do_back(self, block):
        rows = self.rows(block)
        loads = [
            self.copies.load(source, target)
            for source, target in (
                (self.received, self.g_v),
                (self.form2.at[rows], self.form2_v),
                (self.scale2.at[rows], self.scale2_v),
                (self.slope.at[rows], self.slope_v),
                (self.wdown.at[0], self.wdown_v),
                (self.wup.at[0], self.wup_v),
                (self.form1.at[rows], self.form1_v),
                (self.scale1.at[rows], self.scale1_v),
                (self.qkv.at[rows], self.qkv_v),
                (self.weights.at[block], self.weights_v),
                (self.ctx.at[rows], self.ctx_v),
                (self.wout.at[0], self.wout_v),
                (self.wqkv.at[0], self.wqkv_v),
            )
        ]
        for load in loads + self.fetch("gain1", "gain2"):
            load.wait()
        self.norm_back(block)
        self.ffn_back(block)
        self.norm_sums_2(block)
        self.attn_back(block)

    def do_ffn_back(self, block):
        rows = self.rows(block)
        loads = [
            self.copies.load(source, target)
            for source, target in (
                (self.received, self.g_v),
                (self.form2.at[rows], self.form2_v),
                (self.scale2.at[rows], self.scale2_v),
            )
        ]
        loads += self.fetch("gain1", "gain2")
        self.chunk_loads(0, rows)[0].start()
        for load in loads:
            load.wait()
        for load in self.chunk_loads(0, rows)[1:] + self.chunk_loads(1, rows):
            load.start()
        middle = [
            self.copies.load(self.form1.at[rows], self.form1_v),
            self.copies.load(self.scale1.at[rows], self.scale1_v),
        ]
        self.norm_back(block)
        self.norm_sums_2(block)
        self.ffn_back(block, True, middle)
        self.copies.store(self.acc_v, self.residual)

    def do_attn_back(self, block):
        rows = self.rows(block)
        loads = [
            self.copies.load(source, target)
            for source, target in ((self.residual_low.at[rows], self.residual_low_v), (self.wout.at[0], self.wout_v))
        ]
        first = self.copies.take(5 * self.pairs)

        def pair_loads(pair):
            heads = pl.ds(2 * pair, 2)
            sources = [(self.weights.at[block, heads], self.weights_v.at[heads])]
            for source, target, parts in ((self.qkv, self.qkv_v, 3), (self.ctx, self.ctx_v, 1)):
                for part in range(parts):
                    lanes = self.lanes_of(pair, part)
                    sources.append((source.at[rows, lanes], target.at[:, lanes]))
            return [
                pltpu.make_async_copy(source, target, self.sems.at[first + 5 * pair + k])
                for k, (source, target) in enumerate(sources)
            ]

        for pair in range(2):
            for load in pair_loads(pair):
                load.start()
        for load in loads:
            load.wait()
        last = [
            pltpu.make_async_copy(source, target, self.sems.at[self.copies.take()])
            for source, target in ((self.wqkv.at[0], self.wqkv_v), (self.residual, self.acc_v))
        ]

        def next_loads(pair):
            for load in pair_loads(pair):
                load.wait()

            @pl.when(pair + 2 < self.pairs)
            def _():
                for load in pair_loads(pair + 2):
                    load.start()

            @pl.when(pair == self.pairs - 3)
            def _():
                for load in last:
                    load.start()

        self.attn_back(block, next_loads, last)


def layer_kernel(work, phase_on, block, ins, outs, scratch, after_count, kept_count, *refs):
    refs_in, refs = refs[: len(ins)], refs[len(ins) + after_count + kept_count :]
    named = dict(zip(ins, refs_in)) | dict(zip(outs, refs)) | dict(zip(scratch, refs[len(outs) :]))

    @pl.when(named["phase"][0] == phase_on)
    def _():
        layer = Layer(named)
        getattr(layer, f"do_{work}")(block)
        layer.copies.finish()


def layer_step(work, phase_on, block, values, afters, kept, kept_shapes, scratch):
    specs = [SMEM] + [ANY] * (len(values) - 1)
    names = list(scratch)
    kept = list(kept) if kept is not None else []
    sent = jax.ShapeDtypeStruct((BLOCK, values[2].shape[1]), BF16)
    if work == "bias":
        names = ["values_v", "bias_v", "table_v", "buckets_v"]
    count = len(values) + len(afters)
    results = pl.pallas_call(
        functools.partial(
            layer_kernel, work, phase_on, block, INS, KEPT + ("send",), names + ["sems"], len(afters), len(kept)
        ),
        out_shape=list(kept_shapes) + [sent],
        in_specs=specs + [ANY] * (len(afters) + len(kept)),
        out_specs=[ANY] * (len(kept_shapes) + 1),
        scratch_shapes=[pltpu.VMEM(*scratch[name]) for name in names] + [pltpu.SemaphoreType.DMA((96,))],
        input_output_aliases={count + i: i for i in range(len(kept))},
        compiler_params=pltpu.CompilerParams(vmem_limit_bytes=VMEM_BYTES),
        name=f"{work}_{phase_on}_{block}",
    )(*values, *afters, *kept)
    return dict(zip(KEPT, results)), results[-1]


def pack_kernel(ways, buckets_ref, offsets_ref, sums1_ref, sums2_ref, *refs):
    out_ref, turn_v = refs[-2:]
    row_of = lax.broadcasted_iota(jnp.int32, (8, SPAN), 0)
    lines = []
    for head in range(offsets_ref.shape[1]):
        eighth = offsets_ref[0, head] + offsets_ref[1, head]
        for size in (4, 2, 1):
            eighth = jnp.where((row_of & size) != 0, pltpu.roll(eighth, SPAN - size, 1), eighth)
        lines.append(jnp.sum(eighth, 0, keepdims=True))
    lines += [jnp.zeros((1, SPAN), F32)] * (NORM_LANE - len(lines))
    sums = pltpu.roll(jnp.concatenate(lines, 0), SPAN - 1, 1)
    span = buckets_ref.shape[1]
    buckets, depth = out_ref.shape[0] // 3, out_ref.shape[0] // ways
    share = buckets // ways
    bucket_ids = lax.broadcasted_iota(jnp.int32, (buckets, span), 0)
    hot = (bucket_ids == buckets_ref[...]).astype(F32)
    table = lax.dot_general(
        hot, sums[:, :span], (((1,), (1,)), ((), ())), precision=highest, preferred_element_type=F32
    ).astype(BF16)
    turn_v[...] = jnp.zeros(turn_v.shape, F32)
    for i, ref in enumerate((sums1_ref, sums2_ref)):
        at = NORM_LANE + 2 * i
        turn_v[at : at + 2, :] = ref[0, 0:2, :] + ref[1, 0:2, :]
    out_ref[...] = turn_v[...].T.astype(BF16)
    for i in range(ways):
        out_ref[i * depth : i * depth + share, 0:NORM_LANE] = table[i * share : (i + 1) * share, :]


def packed(ways, buckets, offset_buckets, kept, afters):
    width = kept["sums1"].shape[2]
    depth, share = width // ways, buckets // ways
    arrays = (offset_buckets, kept["offsets"], kept["sums1"], kept["sums2"])
    if depth % 16 == 0 and share % 16 == 0 and 3 * buckets == width:
        rows = pl.pallas_call(
            functools.partial(pack_kernel, ways),
            out_shape=jax.ShapeDtypeStruct((width, LANES), BF16),
            in_specs=[VMEM] * len(arrays) + [ANY] * len(afters),
            out_specs=VMEM,
            scratch_shapes=[pltpu.VMEM((LANES, width), F32)],
            compiler_params=pltpu.CompilerParams(vmem_limit_bytes=SMALL_VMEM_BYTES),
            name="pack",
        )(*arrays, *afters)
        return rows.reshape(ways, depth, LANES)
    eighths = jnp.sum(kept["offsets"], 0)
    lines = sum(jnp.roll(eighths[:, i, :], -i, 1) for i in range(8))[:, 1:]
    hot = (offset_buckets[0][None, :] == jnp.arange(buckets, dtype=jnp.int32)[:, None]).astype(F32)
    table = jnp.dot(hot, lines.T, precision=highest).reshape(ways, share, -1)
    table = jnp.pad(table, ((0, 0), (0, depth - share), (0, NORM_LANE - table.shape[2])))
    norms = jnp.concatenate([jnp.sum(kept[name], 0)[:2] for name in ("sums1", "sums2")], 0)
    norms = norms.T.reshape(ways, depth, 4)
    rows = jnp.concatenate([table, norms], 2)
    return jnp.pad(rows, ((0, 0), (0, 0), (0, LANES - rows.shape[2]))).astype(BF16)


def halve_kernel(bits, counts, after_count, through_count, me_ref, *refs):
    outs = refs[2 * sum(counts) + after_count + through_count :]
    for i, count in enumerate(counts):
        pieces, refs = [refs[2 * k : 2 * k + 2] for k in range(count)], refs[2 * count :]
        send_ref, rest_ref = outs[2 * i : 2 * i + 2]
        mine = (me_ref[0] >> bits[i]) & 1

        def total(which):
            parts = [
                (kept[0, which, 0, 0] if len(kept.shape) == 6 else kept[0, which, 0]).astype(F32)
                + arrived[0, which, 0].astype(F32)
                for kept, arrived in pieces
            ]
            return jnp.concatenate(parts, 1)

        send_ref[0, 0] = total(1 - mine).astype(send_ref.dtype)
        rest_ref[0, 0] = total(mine)


def join_kernel(kept_ref, arrived_ref, out_ref, qkv_ref, table_ref, *refs):
    norm_refs, turn_v = refs[:-1], refs[-1]
    total = kept_ref[...] + arrived_ref[...].astype(F32)
    wide = out_ref.shape[1]
    out_ref[...] = total[:, :wide]
    qkv_ref[...] = total[:, wide : 4 * wide]
    small = total[:, 4 * wide :]
    turn_v[...] = jnp.zeros(turn_v.shape, F32)
    turn_v[: small.shape[0], :] = small
    turned = turn_v[...].T
    for head in range(table_ref.shape[0]):
        table_ref[head] = turned[head : head + 1, : table_ref.shape[2]]
    for i, ref in enumerate(norm_refs):
        ref[...] = turned[NORM_LANE + i : NORM_LANE + i + 1, : ref.shape[1]]


class Part:
    def __init__(self, whole):
        self.whole = whole
        self.sent = self.of_core(1 - (lax.axis_index(DP) & 1))
        self.arrived = swapped(self.sent, 0)

    def of_core(self, core):
        split = self.whole.reshape((self.whole.shape[0] // 2, 2) + self.whole.shape[1:])
        return lax.dynamic_index_in_dim(split, core, 1, keepdims=False)


def swapped(array, bit):
    count = lax.axis_size(DP)
    return lax.ppermute(array, DP, [(i, i ^ (1 << bit)) for i in range(count)])


class Share:
    def __init__(self, parts, order):
        self.parts = parts
        self.order = order[1:]
        self.left = sorted(order[1:])
        self.depth = parts[0].whole.shape[1]
        self.wide = sum(part.whole.shape[2] for part in parts)
        self.mine = None

    def swap(self, bit, theirs):
        self.left.remove(bit)
        self.sent = theirs
        self.arrived = swapped(theirs, bit)

    def total(self):
        if self.mine is not None:
            return self.mine + self.arrived.astype(F32)
        here = lax.axis_index(DP) & 1
        return jnp.concatenate(
            [part.of_core(here).astype(F32) + part.arrived.astype(F32) for part in self.parts], 2
        )

    def split_at(self):
        bit = self.order[0]
        axis = len(self.left) - 1 - self.left.index(bit)
        return bit, 2**axis, 2 ** (len(self.left) - 1 - axis)

    def halve(self):
        bit, above, below = self.split_at()
        self.order = self.order[1:]
        split = self.total().reshape(above, 2, below, self.depth, self.wide)
        here = (lax.axis_index(DP) >> bit) & 1
        theirs = lax.dynamic_index_in_dim(split, 1 - here, 1, keepdims=False).astype(BF16)
        mine = lax.dynamic_index_in_dim(split, here, 1, keepdims=False)
        self.mine = mine.reshape(-1, self.depth, self.wide)
        self.swap(bit, theirs.reshape(-1, self.depth, self.wide))


def halve_all(me, shares, afters=(), through=()):
    if any(share.depth % 16 for share in shares):
        for share in shares:
            share.halve()
        return through
    ins, in_specs, outs, out_specs, bits, counts = [], [], [], [], [], []
    for share in shares:
        bit, above, below = share.split_at()
        bits.append(bit)

        def halves(wide, b=below):
            return pl.BlockSpec((1, 2, 1, share.depth, wide), lambda i, me: (i // b, 0, i % b, 0, 0))

        if share.mine is None:
            counts.append(len(share.parts))
            for part in share.parts:
                wide = part.whole.shape[2]
                ins.append(part.whole.reshape(above, 2, below, 2, share.depth, wide))
                in_specs.append(
                    pl.BlockSpec(
                        (1, 2, 1, 1, share.depth, wide),
                        lambda i, me, b=below: (i // b, 0, i % b, me[0] & 1, 0, 0),
                    )
                )
                ins.append(part.arrived.reshape(above, 2, below, share.depth, wide))
                in_specs.append(halves(wide))
        else:
            counts.append(1)
            for array in (share.mine, share.arrived):
                ins.append(array.reshape(above, 2, below, share.depth, share.wide))
                in_specs.append(halves(share.wide))
        outs += [
            jax.ShapeDtypeStruct((above, below, share.depth, share.wide), kind) for kind in (BF16, F32)
        ]
        out_specs += [
            pl.BlockSpec((1, 1, share.depth, share.wide), lambda i, me, b=below: (i // b, i % b, 0, 0))
        ] * 2
        steps = above * below
    results = pl.pallas_call(
        functools.partial(halve_kernel, tuple(bits), tuple(counts), len(afters), len(through)),
        grid_spec=pltpu.PrefetchScalarGridSpec(
            num_scalar_prefetch=1,
            grid=(steps,),
            in_specs=in_specs + [ANY] * (len(afters) + len(through)),
            out_specs=out_specs + [ANY] * len(through),
        ),
        out_shape=outs + [jax.ShapeDtypeStruct(array.shape, array.dtype) for array in through],
        input_output_aliases={
            1 + len(ins) + len(afters) + i: len(outs) + i for i in range(len(through))
        },
        compiler_params=pltpu.CompilerParams(vmem_limit_bytes=SMALL_VMEM_BYTES),
        name="halve",
    )(me, *ins, *afters, *through)
    for i, share in enumerate(shares):
        share.order = share.order[1:]
        share.mine = results[2 * i + 1].reshape(-1, share.depth, share.wide)
        share.swap(bits[i], results[2 * i].reshape(-1, share.depth, share.wide))
    return results[len(outs) :]


def joined(share, width, table_shape):
    shapes = [(share.depth, width), (share.depth, 3 * width), table_shape] + [(1, share.depth)] * 4
    return pl.pallas_call(
        join_kernel,
        out_shape=[jax.ShapeDtypeStruct(dims, F32) for dims in shapes],
        in_specs=[VMEM] * 2,
        out_specs=[VMEM] * len(shapes),
        scratch_shapes=[pltpu.VMEM((LANES, LANES), F32)],
        compiler_params=pltpu.CompilerParams(vmem_limit_bytes=SMALL_VMEM_BYTES),
        name="join",
    )(share.mine[0], share.arrived[0])


def passed_along(x, axis, by):
    length = lax.axis_size(axis)
    pairs = [(i, i + by) for i in range(length) if 0 <= i + by < length]
    return lax.ppermute(x, axis, pairs)


def shards(
    hidden_in, out_grad, qkv_weight, out_weight, rel_table, norm1_gain, norm1_bias,
    up_weight, down_weight, norm2_gain, norm2_bias, seg_ids, pad_mask, rel_buckets,
):
    phase = lax.axis_index(PHASE).astype(jnp.int32).reshape(1)
    ways = lax.axis_size(DP)
    slots, width = hidden_in.shape
    inner = up_weight.shape[2]
    buckets, heads = rel_table.shape[1:]

    def shape(dims, kind):
        return jax.ShapeDtypeStruct(dims, kind)

    rows_of = {
        "xin": (width, BF16), "qkv": (3 * width, BF16), "ctx": (width, BF16), "form1": (width, F32),
        "scale1": (1, F32), "low1": (width, BF16), "slope": (inner, BF16), "act": (inner, BF16),
        "form2": (width, F32), "scale2": (1, F32), "out": (width, BF16),
        "outer_low": (width, BF16), "hidden_low": (inner, BF16), "residual_low": (width, BF16),
        "projected": (3 * width, BF16), "input_grad": (width, BF16),
    }
    kept_shapes = [
        shape((slots, rows_of[name][0]), rows_of[name][1])
        if name in rows_of
        else {
            "weights": shape((MICRO, heads, BLOCK, BLOCK), BF16),
            "sums1": shape((MICRO, 8, width), F32),
            "sums2": shape((MICRO, 8, width), F32),
            "residual": shape((BLOCK, width), F32),
            "offsets": shape((MICRO, heads, 8, SPAN), F32),
            "bias": shape((heads, TILE, SPAN), F32),
        }[name]
        for name in KEPT
    ]
    small = {
        "segments_v": ((1, slots), jnp.int32), "padding_v": ((1, slots), jnp.int32),
        "buckets_v": ((1, rel_buckets.shape[0]), jnp.int32), "table_v": ((heads, 1, buckets), F32),
        "gain1_v": ((1, width), F32), "shift1_v": ((1, width), F32), "gain2_v": ((1, width), F32),
        "shift2_v": ((1, width), F32),
    }
    in_forward = ("qkv", "ctx", "form1", "scale1", "low1", "slope", "act", "form2", "scale2", "out")
    scratch = {f"{name}_v": ((BLOCK, rows_of[name][0]), rows_of[name][1]) for name in in_forward}
    scratch |= small
    scratch |= {
        name: ((BLOCK, width), BF16) for name in ("x_v", "g_v", "outer_v", "residual_low_v", "dctx_v", "grad_v")
    }
    scratch |= {
        "weights_v": ((heads, BLOCK, BLOCK), BF16), "acc_v": ((BLOCK, width), F32), "square_v": ((2, BLOCK, BLOCK), F32),
        "values_v": ((heads, SPAN), F32), "bias_v": ((heads, TILE, SPAN), F32), "sums1_v": ((8, width), F32), "sums2_v": ((8, width), F32),
        "wqkv_v": ((width, 3 * width), BF16), "wout_v": ((width, width), BF16), "wup_v": ((width, inner), BF16),
        "wdown_v": ((inner, width), BF16), "fold_v": ((2, TILE, SPAN), F32), "eighth_v": ((heads, 8, SPAN), F32),
        "half_v": ((2, BLOCK, BLOCK), BF16),
    }

    def step(work, phase_on, block, received, kept, afters=()):
        values = (
            phase, seg_ids[None, :], hidden_in, received, out_grad, rel_table.transpose(2, 0, 1), pad_mask[None, :], rel_buckets[None, :],
            norm1_gain, norm1_bias, norm2_gain, norm2_bias, qkv_weight, out_weight, up_weight, down_weight,
        )
        in_place = None if kept is None else [kept[name] for name in KEPT]
        return layer_step(work, phase_on, block, values, list(afters), in_place, kept_shapes, scratch)

    kept, sent = step("forward", 0, 0, hidden_in, None)
    first = passed_along(sent, PHASE, 1)
    kept, _ = step("bias", 1, 0, hidden_in, kept)
    kept, sent = step("forward", 0, 1, hidden_in, kept)
    second = passed_along(sent, PHASE, 1)
    kept, sent = step("both", 1, 0, first, kept)
    first_back = passed_along(sent, PHASE, -1)
    kept, sent = step("both", 1, 1, second, kept)
    second_back = passed_along(sent, PHASE, -1)
    kept, _ = step("back", 0, 0, first_back, kept)
    kept, _ = step("ffn_back", 0, 1, second_back, kept)

    bits = ways.bit_length() - 1
    near_first = list(range(bits))
    far_first = [0] + list(range(2, bits)) + [1] if bits > 1 else near_first
    me = lax.axis_index(DP).astype(jnp.int32).reshape(1)

    def weight_grad(left, right):
        product = dot_tn(left, right).astype(BF16)
        return product.reshape(ways, product.shape[0] // ways, product.shape[1])

    down = Share([Part(weight_grad(kept["act"], kept["outer_low"]))], near_first)
    up = Share([Part(weight_grad(kept["low1"], kept["hidden_low"]))], far_first)
    out_part = Part(weight_grad(kept["ctx"], kept["residual_low"]))
    halve_all(me, [down])
    halve_all(me, [up])
    kept, _ = step("attn_back", 0, 1, hidden_in, kept, [down.sent, up.sent])
    far_part = Part(weight_grad(kept["xin"], kept["projected"][:, width:]))
    near_part = Part(weight_grad(kept["xin"], kept["projected"][:, :width]))
    halve_all(me, [up, down], [far_part.sent, near_part.sent])
    small_part = Part(packed(ways, buckets, rel_buckets[None, :], kept, [near_part.sent]))
    last = Share([out_part, near_part, far_part, small_part], near_first)
    halve_all(me, [last], [down.sent, up.sent])
    halve_all(me, [last])
    halve_all(me, [up, down], [last.sent])
    while down.order:
        halve_all(me, [up, down])
    while last.order:
        halve_all(me, [last])
    down_share = down.total()[0]
    up_share = up.total()[0]
    out_share, qkv_share, table_share, *norm_shares = joined(last, width, (heads, 1, buckets // ways))
    return (
        kept["out"][None],
        kept["input_grad"][None],
        qkv_share[None],
        out_share[None],
        table_share.transpose(1, 2, 0),
        norm_shares[0],
        norm_shares[1],
        up_share[None],
        down_share[None],
        norm_shares[2],
        norm_shares[3],
    )


def solution(mesh):
    return jax.shard_map(
        shards,
        mesh=mesh,
        in_specs=(
            P(DP, None),
            P(DP, None),
            P(PHASE, None, None),
            P(PHASE, None, None),
            P(PHASE, None, None),
            P(PHASE, None),
            P(PHASE, None),
            P(PHASE, None, None),
            P(PHASE, None, None),
            P(PHASE, None),
            P(PHASE, None),
            P(DP),
            P(DP),
            P(),
        ),
        out_specs=(
            P(PHASE, DP, None),
            P(PHASE, DP, None),
            P(PHASE, DP, None),
            P(PHASE, DP, None),
            P(PHASE, DP, None),
            P(PHASE, DP),
            P(PHASE, DP),
            P(PHASE, DP, None),
            P(PHASE, DP, None),
            P(PHASE, DP),
            P(PHASE, DP),
        ),
        check_vma=False,
    )
```

```python
import functools

import jax
import jax.numpy as jnp
from jax import lax
from jax.experimental import pallas as pl
from jax.experimental.pallas import tpu as pltpu
from jax.sharding import PartitionSpec as P

BLOCK = 512
MICRO = 2
TILE = 128
LANES = 128
CHUNK = 768
SPAN = 2 * BLOCK
VMEM_BYTES = 58 * 1024 * 1024
SMALL_VMEM_BYTES = 20 * 1024 * 1024
NORM_LANE = 16
PHASE, DP = "phase", "dp"

norm_eps = 1e-05
mask_fill = -1000000000.0
score_scale = 0.125
inv_root_two = 0.7071067811865476
inv_root_tau = 0.3989422804014327
log2_e = 1.4426950408889634
highest = lax.Precision.HIGHEST

F32 = jnp.float32
BF16 = jnp.bfloat16
ANY = pl.BlockSpec(memory_space=pl.ANY)
VMEM = pl.BlockSpec(memory_space=pltpu.VMEM)
QUICK = pl.CostEstimate(flops=1, bytes_accessed=1, transcendentals=0)
SMEM = pl.BlockSpec(memory_space=pltpu.SMEM)


def dot_nn(a, b):
    return lax.dot_general(a, b, (((1,), (0,)), ((), ())), preferred_element_type=F32)


def dot_nt(a, b):
    return lax.dot_general(a, b, (((1,), (1,)), ((), ())), preferred_element_type=F32)


def dot_tn(a, b):
    return lax.dot_general(a, b, (((0,), (0,)), ((), ())), preferred_element_type=F32)


def row_mean(rows):
    return jnp.sum(rows, -1, keepdims=True) * (1.0 / rows.shape[-1])


def normal_parts(residual):
    centred = residual - row_mean(residual)
    inv_scale = lax.rsqrt(row_mean(centred * centred) + norm_eps)
    return centred * inv_scale, inv_scale


def norm_backward(grad_rows, normal_form, inv_scale):
    first = row_mean(grad_rows)
    second = row_mean(grad_rows * normal_form)
    return inv_scale * (grad_rows - first - normal_form * second)


def gelu_parts(hidden):
    share = 0.5 + 0.5 * lax.erf(hidden * inv_root_two)
    bell = jnp.exp2(hidden * hidden * (-0.5 * log2_e))
    return hidden * share, share + hidden * bell * inv_root_tau


def half_mask(which, shape):
    lane = lax.broadcasted_iota(jnp.int32, shape, 1)
    return (lane < LANES // 2) if which == 0 else (lane >= LANES // 2)


class Copies:
    def __init__(self, sems):
        self.sems = sems
        self.used = 0
        self.stores = []

    def take(self, count=1):
        self.used += count
        return self.used - count

    def load(self, source, target):
        copy = pltpu.make_async_copy(source, target, self.sems.at[self.take()])
        copy.start()
        return copy

    def store(self, source, target, when=True):
        if when:
            self.stores.append(self.load(source, target))

    def finish(self):
        for copy in self.stores:
            copy.wait()


KEPT = (
    "xin", "qkv", "weights", "ctx", "form1", "scale1", "low1", "slope", "act", "form2", "scale2", "out",
    "bias", "outer_low", "hidden_low", "residual_low", "sums1", "sums2", "residual", "projected", "offsets", "input_grad",
)
INS = (
    "phase", "segments", "hidden_in", "received", "out_grad", "table", "padding", "buckets",
    "gain1", "shift1", "gain2", "shift2",
    "wqkv", "wout", "wup", "wdown",
)


class Layer:
    def __init__(self, refs):
        self.__dict__.update(refs)
        self.copies = Copies(self.sems)
        self.width = self.hidden_in.shape[1]
        self.inner = self.wup.shape[2]
        self.pairs = self.width // LANES
        self.stages = self.inner // (2 * CHUNK)
        self.pair_sems = self.copies.take(self.pairs)
        self.chunk_sems = [self.copies.take(self.stages) for _ in range(3)]

    def fetch(self, *names):
        loads = [self.copies.load(getattr(self, name), getattr(self, f"{name}_v")) for name in names]
        for name in names:
            setattr(self, name, getattr(self, f"{name}_v"))
        return loads

    def lanes_of(self, pair, part):
        return pl.ds(pl.multiple_of(part * self.width + pair * LANES, LANES), LANES)

    def stage(self, i):
        return pl.ds(pl.multiple_of(i * 2 * CHUNK, 2 * CHUNK), 2 * CHUNK)

    def build_bias(self, table_loads):
        for load in table_loads:
            load.wait()
        span = self.buckets.shape[1]
        bucket_ids = lax.broadcasted_iota(jnp.int32, (self.table.shape[2], span), 0)
        hot = (bucket_ids == self.buckets[...]).astype(F32)
        table = jnp.concatenate([self.table[head] for head in range(self.table.shape[0])], 0)
        values = lax.dot_general(
            table, hot, (((1,), (0,)), ((), ())), precision=highest, preferred_element_type=F32
        )
        self.values_v[:, :span] = values
        self.values_v[:, span:] = jnp.zeros((values.shape[0], SPAN - span), F32)

        def one_head(head, carry):
            wide = jnp.broadcast_to(self.values_v[pl.ds(head, 1), :], (TILE, SPAN))
            self.bias_v[head] = pltpu.roll(wide, 1, 1, stride=1, stride_axis=0)
            return carry

        lax.fori_loop(0, values.shape[0], one_head, 0)
        self.copies.store(self.bias_v, self.bias)


    def rows(self, block):
        return pl.ds(block * BLOCK, BLOCK)

    def forward(self, block, keep, built, also=()):
        copies = self.copies
        rows = self.rows(block)
        table_loads = [] if built else self.fetch("table", "buckets")
        load_x = copies.load(self.hidden_in.at[rows] if keep else self.received, self.x_v)
        small = self.fetch("segments", "padding", "gain1", "shift1", "gain2", "shift2")
        width = self.width
        loads = [
            copies.load(self.wqkv.at[0, :, pl.ds(c, width)], self.wqkv_v.at[:, pl.ds(c, width)])
            for c in range(0, 3 * width, width)
        ]
        if not built:
            self.build_bias(table_loads)
        load_x.wait()

        def load_bias(pair):
            heads = pl.ds(2 * pair, 2)
            return pltpu.make_async_copy(self.bias.at[heads], self.bias_v.at[heads], self.sems.at[self.pair_sems + pair])

        for i, c in enumerate(range(0, 3 * width, width)):
            loads[i].wait()
            if built and i == 2:
                for pair in range(self.pairs):
                    load_bias(pair).start()
            self.qkv_v[:, c : c + width] = dot_nn(self.x_v[...], self.wqkv_v[:, c : c + width]).astype(BF16)
        copies.store(self.x_v, self.xin.at[rows])
        copies.store(self.qkv_v, self.qkv.at[rows], keep)
        weights_sem = self.sems.at[copies.take()]
        later_loads = [
            pltpu.make_async_copy(source.at[0], target, self.sems.at[copies.take()])
            for source, target in ((self.wout, self.wout_v), (self.wup, self.wup_v), (self.wdown, self.wdown_v))
        ]

        def own(pair, part, which):
            both = self.qkv_v[:, self.lanes_of(pair, part)]
            return jnp.where(half_mask(which, both.shape), both, jnp.zeros_like(both))

        for load in small:
            load.wait()
        at = block * BLOCK
        single = self.segments[:, at + TILE : at + TILE + 1] == self.segments[:, at : at + 1]
        padding = self.padding[:, block * BLOCK : (block + 1) * BLOCK]
        tile_of = lax.broadcasted_iota(jnp.int32, (1, BLOCK), 1) // TILE
        shut = [
            jnp.where((padding == 1) & (single | (tile_of == tile)), 0.0, mask_fill) for tile in range(BLOCK // TILE)
        ]
        row_id = lax.broadcasted_iota(jnp.int32, (TILE, TILE), 0)
        diagonal = row_id == lax.broadcasted_iota(jnp.int32, (TILE, TILE), 1)

        def bias_rows(head, tile):
            at = BLOCK - tile * TILE
            rows = self.bias_v[head, :, at : at + BLOCK]
            masked = rows + shut[tile]
            own = slice(tile * TILE, (tile + 1) * TILE)
            parts = [masked[:, : own.start], jnp.where(diagonal, rows[:, own], masked[:, own]), masked[:, own.stop :]]
            return jnp.concatenate([part for part in parts if part.shape[1]], 1)

        def weigh(pair, which):
            head = 2 * pair + which
            k_own = own(pair, 1, which)
            for r in range(0, BLOCK, 2 * TILE):
                q_rows = self.qkv_v[r : r + 2 * TILE, self.lanes_of(pair, 0)] * jnp.asarray(score_scale, BF16)
                tiles = [bias_rows(head, tile) for tile in range(r // TILE, r // TILE + 2)]
                logits = dot_nt(q_rows, k_own) + jnp.concatenate(tiles, 0)
                raised = jnp.exp(logits - jnp.max(logits, -1, keepdims=True))
                share = pl.reciprocal(jnp.sum(raised, -1, keepdims=True), approx=True)
                self.weights_v[head, r : r + 2 * TILE, :] = (raised * share).astype(BF16)

        def head_pair(pair, carry):
            if built:
                load_bias(pair).wait()

            @pl.when(pair == 2)
            def _():
                for load in (*later_loads, *also):
                    load.start()

            weigh(pair, 0)
            context = dot_nn(self.weights_v[2 * pair], own(pair, 2, 0))
            weigh(pair, 1)
            context += dot_nn(self.weights_v[2 * pair + 1], own(pair, 2, 1))
            self.ctx_v[:, self.lanes_of(pair, 0)] = context.astype(BF16)
            if keep:
                heads = pl.ds(2 * pair, 2)
                pltpu.make_async_copy(self.weights_v.at[heads], self.weights.at[block, heads], weights_sem).start()
            return carry

        lax.fori_loop(0, self.pairs, head_pair, 0)
        if keep:
            copies.stores.append(pltpu.make_async_copy(self.weights_v, self.weights.at[block], weights_sem))
        copies.store(self.ctx_v, self.ctx.at[rows])
        load_out, load_up, load_down = later_loads
        load_out.wait()
        self.acc_v[...] = dot_nn(self.ctx_v[...], self.wout_v[...])
        for r in range(0, BLOCK, 64):
            tile = slice(r, r + 64)
            form, scale = normal_parts(self.acc_v[tile, :] + self.x_v[tile, :].astype(F32))
            normed = form * self.gain1[...] + self.shift1[...]
            self.form1_v[tile, :] = form
            self.scale1_v[tile, :] = scale
            self.acc_v[tile, :] = normed
            self.low1_v[tile, :] = normed.astype(BF16)
        copies.store(self.form1_v, self.form1.at[rows], keep)
        copies.store(self.scale1_v, self.scale1.at[rows], keep)
        copies.store(self.low1_v, self.low1.at[rows])
        load_up.wait()
        load_down.wait()
        act_sem = self.sems.at[copies.take()]
        slope_sem = self.sems.at[copies.take()]

        def two_chunks(i, carry):
            span = self.stage(i)
            active, grade = gelu_parts(dot_nn(self.low1_v[...], self.wup_v[:, span]))
            active = active.astype(BF16)
            self.act_v[:, span] = active
            self.slope_v[:, span] = grade.astype(BF16)
            self.acc_v[...] += dot_nn(active, self.wdown_v[span, :])
            pltpu.make_async_copy(self.act_v.at[:, span], self.act.at[rows, span], act_sem).start()
            if keep:
                pltpu.make_async_copy(self.slope_v.at[:, span], self.slope.at[rows, span], slope_sem).start()
            return carry

        lax.fori_loop(0, self.stages, two_chunks, 0)
        copies.stores.append(pltpu.make_async_copy(self.act_v, self.act.at[rows], act_sem))
        if keep:
            copies.stores.append(pltpu.make_async_copy(self.slope_v, self.slope.at[rows], slope_sem))
        for r in range(0, BLOCK, 64):
            tile = slice(r, r + 64)
            form, scale = normal_parts(self.acc_v[tile, :])
            self.form2_v[tile, :] = form
            self.scale2_v[tile, :] = scale
            self.out_v[tile, :] = (form * self.gain2[...] + self.shift2[...]).astype(BF16)
        copies.store(self.out_v, self.send, keep)
        copies.store(self.out_v, self.out.at[rows])
        copies.store(self.form2_v, self.form2.at[rows], keep)
        copies.store(self.scale2_v, self.scale2.at[rows], keep)


    def chunk_loads(self, i, rows):
        span = self.stage(i)
        return [
            pltpu.make_async_copy(source, target, self.sems.at[self.chunk_sems[k] + i])
            for k, (source, target) in enumerate(
                (
                    (self.wdown.at[0, span], self.wdown_v.at[span]),
                    (self.slope.at[rows, span], self.slope_v.at[:, span]),
                    (self.wup.at[0, :, span], self.wup_v.at[:, span]),
                )
            )
        ]

    def norm_sums(self, source, form_ref, sums_ref):
        gain_sum = jnp.zeros((1, self.width), F32)
        shift_sum = jnp.zeros((1, self.width), F32)
        for r in range(0, BLOCK, 64):
            grad_rows, form = source[r : r + 64, :].astype(F32), form_ref[r : r + 64, :]
            gain_sum += jnp.sum(grad_rows * form, 0, keepdims=True)
            shift_sum += jnp.sum(grad_rows, 0, keepdims=True)
        sums_ref[...] = jnp.zeros(sums_ref.shape, F32)
        sums_ref[0:1, :] = gain_sum
        sums_ref[1:2, :] = shift_sum

    def norm_back(self, block):
        for r in range(0, BLOCK, 64):
            tile = slice(r, r + 64)
            grad_rows = self.g_v[tile, :].astype(F32) * self.gain2[...]
            grad_outer = norm_backward(grad_rows, self.form2_v[tile, :], self.scale2_v[tile, :])
            self.acc_v[tile, :] = grad_outer
            self.outer_v[tile, :] = grad_outer.astype(BF16)
        self.copies.store(self.outer_v, self.outer_low.at[self.rows(block)])

    def norm_sums_2(self, block):
        self.norm_sums(self.g_v, self.form2_v, self.sums2_v)
        self.copies.store(self.sums2_v, self.sums2.at[block])

    def ffn_back(self, block, staged=False, middle_loads=()):
        copies = self.copies
        rows = self.rows(block)
        hidden_sem = self.sems.at[copies.take()]

        def two_chunks(i, carry):
            span = self.stage(i)
            if staged:
                load_down, load_slope, load_up = self.chunk_loads(i, rows)
                load_down.wait()
                load_slope.wait()

                @pl.when(i + 1 < self.stages)
                def _():
                    for load in self.chunk_loads(i + 1, rows)[:2]:
                        load.start()

            grad_active = dot_nt(self.outer_v[...], self.wdown_v[span, :])
            hidden = (grad_active * self.slope_v[:, span].astype(F32)).astype(BF16)
            self.slope_v[:, span] = hidden
            if staged:
                load_up.wait()

                @pl.when(i + 1 < self.stages)
                def _():
                    self.chunk_loads(i + 1, rows)[2].start()

            self.acc_v[...] += dot_nt(hidden, self.wup_v[:, span])
            pltpu.make_async_copy(self.slope_v.at[:, span], self.hidden_low.at[rows, span], hidden_sem).start()
            return carry

        lax.fori_loop(0, self.stages, two_chunks, 0)
        copies.stores.append(pltpu.make_async_copy(self.slope_v, self.hidden_low.at[rows], hidden_sem))
        for load in middle_loads:
            load.wait()
        self.norm_sums(self.acc_v, self.form1_v, self.sums1_v)
        for r in range(0, BLOCK, 64):
            tile = slice(r, r + 64)
            grad_residual = norm_backward(
                self.acc_v[tile, :] * self.gain1[...], self.form1_v[tile, :], self.scale1_v[tile, :]
            )
            self.acc_v[tile, :] = grad_residual
            self.residual_low_v[tile, :] = grad_residual.astype(BF16)
        copies.store(self.residual_low_v, self.residual_low.at[rows])
        copies.store(self.sums1_v, self.sums1.at[block])

    def attn_back(self, block, next_loads=None, load_in=()):
        copies = self.copies
        rows = self.rows(block)
        self.dctx_v[...] = dot_nt(self.residual_low_v[...], self.wout_v[...]).astype(BF16)
        self.fold_v[:, :, 0:TILE] = jnp.zeros((2, TILE, TILE), F32)

        def head_pair(pair, carry):
            def lanes_of(part):
                return self.lanes_of(pair, part)

            if next_loads is not None:
                next_loads(pair)
            q_pair, k_pair, v_pair = (self.qkv_v[:, lanes_of(part)] for part in range(3))
            grad_pair = self.dctx_v[:, lanes_of(0)]
            crossed = grad_pair.astype(F32) * self.ctx_v[:, lanes_of(0)].astype(F32)
            masks = [half_mask(which, k_pair.shape) for which in range(2)]

            def own(both, which):
                return jnp.where(masks[which], both, jnp.zeros_like(both))

            for which in range(2):
                self.square_v[which] = dot_nt(grad_pair, own(v_pair, which))
            q_grad = k_grad = v_grad = 0.0
            for which in range(2):
                head = 2 * pair + which
                delta = jnp.sum(own(crossed, which), -1, keepdims=True)
                for r in range(0, BLOCK, 64):
                    tile = slice(r, r + 64)
                    score_grad = (
                        self.weights_v[head, tile, :].astype(F32) * (self.square_v[which, tile, :] - delta[tile, :])
                    ).astype(BF16)
                    self.half_v[which, tile, :] = score_grad
                    at = BLOCK - r // TILE * TILE
                    wide = score_grad.astype(F32)
                    half = slice(r % TILE, r % TILE + 64)
                    if r < TILE:
                        self.fold_v[which, half, at : at + BLOCK] = wide
                    else:
                        self.fold_v[which, half, at : at + TILE] = wide[:, :TILE]
                        self.fold_v[which, half, at + TILE : at + BLOCK] += wide[:, TILE:]
                v_grad += dot_tn(self.weights_v[head], own(grad_pair, which))
                q_grad += dot_nn(self.half_v[which], own(k_pair, which))
                k_grad += dot_tn(self.half_v[which], own(q_pair, which))
                folded = self.fold_v[which]
                size = TILE // 2
                while size >= 8:
                    folded = folded[:size, :] + pltpu.roll(folded[size:, :], SPAN - size, 1)
                    size //= 2
                self.eighth_v[head] = folded
            self.qkv_v[:, lanes_of(0)] = (q_grad * score_scale).astype(BF16)
            self.qkv_v[:, lanes_of(1)] = (k_grad * score_scale).astype(BF16)
            self.qkv_v[:, lanes_of(2)] = v_grad.astype(BF16)
            return carry

        lax.fori_loop(0, self.pairs, head_pair, 0)
        copies.store(self.eighth_v, self.offsets.at[block])
        copies.store(self.qkv_v, self.projected.at[rows])
        for load in load_in:
            load.wait()
        self.grad_v[...] = (self.acc_v[...] + dot_nt(self.qkv_v[...], self.wqkv_v[...])).astype(BF16)
        copies.store(self.grad_v, self.send)
        copies.store(self.grad_v, self.input_grad.at[rows])


    def do_forward(self, block):
        self.forward(block, True, block > 0)

    def do_bias(self, block):
        self.build_bias(self.fetch("table", "buckets"))

    def do_both(self, block):
        load = pltpu.make_async_copy(self.out_grad.at[self.rows(block)], self.g_v, self.sems.at[self.copies.take()])
        self.forward(block, False, True, [load])
        load.wait()
        self.norm_back(block)
        self.ffn_back(block)
        self.norm_sums_2(block)
        self.attn_back(block)

    def do_back(self, block):
        rows = self.rows(block)
        loads = [
            self.copies.load(source, target)
            for source, target in (
                (self.received, self.g_v),
                (self.form2.at[rows], self.form2_v),
                (self.scale2.at[rows], self.scale2_v),
                (self.slope.at[rows], self.slope_v),
                (self.wdown.at[0], self.wdown_v),
                (self.wup.at[0], self.wup_v),
                (self.form1.at[rows], self.form1_v),
                (self.scale1.at[rows], self.scale1_v),
                (self.qkv.at[rows], self.qkv_v),
                (self.weights.at[block], self.weights_v),
                (self.ctx.at[rows], self.ctx_v),
                (self.wout.at[0], self.wout_v),
                (self.wqkv.at[0], self.wqkv_v),
            )
        ]
        for load in loads + self.fetch("gain1", "gain2"):
            load.wait()
        self.norm_back(block)
        self.ffn_back(block)
        self.norm_sums_2(block)
        self.attn_back(block)

    def do_ffn_back(self, block):
        rows = self.rows(block)
        loads = [
            self.copies.load(source, target)
            for source, target in (
                (self.received, self.g_v),
                (self.form2.at[rows], self.form2_v),
                (self.scale2.at[rows], self.scale2_v),
            )
        ]
        loads += self.fetch("gain1", "gain2")
        for load in self.chunk_loads(0, rows)[:2]:
            load.start()
        for load in loads:
            load.wait()
        self.chunk_loads(0, rows)[2].start()
        middle = [
            self.copies.load(self.form1.at[rows], self.form1_v),
            self.copies.load(self.scale1.at[rows], self.scale1_v),
        ]
        self.norm_back(block)
        self.norm_sums_2(block)
        self.ffn_back(block, True, middle)
        self.copies.store(self.acc_v, self.residual)

    def do_attn_back(self, block):
        rows = self.rows(block)
        loads = [
            self.copies.load(source, target)
            for source, target in ((self.residual_low.at[rows], self.residual_low_v), (self.wout.at[0], self.wout_v))
        ]
        first = self.copies.take(5 * self.pairs)

        def pair_loads(pair):
            heads = pl.ds(2 * pair, 2)
            sources = [(self.weights.at[block, heads], self.weights_v.at[heads])]
            for source, target, parts in ((self.qkv, self.qkv_v, 3), (self.ctx, self.ctx_v, 1)):
                for part in range(parts):
                    lanes = self.lanes_of(pair, part)
                    sources.append((source.at[rows, lanes], target.at[:, lanes]))
            return [
                pltpu.make_async_copy(source, target, self.sems.at[first + 5 * pair + k])
                for k, (source, target) in enumerate(sources)
            ]

        for pair in range(2):
            for load in pair_loads(pair):
                load.start()
        for load in loads:
            load.wait()
        last = [
            pltpu.make_async_copy(source, target, self.sems.at[self.copies.take()])
            for source, target in ((self.wqkv.at[0], self.wqkv_v), (self.residual, self.acc_v))
        ]

        def next_loads(pair):
            for load in pair_loads(pair):
                load.wait()

            @pl.when(pair + 2 < self.pairs)
            def _():
                for load in pair_loads(pair + 2):
                    load.start()

            @pl.when(pair == self.pairs - 3)
            def _():
                for load in last:
                    load.start()

        self.attn_back(block, next_loads, last)


def layer_kernel(work, phase_on, block, ins, outs, scratch, after_count, kept_count, *refs):
    refs_in, refs = refs[: len(ins)], refs[len(ins) + after_count + kept_count :]
    named = dict(zip(ins, refs_in)) | dict(zip(outs, refs)) | dict(zip(scratch, refs[len(outs) :]))

    @pl.when(named["phase"][0] == phase_on)
    def _():
        layer = Layer(named)
        getattr(layer, f"do_{work}")(block)
        layer.copies.finish()


def layer_step(work, phase_on, block, values, afters, kept, kept_shapes, scratch):
    specs = [SMEM] + [ANY] * (len(values) - 1)
    names = list(scratch)
    kept = list(kept) if kept is not None else []
    sent = jax.ShapeDtypeStruct((BLOCK, values[2].shape[1]), BF16)
    if work == "bias":
        names = ["values_v", "bias_v", "table_v", "buckets_v"]
    count = len(values) + len(afters)
    results = pl.pallas_call(
        functools.partial(
            layer_kernel, work, phase_on, block, INS, KEPT + ("send",), names + ["sems"], len(afters), len(kept)
        ),
        out_shape=list(kept_shapes) + [sent],
        in_specs=specs + [ANY] * (len(afters) + len(kept)),
        out_specs=[ANY] * (len(kept_shapes) + 1),
        scratch_shapes=[pltpu.VMEM(*scratch[name]) for name in names] + [pltpu.SemaphoreType.DMA((96,))],
        input_output_aliases={count + i: i for i in range(len(kept))},
        compiler_params=pltpu.CompilerParams(vmem_limit_bytes=VMEM_BYTES),
        name=f"{work}_{phase_on}_{block}",
    )(*values, *afters, *kept)
    return dict(zip(KEPT, results)), results[-1]


def pack_kernel(ways, buckets_ref, offsets_ref, sums1_ref, sums2_ref, *refs):
    out_ref, turn_v = refs[-2:]
    row_of = lax.broadcasted_iota(jnp.int32, (8, SPAN), 0)
    lines = []
    for head in range(offsets_ref.shape[1]):
        eighth = offsets_ref[0, head] + offsets_ref[1, head]
        for size in (4, 2, 1):
            eighth = jnp.where((row_of & size) != 0, pltpu.roll(eighth, SPAN - size, 1), eighth)
        lines.append(jnp.sum(eighth, 0, keepdims=True))
    lines += [jnp.zeros((1, SPAN), F32)] * (NORM_LANE - len(lines))
    sums = pltpu.roll(jnp.concatenate(lines, 0), SPAN - 1, 1)
    span = buckets_ref.shape[1]
    buckets, depth = out_ref.shape[0] // 3, out_ref.shape[0] // ways
    share = buckets // ways
    bucket_ids = lax.broadcasted_iota(jnp.int32, (buckets, span), 0)
    hot = (bucket_ids == buckets_ref[...]).astype(F32)
    table = lax.dot_general(
        hot, sums[:, :span], (((1,), (1,)), ((), ())), precision=highest, preferred_element_type=F32
    ).astype(BF16)
    turn_v[...] = jnp.zeros(turn_v.shape, F32)
    for i, ref in enumerate((sums1_ref, sums2_ref)):
        at = NORM_LANE + 2 * i
        turn_v[at : at + 2, :] = ref[0, 0:2, :] + ref[1, 0:2, :]
    out_ref[...] = turn_v[...].T.astype(BF16)
    for i in range(ways):
        out_ref[i * depth : i * depth + share, 0:NORM_LANE] = table[i * share : (i + 1) * share, :]


def packed(ways, buckets, offset_buckets, kept, afters):
    width = kept["sums1"].shape[2]
    depth, share = width // ways, buckets // ways
    arrays = (offset_buckets, kept["offsets"], kept["sums1"], kept["sums2"])
    if depth % 16 == 0 and share % 16 == 0 and 3 * buckets == width:
        rows = pl.pallas_call(
            functools.partial(pack_kernel, ways),
            out_shape=jax.ShapeDtypeStruct((width, LANES), BF16),
            in_specs=[VMEM] * len(arrays) + [ANY] * len(afters),
            out_specs=VMEM,
            scratch_shapes=[pltpu.VMEM((LANES, width), F32)],
            compiler_params=pltpu.CompilerParams(vmem_limit_bytes=SMALL_VMEM_BYTES),
            name="pack",
        )(*arrays, *afters)
        return rows.reshape(ways, depth, LANES)
    eighths = jnp.sum(kept["offsets"], 0)
    lines = sum(jnp.roll(eighths[:, i, :], -i, 1) for i in range(8))[:, 1:]
    hot = (offset_buckets[0][None, :] == jnp.arange(buckets, dtype=jnp.int32)[:, None]).astype(F32)
    table = jnp.dot(hot, lines.T, precision=highest).reshape(ways, share, -1)
    table = jnp.pad(table, ((0, 0), (0, depth - share), (0, NORM_LANE - table.shape[2])))
    norms = jnp.concatenate([jnp.sum(kept[name], 0)[:2] for name in ("sums1", "sums2")], 0)
    norms = norms.T.reshape(ways, depth, 4)
    rows = jnp.concatenate([table, norms], 2)
    return jnp.pad(rows, ((0, 0), (0, 0), (0, LANES - rows.shape[2]))).astype(BF16)


def halve_kernel(bits, counts, after_count, through_count, me_ref, *refs):
    outs = refs[2 * sum(counts) + after_count + through_count :]
    for i, count in enumerate(counts):
        pieces, refs = [refs[2 * k : 2 * k + 2] for k in range(count)], refs[2 * count :]
        send_ref, rest_ref = outs[2 * i : 2 * i + 2]
        mine = (me_ref[0] >> bits[i]) & 1

        def total(which):
            parts = [
                (kept[0, which, 0, 0] if len(kept.shape) == 6 else kept[0, which, 0]).astype(F32)
                + arrived[0, which, 0].astype(F32)
                for kept, arrived in pieces
            ]
            return jnp.concatenate(parts, 1)

        send_ref[0, 0] = total(1 - mine).astype(send_ref.dtype)
        rest_ref[0, 0] = total(mine)


def join_kernel(kept_ref, arrived_ref, out_ref, qkv_ref, table_ref, *refs):
    norm_refs, turn_v = refs[:-1], refs[-1]
    total = kept_ref[...] + arrived_ref[...].astype(F32)
    wide = out_ref.shape[1]
    out_ref[...] = total[:, :wide]
    qkv_ref[...] = total[:, wide : 4 * wide]
    small = total[:, 4 * wide :]
    turn_v[...] = jnp.zeros(turn_v.shape, F32)
    turn_v[: small.shape[0], :] = small
    turned = turn_v[...].T
    for head in range(table_ref.shape[0]):
        table_ref[head] = turned[head : head + 1, : table_ref.shape[2]]
    for i, ref in enumerate(norm_refs):
        ref[...] = turned[NORM_LANE + i : NORM_LANE + i + 1, : ref.shape[1]]


class Part:
    def __init__(self, whole):
        self.whole = whole
        self.sent = self.of_core(1 - (lax.axis_index(DP) & 1))
        self.arrived = swapped(self.sent, 0)

    def of_core(self, core):
        split = self.whole.reshape((self.whole.shape[0] // 2, 2) + self.whole.shape[1:])
        return lax.dynamic_index_in_dim(split, core, 1, keepdims=False)


def swapped(array, bit):
    count = lax.axis_size(DP)
    return lax.ppermute(array, DP, [(i, i ^ (1 << bit)) for i in range(count)])


class Share:
    def __init__(self, parts, order):
        self.parts = parts
        self.order = order[1:]
        self.left = sorted(order[1:])
        self.depth = parts[0].whole.shape[1]
        self.wide = sum(part.whole.shape[2] for part in parts)
        self.mine = None

    def swap(self, bit, theirs):
        self.left.remove(bit)
        self.sent = theirs
        self.arrived = swapped(theirs, bit)

    def total(self):
        if self.mine is not None:
            return self.mine + self.arrived.astype(F32)
        here = lax.axis_index(DP) & 1
        return jnp.concatenate(
            [part.of_core(here).astype(F32) + part.arrived.astype(F32) for part in self.parts], 2
        )

    def split_at(self):
        bit = self.order[0]
        axis = len(self.left) - 1 - self.left.index(bit)
        return bit, 2**axis, 2 ** (len(self.left) - 1 - axis)

    def halve(self):
        bit, above, below = self.split_at()
        self.order = self.order[1:]
        split = self.total().reshape(above, 2, below, self.depth, self.wide)
        here = (lax.axis_index(DP) >> bit) & 1
        theirs = lax.dynamic_index_in_dim(split, 1 - here, 1, keepdims=False).astype(BF16)
        mine = lax.dynamic_index_in_dim(split, here, 1, keepdims=False)
        self.mine = mine.reshape(-1, self.depth, self.wide)
        self.swap(bit, theirs.reshape(-1, self.depth, self.wide))


def halve_all(me, shares, afters=(), through=()):
    if any(share.depth % 16 for share in shares):
        for share in shares:
            share.halve()
        return through
    ins, in_specs, outs, out_specs, bits, counts = [], [], [], [], [], []
    for share in shares:
        bit, above, below = share.split_at()
        bits.append(bit)

        def halves(wide, b=below):
            return pl.BlockSpec((1, 2, 1, share.depth, wide), lambda i, me: (i // b, 0, i % b, 0, 0))

        if share.mine is None:
            counts.append(len(share.parts))
            for part in share.parts:
                wide = part.whole.shape[2]
                ins.append(part.whole.reshape(above, 2, below, 2, share.depth, wide))
                in_specs.append(
                    pl.BlockSpec(
                        (1, 2, 1, 1, share.depth, wide),
                        lambda i, me, b=below: (i // b, 0, i % b, me[0] & 1, 0, 0),
                    )
                )
                ins.append(part.arrived.reshape(above, 2, below, share.depth, wide))
                in_specs.append(halves(wide))
        else:
            counts.append(1)
            for array in (share.mine, share.arrived):
                ins.append(array.reshape(above, 2, below, share.depth, share.wide))
                in_specs.append(halves(share.wide))
        outs += [
            jax.ShapeDtypeStruct((above, below, share.depth, share.wide), kind) for kind in (BF16, F32)
        ]
        out_specs += [
            pl.BlockSpec((1, 1, share.depth, share.wide), lambda i, me, b=below: (i // b, i % b, 0, 0))
        ] * 2
        steps = above * below
    results = pl.pallas_call(
        functools.partial(halve_kernel, tuple(bits), tuple(counts), len(afters), len(through)),
        grid_spec=pltpu.PrefetchScalarGridSpec(
            num_scalar_prefetch=1,
            grid=(steps,),
            in_specs=in_specs + [ANY] * (len(afters) + len(through)),
            out_specs=out_specs + [ANY] * len(through),
        ),
        out_shape=outs + [jax.ShapeDtypeStruct(array.shape, array.dtype) for array in through],
        input_output_aliases={
            1 + len(ins) + len(afters) + i: len(outs) + i for i in range(len(through))
        },
        compiler_params=pltpu.CompilerParams(vmem_limit_bytes=SMALL_VMEM_BYTES),
        name="halve",
    )(me, *ins, *afters, *through)
    for i, share in enumerate(shares):
        share.order = share.order[1:]
        share.mine = results[2 * i + 1].reshape(-1, share.depth, share.wide)
        share.swap(bits[i], results[2 * i].reshape(-1, share.depth, share.wide))
    return results[len(outs) :]


def joined(share, width, table_shape):
    shapes = [(share.depth, width), (share.depth, 3 * width), table_shape] + [(1, share.depth)] * 4
    return pl.pallas_call(
        join_kernel,
        out_shape=[jax.ShapeDtypeStruct(dims, F32) for dims in shapes],
        in_specs=[VMEM] * 2,
        out_specs=[VMEM] * len(shapes),
        scratch_shapes=[pltpu.VMEM((LANES, LANES), F32)],
        compiler_params=pltpu.CompilerParams(vmem_limit_bytes=SMALL_VMEM_BYTES),
        name="join",
    )(share.mine[0], share.arrived[0])


def passed_along(x, axis, by):
    length = lax.axis_size(axis)
    pairs = [(i, i + by) for i in range(length) if 0 <= i + by < length]
    return lax.ppermute(x, axis, pairs)


def shards(
    hidden_in, out_grad, qkv_weight, out_weight, rel_table, norm1_gain, norm1_bias,
    up_weight, down_weight, norm2_gain, norm2_bias, seg_ids, pad_mask, rel_buckets,
):
    phase = lax.axis_index(PHASE).astype(jnp.int32).reshape(1)
    ways = lax.axis_size(DP)
    slots, width = hidden_in.shape
    inner = up_weight.shape[2]
    buckets, heads = rel_table.shape[1:]

    def shape(dims, kind):
        return jax.ShapeDtypeStruct(dims, kind)

    rows_of = {
        "xin": (width, BF16), "qkv": (3 * width, BF16), "ctx": (width, BF16), "form1": (width, F32),
        "scale1": (1, F32), "low1": (width, BF16), "slope": (inner, BF16), "act": (inner, BF16),
        "form2": (width, F32), "scale2": (1, F32), "out": (width, BF16),
        "outer_low": (width, BF16), "hidden_low": (inner, BF16), "residual_low": (width, BF16),
        "projected": (3 * width, BF16), "input_grad": (width, BF16),
    }
    kept_shapes = [
        shape((slots, rows_of[name][0]), rows_of[name][1])
        if name in rows_of
        else {
            "weights": shape((MICRO, heads, BLOCK, BLOCK), BF16),
            "sums1": shape((MICRO, 8, width), F32),
            "sums2": shape((MICRO, 8, width), F32),
            "residual": shape((BLOCK, width), F32),
            "offsets": shape((MICRO, heads, 8, SPAN), F32),
            "bias": shape((heads, TILE, SPAN), F32),
        }[name]
        for name in KEPT
    ]
    small = {
        "segments_v": ((1, slots), jnp.int32), "padding_v": ((1, slots), jnp.int32),
        "buckets_v": ((1, rel_buckets.shape[0]), jnp.int32), "table_v": ((heads, 1, buckets), F32),
        "gain1_v": ((1, width), F32), "shift1_v": ((1, width), F32), "gain2_v": ((1, width), F32),
        "shift2_v": ((1, width), F32),
    }
    in_forward = ("qkv", "ctx", "form1", "scale1", "low1", "slope", "act", "form2", "scale2", "out")
    scratch = {f"{name}_v": ((BLOCK, rows_of[name][0]), rows_of[name][1]) for name in in_forward}
    scratch |= small
    scratch |= {
        name: ((BLOCK, width), BF16) for name in ("x_v", "g_v", "outer_v", "residual_low_v", "dctx_v", "grad_v")
    }
    scratch |= {
        "weights_v": ((heads, BLOCK, BLOCK), BF16), "acc_v": ((BLOCK, width), F32), "square_v": ((2, BLOCK, BLOCK), F32),
        "values_v": ((heads, SPAN), F32), "bias_v": ((heads, TILE, SPAN), F32), "sums1_v": ((8, width), F32), "sums2_v": ((8, width), F32),
        "wqkv_v": ((width, 3 * width), BF16), "wout_v": ((width, width), BF16), "wup_v": ((width, inner), BF16),
        "wdown_v": ((inner, width), BF16), "fold_v": ((2, TILE, SPAN), F32), "eighth_v": ((heads, 8, SPAN), F32),
        "half_v": ((2, BLOCK, BLOCK), BF16),
    }

    def step(work, phase_on, block, received, kept, afters=()):
        values = (
            phase, seg_ids[None, :], hidden_in, received, out_grad, rel_table.transpose(2, 0, 1), pad_mask[None, :], rel_buckets[None, :],
            norm1_gain, norm1_bias, norm2_gain, norm2_bias, qkv_weight, out_weight, up_weight, down_weight,
        )
        in_place = None if kept is None else [kept[name] for name in KEPT]
        return layer_step(work, phase_on, block, values, list(afters), in_place, kept_shapes, scratch)

    kept, sent = step("forward", 0, 0, hidden_in, None)
    first = passed_along(sent, PHASE, 1)
    kept, _ = step("bias", 1, 0, hidden_in, kept)
    kept, sent = step("forward", 0, 1, hidden_in, kept)
    second = passed_along(sent, PHASE, 1)
    kept, sent = step("both", 1, 0, first, kept)
    first_back = passed_along(sent, PHASE, -1)
    kept, sent = step("both", 1, 1, second, kept)
    second_back = passed_along(sent, PHASE, -1)
    kept, _ = step("back", 0, 0, first_back, kept)
    kept, _ = step("ffn_back", 0, 1, second_back, kept)

    bits = ways.bit_length() - 1
    near_first = list(range(bits))
    far_first = [0] + list(range(2, bits)) + [1] if bits > 1 else near_first
    me = lax.axis_index(DP).astype(jnp.int32).reshape(1)

    def weight_grad(left, right):
        product = dot_tn(left, right).astype(BF16)
        return product.reshape(ways, product.shape[0] // ways, product.shape[1])

    down = Share([Part(weight_grad(kept["act"], kept["outer_low"]))], near_first)
    up = Share([Part(weight_grad(kept["low1"], kept["hidden_low"]))], far_first)
    out_part = Part(weight_grad(kept["ctx"], kept["residual_low"]))
    halve_all(me, [down])
    halve_all(me, [up])
    kept, _ = step("attn_back", 0, 1, hidden_in, kept, [down.sent, up.sent])
    far_part = Part(weight_grad(kept["xin"], kept["projected"][:, width:]))
    near_part = Part(weight_grad(kept["xin"], kept["projected"][:, :width]))
    halve_all(me, [up, down], [far_part.sent, near_part.sent])
    small_part = Part(packed(ways, buckets, rel_buckets[None, :], kept, [near_part.sent]))
    last = Share([out_part, near_part, far_part, small_part], near_first)
    halve_all(me, [last], [down.sent, up.sent])
    halve_all(me, [last])
    halve_all(me, [up, down], [last.sent])
    while down.order:
        halve_all(me, [up, down])
    while last.order:
        halve_all(me, [last])
    down_share = down.total()[0]
    up_share = up.total()[0]
    out_share, qkv_share, table_share, *norm_shares = joined(last, width, (heads, 1, buckets // ways))
    return (
        kept["out"][None],
        kept["input_grad"][None],
        qkv_share[None],
        out_share[None],
        table_share.transpose(1, 2, 0),
        norm_shares[0],
        norm_shares[1],
        up_share[None],
        down_share[None],
        norm_shares[2],
        norm_shares[3],
    )


def solution(mesh):
    return jax.shard_map(
        shards,
        mesh=mesh,
        in_specs=(
            P(DP, None),
            P(DP, None),
            P(PHASE, None, None),
            P(PHASE, None, None),
            P(PHASE, None, None),
            P(PHASE, None),
            P(PHASE, None),
            P(PHASE, None, None),
            P(PHASE, None, None),
            P(PHASE, None),
            P(PHASE, None),
            P(DP),
            P(DP),
            P(),
        ),
        out_specs=(
            P(PHASE, DP, None),
            P(PHASE, DP, None),
            P(PHASE, DP, None),
            P(PHASE, DP, None),
            P(PHASE, DP, None),
            P(PHASE, DP),
            P(PHASE, DP),
            P(PHASE, DP, None),
            P(PHASE, DP, None),
            P(PHASE, DP),
            P(PHASE, DP),
        ),
        check_vma=False,
    )
```

```python
import functools

import jax
import jax.numpy as jnp
from jax import lax
from jax.experimental import pallas as pl
from jax.experimental.pallas import tpu as pltpu
from jax.sharding import PartitionSpec as P

BLOCK = 512
MICRO = 2
TILE = 128
LANES = 128
CHUNK = 768
SPAN = 2 * BLOCK
VMEM_BYTES = 58 * 1024 * 1024
SMALL_VMEM_BYTES = 20 * 1024 * 1024
NORM_LANE = 16
PHASE, DP = "phase", "dp"

norm_eps = 1e-05
mask_fill = -1000000000.0
score_scale = 0.125
inv_root_two = 0.7071067811865476
inv_root_tau = 0.3989422804014327
log2_e = 1.4426950408889634
highest = lax.Precision.HIGHEST

F32 = jnp.float32
BF16 = jnp.bfloat16
ANY = pl.BlockSpec(memory_space=pl.ANY)
VMEM = pl.BlockSpec(memory_space=pltpu.VMEM)
QUICK = pl.CostEstimate(flops=1, bytes_accessed=1, transcendentals=0)
SMEM = pl.BlockSpec(memory_space=pltpu.SMEM)


def dot_nn(a, b):
    return lax.dot_general(a, b, (((1,), (0,)), ((), ())), preferred_element_type=F32)


def dot_nt(a, b):
    return lax.dot_general(a, b, (((1,), (1,)), ((), ())), preferred_element_type=F32)


def dot_tn(a, b):
    return lax.dot_general(a, b, (((0,), (0,)), ((), ())), preferred_element_type=F32)


def row_mean(rows):
    return jnp.sum(rows, -1, keepdims=True) * (1.0 / rows.shape[-1])


def normal_parts(residual):
    centred = residual - row_mean(residual)
    inv_scale = lax.rsqrt(row_mean(centred * centred) + norm_eps)
    return centred * inv_scale, inv_scale


def norm_backward(grad_rows, normal_form, inv_scale):
    first = row_mean(grad_rows)
    second = row_mean(grad_rows * normal_form)
    return inv_scale * (grad_rows - first - normal_form * second)


def gelu_parts(hidden):
    share = 0.5 + 0.5 * lax.erf(hidden * inv_root_two)
    bell = jnp.exp2(hidden * hidden * (-0.5 * log2_e))
    return hidden * share, share + hidden * bell * inv_root_tau


def half_mask(which, shape):
    lane = lax.broadcasted_iota(jnp.int32, shape, 1)
    return (lane < LANES // 2) if which == 0 else (lane >= LANES // 2)


class Copies:
    def __init__(self, sems):
        self.sems = sems
        self.used = 0
        self.stores = []

    def take(self, count=1):
        self.used += count
        return self.used - count

    def load(self, source, target):
        copy = pltpu.make_async_copy(source, target, self.sems.at[self.take()])
        copy.start()
        return copy

    def store(self, source, target, when=True):
        if when:
            self.stores.append(self.load(source, target))

    def finish(self):
        for copy in self.stores:
            copy.wait()


KEPT = (
    "xin", "qkv", "weights", "ctx", "form1", "scale1", "low1", "slope", "act", "form2", "scale2", "out",
    "bias", "outer_low", "hidden_low", "residual_low", "sums1", "sums2", "residual", "projected", "offsets", "input_grad",
)
INS = (
    "phase", "segments", "hidden_in", "received", "out_grad", "table", "padding", "buckets",
    "gain1", "shift1", "gain2", "shift2",
    "wqkv", "wout", "wup", "wdown",
)


class Layer:
    def __init__(self, refs):
        self.__dict__.update(refs)
        self.copies = Copies(self.sems)
        self.width = self.hidden_in.shape[1]
        self.inner = self.wup.shape[2]
        self.pairs = self.width // LANES
        self.stages = self.inner // (2 * CHUNK)
        self.pair_sems = self.copies.take(self.pairs)
        self.chunk_sems = [self.copies.take(self.stages) for _ in range(3)]

    def fetch(self, *names):
        loads = [self.copies.load(getattr(self, name), getattr(self, f"{name}_v")) for name in names]
        for name in names:
            setattr(self, name, getattr(self, f"{name}_v"))
        return loads

    def lanes_of(self, pair, part):
        return pl.ds(pl.multiple_of(part * self.width + pair * LANES, LANES), LANES)

    def stage(self, i):
        return pl.ds(pl.multiple_of(i * 2 * CHUNK, 2 * CHUNK), 2 * CHUNK)

    def build_bias(self, table_loads):
        for load in table_loads:
            load.wait()
        span = self.buckets.shape[1]
        bucket_ids = lax.broadcasted_iota(jnp.int32, (self.table.shape[2], span), 0)
        hot = (bucket_ids == self.buckets[...]).astype(F32)
        table = jnp.concatenate([self.table[head] for head in range(self.table.shape[0])], 0)
        values = lax.dot_general(
            table, hot, (((1,), (0,)), ((), ())), precision=highest, preferred_element_type=F32
        )
        self.values_v[:, :span] = values
        self.values_v[:, span:] = jnp.zeros((values.shape[0], SPAN - span), F32)

        def one_head(head, carry):
            wide = jnp.broadcast_to(self.values_v[pl.ds(head, 1), :], (TILE, SPAN))
            self.bias_v[head] = pltpu.roll(wide, 1, 1, stride=1, stride_axis=0)
            return carry

        lax.fori_loop(0, values.shape[0], one_head, 0)
        self.copies.store(self.bias_v, self.bias)

    def over_pairs(self, head_pair):
        def two_pairs(i, carry):
            for k in range(2):
                head_pair(2 * i + k, carry)
            return carry

        lax.fori_loop(0, self.pairs // 2, two_pairs, 0)


    def rows(self, block):
        return pl.ds(block * BLOCK, BLOCK)

    def forward(self, block, keep, built, also=()):
        copies = self.copies
        rows = self.rows(block)
        table_loads = [] if built else self.fetch("table", "buckets")
        load_x = copies.load(self.hidden_in.at[rows] if keep else self.received, self.x_v)
        small = self.fetch("segments", "padding", "gain1", "shift1", "gain2", "shift2")
        width = self.width
        loads = [
            copies.load(self.wqkv.at[0, :, pl.ds(c, width)], self.wqkv_v.at[:, pl.ds(c, width)])
            for c in range(0, 3 * width, width)
        ]
        if not built:
            self.build_bias(table_loads)
        load_x.wait()

        def load_bias(pair):
            heads = pl.ds(2 * pair, 2)
            return pltpu.make_async_copy(self.bias.at[heads], self.bias_v.at[heads], self.sems.at[self.pair_sems + pair])

        for i, c in enumerate(range(0, 3 * width, width)):
            loads[i].wait()
            if built and i == 2:
                for pair in range(self.pairs):
                    load_bias(pair).start()
            self.qkv_v[:, c : c + width] = dot_nn(self.x_v[...], self.wqkv_v[:, c : c + width]).astype(BF16)
        copies.store(self.x_v, self.xin.at[rows])
        copies.store(self.qkv_v, self.qkv.at[rows], keep)
        weights_sem = self.sems.at[copies.take()]
        later_loads = [
            pltpu.make_async_copy(source.at[0], target, self.sems.at[copies.take()])
            for source, target in ((self.wout, self.wout_v), (self.wup, self.wup_v), (self.wdown, self.wdown_v))
        ]

        def own(pair, part, which):
            both = self.qkv_v[:, self.lanes_of(pair, part)]
            return jnp.where(half_mask(which, both.shape), both, jnp.zeros_like(both))

        for load in small:
            load.wait()
        at = block * BLOCK
        single = self.segments[:, at + TILE : at + TILE + 1] == self.segments[:, at : at + 1]
        padding = self.padding[:, block * BLOCK : (block + 1) * BLOCK]
        tile_of = lax.broadcasted_iota(jnp.int32, (1, BLOCK), 1) // TILE
        shut = [
            jnp.where((padding == 1) & (single | (tile_of == tile)), 0.0, mask_fill) for tile in range(BLOCK // TILE)
        ]
        row_id = lax.broadcasted_iota(jnp.int32, (TILE, TILE), 0)
        diagonal = row_id == lax.broadcasted_iota(jnp.int32, (TILE, TILE), 1)

        def bias_rows(head, tile):
            at = BLOCK - tile * TILE
            rows = self.bias_v[head, :, at : at + BLOCK]
            masked = rows + shut[tile]
            own = slice(tile * TILE, (tile + 1) * TILE)
            parts = [masked[:, : own.start], jnp.where(diagonal, rows[:, own], masked[:, own]), masked[:, own.stop :]]
            return jnp.concatenate([part for part in parts if part.shape[1]], 1)

        def weigh(pair, which):
            head = 2 * pair + which
            k_own = own(pair, 1, which)
            for r in range(0, BLOCK, 2 * TILE):
                q_rows = self.qkv_v[r : r + 2 * TILE, self.lanes_of(pair, 0)] * jnp.asarray(score_scale, BF16)
                tiles = [bias_rows(head, tile) for tile in range(r // TILE, r // TILE + 2)]
                logits = dot_nt(q_rows, k_own) + jnp.concatenate(tiles, 0)
                raised = jnp.exp(logits - jnp.max(logits, -1, keepdims=True))
                share = pl.reciprocal(jnp.sum(raised, -1, keepdims=True), approx=True)
                self.weights_v[head, r : r + 2 * TILE, :] = (raised * share).astype(BF16)

        def head_pair(pair, carry):
            if built:
                load_bias(pair).wait()

            @pl.when(pair == 2)
            def _():
                for load in (*later_loads, *also):
                    load.start()

            weigh(pair, 0)
            context = dot_nn(self.weights_v[2 * pair], own(pair, 2, 0))
            weigh(pair, 1)
            context += dot_nn(self.weights_v[2 * pair + 1], own(pair, 2, 1))
            self.ctx_v[:, self.lanes_of(pair, 0)] = context.astype(BF16)
            if keep:
                heads = pl.ds(2 * pair, 2)
                pltpu.make_async_copy(self.weights_v.at[heads], self.weights.at[block, heads], weights_sem).start()
            return carry

        self.over_pairs(head_pair)
        if keep:
            copies.stores.append(pltpu.make_async_copy(self.weights_v, self.weights.at[block], weights_sem))
        copies.store(self.ctx_v, self.ctx.at[rows])
        load_out, load_up, load_down = later_loads
        load_out.wait()
        self.acc_v[...] = dot_nn(self.ctx_v[...], self.wout_v[...])
        for r in range(0, BLOCK, 64):
            tile = slice(r, r + 64)
            form, scale = normal_parts(self.acc_v[tile, :] + self.x_v[tile, :].astype(F32))
            normed = form * self.gain1[...] + self.shift1[...]
            self.form1_v[tile, :] = form
            self.scale1_v[tile, :] = scale
            self.acc_v[tile, :] = normed
            self.low1_v[tile, :] = normed.astype(BF16)
        copies.store(self.form1_v, self.form1.at[rows], keep)
        copies.store(self.scale1_v, self.scale1.at[rows], keep)
        copies.store(self.low1_v, self.low1.at[rows])
        load_up.wait()
        load_down.wait()
        act_sem = self.sems.at[copies.take()]
        slope_sem = self.sems.at[copies.take()]

        def two_chunks(i, carry):
            span = self.stage(i)
            active, grade = gelu_parts(dot_nn(self.low1_v[...], self.wup_v[:, span]))
            active = active.astype(BF16)
            self.act_v[:, span] = active
            self.slope_v[:, span] = grade.astype(BF16)
            self.acc_v[...] += dot_nn(active, self.wdown_v[span, :])
            pltpu.make_async_copy(self.act_v.at[:, span], self.act.at[rows, span], act_sem).start()
            if keep:
                pltpu.make_async_copy(self.slope_v.at[:, span], self.slope.at[rows, span], slope_sem).start()
            return carry

        lax.fori_loop(0, self.stages, two_chunks, 0)
        copies.stores.append(pltpu.make_async_copy(self.act_v, self.act.at[rows], act_sem))
        if keep:
            copies.stores.append(pltpu.make_async_copy(self.slope_v, self.slope.at[rows], slope_sem))
        for r in range(0, BLOCK, 64):
            tile = slice(r, r + 64)
            form, scale = normal_parts(self.acc_v[tile, :])
            self.form2_v[tile, :] = form
            self.scale2_v[tile, :] = scale
            self.out_v[tile, :] = (form * self.gain2[...] + self.shift2[...]).astype(BF16)
        copies.store(self.out_v, self.send, keep)
        copies.store(self.out_v, self.out.at[rows])
        copies.store(self.form2_v, self.form2.at[rows], keep)
        copies.store(self.scale2_v, self.scale2.at[rows], keep)


    def chunk_loads(self, i, rows):
        span = self.stage(i)
        return [
            pltpu.make_async_copy(source, target, self.sems.at[self.chunk_sems[k] + i])
            for k, (source, target) in enumerate(
                (
                    (self.wdown.at[0, span], self.wdown_v.at[span]),
                    (self.slope.at[rows, span], self.slope_v.at[:, span]),
                    (self.wup.at[0, :, span], self.wup_v.at[:, span]),
                )
            )
        ]

    def norm_sums(self, source, form_ref, sums_ref):
        gain_sum = jnp.zeros((1, self.width), F32)
        shift_sum = jnp.zeros((1, self.width), F32)
        for r in range(0, BLOCK, 64):
            grad_rows, form = source[r : r + 64, :].astype(F32), form_ref[r : r + 64, :]
            gain_sum += jnp.sum(grad_rows * form, 0, keepdims=True)
            shift_sum += jnp.sum(grad_rows, 0, keepdims=True)
        sums_ref[...] = jnp.zeros(sums_ref.shape, F32)
        sums_ref[0:1, :] = gain_sum
        sums_ref[1:2, :] = shift_sum

    def norm_back(self, block):
        for r in range(0, BLOCK, 64):
            tile = slice(r, r + 64)
            grad_rows = self.g_v[tile, :].astype(F32) * self.gain2[...]
            grad_outer = norm_backward(grad_rows, self.form2_v[tile, :], self.scale2_v[tile, :])
            self.acc_v[tile, :] = grad_outer
            self.outer_v[tile, :] = grad_outer.astype(BF16)
        self.copies.store(self.outer_v, self.outer_low.at[self.rows(block)])

    def norm_sums_2(self, block):
        self.norm_sums(self.g_v, self.form2_v, self.sums2_v)
        self.copies.store(self.sums2_v, self.sums2.at[block])

    def ffn_back(self, block, staged=False, middle_loads=()):
        copies = self.copies
        rows = self.rows(block)
        hidden_sem = self.sems.at[copies.take()]

        def two_chunks(i, carry):
            span = self.stage(i)
            if staged:
                load_down, load_slope, load_up = self.chunk_loads(i, rows)
                load_down.wait()
                load_slope.wait()

                @pl.when(i + 1 < self.stages)
                def _():
                    for load in self.chunk_loads(i + 1, rows)[:2]:
                        load.start()

            grad_active = dot_nt(self.outer_v[...], self.wdown_v[span, :])
            hidden = (grad_active * self.slope_v[:, span].astype(F32)).astype(BF16)
            self.slope_v[:, span] = hidden
            if staged:
                load_up.wait()

                @pl.when(i + 1 < self.stages)
                def _():
                    self.chunk_loads(i + 1, rows)[2].start()

            self.acc_v[...] += dot_nt(hidden, self.wup_v[:, span])
            pltpu.make_async_copy(self.slope_v.at[:, span], self.hidden_low.at[rows, span], hidden_sem).start()
            return carry

        lax.fori_loop(0, self.stages, two_chunks, 0)
        copies.stores.append(pltpu.make_async_copy(self.slope_v, self.hidden_low.at[rows], hidden_sem))
        for load in middle_loads:
            load.wait()
        self.norm_sums(self.acc_v, self.form1_v, self.sums1_v)
        for r in range(0, BLOCK, 64):
            tile = slice(r, r + 64)
            grad_residual = norm_backward(
                self.acc_v[tile, :] * self.gain1[...], self.form1_v[tile, :], self.scale1_v[tile, :]
            )
            self.acc_v[tile, :] = grad_residual
            self.residual_low_v[tile, :] = grad_residual.astype(BF16)
        copies.store(self.residual_low_v, self.residual_low.at[rows])
        copies.store(self.sums1_v, self.sums1.at[block])

    def attn_back(self, block, next_loads=None, load_in=()):
        copies = self.copies
        rows = self.rows(block)
        self.dctx_v[...] = dot_nt(self.residual_low_v[...], self.wout_v[...]).astype(BF16)
        self.fold_v[:, :, 0:TILE] = jnp.zeros((2, TILE, TILE), F32)

        def head_pair(pair, carry):
            def lanes_of(part):
                return self.lanes_of(pair, part)

            if next_loads is not None:
                next_loads(pair)
            q_pair, k_pair, v_pair = (self.qkv_v[:, lanes_of(part)] for part in range(3))
            grad_pair = self.dctx_v[:, lanes_of(0)]
            crossed = grad_pair.astype(F32) * self.ctx_v[:, lanes_of(0)].astype(F32)
            masks = [half_mask(which, k_pair.shape) for which in range(2)]

            def own(both, which):
                return jnp.where(masks[which], both, jnp.zeros_like(both))

            for which in range(2):
                self.square_v[which] = dot_nt(grad_pair, own(v_pair, which))
            q_grad = k_grad = v_grad = 0.0
            for which in range(2):
                head = 2 * pair + which
                delta = jnp.sum(own(crossed, which), -1, keepdims=True)
                for r in range(0, BLOCK, 64):
                    tile = slice(r, r + 64)
                    score_grad = (
                        self.weights_v[head, tile, :].astype(F32) * (self.square_v[which, tile, :] - delta[tile, :])
                    ).astype(BF16)
                    self.half_v[which, tile, :] = score_grad
                    at = BLOCK - r // TILE * TILE
                    wide = score_grad.astype(F32)
                    half = slice(r % TILE, r % TILE + 64)
                    if r < TILE:
                        self.fold_v[which, half, at : at + BLOCK] = wide
                    else:
                        self.fold_v[which, half, at : at + TILE] = wide[:, :TILE]
                        self.fold_v[which, half, at + TILE : at + BLOCK] += wide[:, TILE:]
                v_grad += dot_tn(self.weights_v[head], own(grad_pair, which))
                q_grad += dot_nn(self.half_v[which], own(k_pair, which))
                k_grad += dot_tn(self.half_v[which], own(q_pair, which))
                folded = self.fold_v[which]
                size = TILE // 2
                while size >= 8:
                    folded = folded[:size, :] + pltpu.roll(folded[size:, :], SPAN - size, 1)
                    size //= 2
                self.eighth_v[head] = folded
            self.qkv_v[:, lanes_of(0)] = (q_grad * score_scale).astype(BF16)
            self.qkv_v[:, lanes_of(1)] = (k_grad * score_scale).astype(BF16)
            self.qkv_v[:, lanes_of(2)] = v_grad.astype(BF16)
            return carry

        self.over_pairs(head_pair)
        copies.store(self.eighth_v, self.offsets.at[block])
        copies.store(self.qkv_v, self.projected.at[rows])
        for load in load_in:
            load.wait()
        self.grad_v[...] = (self.acc_v[...] + dot_nt(self.qkv_v[...], self.wqkv_v[...])).astype(BF16)
        copies.store(self.grad_v, self.send)
        copies.store(self.grad_v, self.input_grad.at[rows])


    def do_forward(self, block):
        self.forward(block, True, block > 0)

    def do_bias(self, block):
        self.build_bias(self.fetch("table", "buckets"))

    def do_both(self, block):
        load = pltpu.make_async_copy(self.out_grad.at[self.rows(block)], self.g_v, self.sems.at[self.copies.take()])
        self.forward(block, False, True, [load])
        load.wait()
        self.norm_back(block)
        self.ffn_back(block)
        self.norm_sums_2(block)
        self.attn_back(block)

    def do_back(self, block):
        rows = self.rows(block)
        loads = [
            self.copies.load(source, target)
            for source, target in (
                (self.received, self.g_v),
                (self.form2.at[rows], self.form2_v),
                (self.scale2.at[rows], self.scale2_v),
                (self.slope.at[rows], self.slope_v),
                (self.wdown.at[0], self.wdown_v),
                (self.wup.at[0], self.wup_v),
                (self.form1.at[rows], self.form1_v),
                (self.scale1.at[rows], self.scale1_v),
                (self.qkv.at[rows], self.qkv_v),
                (self.weights.at[block], self.weights_v),
                (self.ctx.at[rows], self.ctx_v),
                (self.wout.at[0], self.wout_v),
                (self.wqkv.at[0], self.wqkv_v),
            )
        ]
        for load in loads + self.fetch("gain1", "gain2"):
            load.wait()
        self.norm_back(block)
        self.ffn_back(block)
        self.norm_sums_2(block)
        self.attn_back(block)

    def do_ffn_back(self, block):
        rows = self.rows(block)
        loads = [
            self.copies.load(source, target)
            for source, target in (
                (self.received, self.g_v),
                (self.form2.at[rows], self.form2_v),
                (self.scale2.at[rows], self.scale2_v),
            )
        ]
        loads += self.fetch("gain1", "gain2")
        for load in self.chunk_loads(0, rows)[:2]:
            load.start()
        for load in loads:
            load.wait()
        self.chunk_loads(0, rows)[2].start()
        middle = [
            self.copies.load(self.form1.at[rows], self.form1_v),
            self.copies.load(self.scale1.at[rows], self.scale1_v),
        ]
        self.norm_back(block)
        self.norm_sums_2(block)
        self.ffn_back(block, True, middle)
        self.copies.store(self.acc_v, self.residual)

    def do_attn_back(self, block):
        rows = self.rows(block)
        loads = [
            self.copies.load(source, target)
            for source, target in ((self.residual_low.at[rows], self.residual_low_v), (self.wout.at[0], self.wout_v))
        ]
        first = self.copies.take(5 * self.pairs)

        def pair_loads(pair):
            heads = pl.ds(2 * pair, 2)
            sources = [(self.weights.at[block, heads], self.weights_v.at[heads])]
            for source, target, parts in ((self.qkv, self.qkv_v, 3), (self.ctx, self.ctx_v, 1)):
                for part in range(parts):
                    lanes = self.lanes_of(pair, part)
                    sources.append((source.at[rows, lanes], target.at[:, lanes]))
            return [
                pltpu.make_async_copy(source, target, self.sems.at[first + 5 * pair + k])
                for k, (source, target) in enumerate(sources)
            ]

        for pair in range(2):
            for load in pair_loads(pair):
                load.start()
        for load in loads:
            load.wait()
        last = [
            pltpu.make_async_copy(source, target, self.sems.at[self.copies.take()])
            for source, target in ((self.wqkv.at[0], self.wqkv_v), (self.residual, self.acc_v))
        ]

        def next_loads(pair):
            for load in pair_loads(pair):
                load.wait()

            @pl.when(pair + 2 < self.pairs)
            def _():
                for load in pair_loads(pair + 2):
                    load.start()

            @pl.when(pair == self.pairs - 3)
            def _():
                for load in last:
                    load.start()

        self.attn_back(block, next_loads, last)


def layer_kernel(work, phase_on, block, ins, outs, scratch, after_count, kept_count, *refs):
    refs_in, refs = refs[: len(ins)], refs[len(ins) + after_count + kept_count :]
    named = dict(zip(ins, refs_in)) | dict(zip(outs, refs)) | dict(zip(scratch, refs[len(outs) :]))

    @pl.when(named["phase"][0] == phase_on)
    def _():
        layer = Layer(named)
        getattr(layer, f"do_{work}")(block)
        layer.copies.finish()


def layer_step(work, phase_on, block, values, afters, kept, kept_shapes, scratch):
    specs = [SMEM] + [ANY] * (len(values) - 1)
    names = list(scratch)
    kept = list(kept) if kept is not None else []
    sent = jax.ShapeDtypeStruct((BLOCK, values[2].shape[1]), BF16)
    if work == "bias":
        names = ["values_v", "bias_v", "table_v", "buckets_v"]
    count = len(values) + len(afters)
    results = pl.pallas_call(
        functools.partial(
            layer_kernel, work, phase_on, block, INS, KEPT + ("send",), names + ["sems"], len(afters), len(kept)
        ),
        out_shape=list(kept_shapes) + [sent],
        in_specs=specs + [ANY] * (len(afters) + len(kept)),
        out_specs=[ANY] * (len(kept_shapes) + 1),
        scratch_shapes=[pltpu.VMEM(*scratch[name]) for name in names] + [pltpu.SemaphoreType.DMA((96,))],
        input_output_aliases={count + i: i for i in range(len(kept))},
        compiler_params=pltpu.CompilerParams(vmem_limit_bytes=VMEM_BYTES),
        name=f"{work}_{phase_on}_{block}",
    )(*values, *afters, *kept)
    return dict(zip(KEPT, results)), results[-1]


def pack_kernel(ways, buckets_ref, offsets_ref, sums1_ref, sums2_ref, *refs):
    out_ref, turn_v = refs[-2:]
    row_of = lax.broadcasted_iota(jnp.int32, (8, SPAN), 0)
    lines = []
    for head in range(offsets_ref.shape[1]):
        eighth = offsets_ref[0, head] + offsets_ref[1, head]
        for size in (4, 2, 1):
            eighth = jnp.where((row_of & size) != 0, pltpu.roll(eighth, SPAN - size, 1), eighth)
        lines.append(jnp.sum(eighth, 0, keepdims=True))
    lines += [jnp.zeros((1, SPAN), F32)] * (NORM_LANE - len(lines))
    sums = pltpu.roll(jnp.concatenate(lines, 0), SPAN - 1, 1)
    span = buckets_ref.shape[1]
    buckets, depth = out_ref.shape[0] // 3, out_ref.shape[0] // ways
    share = buckets // ways
    bucket_ids = lax.broadcasted_iota(jnp.int32, (buckets, span), 0)
    hot = (bucket_ids == buckets_ref[...]).astype(F32)
    table = lax.dot_general(
        hot, sums[:, :span], (((1,), (1,)), ((), ())), precision=highest, preferred_element_type=F32
    ).astype(BF16)
    turn_v[...] = jnp.zeros(turn_v.shape, F32)
    for i, ref in enumerate((sums1_ref, sums2_ref)):
        at = NORM_LANE + 2 * i
        turn_v[at : at + 2, :] = ref[0, 0:2, :] + ref[1, 0:2, :]
    out_ref[...] = turn_v[...].T.astype(BF16)
    for i in range(ways):
        out_ref[i * depth : i * depth + share, 0:NORM_LANE] = table[i * share : (i + 1) * share, :]


def packed(ways, buckets, offset_buckets, kept, afters):
    width = kept["sums1"].shape[2]
    depth, share = width // ways, buckets // ways
    arrays = (offset_buckets, kept["offsets"], kept["sums1"], kept["sums2"])
    if depth % 16 == 0 and share % 16 == 0 and 3 * buckets == width:
        rows = pl.pallas_call(
            functools.partial(pack_kernel, ways),
            out_shape=jax.ShapeDtypeStruct((width, LANES), BF16),
            in_specs=[VMEM] * len(arrays) + [ANY] * len(afters),
            out_specs=VMEM,
            scratch_shapes=[pltpu.VMEM((LANES, width), F32)],
            compiler_params=pltpu.CompilerParams(vmem_limit_bytes=SMALL_VMEM_BYTES),
            name="pack",
        )(*arrays, *afters)
        return rows.reshape(ways, depth, LANES)
    eighths = jnp.sum(kept["offsets"], 0)
    lines = sum(jnp.roll(eighths[:, i, :], -i, 1) for i in range(8))[:, 1:]
    hot = (offset_buckets[0][None, :] == jnp.arange(buckets, dtype=jnp.int32)[:, None]).astype(F32)
    table = jnp.dot(hot, lines.T, precision=highest).reshape(ways, share, -1)
    table = jnp.pad(table, ((0, 0), (0, depth - share), (0, NORM_LANE - table.shape[2])))
    norms = jnp.concatenate([jnp.sum(kept[name], 0)[:2] for name in ("sums1", "sums2")], 0)
    norms = norms.T.reshape(ways, depth, 4)
    rows = jnp.concatenate([table, norms], 2)
    return jnp.pad(rows, ((0, 0), (0, 0), (0, LANES - rows.shape[2]))).astype(BF16)


def halve_kernel(bits, counts, after_count, through_count, me_ref, *refs):
    outs = refs[2 * sum(counts) + after_count + through_count :]
    for i, count in enumerate(counts):
        pieces, refs = [refs[2 * k : 2 * k + 2] for k in range(count)], refs[2 * count :]
        send_ref, rest_ref = outs[2 * i : 2 * i + 2]
        mine = (me_ref[0] >> bits[i]) & 1

        def total(which):
            parts = [
                (kept[0, which, 0, 0] if len(kept.shape) == 6 else kept[0, which, 0]).astype(F32)
                + arrived[0, which, 0].astype(F32)
                for kept, arrived in pieces
            ]
            return jnp.concatenate(parts, 1)

        send_ref[0, 0] = total(1 - mine).astype(send_ref.dtype)
        rest_ref[0, 0] = total(mine)


def join_kernel(kept_ref, arrived_ref, out_ref, qkv_ref, table_ref, *refs):
    norm_refs, turn_v = refs[:-1], refs[-1]
    total = kept_ref[...] + arrived_ref[...].astype(F32)
    wide = out_ref.shape[1]
    out_ref[...] = total[:, :wide]
    qkv_ref[...] = total[:, wide : 4 * wide]
    small = total[:, 4 * wide :]
    turn_v[...] = jnp.zeros(turn_v.shape, F32)
    turn_v[: small.shape[0], :] = small
    turned = turn_v[...].T
    for head in range(table_ref.shape[0]):
        table_ref[head] = turned[head : head + 1, : table_ref.shape[2]]
    for i, ref in enumerate(norm_refs):
        ref[...] = turned[NORM_LANE + i : NORM_LANE + i + 1, : ref.shape[1]]


class Part:
    def __init__(self, whole):
        self.whole = whole
        self.sent = self.of_core(1 - (lax.axis_index(DP) & 1))
        self.arrived = swapped(self.sent, 0)

    def of_core(self, core):
        split = self.whole.reshape((self.whole.shape[0] // 2, 2) + self.whole.shape[1:])
        return lax.dynamic_index_in_dim(split, core, 1, keepdims=False)


def swapped(array, bit):
    count = lax.axis_size(DP)
    return lax.ppermute(array, DP, [(i, i ^ (1 << bit)) for i in range(count)])


class Share:
    def __init__(self, parts, order):
        self.parts = parts
        self.order = order[1:]
        self.left = sorted(order[1:])
        self.depth = parts[0].whole.shape[1]
        self.wide = sum(part.whole.shape[2] for part in parts)
        self.mine = None

    def swap(self, bit, theirs):
        self.left.remove(bit)
        self.sent = theirs
        self.arrived = swapped(theirs, bit)

    def total(self):
        if self.mine is not None:
            return self.mine + self.arrived.astype(F32)
        here = lax.axis_index(DP) & 1
        return jnp.concatenate(
            [part.of_core(here).astype(F32) + part.arrived.astype(F32) for part in self.parts], 2
        )

    def split_at(self):
        bit = self.order[0]
        axis = len(self.left) - 1 - self.left.index(bit)
        return bit, 2**axis, 2 ** (len(self.left) - 1 - axis)

    def halve(self):
        bit, above, below = self.split_at()
        self.order = self.order[1:]
        split = self.total().reshape(above, 2, below, self.depth, self.wide)
        here = (lax.axis_index(DP) >> bit) & 1
        theirs = lax.dynamic_index_in_dim(split, 1 - here, 1, keepdims=False).astype(BF16)
        mine = lax.dynamic_index_in_dim(split, here, 1, keepdims=False)
        self.mine = mine.reshape(-1, self.depth, self.wide)
        self.swap(bit, theirs.reshape(-1, self.depth, self.wide))


def halve_all(me, shares, afters=(), through=()):
    if any(share.depth % 16 for share in shares):
        for share in shares:
            share.halve()
        return through
    ins, in_specs, outs, out_specs, bits, counts = [], [], [], [], [], []
    for share in shares:
        bit, above, below = share.split_at()
        bits.append(bit)

        def halves(wide, b=below):
            return pl.BlockSpec((1, 2, 1, share.depth, wide), lambda i, me: (i // b, 0, i % b, 0, 0))

        if share.mine is None:
            counts.append(len(share.parts))
            for part in share.parts:
                wide = part.whole.shape[2]
                ins.append(part.whole.reshape(above, 2, below, 2, share.depth, wide))
                in_specs.append(
                    pl.BlockSpec(
                        (1, 2, 1, 1, share.depth, wide),
                        lambda i, me, b=below: (i // b, 0, i % b, me[0] & 1, 0, 0),
                    )
                )
                ins.append(part.arrived.reshape(above, 2, below, share.depth, wide))
                in_specs.append(halves(wide))
        else:
            counts.append(1)
            for array in (share.mine, share.arrived):
                ins.append(array.reshape(above, 2, below, share.depth, share.wide))
                in_specs.append(halves(share.wide))
        outs += [
            jax.ShapeDtypeStruct((above, below, share.depth, share.wide), kind) for kind in (BF16, F32)
        ]
        out_specs += [
            pl.BlockSpec((1, 1, share.depth, share.wide), lambda i, me, b=below: (i // b, i % b, 0, 0))
        ] * 2
        steps = above * below
    results = pl.pallas_call(
        functools.partial(halve_kernel, tuple(bits), tuple(counts), len(afters), len(through)),
        grid_spec=pltpu.PrefetchScalarGridSpec(
            num_scalar_prefetch=1,
            grid=(steps,),
            in_specs=in_specs + [ANY] * (len(afters) + len(through)),
            out_specs=out_specs + [ANY] * len(through),
        ),
        out_shape=outs + [jax.ShapeDtypeStruct(array.shape, array.dtype) for array in through],
        input_output_aliases={
            1 + len(ins) + len(afters) + i: len(outs) + i for i in range(len(through))
        },
        compiler_params=pltpu.CompilerParams(vmem_limit_bytes=SMALL_VMEM_BYTES),
        name="halve",
    )(me, *ins, *afters, *through)
    for i, share in enumerate(shares):
        share.order = share.order[1:]
        share.mine = results[2 * i + 1].reshape(-1, share.depth, share.wide)
        share.swap(bits[i], results[2 * i].reshape(-1, share.depth, share.wide))
    return results[len(outs) :]


def joined(share, width, table_shape):
    shapes = [(share.depth, width), (share.depth, 3 * width), table_shape] + [(1, share.depth)] * 4
    return pl.pallas_call(
        join_kernel,
        out_shape=[jax.ShapeDtypeStruct(dims, F32) for dims in shapes],
        in_specs=[VMEM] * 2,
        out_specs=[VMEM] * len(shapes),
        scratch_shapes=[pltpu.VMEM((LANES, LANES), F32)],
        compiler_params=pltpu.CompilerParams(vmem_limit_bytes=SMALL_VMEM_BYTES),
        name="join",
    )(share.mine[0], share.arrived[0])


def passed_along(x, axis, by):
    length = lax.axis_size(axis)
    pairs = [(i, i + by) for i in range(length) if 0 <= i + by < length]
    return lax.ppermute(x, axis, pairs)


def shards(
    hidden_in, out_grad, qkv_weight, out_weight, rel_table, norm1_gain, norm1_bias,
    up_weight, down_weight, norm2_gain, norm2_bias, seg_ids, pad_mask, rel_buckets,
):
    phase = lax.axis_index(PHASE).astype(jnp.int32).reshape(1)
    ways = lax.axis_size(DP)
    slots, width = hidden_in.shape
    inner = up_weight.shape[2]
    buckets, heads = rel_table.shape[1:]

    def shape(dims, kind):
        return jax.ShapeDtypeStruct(dims, kind)

    rows_of = {
        "xin": (width, BF16), "qkv": (3 * width, BF16), "ctx": (width, BF16), "form1": (width, F32),
        "scale1": (1, F32), "low1": (width, BF16), "slope": (inner, BF16), "act": (inner, BF16),
        "form2": (width, F32), "scale2": (1, F32), "out": (width, BF16),
        "outer_low": (width, BF16), "hidden_low": (inner, BF16), "residual_low": (width, BF16),
        "projected": (3 * width, BF16), "input_grad": (width, BF16),
    }
    kept_shapes = [
        shape((slots, rows_of[name][0]), rows_of[name][1])
        if name in rows_of
        else {
            "weights": shape((MICRO, heads, BLOCK, BLOCK), BF16),
            "sums1": shape((MICRO, 8, width), F32),
            "sums2": shape((MICRO, 8, width), F32),
            "residual": shape((BLOCK, width), F32),
            "offsets": shape((MICRO, heads, 8, SPAN), F32),
            "bias": shape((heads, TILE, SPAN), F32),
        }[name]
        for name in KEPT
    ]
    small = {
        "segments_v": ((1, slots), jnp.int32), "padding_v": ((1, slots), jnp.int32),
        "buckets_v": ((1, rel_buckets.shape[0]), jnp.int32), "table_v": ((heads, 1, buckets), F32),
        "gain1_v": ((1, width), F32), "shift1_v": ((1, width), F32), "gain2_v": ((1, width), F32),
        "shift2_v": ((1, width), F32),
    }
    in_forward = ("qkv", "ctx", "form1", "scale1", "low1", "slope", "act", "form2", "scale2", "out")
    scratch = {f"{name}_v": ((BLOCK, rows_of[name][0]), rows_of[name][1]) for name in in_forward}
    scratch |= small
    scratch |= {
        name: ((BLOCK, width), BF16) for name in ("x_v", "g_v", "outer_v", "residual_low_v", "dctx_v", "grad_v")
    }
    scratch |= {
        "weights_v": ((heads, BLOCK, BLOCK), BF16), "acc_v": ((BLOCK, width), F32), "square_v": ((2, BLOCK, BLOCK), F32),
        "values_v": ((heads, SPAN), F32), "bias_v": ((heads, TILE, SPAN), F32), "sums1_v": ((8, width), F32), "sums2_v": ((8, width), F32),
        "wqkv_v": ((width, 3 * width), BF16), "wout_v": ((width, width), BF16), "wup_v": ((width, inner), BF16),
        "wdown_v": ((inner, width), BF16), "fold_v": ((2, TILE, SPAN), F32), "eighth_v": ((heads, 8, SPAN), F32),
        "half_v": ((2, BLOCK, BLOCK), BF16),
    }

    def step(work, phase_on, block, received, kept, afters=()):
        values = (
            phase, seg_ids[None, :], hidden_in, received, out_grad, rel_table.transpose(2, 0, 1), pad_mask[None, :], rel_buckets[None, :],
            norm1_gain, norm1_bias, norm2_gain, norm2_bias, qkv_weight, out_weight, up_weight, down_weight,
        )
        in_place = None if kept is None else [kept[name] for name in KEPT]
        return layer_step(work, phase_on, block, values, list(afters), in_place, kept_shapes, scratch)

    kept, sent = step("forward", 0, 0, hidden_in, None)
    first = passed_along(sent, PHASE, 1)
    kept, _ = step("bias", 1, 0, hidden_in, kept)
    kept, sent = step("forward", 0, 1, hidden_in, kept)
    second = passed_along(sent, PHASE, 1)
    kept, sent = step("both", 1, 0, first, kept)
    first_back = passed_along(sent, PHASE, -1)
    kept, sent = step("both", 1, 1, second, kept)
    second_back = passed_along(sent, PHASE, -1)
    kept, _ = step("back", 0, 0, first_back, kept)
    kept, _ = step("ffn_back", 0, 1, second_back, kept)

    bits = ways.bit_length() - 1
    near_first = list(range(bits))
    far_first = [0] + list(range(2, bits)) + [1] if bits > 1 else near_first
    me = lax.axis_index(DP).astype(jnp.int32).reshape(1)

    def weight_grad(left, right):
        product = dot_tn(left, right).astype(BF16)
        return product.reshape(ways, product.shape[0] // ways, product.shape[1])

    down = Share([Part(weight_grad(kept["act"], kept["outer_low"]))], near_first)
    up = Share([Part(weight_grad(kept["low1"], kept["hidden_low"]))], far_first)
    out_part = Part(weight_grad(kept["ctx"], kept["residual_low"]))
    halve_all(me, [down])
    halve_all(me, [up])
    kept, _ = step("attn_back", 0, 1, hidden_in, kept, [down.sent, up.sent])
    far_part = Part(weight_grad(kept["xin"], kept["projected"][:, width:]))
    near_part = Part(weight_grad(kept["xin"], kept["projected"][:, :width]))
    halve_all(me, [up, down], [far_part.sent, near_part.sent])
    small_part = Part(packed(ways, buckets, rel_buckets[None, :], kept, [near_part.sent]))
    last = Share([out_part, near_part, far_part, small_part], near_first)
    halve_all(me, [last], [down.sent, up.sent])
    halve_all(me, [last])
    halve_all(me, [up, down], [last.sent])
    while down.order:
        halve_all(me, [up, down])
    while last.order:
        halve_all(me, [last])
    down_share = down.total()[0]
    up_share = up.total()[0]
    out_share, qkv_share, table_share, *norm_shares = joined(last, width, (heads, 1, buckets // ways))
    return (
        kept["out"][None],
        kept["input_grad"][None],
        qkv_share[None],
        out_share[None],
        table_share.transpose(1, 2, 0),
        norm_shares[0],
        norm_shares[1],
        up_share[None],
        down_share[None],
        norm_shares[2],
        norm_shares[3],
    )


def solution(mesh):
    return jax.shard_map(
        shards,
        mesh=mesh,
        in_specs=(
            P(DP, None),
            P(DP, None),
            P(PHASE, None, None),
            P(PHASE, None, None),
            P(PHASE, None, None),
            P(PHASE, None),
            P(PHASE, None),
            P(PHASE, None, None),
            P(PHASE, None, None),
            P(PHASE, None),
            P(PHASE, None),
            P(DP),
            P(DP),
            P(),
        ),
        out_specs=(
            P(PHASE, DP, None),
            P(PHASE, DP, None),
            P(PHASE, DP, None),
            P(PHASE, DP, None),
            P(PHASE, DP, None),
            P(PHASE, DP),
            P(PHASE, DP),
            P(PHASE, DP, None),
            P(PHASE, DP, None),
            P(PHASE, DP),
            P(PHASE, DP),
        ),
        check_vma=False,
    )
```

```python
import functools

import jax
import jax.numpy as jnp
from jax import lax
from jax.experimental import pallas as pl
from jax.experimental.pallas import tpu as pltpu
from jax.sharding import PartitionSpec as P

BLOCK = 512
MICRO = 2
TILE = 128
LANES = 128
CHUNK = 768
SPAN = 2 * BLOCK
VMEM_BYTES = 58 * 1024 * 1024
SMALL_VMEM_BYTES = 20 * 1024 * 1024
NORM_LANE = 16
PHASE, DP = "phase", "dp"

norm_eps = 1e-05
mask_fill = -1000000000.0
score_scale = 0.125
inv_root_two = 0.7071067811865476
inv_root_tau = 0.3989422804014327
log2_e = 1.4426950408889634
highest = lax.Precision.HIGHEST

F32 = jnp.float32
BF16 = jnp.bfloat16
ANY = pl.BlockSpec(memory_space=pl.ANY)
VMEM = pl.BlockSpec(memory_space=pltpu.VMEM)
QUICK = pl.CostEstimate(flops=1, bytes_accessed=1, transcendentals=0)
SMEM = pl.BlockSpec(memory_space=pltpu.SMEM)


def dot_nn(a, b):
    return lax.dot_general(a, b, (((1,), (0,)), ((), ())), preferred_element_type=F32)


def dot_nt(a, b):
    return lax.dot_general(a, b, (((1,), (1,)), ((), ())), preferred_element_type=F32)


def dot_tn(a, b):
    return lax.dot_general(a, b, (((0,), (0,)), ((), ())), preferred_element_type=F32)


def row_mean(rows):
    return jnp.sum(rows, -1, keepdims=True) * (1.0 / rows.shape[-1])


def normal_parts(residual):
    centred = residual - row_mean(residual)
    inv_scale = lax.rsqrt(row_mean(centred * centred) + norm_eps)
    return centred * inv_scale, inv_scale


def norm_backward(grad_rows, normal_form, inv_scale):
    first = row_mean(grad_rows)
    second = row_mean(grad_rows * normal_form)
    return inv_scale * (grad_rows - first - normal_form * second)


def gelu_parts(hidden):
    share = 0.5 + 0.5 * lax.erf(hidden * inv_root_two)
    bell = jnp.exp2(hidden * hidden * (-0.5 * log2_e))
    return hidden * share, share + hidden * bell * inv_root_tau


def half_mask(which, shape):
    lane = lax.broadcasted_iota(jnp.int32, shape, 1)
    return (lane < LANES // 2) if which == 0 else (lane >= LANES // 2)


class Copies:
    def __init__(self, sems):
        self.sems = sems
        self.used = 0
        self.stores = []

    def take(self, count=1):
        self.used += count
        return self.used - count

    def load(self, source, target):
        copy = pltpu.make_async_copy(source, target, self.sems.at[self.take()])
        copy.start()
        return copy

    def store(self, source, target, when=True):
        if when:
            self.stores.append(self.load(source, target))

    def finish(self):
        for copy in self.stores:
            copy.wait()


KEPT = (
    "xin", "qkv", "weights", "ctx", "form1", "scale1", "low1", "slope", "act", "form2", "scale2", "out",
    "bias", "outer_low", "hidden_low", "residual_low", "sums1", "sums2", "residual", "projected", "offsets", "input_grad",
)
INS = (
    "phase", "segments", "hidden_in", "received", "out_grad", "table", "padding", "buckets",
    "gain1", "shift1", "gain2", "shift2",
    "wqkv", "wout", "wup", "wdown",
)


class Layer:
    def __init__(self, refs):
        self.__dict__.update(refs)
        self.copies = Copies(self.sems)
        self.width = self.hidden_in.shape[1]
        self.inner = self.wup.shape[2]
        self.pairs = self.width // LANES
        self.stages = self.inner // (2 * CHUNK)
        self.pair_sems = self.copies.take(self.pairs)
        self.chunk_sems = [self.copies.take(self.stages) for _ in range(3)]

    def fetch(self, *names):
        loads = [self.copies.load(getattr(self, name), getattr(self, f"{name}_v")) for name in names]
        for name in names:
            setattr(self, name, getattr(self, f"{name}_v"))
        return loads

    def lanes_of(self, pair, part):
        return pl.ds(pl.multiple_of(part * self.width + pair * LANES, LANES), LANES)

    def stage(self, i):
        return pl.ds(pl.multiple_of(i * 2 * CHUNK, 2 * CHUNK), 2 * CHUNK)

    def build_bias(self, table_loads):
        for load in table_loads:
            load.wait()
        span = self.buckets.shape[1]
        bucket_ids = lax.broadcasted_iota(jnp.int32, (self.table.shape[2], span), 0)
        hot = (bucket_ids == self.buckets[...]).astype(F32)
        table = jnp.concatenate([self.table[head] for head in range(self.table.shape[0])], 0)
        values = lax.dot_general(
            table, hot, (((1,), (0,)), ((), ())), precision=highest, preferred_element_type=F32
        )
        self.values_v[:, :span] = values
        self.values_v[:, span:] = jnp.zeros((values.shape[0], SPAN - span), F32)

        def one_head(head, carry):
            wide = jnp.broadcast_to(self.values_v[pl.ds(head, 1), :], (TILE, SPAN))
            self.bias_v[head] = pltpu.roll(wide, 1, 1, stride=1, stride_axis=0)
            return carry

        lax.fori_loop(0, values.shape[0], one_head, 0)
        self.copies.store(self.bias_v, self.bias)


    def rows(self, block):
        return pl.ds(block * BLOCK, BLOCK)

    def forward(self, block, keep, built, also=()):
        copies = self.copies
        rows = self.rows(block)
        table_loads = [] if built else self.fetch("table", "buckets")
        load_x = copies.load(self.hidden_in.at[rows] if keep else self.received, self.x_v)
        small = self.fetch("segments", "padding", "gain1", "shift1", "gain2", "shift2")
        width = self.width
        loads = [
            copies.load(self.wqkv.at[0, :, pl.ds(c, width)], self.wqkv_v.at[:, pl.ds(c, width)])
            for c in range(0, 3 * width, width)
        ]
        if not built:
            self.build_bias(table_loads)
        load_x.wait()

        def load_bias(pair):
            heads = pl.ds(2 * pair, 2)
            return pltpu.make_async_copy(self.bias.at[heads], self.bias_v.at[heads], self.sems.at[self.pair_sems + pair])

        for i, c in enumerate(range(0, 3 * width, width)):
            loads[i].wait()
            if built and i == 2:
                for pair in range(self.pairs):
                    load_bias(pair).start()
            self.qkv_v[:, c : c + width] = dot_nn(self.x_v[...], self.wqkv_v[:, c : c + width]).astype(BF16)
        copies.store(self.x_v, self.xin.at[rows])
        copies.store(self.qkv_v, self.qkv.at[rows], keep)
        weights_sem = self.sems.at[copies.take()]
        later_loads = [
            pltpu.make_async_copy(source.at[0], target, self.sems.at[copies.take()])
            for source, target in ((self.wout, self.wout_v), (self.wup, self.wup_v), (self.wdown, self.wdown_v))
        ]

        def own(pair, part, which):
            both = self.qkv_v[:, self.lanes_of(pair, part)]
            return jnp.where(half_mask(which, both.shape), both, jnp.zeros_like(both))

        for load in small:
            load.wait()
        at = block * BLOCK
        single = self.segments[:, at + TILE : at + TILE + 1] == self.segments[:, at : at + 1]
        padding = self.padding[:, block * BLOCK : (block + 1) * BLOCK]
        tile_of = lax.broadcasted_iota(jnp.int32, (1, BLOCK), 1) // TILE
        shut = [
            jnp.where((padding == 1) & (single | (tile_of == tile)), 0.0, mask_fill) for tile in range(BLOCK // TILE)
        ]
        row_id = lax.broadcasted_iota(jnp.int32, (TILE, TILE), 0)
        diagonal = row_id == lax.broadcasted_iota(jnp.int32, (TILE, TILE), 1)

        def bias_rows(head, tile):
            at = BLOCK - tile * TILE
            rows = self.bias_v[head, :, at : at + BLOCK]
            masked = rows + shut[tile]
            own = slice(tile * TILE, (tile + 1) * TILE)
            parts = [masked[:, : own.start], jnp.where(diagonal, rows[:, own], masked[:, own]), masked[:, own.stop :]]
            return jnp.concatenate([part for part in parts if part.shape[1]], 1)

        def weigh(pair, which):
            head = 2 * pair + which
            k_own = own(pair, 1, which)
            for r in range(0, BLOCK, 2 * TILE):
                q_rows = self.qkv_v[r : r + 2 * TILE, self.lanes_of(pair, 0)] * jnp.asarray(score_scale, BF16)
                tiles = [bias_rows(head, tile) for tile in range(r // TILE, r // TILE + 2)]
                logits = dot_nt(q_rows, k_own) + jnp.concatenate(tiles, 0)
                raised = jnp.exp(logits - jnp.max(logits, -1, keepdims=True))
                share = pl.reciprocal(jnp.sum(raised, -1, keepdims=True), approx=True)
                self.weights_v[head, r : r + 2 * TILE, :] = (raised * share).astype(BF16)

        def head_pair(pair, carry):
            if built:
                load_bias(pair).wait()

            @pl.when(pair == 2)
            def _():
                for load in (*later_loads, *also):
                    load.start()

            weigh(pair, 0)
            context = dot_nn(self.weights_v[2 * pair], own(pair, 2, 0))
            weigh(pair, 1)
            context += dot_nn(self.weights_v[2 * pair + 1], own(pair, 2, 1))
            self.ctx_v[:, self.lanes_of(pair, 0)] = context.astype(BF16)
            if keep:
                heads = pl.ds(2 * pair, 2)
                pltpu.make_async_copy(self.weights_v.at[heads], self.weights.at[block, heads], weights_sem).start()
            return carry

        lax.fori_loop(0, self.pairs, head_pair, 0)
        if keep:
            copies.stores.append(pltpu.make_async_copy(self.weights_v, self.weights.at[block], weights_sem))
        copies.store(self.ctx_v, self.ctx.at[rows])
        load_out, load_up, load_down = later_loads
        load_out.wait()
        self.acc_v[...] = dot_nn(self.ctx_v[...], self.wout_v[...])
        for r in range(0, BLOCK, 64):
            tile = slice(r, r + 64)
            form, scale = normal_parts(self.acc_v[tile, :] + self.x_v[tile, :].astype(F32))
            normed = form * self.gain1[...] + self.shift1[...]
            self.form1_v[tile, :] = form
            self.scale1_v[tile, :] = scale
            self.acc_v[tile, :] = normed
            self.low1_v[tile, :] = normed.astype(BF16)
        copies.store(self.form1_v, self.form1.at[rows], keep)
        copies.store(self.scale1_v, self.scale1.at[rows], keep)
        copies.store(self.low1_v, self.low1.at[rows])
        load_up.wait()
        load_down.wait()
        act_sem = self.sems.at[copies.take()]
        slope_sem = self.sems.at[copies.take()]

        def two_chunks(i, carry):
            span = self.stage(i)
            active, grade = gelu_parts(dot_nn(self.low1_v[...], self.wup_v[:, span]))
            active = active.astype(BF16)
            self.act_v[:, span] = active
            self.slope_v[:, span] = grade.astype(BF16)
            self.acc_v[...] += dot_nn(active, self.wdown_v[span, :])
            pltpu.make_async_copy(self.act_v.at[:, span], self.act.at[rows, span], act_sem).start()
            if keep:
                pltpu.make_async_copy(self.slope_v.at[:, span], self.slope.at[rows, span], slope_sem).start()
            return carry

        lax.fori_loop(0, self.stages, two_chunks, 0)
        copies.stores.append(pltpu.make_async_copy(self.act_v, self.act.at[rows], act_sem))
        if keep:
            copies.stores.append(pltpu.make_async_copy(self.slope_v, self.slope.at[rows], slope_sem))
        for r in range(0, BLOCK, 64):
            tile = slice(r, r + 64)
            form, scale = normal_parts(self.acc_v[tile, :])
            self.form2_v[tile, :] = form
            self.scale2_v[tile, :] = scale
            self.out_v[tile, :] = (form * self.gain2[...] + self.shift2[...]).astype(BF16)
        copies.store(self.out_v, self.send, keep)
        copies.store(self.out_v, self.out.at[rows])
        copies.store(self.form2_v, self.form2.at[rows], keep)
        copies.store(self.scale2_v, self.scale2.at[rows], keep)


    def chunk_loads(self, i, rows):
        span = self.stage(i)
        return [
            pltpu.make_async_copy(source, target, self.sems.at[self.chunk_sems[k] + i])
            for k, (source, target) in enumerate(
                (
                    (self.wdown.at[0, span], self.wdown_v.at[span]),
                    (self.slope.at[rows, span], self.slope_v.at[:, span]),
                    (self.wup.at[0, :, span], self.wup_v.at[:, span]),
                )
            )
        ]

    def norm_sums(self, source, form_ref, sums_ref):
        gain_sum = jnp.zeros((1, self.width), F32)
        shift_sum = jnp.zeros((1, self.width), F32)
        for r in range(0, BLOCK, 64):
            grad_rows, form = source[r : r + 64, :].astype(F32), form_ref[r : r + 64, :]
            gain_sum += jnp.sum(grad_rows * form, 0, keepdims=True)
            shift_sum += jnp.sum(grad_rows, 0, keepdims=True)
        sums_ref[...] = jnp.zeros(sums_ref.shape, F32)
        sums_ref[0:1, :] = gain_sum
        sums_ref[1:2, :] = shift_sum

    def norm_back(self, block):
        for r in range(0, BLOCK, 64):
            tile = slice(r, r + 64)
            grad_rows = self.g_v[tile, :].astype(F32) * self.gain2[...]
            grad_outer = norm_backward(grad_rows, self.form2_v[tile, :], self.scale2_v[tile, :])
            self.acc_v[tile, :] = grad_outer
            self.outer_v[tile, :] = grad_outer.astype(BF16)
        self.copies.store(self.outer_v, self.outer_low.at[self.rows(block)])

    def norm_sums_2(self, block):
        self.norm_sums(self.g_v, self.form2_v, self.sums2_v)
        self.copies.store(self.sums2_v, self.sums2.at[block])

    def ffn_back(self, block, staged=False, middle_loads=()):
        copies = self.copies
        rows = self.rows(block)
        hidden_sem = self.sems.at[copies.take()]

        def two_chunks(i, carry):
            span = self.stage(i)
            if staged:
                load_down, load_slope, load_up = self.chunk_loads(i, rows)
                load_down.wait()
                load_slope.wait()

                @pl.when(i + 1 < self.stages)
                def _():
                    for load in self.chunk_loads(i + 1, rows)[:2]:
                        load.start()

            grad_active = dot_nt(self.outer_v[...], self.wdown_v[span, :])
            hidden = (grad_active * self.slope_v[:, span].astype(F32)).astype(BF16)
            self.slope_v[:, span] = hidden
            if staged:
                load_up.wait()

                @pl.when(i + 1 < self.stages)
                def _():
                    self.chunk_loads(i + 1, rows)[2].start()

            self.acc_v[...] += dot_nt(hidden, self.wup_v[:, span])
            pltpu.make_async_copy(self.slope_v.at[:, span], self.hidden_low.at[rows, span], hidden_sem).start()
            return carry

        lax.fori_loop(0, self.stages, two_chunks, 0)
        copies.stores.append(pltpu.make_async_copy(self.slope_v, self.hidden_low.at[rows], hidden_sem))
        for load in middle_loads:
            load.wait()
        self.norm_sums(self.acc_v, self.form1_v, self.sums1_v)
        for r in range(0, BLOCK, 64):
            tile = slice(r, r + 64)
            grad_residual = norm_backward(
                self.acc_v[tile, :] * self.gain1[...], self.form1_v[tile, :], self.scale1_v[tile, :]
            )
            self.acc_v[tile, :] = grad_residual
            self.residual_low_v[tile, :] = grad_residual.astype(BF16)
        copies.store(self.residual_low_v, self.residual_low.at[rows])
        copies.store(self.sums1_v, self.sums1.at[block])

    def attn_back(self, block, next_loads=None, load_in=()):
        copies = self.copies
        rows = self.rows(block)
        self.dctx_v[...] = dot_nt(self.residual_low_v[...], self.wout_v[...]).astype(BF16)
        self.fold_v[:, :, 0:TILE] = jnp.zeros((2, TILE, TILE), F32)

        def head_pair(pair, carry):
            def lanes_of(part):
                return self.lanes_of(pair, part)

            if next_loads is not None:
                next_loads(pair)
            q_pair, k_pair, v_pair = (self.qkv_v[:, lanes_of(part)] for part in range(3))
            grad_pair = self.dctx_v[:, lanes_of(0)]
            crossed = grad_pair.astype(F32) * self.ctx_v[:, lanes_of(0)].astype(F32)
            masks = [half_mask(which, k_pair.shape) for which in range(2)]

            def own(both, which):
                return jnp.where(masks[which], both, jnp.zeros_like(both))

            for which in range(2):
                self.square_v[which] = dot_nt(grad_pair, own(v_pair, which))
            q_grad = k_grad = v_grad = 0.0
            for which in range(2):
                head = 2 * pair + which
                delta = jnp.sum(own(crossed, which), -1, keepdims=True)
                for r in range(0, BLOCK, 64):
                    tile = slice(r, r + 64)
                    score_grad = (
                        self.weights_v[head, tile, :].astype(F32) * (self.square_v[which, tile, :] - delta[tile, :])
                    ).astype(BF16)
                    self.half_v[which, tile, :] = score_grad
                    at = BLOCK - r // TILE * TILE
                    wide = score_grad.astype(F32)
                    half = slice(r % TILE, r % TILE + 64)
                    if r < TILE:
                        self.fold_v[which, half, at : at + BLOCK] = wide
                    else:
                        self.fold_v[which, half, at : at + TILE] = wide[:, :TILE]
                        self.fold_v[which, half, at + TILE : at + BLOCK] += wide[:, TILE:]
                v_grad += dot_tn(self.weights_v[head], own(grad_pair, which))
                q_grad += dot_nn(self.half_v[which], own(k_pair, which))
                k_grad += dot_tn(self.half_v[which], own(q_pair, which))
                folded = self.fold_v[which]
                size = TILE // 2
                while size >= 8:
                    folded = folded[:size, :] + pltpu.roll(folded[size:, :], SPAN - size, 1)
                    size //= 2
                self.eighth_v[head] = folded
            self.qkv_v[:, lanes_of(0)] = (q_grad * score_scale).astype(BF16)
            self.qkv_v[:, lanes_of(1)] = (k_grad * score_scale).astype(BF16)
            self.qkv_v[:, lanes_of(2)] = v_grad.astype(BF16)
            return carry

        lax.fori_loop(0, self.pairs, head_pair, 0)
        copies.store(self.eighth_v, self.offsets.at[block])
        copies.store(self.qkv_v, self.projected.at[rows])
        for load in load_in:
            load.wait()
        self.grad_v[...] = (self.acc_v[...] + dot_nt(self.qkv_v[...], self.wqkv_v[...])).astype(BF16)
        copies.store(self.grad_v, self.send)
        copies.store(self.grad_v, self.input_grad.at[rows])


    def do_forward(self, block):
        self.forward(block, True, block > 0)

    def do_bias(self, block):
        self.build_bias(self.fetch("table", "buckets"))

    def do_both(self, block):
        load = pltpu.make_async_copy(self.out_grad.at[self.rows(block)], self.g_v, self.sems.at[self.copies.take()])
        self.forward(block, False, True, [load])
        load.wait()
        self.norm_back(block)
        self.ffn_back(block)
        self.norm_sums_2(block)
        self.attn_back(block)

    def do_back(self, block):
        rows = self.rows(block)
        loads = [
            self.copies.load(source, target)
            for source, target in (
                (self.received, self.g_v),
                (self.form2.at[rows], self.form2_v),
                (self.scale2.at[rows], self.scale2_v),
                (self.slope.at[rows], self.slope_v),
                (self.wdown.at[0], self.wdown_v),
                (self.wup.at[0], self.wup_v),
                (self.form1.at[rows], self.form1_v),
                (self.scale1.at[rows], self.scale1_v),
                (self.qkv.at[rows], self.qkv_v),
                (self.weights.at[block], self.weights_v),
                (self.ctx.at[rows], self.ctx_v),
                (self.wout.at[0], self.wout_v),
                (self.wqkv.at[0], self.wqkv_v),
            )
        ]
        for load in loads + self.fetch("gain1", "gain2"):
            load.wait()
        self.norm_back(block)
        self.ffn_back(block)
        self.norm_sums_2(block)
        self.attn_back(block)

    def do_ffn_back(self, block):
        rows = self.rows(block)
        loads = [
            self.copies.load(source, target)
            for source, target in (
                (self.received, self.g_v),
                (self.form2.at[rows], self.form2_v),
                (self.scale2.at[rows], self.scale2_v),
            )
        ]
        loads += self.fetch("gain1", "gain2")
        for load in self.chunk_loads(0, rows)[:2]:
            load.start()
        for load in loads:
            load.wait()
        self.chunk_loads(0, rows)[2].start()
        middle = [
            self.copies.load(self.form1.at[rows], self.form1_v),
            self.copies.load(self.scale1.at[rows], self.scale1_v),
        ]
        self.norm_back(block)
        self.norm_sums_2(block)
        self.ffn_back(block, True, middle)
        self.copies.store(self.acc_v, self.residual)

    def do_attn_back(self, block):
        rows = self.rows(block)
        loads = [
            self.copies.load(source, target)
            for source, target in ((self.residual_low.at[rows], self.residual_low_v), (self.wout.at[0], self.wout_v))
        ]
        first = self.copies.take(5 * self.pairs)

        def pair_loads(pair):
            heads = pl.ds(2 * pair, 2)
            sources = [(self.weights.at[block, heads], self.weights_v.at[heads])]
            for source, target, parts in ((self.qkv, self.qkv_v, 3), (self.ctx, self.ctx_v, 1)):
                for part in range(parts):
                    lanes = self.lanes_of(pair, part)
                    sources.append((source.at[rows, lanes], target.at[:, lanes]))
            return [
                pltpu.make_async_copy(source, target, self.sems.at[first + 5 * pair + k])
                for k, (source, target) in enumerate(sources)
            ]

        for pair in range(2):
            for load in pair_loads(pair):
                load.start()
        for load in loads:
            load.wait()
        last = [
            pltpu.make_async_copy(source, target, self.sems.at[self.copies.take()])
            for source, target in ((self.wqkv.at[0], self.wqkv_v), (self.residual, self.acc_v))
        ]

        def next_loads(pair):
            for load in pair_loads(pair):
                load.wait()

            @pl.when(pair + 2 < self.pairs)
            def _():
                for load in pair_loads(pair + 2):
                    load.start()

            @pl.when(pair == self.pairs - 3)
            def _():
                for load in last:
                    load.start()

        self.attn_back(block, next_loads, last)


def layer_kernel(work, phase_on, block, ins, outs, scratch, after_count, kept_count, *refs):
    refs_in, refs = refs[: len(ins)], refs[len(ins) + after_count + kept_count :]
    named = dict(zip(ins, refs_in)) | dict(zip(outs, refs)) | dict(zip(scratch, refs[len(outs) :]))

    @pl.when(named["phase"][0] == phase_on)
    def _():
        layer = Layer(named)
        getattr(layer, f"do_{work}")(block)
        layer.copies.finish()


def layer_step(work, phase_on, block, values, afters, kept, kept_shapes, scratch):
    specs = [SMEM] + [ANY] * (len(values) - 1)
    names = list(scratch)
    kept = list(kept) if kept is not None else []
    sent = jax.ShapeDtypeStruct((BLOCK, values[2].shape[1]), BF16)
    if work == "bias":
        names = ["values_v", "bias_v", "table_v", "buckets_v"]
    count = len(values) + len(afters)
    results = pl.pallas_call(
        functools.partial(
            layer_kernel, work, phase_on, block, INS, KEPT + ("send",), names + ["sems"], len(afters), len(kept)
        ),
        out_shape=list(kept_shapes) + [sent],
        in_specs=specs + [ANY] * (len(afters) + len(kept)),
        out_specs=[ANY] * (len(kept_shapes) + 1),
        scratch_shapes=[pltpu.VMEM(*scratch[name]) for name in names] + [pltpu.SemaphoreType.DMA((96,))],
        input_output_aliases={count + i: i for i in range(len(kept))},
        compiler_params=pltpu.CompilerParams(vmem_limit_bytes=VMEM_BYTES),
        name=f"{work}_{phase_on}_{block}",
    )(*values, *afters, *kept)
    return dict(zip(KEPT, results)), results[-1]


def pack_kernel(ways, buckets_ref, offsets_ref, sums1_ref, sums2_ref, *refs):
    out_ref, turn_v = refs[-2:]
    row_of = lax.broadcasted_iota(jnp.int32, (8, SPAN), 0)
    lines = []
    for head in range(offsets_ref.shape[1]):
        eighth = offsets_ref[0, head] + offsets_ref[1, head]
        for size in (4, 2, 1):
            eighth = jnp.where((row_of & size) != 0, pltpu.roll(eighth, SPAN - size, 1), eighth)
        lines.append(jnp.sum(eighth, 0, keepdims=True))
    lines += [jnp.zeros((1, SPAN), F32)] * (NORM_LANE - len(lines))
    sums = pltpu.roll(jnp.concatenate(lines, 0), SPAN - 1, 1)
    span = buckets_ref.shape[1]
    buckets, depth = out_ref.shape[0] // 3, out_ref.shape[0] // ways
    share = buckets // ways
    bucket_ids = lax.broadcasted_iota(jnp.int32, (buckets, span), 0)
    hot = (bucket_ids == buckets_ref[...]).astype(F32)
    table = lax.dot_general(
        hot, sums[:, :span], (((1,), (1,)), ((), ())), precision=highest, preferred_element_type=F32
    ).astype(BF16)
    turn_v[...] = jnp.zeros(turn_v.shape, F32)
    for i, ref in enumerate((sums1_ref, sums2_ref)):
        at = NORM_LANE + 2 * i
        turn_v[at : at + 2, :] = ref[0, 0:2, :] + ref[1, 0:2, :]
    out_ref[...] = turn_v[...].T.astype(BF16)
    for i in range(ways):
        out_ref[i * depth : i * depth + share, 0:NORM_LANE] = table[i * share : (i + 1) * share, :]


def packed(ways, buckets, offset_buckets, kept, afters):
    width = kept["sums1"].shape[2]
    depth, share = width // ways, buckets // ways
    arrays = (offset_buckets, kept["offsets"], kept["sums1"], kept["sums2"])
    if depth % 16 == 0 and share % 16 == 0 and 3 * buckets == width:
        rows = pl.pallas_call(
            functools.partial(pack_kernel, ways),
            out_shape=jax.ShapeDtypeStruct((width, LANES), BF16),
            in_specs=[VMEM] * len(arrays) + [ANY] * len(afters),
            out_specs=VMEM,
            scratch_shapes=[pltpu.VMEM((LANES, width), F32)],
            compiler_params=pltpu.CompilerParams(vmem_limit_bytes=SMALL_VMEM_BYTES),
            name="pack",
        )(*arrays, *afters)
        return rows.reshape(ways, depth, LANES)
    eighths = jnp.sum(kept["offsets"], 0)
    lines = sum(jnp.roll(eighths[:, i, :], -i, 1) for i in range(8))[:, 1:]
    hot = (offset_buckets[0][None, :] == jnp.arange(buckets, dtype=jnp.int32)[:, None]).astype(F32)
    table = jnp.dot(hot, lines.T, precision=highest).reshape(ways, share, -1)
    table = jnp.pad(table, ((0, 0), (0, depth - share), (0, NORM_LANE - table.shape[2])))
    norms = jnp.concatenate([jnp.sum(kept[name], 0)[:2] for name in ("sums1", "sums2")], 0)
    norms = norms.T.reshape(ways, depth, 4)
    rows = jnp.concatenate([table, norms], 2)
    return jnp.pad(rows, ((0, 0), (0, 0), (0, LANES - rows.shape[2]))).astype(BF16)


def halve_kernel(bits, counts, after_count, through_count, me_ref, *refs):
    outs = refs[2 * sum(counts) + after_count + through_count :]
    for i, count in enumerate(counts):
        pieces, refs = [refs[2 * k : 2 * k + 2] for k in range(count)], refs[2 * count :]
        send_ref, rest_ref = outs[2 * i : 2 * i + 2]
        mine = (me_ref[0] >> bits[i]) & 1

        def total(which):
            parts = [
                (kept[0, which, 0, 0] if len(kept.shape) == 6 else kept[0, which, 0]).astype(F32)
                + arrived[0, which, 0].astype(F32)
                for kept, arrived in pieces
            ]
            return jnp.concatenate(parts, 1)

        send_ref[0, 0] = total(1 - mine).astype(send_ref.dtype)
        rest_ref[0, 0] = total(mine)


def join_kernel(kept_ref, arrived_ref, out_ref, qkv_ref, table_ref, *refs):
    norm_refs, turn_v = refs[:-1], refs[-1]
    total = kept_ref[...] + arrived_ref[...].astype(F32)
    wide = out_ref.shape[1]
    out_ref[...] = total[:, :wide]
    qkv_ref[...] = total[:, wide : 4 * wide]
    small = total[:, 4 * wide :]
    turn_v[...] = jnp.zeros(turn_v.shape, F32)
    turn_v[: small.shape[0], :] = small
    turned = turn_v[...].T
    for head in range(table_ref.shape[0]):
        table_ref[head] = turned[head : head + 1, : table_ref.shape[2]]
    for i, ref in enumerate(norm_refs):
        ref[...] = turned[NORM_LANE + i : NORM_LANE + i + 1, : ref.shape[1]]


class Part:
    def __init__(self, whole):
        self.whole = whole
        self.sent = self.of_core(1 - (lax.axis_index(DP) & 1))
        self.arrived = swapped(self.sent, 0)

    def of_core(self, core):
        split = self.whole.reshape((self.whole.shape[0] // 2, 2) + self.whole.shape[1:])
        return lax.dynamic_index_in_dim(split, core, 1, keepdims=False)


def swapped(array, bit):
    count = lax.axis_size(DP)
    return lax.ppermute(array, DP, [(i, i ^ (1 << bit)) for i in range(count)])


class Share:
    def __init__(self, parts, order):
        self.parts = parts
        self.order = order[1:]
        self.left = sorted(order[1:])
        self.depth = parts[0].whole.shape[1]
        self.wide = sum(part.whole.shape[2] for part in parts)
        self.mine = None

    def swap(self, bit, theirs):
        self.left.remove(bit)
        self.sent = theirs
        self.arrived = swapped(theirs, bit)

    def total(self):
        if self.mine is not None:
            return self.mine + self.arrived.astype(F32)
        here = lax.axis_index(DP) & 1
        return jnp.concatenate(
            [part.of_core(here).astype(F32) + part.arrived.astype(F32) for part in self.parts], 2
        )

    def split_at(self):
        bit = self.order[0]
        axis = len(self.left) - 1 - self.left.index(bit)
        return bit, 2**axis, 2 ** (len(self.left) - 1 - axis)

    def halve(self):
        bit, above, below = self.split_at()
        self.order = self.order[1:]
        split = self.total().reshape(above, 2, below, self.depth, self.wide)
        here = (lax.axis_index(DP) >> bit) & 1
        theirs = lax.dynamic_index_in_dim(split, 1 - here, 1, keepdims=False).astype(BF16)
        mine = lax.dynamic_index_in_dim(split, here, 1, keepdims=False)
        self.mine = mine.reshape(-1, self.depth, self.wide)
        self.swap(bit, theirs.reshape(-1, self.depth, self.wide))


def halve_all(me, shares, afters=(), through=()):
    if any(share.depth % 16 for share in shares):
        for share in shares:
            share.halve()
        return through
    ins, in_specs, outs, out_specs, bits, counts = [], [], [], [], [], []
    for share in shares:
        bit, above, below = share.split_at()
        bits.append(bit)

        def halves(wide, b=below):
            return pl.BlockSpec((1, 2, 1, share.depth, wide), lambda i, me: (i // b, 0, i % b, 0, 0))

        if share.mine is None:
            counts.append(len(share.parts))
            for part in share.parts:
                wide = part.whole.shape[2]
                ins.append(part.whole.reshape(above, 2, below, 2, share.depth, wide))
                in_specs.append(
                    pl.BlockSpec(
                        (1, 2, 1, 1, share.depth, wide),
                        lambda i, me, b=below: (i // b, 0, i % b, me[0] & 1, 0, 0),
                    )
                )
                ins.append(part.arrived.reshape(above, 2, below, share.depth, wide))
                in_specs.append(halves(wide))
        else:
            counts.append(1)
            for array in (share.mine, share.arrived):
                ins.append(array.reshape(above, 2, below, share.depth, share.wide))
                in_specs.append(halves(share.wide))
        outs += [
            jax.ShapeDtypeStruct((above, below, share.depth, share.wide), kind) for kind in (BF16, F32)
        ]
        out_specs += [
            pl.BlockSpec((1, 1, share.depth, share.wide), lambda i, me, b=below: (i // b, i % b, 0, 0))
        ] * 2
        steps = above * below
    results = pl.pallas_call(
        functools.partial(halve_kernel, tuple(bits), tuple(counts), len(afters), len(through)),
        grid_spec=pltpu.PrefetchScalarGridSpec(
            num_scalar_prefetch=1,
            grid=(steps,),
            in_specs=in_specs + [ANY] * (len(afters) + len(through)),
            out_specs=out_specs + [ANY] * len(through),
        ),
        out_shape=outs + [jax.ShapeDtypeStruct(array.shape, array.dtype) for array in through],
        input_output_aliases={
            1 + len(ins) + len(afters) + i: len(outs) + i for i in range(len(through))
        },
        compiler_params=pltpu.CompilerParams(vmem_limit_bytes=SMALL_VMEM_BYTES),
        name="halve",
    )(me, *ins, *afters, *through)
    for i, share in enumerate(shares):
        share.order = share.order[1:]
        share.mine = results[2 * i + 1].reshape(-1, share.depth, share.wide)
        share.swap(bits[i], results[2 * i].reshape(-1, share.depth, share.wide))
    return results[len(outs) :]


def joined(share, width, table_shape):
    shapes = [(share.depth, width), (share.depth, 3 * width), table_shape] + [(1, share.depth)] * 4
    return pl.pallas_call(
        join_kernel,
        out_shape=[jax.ShapeDtypeStruct(dims, F32) for dims in shapes],
        in_specs=[VMEM] * 2,
        out_specs=[VMEM] * len(shapes),
        scratch_shapes=[pltpu.VMEM((LANES, LANES), F32)],
        compiler_params=pltpu.CompilerParams(vmem_limit_bytes=SMALL_VMEM_BYTES),
        name="join",
    )(share.mine[0], share.arrived[0])


def passed_along(x, axis, by):
    length = lax.axis_size(axis)
    pairs = [(i, i + by) for i in range(length) if 0 <= i + by < length]
    return lax.ppermute(x, axis, pairs)


def shards(
    hidden_in, out_grad, qkv_weight, out_weight, rel_table, norm1_gain, norm1_bias,
    up_weight, down_weight, norm2_gain, norm2_bias, seg_ids, pad_mask, rel_buckets,
):
    phase = lax.axis_index(PHASE).astype(jnp.int32).reshape(1)
    ways = lax.axis_size(DP)
    slots, width = hidden_in.shape
    inner = up_weight.shape[2]
    buckets, heads = rel_table.shape[1:]

    def shape(dims, kind):
        return jax.ShapeDtypeStruct(dims, kind)

    rows_of = {
        "xin": (width, BF16), "qkv": (3 * width, BF16), "ctx": (width, BF16), "form1": (width, F32),
        "scale1": (1, F32), "low1": (width, BF16), "slope": (inner, BF16), "act": (inner, BF16),
        "form2": (width, F32), "scale2": (1, F32), "out": (width, BF16),
        "outer_low": (width, BF16), "hidden_low": (inner, BF16), "residual_low": (width, BF16),
        "projected": (3 * width, BF16), "input_grad": (width, BF16),
    }
    kept_shapes = [
        shape((slots, rows_of[name][0]), rows_of[name][1])
        if name in rows_of
        else {
            "weights": shape((MICRO, heads, BLOCK, BLOCK), BF16),
            "sums1": shape((MICRO, 8, width), F32),
            "sums2": shape((MICRO, 8, width), F32),
            "residual": shape((BLOCK, width), F32),
            "offsets": shape((MICRO, heads, 8, SPAN), F32),
            "bias": shape((heads, TILE, SPAN), F32),
        }[name]
        for name in KEPT
    ]
    small = {
        "segments_v": ((1, slots), jnp.int32), "padding_v": ((1, slots), jnp.int32),
        "buckets_v": ((1, rel_buckets.shape[0]), jnp.int32), "table_v": ((heads, 1, buckets), F32),
        "gain1_v": ((1, width), F32), "shift1_v": ((1, width), F32), "gain2_v": ((1, width), F32),
        "shift2_v": ((1, width), F32),
    }
    in_forward = ("qkv", "ctx", "form1", "scale1", "low1", "slope", "act", "form2", "scale2", "out")
    scratch = {f"{name}_v": ((BLOCK, rows_of[name][0]), rows_of[name][1]) for name in in_forward}
    scratch |= small
    scratch |= {
        name: ((BLOCK, width), BF16) for name in ("x_v", "g_v", "outer_v", "residual_low_v", "dctx_v", "grad_v")
    }
    scratch |= {
        "weights_v": ((heads, BLOCK, BLOCK), BF16), "acc_v": ((BLOCK, width), F32), "square_v": ((2, BLOCK, BLOCK), F32),
        "values_v": ((heads, SPAN), F32), "bias_v": ((heads, TILE, SPAN), F32), "sums1_v": ((8, width), F32), "sums2_v": ((8, width), F32),
        "wqkv_v": ((width, 3 * width), BF16), "wout_v": ((width, width), BF16), "wup_v": ((width, inner), BF16),
        "wdown_v": ((inner, width), BF16), "fold_v": ((2, TILE, SPAN), F32), "eighth_v": ((heads, 8, SPAN), F32),
        "half_v": ((2, BLOCK, BLOCK), BF16),
    }

    def step(work, phase_on, block, received, kept, afters=()):
        values = (
            phase, seg_ids[None, :], hidden_in, received, out_grad, rel_table.transpose(2, 0, 1), pad_mask[None, :], rel_buckets[None, :],
            norm1_gain, norm1_bias, norm2_gain, norm2_bias, qkv_weight, out_weight, up_weight, down_weight,
        )
        in_place = None if kept is None else [kept[name] for name in KEPT]
        return layer_step(work, phase_on, block, values, list(afters), in_place, kept_shapes, scratch)

    kept, sent = step("forward", 0, 0, hidden_in, None)
    first = passed_along(sent, PHASE, 1)
    kept, _ = step("bias", 1, 0, hidden_in, kept)
    kept, sent = step("forward", 0, 1, hidden_in, kept)
    second = passed_along(sent, PHASE, 1)
    kept, sent = step("both", 1, 0, first, kept)
    first_back = passed_along(sent, PHASE, -1)
    kept, sent = step("both", 1, 1, second, kept)
    second_back = passed_along(sent, PHASE, -1)
    kept, _ = step("back", 0, 0, first_back, kept)
    def early(left, right):
        return dot_tn(left[:BLOCK], right[:BLOCK]).astype(BF16)

    up_base = early(kept["low1"], kept["hidden_low"])
    qkv_base = early(kept["xin"], kept["projected"])
    kept, _ = step("ffn_back", 0, 1, second_back, kept, [up_base, qkv_base])

    bits = ways.bit_length() - 1
    near_first = list(range(bits))
    far_first = [0] + list(range(2, bits)) + [1] if bits > 1 else near_first
    me = lax.axis_index(DP).astype(jnp.int32).reshape(1)

    def weight_grad(left, right, base=None):
        if base is None:
            product = dot_tn(left, right)
        else:
            product = dot_tn(left[BLOCK:], right[BLOCK:]) + base.astype(F32)
        product = product.astype(BF16)
        return product.reshape(ways, product.shape[0] // ways, product.shape[1])

    down = Share([Part(weight_grad(kept["act"], kept["outer_low"]))], near_first)
    up = Share([Part(weight_grad(kept["low1"], kept["hidden_low"], up_base))], far_first)
    out_part = Part(weight_grad(kept["ctx"], kept["residual_low"]))
    halve_all(me, [down])
    halve_all(me, [up])
    kept, _ = step("attn_back", 0, 1, hidden_in, kept, [down.sent, up.sent])
    far_part = Part(weight_grad(kept["xin"], kept["projected"][:, width:], qkv_base[:, width:]))
    near_part = Part(weight_grad(kept["xin"], kept["projected"][:, :width], qkv_base[:, :width]))
    halve_all(me, [up, down], [far_part.sent, near_part.sent])
    small_part = Part(packed(ways, buckets, rel_buckets[None, :], kept, [near_part.sent]))
    last = Share([out_part, near_part, far_part, small_part], near_first)
    halve_all(me, [last], [down.sent, up.sent])
    halve_all(me, [last])
    halve_all(me, [up, down], [last.sent])
    while down.order:
        halve_all(me, [up, down])
    while last.order:
        halve_all(me, [last])
    down_share = down.total()[0]
    up_share = up.total()[0]
    out_share, qkv_share, table_share, *norm_shares = joined(last, width, (heads, 1, buckets // ways))
    return (
        kept["out"][None],
        kept["input_grad"][None],
        qkv_share[None],
        out_share[None],
        table_share.transpose(1, 2, 0),
        norm_shares[0],
        norm_shares[1],
        up_share[None],
        down_share[None],
        norm_shares[2],
        norm_shares[3],
    )


def solution(mesh):
    return jax.shard_map(
        shards,
        mesh=mesh,
        in_specs=(
            P(DP, None),
            P(DP, None),
            P(PHASE, None, None),
            P(PHASE, None, None),
            P(PHASE, None, None),
            P(PHASE, None),
            P(PHASE, None),
            P(PHASE, None, None),
            P(PHASE, None, None),
            P(PHASE, None),
            P(PHASE, None),
            P(DP),
            P(DP),
            P(),
        ),
        out_specs=(
            P(PHASE, DP, None),
            P(PHASE, DP, None),
            P(PHASE, DP, None),
            P(PHASE, DP, None),
            P(PHASE, DP, None),
            P(PHASE, DP),
            P(PHASE, DP),
            P(PHASE, DP, None),
            P(PHASE, DP, None),
            P(PHASE, DP),
            P(PHASE, DP),
        ),
        check_vma=False,
    )
```

```python
import functools

import jax
import jax.numpy as jnp
from jax import lax
from jax.experimental import pallas as pl
from jax.experimental.pallas import tpu as pltpu
from jax.sharding import PartitionSpec as P

BLOCK = 512
MICRO = 2
TILE = 128
LANES = 128
CHUNK = 768
SPAN = 2 * BLOCK
VMEM_BYTES = 58 * 1024 * 1024
SMALL_VMEM_BYTES = 20 * 1024 * 1024
NORM_LANE = 16
PHASE, DP = "phase", "dp"

norm_eps = 1e-05
mask_fill = -1000000000.0
score_scale = 0.125
inv_root_two = 0.7071067811865476
inv_root_tau = 0.3989422804014327
log2_e = 1.4426950408889634
highest = lax.Precision.HIGHEST

F32 = jnp.float32
BF16 = jnp.bfloat16
ANY = pl.BlockSpec(memory_space=pl.ANY)
VMEM = pl.BlockSpec(memory_space=pltpu.VMEM)
QUICK = pl.CostEstimate(flops=1, bytes_accessed=1, transcendentals=0)
SMEM = pl.BlockSpec(memory_space=pltpu.SMEM)


def dot_nn(a, b):
    return lax.dot_general(a, b, (((1,), (0,)), ((), ())), preferred_element_type=F32)


def dot_nt(a, b):
    return lax.dot_general(a, b, (((1,), (1,)), ((), ())), preferred_element_type=F32)


def dot_tn(a, b):
    return lax.dot_general(a, b, (((0,), (0,)), ((), ())), preferred_element_type=F32)


def row_mean(rows):
    return jnp.sum(rows, -1, keepdims=True) * (1.0 / rows.shape[-1])


def normal_parts(residual):
    centred = residual - row_mean(residual)
    inv_scale = lax.rsqrt(row_mean(centred * centred) + norm_eps)
    return centred * inv_scale, inv_scale


def norm_backward(grad_rows, normal_form, inv_scale):
    first = row_mean(grad_rows)
    second = row_mean(grad_rows * normal_form)
    return inv_scale * (grad_rows - first - normal_form * second)


def gelu_parts(hidden):
    share = 0.5 + 0.5 * lax.erf(hidden * inv_root_two)
    bell = jnp.exp2(hidden * hidden * (-0.5 * log2_e))
    return hidden * share, share + hidden * bell * inv_root_tau


def half_mask(which, shape):
    lane = lax.broadcasted_iota(jnp.int32, shape, 1)
    return (lane < LANES // 2) if which == 0 else (lane >= LANES // 2)


class Copies:
    def __init__(self, sems):
        self.sems = sems
        self.used = 0
        self.stores = []

    def take(self, count=1):
        self.used += count
        return self.used - count

    def load(self, source, target):
        copy = pltpu.make_async_copy(source, target, self.sems.at[self.take()])
        copy.start()
        return copy

    def store(self, source, target, when=True):
        if when:
            self.stores.append(self.load(source, target))

    def finish(self):
        for copy in self.stores:
            copy.wait()


KEPT = (
    "xin", "qkv", "weights", "ctx", "form1", "scale1", "low1", "slope", "act", "form2", "scale2", "out",
    "bias", "outer_low", "hidden_low", "residual_low", "sums1", "sums2", "residual", "projected", "offsets", "input_grad",
)
INS = (
    "phase", "segments", "hidden_in", "received", "out_grad", "table", "padding", "buckets",
    "gain1", "shift1", "gain2", "shift2",
    "wqkv", "wout", "wup", "wdown",
)


class Layer:
    def __init__(self, refs):
        self.__dict__.update(refs)
        self.copies = Copies(self.sems)
        self.width = self.hidden_in.shape[1]
        self.inner = self.wup.shape[2]
        self.pairs = self.width // LANES
        self.stages = self.inner // (2 * CHUNK)
        self.pair_sems = self.copies.take(self.pairs)
        self.chunk_sems = [self.copies.take(self.stages) for _ in range(3)]

    def fetch(self, *names):
        loads = [self.copies.load(getattr(self, name), getattr(self, f"{name}_v")) for name in names]
        for name in names:
            setattr(self, name, getattr(self, f"{name}_v"))
        return loads

    def lanes_of(self, pair, part):
        return pl.ds(pl.multiple_of(part * self.width + pair * LANES, LANES), LANES)

    def stage(self, i):
        return pl.ds(pl.multiple_of(i * 2 * CHUNK, 2 * CHUNK), 2 * CHUNK)

    def build_bias(self, table_loads):
        for load in table_loads:
            load.wait()
        span = self.buckets.shape[1]
        bucket_ids = lax.broadcasted_iota(jnp.int32, (self.table.shape[2], span), 0)
        hot = (bucket_ids == self.buckets[...]).astype(F32)
        table = jnp.concatenate([self.table[head] for head in range(self.table.shape[0])], 0)
        values = lax.dot_general(
            table, hot, (((1,), (0,)), ((), ())), precision=highest, preferred_element_type=F32
        )
        self.values_v[:, :span] = values
        self.values_v[:, span:] = jnp.zeros((values.shape[0], SPAN - span), F32)

        def one_head(head, carry):
            wide = jnp.broadcast_to(self.values_v[pl.ds(head, 1), :], (TILE, SPAN))
            self.bias_v[head] = pltpu.roll(wide, 1, 1, stride=1, stride_axis=0)
            return carry

        lax.fori_loop(0, values.shape[0], one_head, 0)
        self.copies.store(self.bias_v, self.bias)


    def rows(self, block):
        return pl.ds(block * BLOCK, BLOCK)

    def forward(self, block, keep, built, also=()):
        copies = self.copies
        rows = self.rows(block)
        table_loads = [] if built else self.fetch("table", "buckets")
        load_x = copies.load(self.hidden_in.at[rows] if keep else self.received, self.x_v)
        small = self.fetch("segments", "padding", "gain1", "shift1", "gain2", "shift2")
        width = self.width
        loads = [
            copies.load(self.wqkv.at[0, :, pl.ds(c, width)], self.wqkv_v.at[:, pl.ds(c, width)])
            for c in range(0, 3 * width, width)
        ]
        if not built:
            self.build_bias(table_loads)
        load_x.wait()

        def load_bias(pair):
            heads = pl.ds(2 * pair, 2)
            return pltpu.make_async_copy(self.bias.at[heads], self.bias_v.at[heads], self.sems.at[self.pair_sems + pair])

        for i, c in enumerate(range(0, 3 * width, width)):
            loads[i].wait()
            if built and i == 2:
                for pair in range(self.pairs):
                    load_bias(pair).start()
            self.qkv_v[:, c : c + width] = dot_nn(self.x_v[...], self.wqkv_v[:, c : c + width]).astype(BF16)
        copies.store(self.x_v, self.xin.at[rows])
        copies.store(self.qkv_v, self.qkv.at[rows], keep)
        weights_sem = self.sems.at[copies.take()]
        later_loads = [
            pltpu.make_async_copy(source.at[0], target, self.sems.at[copies.take()])
            for source, target in ((self.wout, self.wout_v), (self.wup, self.wup_v), (self.wdown, self.wdown_v))
        ]

        def own(pair, part, which):
            both = self.qkv_v[:, self.lanes_of(pair, part)]
            return jnp.where(half_mask(which, both.shape), both, jnp.zeros_like(both))

        for load in small:
            load.wait()
        at = block * BLOCK
        single = self.segments[:, at + TILE : at + TILE + 1] == self.segments[:, at : at + 1]
        padding = self.padding[:, block * BLOCK : (block + 1) * BLOCK]
        tile_of = lax.broadcasted_iota(jnp.int32, (1, BLOCK), 1) // TILE
        shut = [
            jnp.where((padding == 1) & (single | (tile_of == tile)), 0.0, mask_fill) for tile in range(BLOCK // TILE)
        ]
        row_id = lax.broadcasted_iota(jnp.int32, (TILE, TILE), 0)
        diagonal = row_id == lax.broadcasted_iota(jnp.int32, (TILE, TILE), 1)

        def bias_rows(head, tile):
            at = BLOCK - tile * TILE
            rows = self.bias_v[head, :, at : at + BLOCK]
            masked = rows + shut[tile]
            own = slice(tile * TILE, (tile + 1) * TILE)
            parts = [masked[:, : own.start], jnp.where(diagonal, rows[:, own], masked[:, own]), masked[:, own.stop :]]
            return jnp.concatenate([part for part in parts if part.shape[1]], 1)

        def weigh(pair, which):
            head = 2 * pair + which
            k_own = own(pair, 1, which)
            for r in range(0, BLOCK, 2 * TILE):
                q_rows = self.qkv_v[r : r + 2 * TILE, self.lanes_of(pair, 0)] * jnp.asarray(score_scale, BF16)
                tiles = [bias_rows(head, tile) for tile in range(r // TILE, r // TILE + 2)]
                logits = dot_nt(q_rows, k_own) + jnp.concatenate(tiles, 0)
                raised = jnp.exp(logits - jnp.max(logits, -1, keepdims=True))
                share = pl.reciprocal(jnp.sum(raised, -1, keepdims=True), approx=True)
                self.weights_v[head, r : r + 2 * TILE, :] = (raised * share).astype(BF16)

        def head_pair(pair, carry):
            if built:
                load_bias(pair).wait()

            @pl.when(pair == 2)
            def _():
                for load in (*later_loads, *also):
                    load.start()

            weigh(pair, 0)
            context = dot_nn(self.weights_v[2 * pair], own(pair, 2, 0))
            weigh(pair, 1)
            context += dot_nn(self.weights_v[2 * pair + 1], own(pair, 2, 1))
            self.ctx_v[:, self.lanes_of(pair, 0)] = context.astype(BF16)
            if keep:
                heads = pl.ds(2 * pair, 2)
                pltpu.make_async_copy(self.weights_v.at[heads], self.weights.at[block, heads], weights_sem).start()
            return carry

        lax.fori_loop(0, self.pairs, head_pair, 0)
        if keep:
            copies.stores.append(pltpu.make_async_copy(self.weights_v, self.weights.at[block], weights_sem))
        copies.store(self.ctx_v, self.ctx.at[rows])
        load_out, load_up, load_down = later_loads
        load_out.wait()
        self.acc_v[...] = dot_nn(self.ctx_v[...], self.wout_v[...])
        for r in range(0, BLOCK, 64):
            tile = slice(r, r + 64)
            form, scale = normal_parts(self.acc_v[tile, :] + self.x_v[tile, :].astype(F32))
            normed = form * self.gain1[...] + self.shift1[...]
            self.form1_v[tile, :] = form
            self.scale1_v[tile, :] = scale
            self.acc_v[tile, :] = normed
            self.low1_v[tile, :] = normed.astype(BF16)
        copies.store(self.form1_v, self.form1.at[rows], keep)
        copies.store(self.scale1_v, self.scale1.at[rows], keep)
        copies.store(self.low1_v, self.low1.at[rows])
        load_up.wait()
        load_down.wait()
        act_sem = self.sems.at[copies.take()]
        slope_sem = self.sems.at[copies.take()]

        def two_chunks(i, carry):
            span = self.stage(i)
            active, grade = gelu_parts(dot_nn(self.low1_v[...], self.wup_v[:, span]))
            active = active.astype(BF16)
            self.act_v[:, span] = active
            self.slope_v[:, span] = grade.astype(BF16)
            self.acc_v[...] += dot_nn(active, self.wdown_v[span, :])
            pltpu.make_async_copy(self.act_v.at[:, span], self.act.at[rows, span], act_sem).start()
            if keep:
                pltpu.make_async_copy(self.slope_v.at[:, span], self.slope.at[rows, span], slope_sem).start()
            return carry

        lax.fori_loop(0, self.stages, two_chunks, 0)
        copies.stores.append(pltpu.make_async_copy(self.act_v, self.act.at[rows], act_sem))
        if keep:
            copies.stores.append(pltpu.make_async_copy(self.slope_v, self.slope.at[rows], slope_sem))
        for r in range(0, BLOCK, 64):
            tile = slice(r, r + 64)
            form, scale = normal_parts(self.acc_v[tile, :])
            self.form2_v[tile, :] = form
            self.scale2_v[tile, :] = scale
            self.out_v[tile, :] = (form * self.gain2[...] + self.shift2[...]).astype(BF16)
        copies.store(self.out_v, self.send, keep)
        copies.store(self.out_v, self.out.at[rows])
        copies.store(self.form2_v, self.form2.at[rows], keep)
        copies.store(self.scale2_v, self.scale2.at[rows], keep)


    def chunk_loads(self, i, rows):
        span = self.stage(i)
        return [
            pltpu.make_async_copy(source, target, self.sems.at[self.chunk_sems[k] + i])
            for k, (source, target) in enumerate(
                (
                    (self.wdown.at[0, span], self.wdown_v.at[span]),
                    (self.slope.at[rows, span], self.slope_v.at[:, span]),
                    (self.wup.at[0, :, span], self.wup_v.at[:, span]),
                )
            )
        ]

    def norm_sums(self, source, form_ref, sums_ref):
        gain_sum = jnp.zeros((1, self.width), F32)
        shift_sum = jnp.zeros((1, self.width), F32)
        for r in range(0, BLOCK, 64):
            grad_rows, form = source[r : r + 64, :].astype(F32), form_ref[r : r + 64, :]
            gain_sum += jnp.sum(grad_rows * form, 0, keepdims=True)
            shift_sum += jnp.sum(grad_rows, 0, keepdims=True)
        sums_ref[...] = jnp.zeros(sums_ref.shape, F32)
        sums_ref[0:1, :] = gain_sum
        sums_ref[1:2, :] = shift_sum

    def norm_back(self, block):
        for r in range(0, BLOCK, 64):
            tile = slice(r, r + 64)
            grad_rows = self.g_v[tile, :].astype(F32) * self.gain2[...]
            grad_outer = norm_backward(grad_rows, self.form2_v[tile, :], self.scale2_v[tile, :])
            self.acc_v[tile, :] = grad_outer
            self.outer_v[tile, :] = grad_outer.astype(BF16)
        self.copies.store(self.outer_v, self.outer_low.at[self.rows(block)])

    def norm_sums_2(self, block):
        self.norm_sums(self.g_v, self.form2_v, self.sums2_v)
        self.copies.store(self.sums2_v, self.sums2.at[block])

    def ffn_back(self, block, staged=False, middle_loads=()):
        copies = self.copies
        rows = self.rows(block)
        hidden_sem = self.sems.at[copies.take()]

        def two_chunks(i, carry):
            span = self.stage(i)
            if staged:
                load_down, load_slope, load_up = self.chunk_loads(i, rows)
                load_down.wait()
                load_slope.wait()

                @pl.when(i + 1 < self.stages)
                def _():
                    for load in self.chunk_loads(i + 1, rows)[:2]:
                        load.start()

            grad_active = dot_nt(self.outer_v[...], self.wdown_v[span, :])
            hidden = (grad_active * self.slope_v[:, span].astype(F32)).astype(BF16)
            self.slope_v[:, span] = hidden
            if staged:
                load_up.wait()

                @pl.when(i + 1 < self.stages)
                def _():
                    self.chunk_loads(i + 1, rows)[2].start()

            self.acc_v[...] += dot_nt(hidden, self.wup_v[:, span])
            pltpu.make_async_copy(self.slope_v.at[:, span], self.hidden_low.at[rows, span], hidden_sem).start()
            return carry

        lax.fori_loop(0, self.stages, two_chunks, 0)
        copies.stores.append(pltpu.make_async_copy(self.slope_v, self.hidden_low.at[rows], hidden_sem))
        for load in middle_loads:
            load.wait()
        self.norm_sums(self.acc_v, self.form1_v, self.sums1_v)
        for r in range(0, BLOCK, 64):
            tile = slice(r, r + 64)
            grad_residual = norm_backward(
                self.acc_v[tile, :] * self.gain1[...], self.form1_v[tile, :], self.scale1_v[tile, :]
            )
            self.acc_v[tile, :] = grad_residual
            self.residual_low_v[tile, :] = grad_residual.astype(BF16)
        copies.store(self.residual_low_v, self.residual_low.at[rows])
        copies.store(self.sums1_v, self.sums1.at[block])

    def attn_back(self, block, next_loads=None, load_in=()):
        copies = self.copies
        rows = self.rows(block)
        self.dctx_v[...] = dot_nt(self.residual_low_v[...], self.wout_v[...]).astype(BF16)
        self.fold_v[:, :, 0:TILE] = jnp.zeros((2, TILE, TILE), F32)

        def head_pair(pair, carry):
            def lanes_of(part):
                return self.lanes_of(pair, part)

            if next_loads is not None:
                next_loads(pair)
            q_pair, k_pair, v_pair = (self.qkv_v[:, lanes_of(part)] for part in range(3))
            grad_pair = self.dctx_v[:, lanes_of(0)]
            crossed = grad_pair.astype(F32) * self.ctx_v[:, lanes_of(0)].astype(F32)
            masks = [half_mask(which, k_pair.shape) for which in range(2)]

            def own(both, which):
                return jnp.where(masks[which], both, jnp.zeros_like(both))

            for which in range(2):
                self.square_v[which] = dot_nt(grad_pair, own(v_pair, which))
            q_grad = k_grad = v_grad = 0.0
            for which in range(2):
                head = 2 * pair + which
                delta = jnp.sum(own(crossed, which), -1, keepdims=True)
                for r in range(0, BLOCK, 64):
                    tile = slice(r, r + 64)
                    score_grad = (
                        self.weights_v[head, tile, :].astype(F32) * (self.square_v[which, tile, :] - delta[tile, :])
                    ).astype(BF16)
                    self.half_v[which, tile, :] = score_grad
                    at = BLOCK - r // TILE * TILE
                    wide = score_grad.astype(F32)
                    half = slice(r % TILE, r % TILE + 64)
                    if r < TILE:
                        self.fold_v[which, half, at : at + BLOCK] = wide
                    else:
                        self.fold_v[which, half, at : at + TILE] = wide[:, :TILE]
                        self.fold_v[which, half, at + TILE : at + BLOCK] += wide[:, TILE:]
                v_grad += dot_tn(self.weights_v[head], own(grad_pair, which))
                q_grad += dot_nn(self.half_v[which], own(k_pair, which))
                k_grad += dot_tn(self.half_v[which], own(q_pair, which))
                folded = self.fold_v[which]
                size = TILE // 2
                while size >= 8:
                    folded = folded[:size, :] + pltpu.roll(folded[size:, :], SPAN - size, 1)
                    size //= 2
                self.eighth_v[head] = folded
            self.qkv_v[:, lanes_of(0)] = (q_grad * score_scale).astype(BF16)
            self.qkv_v[:, lanes_of(1)] = (k_grad * score_scale).astype(BF16)
            self.qkv_v[:, lanes_of(2)] = v_grad.astype(BF16)
            return carry

        lax.fori_loop(0, self.pairs, head_pair, 0)
        copies.store(self.eighth_v, self.offsets.at[block])
        copies.store(self.qkv_v, self.projected.at[rows])
        for load in load_in:
            load.wait()
        self.grad_v[...] = (self.acc_v[...] + dot_nt(self.qkv_v[...], self.wqkv_v[...])).astype(BF16)
        copies.store(self.grad_v, self.send)
        copies.store(self.grad_v, self.input_grad.at[rows])


    def do_forward(self, block):
        self.forward(block, True, block > 0)

    def do_bias(self, block):
        self.build_bias(self.fetch("table", "buckets"))

    def do_both(self, block):
        load = pltpu.make_async_copy(self.out_grad.at[self.rows(block)], self.g_v, self.sems.at[self.copies.take()])
        self.forward(block, False, True, [load])
        load.wait()
        self.norm_back(block)
        self.ffn_back(block)
        self.norm_sums_2(block)
        self.attn_back(block)

    def do_back(self, block):
        rows = self.rows(block)
        loads = [
            self.copies.load(source, target)
            for source, target in (
                (self.received, self.g_v),
                (self.form2.at[rows], self.form2_v),
                (self.scale2.at[rows], self.scale2_v),
                (self.slope.at[rows], self.slope_v),
                (self.wdown.at[0], self.wdown_v),
                (self.wup.at[0], self.wup_v),
                (self.form1.at[rows], self.form1_v),
                (self.scale1.at[rows], self.scale1_v),
                (self.qkv.at[rows], self.qkv_v),
                (self.weights.at[block], self.weights_v),
                (self.ctx.at[rows], self.ctx_v),
                (self.wout.at[0], self.wout_v),
                (self.wqkv.at[0], self.wqkv_v),
            )
        ]
        for load in loads + self.fetch("gain1", "gain2"):
            load.wait()
        self.norm_back(block)
        self.ffn_back(block)
        self.norm_sums_2(block)
        self.attn_back(block)

    def do_ffn_back(self, block):
        rows = self.rows(block)
        loads = [
            self.copies.load(source, target)
            for source, target in (
                (self.received, self.g_v),
                (self.form2.at[rows], self.form2_v),
                (self.scale2.at[rows], self.scale2_v),
            )
        ]
        loads += self.fetch("gain1", "gain2")
        for load in self.chunk_loads(0, rows)[:2]:
            load.start()
        for load in loads:
            load.wait()
        self.chunk_loads(0, rows)[2].start()
        middle = [
            self.copies.load(self.form1.at[rows], self.form1_v),
            self.copies.load(self.scale1.at[rows], self.scale1_v),
        ]
        self.norm_back(block)
        self.norm_sums_2(block)
        self.ffn_back(block, True, middle)
        self.copies.store(self.acc_v, self.residual)

    def do_attn_back(self, block):
        rows = self.rows(block)
        loads = [
            self.copies.load(source, target)
            for source, target in ((self.residual_low.at[rows], self.residual_low_v), (self.wout.at[0], self.wout_v))
        ]
        first = self.copies.take(5 * self.pairs)

        def pair_loads(pair):
            heads = pl.ds(2 * pair, 2)
            sources = [(self.weights.at[block, heads], self.weights_v.at[heads])]
            for source, target, parts in ((self.qkv, self.qkv_v, 3), (self.ctx, self.ctx_v, 1)):
                for part in range(parts):
                    lanes = self.lanes_of(pair, part)
                    sources.append((source.at[rows, lanes], target.at[:, lanes]))
            return [
                pltpu.make_async_copy(source, target, self.sems.at[first + 5 * pair + k])
                for k, (source, target) in enumerate(sources)
            ]

        for pair in range(2):
            for load in pair_loads(pair):
                load.start()
        for load in loads:
            load.wait()
        last = [
            pltpu.make_async_copy(source, target, self.sems.at[self.copies.take()])
            for source, target in ((self.wqkv.at[0], self.wqkv_v), (self.residual, self.acc_v))
        ]

        def next_loads(pair):
            for load in pair_loads(pair):
                load.wait()

            @pl.when(pair + 2 < self.pairs)
            def _():
                for load in pair_loads(pair + 2):
                    load.start()

            @pl.when(pair == self.pairs - 3)
            def _():
                for load in last:
                    load.start()

        self.attn_back(block, next_loads, last)


def layer_kernel(work, phase_on, block, ins, outs, scratch, after_count, kept_count, *refs):
    refs_in, refs = refs[: len(ins)], refs[len(ins) + after_count + kept_count :]
    named = dict(zip(ins, refs_in)) | dict(zip(outs, refs)) | dict(zip(scratch, refs[len(outs) :]))

    @pl.when(named["phase"][0] == phase_on)
    def _():
        layer = Layer(named)
        getattr(layer, f"do_{work}")(block)
        layer.copies.finish()


def layer_step(work, phase_on, block, values, afters, kept, kept_shapes, scratch):
    specs = [SMEM] + [ANY] * (len(values) - 1)
    names = list(scratch)
    kept = list(kept) if kept is not None else []
    sent = jax.ShapeDtypeStruct((BLOCK, values[2].shape[1]), BF16)
    if work == "bias":
        names = ["values_v", "bias_v", "table_v", "buckets_v"]
    count = len(values) + len(afters)
    results = pl.pallas_call(
        functools.partial(
            layer_kernel, work, phase_on, block, INS, KEPT + ("send",), names + ["sems"], len(afters), len(kept)
        ),
        out_shape=list(kept_shapes) + [sent],
        in_specs=specs + [ANY] * (len(afters) + len(kept)),
        out_specs=[ANY] * (len(kept_shapes) + 1),
        scratch_shapes=[pltpu.VMEM(*scratch[name]) for name in names] + [pltpu.SemaphoreType.DMA((96,))],
        input_output_aliases={count + i: i for i in range(len(kept))},
        compiler_params=pltpu.CompilerParams(vmem_limit_bytes=VMEM_BYTES),
        name=f"{work}_{phase_on}_{block}",
    )(*values, *afters, *kept)
    return dict(zip(KEPT, results)), results[-1]


def pack_kernel(ways, buckets_ref, offsets_ref, sums1_ref, sums2_ref, *refs):
    out_ref, turn_v = refs[-3], refs[-1]
    row_of = lax.broadcasted_iota(jnp.int32, (8, SPAN), 0)
    lines = []
    for head in range(offsets_ref.shape[1]):
        eighth = offsets_ref[0, head] + offsets_ref[1, head]
        for size in (4, 2, 1):
            eighth = jnp.where((row_of & size) != 0, pltpu.roll(eighth, SPAN - size, 1), eighth)
        lines.append(jnp.sum(eighth, 0, keepdims=True))
    lines += [jnp.zeros((1, SPAN), F32)] * (NORM_LANE - len(lines))
    sums = pltpu.roll(jnp.concatenate(lines, 0), SPAN - 1, 1)
    span = buckets_ref.shape[1]
    buckets, depth = out_ref.shape[0] // 3, out_ref.shape[0] // ways
    share = buckets // ways
    bucket_ids = lax.broadcasted_iota(jnp.int32, (buckets, span), 0)
    hot = (bucket_ids == buckets_ref[...]).astype(F32)
    table = lax.dot_general(
        hot, sums[:, :span], (((1,), (1,)), ((), ())), precision=highest, preferred_element_type=F32
    ).astype(BF16)
    turn_v[...] = jnp.zeros(turn_v.shape, F32)
    for i, ref in enumerate((sums1_ref, sums2_ref)):
        at = NORM_LANE + 2 * i
        turn_v[at : at + 2, :] = ref[0, 0:2, :] + ref[1, 0:2, :]
    out_ref[...] = turn_v[...].T.astype(BF16)
    for i in range(ways):
        out_ref[i * depth : i * depth + share, 0:NORM_LANE] = table[i * share : (i + 1) * share, :]


def packed(ways, buckets, offset_buckets, kept, afters, through):
    width = kept["sums1"].shape[2]
    depth, share = width // ways, buckets // ways
    arrays = (offset_buckets, kept["offsets"], kept["sums1"], kept["sums2"])
    if depth % 16 == 0 and share % 16 == 0 and 3 * buckets == width:
        rows, through = pl.pallas_call(
            functools.partial(pack_kernel, ways),
            out_shape=[jax.ShapeDtypeStruct((width, LANES), BF16), jax.ShapeDtypeStruct(through.shape, through.dtype)],
            in_specs=[VMEM] * len(arrays) + [ANY] * (len(afters) + 1),
            out_specs=[VMEM, ANY],
            input_output_aliases={len(arrays) + len(afters): 1},
            scratch_shapes=[pltpu.VMEM((LANES, width), F32)],
            compiler_params=pltpu.CompilerParams(vmem_limit_bytes=SMALL_VMEM_BYTES),
            name="pack",
        )(*arrays, *afters, through)
        return rows.reshape(ways, depth, LANES), through
    eighths = jnp.sum(kept["offsets"], 0)
    lines = sum(jnp.roll(eighths[:, i, :], -i, 1) for i in range(8))[:, 1:]
    hot = (offset_buckets[0][None, :] == jnp.arange(buckets, dtype=jnp.int32)[:, None]).astype(F32)
    table = jnp.dot(hot, lines.T, precision=highest).reshape(ways, share, -1)
    table = jnp.pad(table, ((0, 0), (0, depth - share), (0, NORM_LANE - table.shape[2])))
    norms = jnp.concatenate([jnp.sum(kept[name], 0)[:2] for name in ("sums1", "sums2")], 0)
    norms = norms.T.reshape(ways, depth, 4)
    rows = jnp.concatenate([table, norms], 2)
    return jnp.pad(rows, ((0, 0), (0, 0), (0, LANES - rows.shape[2]))).astype(BF16), through


def halve_kernel(bits, counts, after_count, through_count, me_ref, *refs):
    outs = refs[2 * sum(counts) + after_count + through_count :]
    for i, count in enumerate(counts):
        pieces, refs = [refs[2 * k : 2 * k + 2] for k in range(count)], refs[2 * count :]
        send_ref, rest_ref = outs[2 * i : 2 * i + 2]
        mine = (me_ref[0] >> bits[i]) & 1

        def total(which):
            parts = [
                (kept[0, which, 0, 0] if len(kept.shape) == 6 else kept[0, which, 0]).astype(F32)
                + arrived[0, which, 0].astype(F32)
                for kept, arrived in pieces
            ]
            return jnp.concatenate(parts, 1)

        send_ref[0, 0] = total(1 - mine).astype(send_ref.dtype)
        rest_ref[0, 0] = total(mine)


def join_kernel(kept_ref, arrived_ref, out_ref, qkv_ref, table_ref, *refs):
    norm_refs, turn_v = refs[:-1], refs[-1]
    total = kept_ref[...] + arrived_ref[...].astype(F32)
    wide = out_ref.shape[1]
    out_ref[...] = total[:, :wide]
    qkv_ref[...] = total[:, wide : 4 * wide]
    small = total[:, 4 * wide :]
    turn_v[...] = jnp.zeros(turn_v.shape, F32)
    turn_v[: small.shape[0], :] = small
    turned = turn_v[...].T
    for head in range(table_ref.shape[0]):
        table_ref[head] = turned[head : head + 1, : table_ref.shape[2]]
    for i, ref in enumerate(norm_refs):
        ref[...] = turned[NORM_LANE + i : NORM_LANE + i + 1, : ref.shape[1]]


class Part:
    def __init__(self, whole):
        self.whole = whole
        self.sent = self.of_core(1 - (lax.axis_index(DP) & 1))
        self.arrived = swapped(self.sent, 0)

    def of_core(self, core):
        split = self.whole.reshape((self.whole.shape[0] // 2, 2) + self.whole.shape[1:])
        return lax.dynamic_index_in_dim(split, core, 1, keepdims=False)


def swapped(array, bit):
    count = lax.axis_size(DP)
    return lax.ppermute(array, DP, [(i, i ^ (1 << bit)) for i in range(count)])


class Share:
    def __init__(self, parts, order):
        self.parts = parts
        self.order = order[1:]
        self.left = sorted(order[1:])
        self.depth = parts[0].whole.shape[1]
        self.wide = sum(part.whole.shape[2] for part in parts)
        self.mine = None

    def swap(self, bit, theirs):
        self.left.remove(bit)
        self.sent = theirs
        self.arrived = swapped(theirs, bit)

    def total(self):
        if self.mine is not None:
            return self.mine + self.arrived.astype(F32)
        here = lax.axis_index(DP) & 1
        return jnp.concatenate(
            [part.of_core(here).astype(F32) + part.arrived.astype(F32) for part in self.parts], 2
        )

    def split_at(self):
        bit = self.order[0]
        axis = len(self.left) - 1 - self.left.index(bit)
        return bit, 2**axis, 2 ** (len(self.left) - 1 - axis)

    def halve(self):
        bit, above, below = self.split_at()
        self.order = self.order[1:]
        split = self.total().reshape(above, 2, below, self.depth, self.wide)
        here = (lax.axis_index(DP) >> bit) & 1
        theirs = lax.dynamic_index_in_dim(split, 1 - here, 1, keepdims=False).astype(BF16)
        mine = lax.dynamic_index_in_dim(split, here, 1, keepdims=False)
        self.mine = mine.reshape(-1, self.depth, self.wide)
        self.swap(bit, theirs.reshape(-1, self.depth, self.wide))


def halve_all(me, shares, afters=(), through=()):
    if any(share.depth % 16 for share in shares):
        for share in shares:
            share.halve()
        return through
    ins, in_specs, outs, out_specs, bits, counts = [], [], [], [], [], []
    for share in shares:
        bit, above, below = share.split_at()
        bits.append(bit)

        def halves(wide, b=below):
            return pl.BlockSpec((1, 2, 1, share.depth, wide), lambda i, me: (i // b, 0, i % b, 0, 0))

        if share.mine is None:
            counts.append(len(share.parts))
            for part in share.parts:
                wide = part.whole.shape[2]
                ins.append(part.whole.reshape(above, 2, below, 2, share.depth, wide))
                in_specs.append(
                    pl.BlockSpec(
                        (1, 2, 1, 1, share.depth, wide),
                        lambda i, me, b=below: (i // b, 0, i % b, me[0] & 1, 0, 0),
                    )
                )
                ins.append(part.arrived.reshape(above, 2, below, share.depth, wide))
                in_specs.append(halves(wide))
        else:
            counts.append(1)
            for array in (share.mine, share.arrived):
                ins.append(array.reshape(above, 2, below, share.depth, share.wide))
                in_specs.append(halves(share.wide))
        outs += [
            jax.ShapeDtypeStruct((above, below, share.depth, share.wide), kind) for kind in (BF16, F32)
        ]
        out_specs += [
            pl.BlockSpec((1, 1, share.depth, share.wide), lambda i, me, b=below: (i // b, i % b, 0, 0))
        ] * 2
        steps = above * below
    results = pl.pallas_call(
        functools.partial(halve_kernel, tuple(bits), tuple(counts), len(afters), len(through)),
        grid_spec=pltpu.PrefetchScalarGridSpec(
            num_scalar_prefetch=1,
            grid=(steps,),
            in_specs=in_specs + [ANY] * (len(afters) + len(through)),
            out_specs=out_specs + [ANY] * len(through),
        ),
        out_shape=outs + [jax.ShapeDtypeStruct(array.shape, array.dtype) for array in through],
        input_output_aliases={
            1 + len(ins) + len(afters) + i: len(outs) + i for i in range(len(through))
        },
        compiler_params=pltpu.CompilerParams(vmem_limit_bytes=SMALL_VMEM_BYTES),
        name="halve",
    )(me, *ins, *afters, *through)
    for i, share in enumerate(shares):
        share.order = share.order[1:]
        share.mine = results[2 * i + 1].reshape(-1, share.depth, share.wide)
        share.swap(bits[i], results[2 * i].reshape(-1, share.depth, share.wide))
    return results[len(outs) :]


def joined(share, width, table_shape):
    shapes = [(share.depth, width), (share.depth, 3 * width), table_shape] + [(1, share.depth)] * 4
    return pl.pallas_call(
        join_kernel,
        out_shape=[jax.ShapeDtypeStruct(dims, F32) for dims in shapes],
        in_specs=[VMEM] * 2,
        out_specs=[VMEM] * len(shapes),
        scratch_shapes=[pltpu.VMEM((LANES, LANES), F32)],
        compiler_params=pltpu.CompilerParams(vmem_limit_bytes=SMALL_VMEM_BYTES),
        name="join",
    )(share.mine[0], share.arrived[0])


def passed_along(x, axis, by):
    length = lax.axis_size(axis)
    pairs = [(i, i + by) for i in range(length) if 0 <= i + by < length]
    return lax.ppermute(x, axis, pairs)


def shards(
    hidden_in, out_grad, qkv_weight, out_weight, rel_table, norm1_gain, norm1_bias,
    up_weight, down_weight, norm2_gain, norm2_bias, seg_ids, pad_mask, rel_buckets,
):
    phase = lax.axis_index(PHASE).astype(jnp.int32).reshape(1)
    ways = lax.axis_size(DP)
    slots, width = hidden_in.shape
    inner = up_weight.shape[2]
    buckets, heads = rel_table.shape[1:]

    def shape(dims, kind):
        return jax.ShapeDtypeStruct(dims, kind)

    rows_of = {
        "xin": (width, BF16), "qkv": (3 * width, BF16), "ctx": (width, BF16), "form1": (width, F32),
        "scale1": (1, F32), "low1": (width, BF16), "slope": (inner, BF16), "act": (inner, BF16),
        "form2": (width, F32), "scale2": (1, F32), "out": (width, BF16),
        "outer_low": (width, BF16), "hidden_low": (inner, BF16), "residual_low": (width, BF16),
        "projected": (3 * width, BF16), "input_grad": (width, BF16),
    }
    kept_shapes = [
        shape((slots, rows_of[name][0]), rows_of[name][1])
        if name in rows_of
        else {
            "weights": shape((MICRO, heads, BLOCK, BLOCK), BF16),
            "sums1": shape((MICRO, 8, width), F32),
            "sums2": shape((MICRO, 8, width), F32),
            "residual": shape((BLOCK, width), F32),
            "offsets": shape((MICRO, heads, 8, SPAN), F32),
            "bias": shape((heads, TILE, SPAN), F32),
        }[name]
        for name in KEPT
    ]
    small = {
        "segments_v": ((1, slots), jnp.int32), "padding_v": ((1, slots), jnp.int32),
        "buckets_v": ((1, rel_buckets.shape[0]), jnp.int32), "table_v": ((heads, 1, buckets), F32),
        "gain1_v": ((1, width), F32), "shift1_v": ((1, width), F32), "gain2_v": ((1, width), F32),
        "shift2_v": ((1, width), F32),
    }
    in_forward = ("qkv", "ctx", "form1", "scale1", "low1", "slope", "act", "form2", "scale2", "out")
    scratch = {f"{name}_v": ((BLOCK, rows_of[name][0]), rows_of[name][1]) for name in in_forward}
    scratch |= small
    scratch |= {
        name: ((BLOCK, width), BF16) for name in ("x_v", "g_v", "outer_v", "residual_low_v", "dctx_v", "grad_v")
    }
    scratch |= {
        "weights_v": ((heads, BLOCK, BLOCK), BF16), "acc_v": ((BLOCK, width), F32), "square_v": ((2, BLOCK, BLOCK), F32),
        "values_v": ((heads, SPAN), F32), "bias_v": ((heads, TILE, SPAN), F32), "sums1_v": ((8, width), F32), "sums2_v": ((8, width), F32),
        "wqkv_v": ((width, 3 * width), BF16), "wout_v": ((width, width), BF16), "wup_v": ((width, inner), BF16),
        "wdown_v": ((inner, width), BF16), "fold_v": ((2, TILE, SPAN), F32), "eighth_v": ((heads, 8, SPAN), F32),
        "half_v": ((2, BLOCK, BLOCK), BF16),
    }

    def step(work, phase_on, block, received, kept, afters=()):
        values = (
            phase, seg_ids[None, :], hidden_in, received, out_grad, rel_table.transpose(2, 0, 1), pad_mask[None, :], rel_buckets[None, :],
            norm1_gain, norm1_bias, norm2_gain, norm2_bias, qkv_weight, out_weight, up_weight, down_weight,
        )
        in_place = None if kept is None else [kept[name] for name in KEPT]
        return layer_step(work, phase_on, block, values, list(afters), in_place, kept_shapes, scratch)

    kept, sent = step("forward", 0, 0, hidden_in, None)
    first = passed_along(sent, PHASE, 1)
    kept, _ = step("bias", 1, 0, hidden_in, kept)
    kept, sent = step("forward", 0, 1, hidden_in, kept)
    second = passed_along(sent, PHASE, 1)
    kept, sent = step("both", 1, 0, first, kept)
    first_back = passed_along(sent, PHASE, -1)
    kept, sent = step("both", 1, 1, second, kept)
    second_back = passed_along(sent, PHASE, -1)
    kept, _ = step("back", 0, 0, first_back, kept)
    def early(left, right):
        return dot_tn(left[:BLOCK], right[:BLOCK]).astype(BF16)

    up_base = early(kept["low1"], kept["hidden_low"])
    qkv_base = early(kept["xin"], kept["projected"])
    kept, _ = step("ffn_back", 0, 1, second_back, kept, [up_base, qkv_base])

    bits = ways.bit_length() - 1
    near_first = list(range(bits))
    far_first = [0] + list(range(2, bits)) + [1] if bits > 1 else near_first
    me = lax.axis_index(DP).astype(jnp.int32).reshape(1)

    def weight_grad(left, right, base=None):
        if base is None:
            product = dot_tn(left, right)
        else:
            product = dot_tn(left[BLOCK:], right[BLOCK:]) + base.astype(F32)
        product = product.astype(BF16)
        return product.reshape(ways, product.shape[0] // ways, product.shape[1])

    down = Share([Part(weight_grad(kept["act"], kept["outer_low"]))], near_first)
    up = Share([Part(weight_grad(kept["low1"], kept["hidden_low"], up_base))], far_first)
    out_part = Part(weight_grad(kept["ctx"], kept["residual_low"]))
    halve_all(me, [down])
    halve_all(me, [up])
    kept, _ = step("attn_back", 0, 1, hidden_in, kept, [down.sent, up.sent])
    far_part = Part(weight_grad(kept["xin"], kept["projected"][:, width:], qkv_base[:, width:]))
    small, slots_in = packed(ways, buckets, rel_buckets[None, :], kept, [far_part.sent], kept["xin"])
    small_part = Part(small)
    near_part = Part(weight_grad(slots_in, kept["projected"][:, :width], qkv_base[:, :width]))
    halve_all(me, [up, down], [far_part.sent, near_part.sent])
    last = Share([out_part, near_part, far_part, small_part], near_first)
    halve_all(me, [last], [down.sent, up.sent])
    halve_all(me, [last])
    halve_all(me, [up, down], [last.sent])
    while down.order:
        halve_all(me, [up, down])
    while last.order:
        halve_all(me, [last])
    down_share = down.total()[0]
    up_share = up.total()[0]
    out_share, qkv_share, table_share, *norm_shares = joined(last, width, (heads, 1, buckets // ways))
    return (
        kept["out"][None],
        kept["input_grad"][None],
        qkv_share[None],
        out_share[None],
        table_share.transpose(1, 2, 0),
        norm_shares[0],
        norm_shares[1],
        up_share[None],
        down_share[None],
        norm_shares[2],
        norm_shares[3],
    )


def solution(mesh):
    return jax.shard_map(
        shards,
        mesh=mesh,
        in_specs=(
            P(DP, None),
            P(DP, None),
            P(PHASE, None, None),
            P(PHASE, None, None),
            P(PHASE, None, None),
            P(PHASE, None),
            P(PHASE, None),
            P(PHASE, None, None),
            P(PHASE, None, None),
            P(PHASE, None),
            P(PHASE, None),
            P(DP),
            P(DP),
            P(),
        ),
        out_specs=(
            P(PHASE, DP, None),
            P(PHASE, DP, None),
            P(PHASE, DP, None),
            P(PHASE, DP, None),
            P(PHASE, DP, None),
            P(PHASE, DP),
            P(PHASE, DP),
            P(PHASE, DP, None),
            P(PHASE, DP, None),
            P(PHASE, DP),
            P(PHASE, DP),
        ),
        check_vma=False,
    )
```
